32 devices in a mesh: ctx: 8 (over z, y), head: 4 (over x, core).
Axes of the slice: x: 2, y: 2, z: 4, core: 2. Of those that a mesh axis runs over, the one named last changes fastest.
Arguments:
- queries: bfloat16 [2048, 2048], P('ctx', 'head'), may hold values from -32 to 32
- keys: bfloat16 [2048, 1024], P('ctx', 'head'), may hold values from -32 to 32
- values: bfloat16 [2048, 1024], P('ctx', 'head'), may hold values from -6 to 6
- doc_ids: int32 [16], replicated, may hold values from 0 to 2, as said below
- out_weight: bfloat16 [2048, 5376], P('head'), may hold values from -1 to 1
Outputs:
- projected: bfloat16 [2048, 5376], P(('ctx', 'head'))
The draws below stay inside these ranges and needn't reach their ends.
Inputs may be any that keep to these rules, and one draw needn't show every extreme that they name: doc_ids is non-decreasing along the sequence and starts at 0; the first document spans exactly 12 blocks, every other one 1 or more blocks.
All inputs are finite; a program needn't handle non-finite values.
Results may differ from the reference program's by a relative error of at most 0.015.
Values may be sent and summed in bfloat16 or wider, within the bound.
No kernel may reach another device: no remote copies, remote signals or barrier semaphores. Data moves between devices by JAX's collectives and lax.ppermute only.
A program may use at most 64 MiB of HBM per device.

```python
import math
import jax
import jax.numpy as jnp
from jax import lax

D = 5376
QUERY_HEADS = 16
KEY_VALUE_HEADS = 8
HEAD_SIZE = 128
BLOCK = 128
PACKED_TOKENS = 2048
NBLK = 16
DOCS = 3
LONGEST = 12


def draw_queries(key, part):
    key = jax.random.fold_in(key, 1)
    query_group = QUERY_HEADS // KEY_VALUE_HEADS
    main_portion = jax.random.normal(key, (PACKED_TOKENS, KEY_VALUE_HEADS, query_group, HEAD_SIZE), jnp.float32)
    return main_portion.reshape(PACKED_TOKENS, QUERY_HEADS * HEAD_SIZE).astype(jnp.bfloat16)


def draw_keys(key, part):
    key = jax.random.fold_in(key, 2)
    main_portion = jax.random.normal(key, (PACKED_TOKENS, KEY_VALUE_HEADS, HEAD_SIZE), jnp.float32)
    return main_portion.reshape(PACKED_TOKENS, KEY_VALUE_HEADS * HEAD_SIZE).astype(jnp.bfloat16)


def draw_doc_ids(key, part):
    key = jax.random.fold_in(key, 3)
    candidates = NBLK - LONGEST - 1
    order = jax.random.permutation(key, candidates).astype(jnp.int32)
    chosen = order[:DOCS - 2] + LONGEST + 1
    blocks = jnp.arange(NBLK, dtype=jnp.int32)
    after_first = (blocks >= LONGEST).astype(jnp.int32)
    past_cuts = jnp.sum((blocks[:, None] >= chosen[None, :]).astype(jnp.int32), axis=1)
    return (after_first + past_cuts).astype(jnp.int32)


def shard_levels(rng, shape, pieces, smallest, largest):
    level, own = 1.0, jax.random.fold_in(rng, 6)
    for position, blocks in pieces:
        draws = jnp.exp(jax.random.uniform(jax.random.fold_in(own, position), (blocks,), jnp.float32, smallest / len(pieces), largest / len(pieces)))
        level = level * jnp.repeat(draws, shape[position] // blocks).reshape([-1 if axis == position else 1 for axis in range(len(shape))])
    return level


def normal_values(rng, extent, deviation, reach, shards=(), kind=jnp.bfloat16):
    values = jax.random.normal(rng, extent, jnp.float32) * deviation
    if len(shards) > 0:
        values = shard_levels(rng, extent, shards, -0.22, 0.18) * values
    return jnp.clip(values, min=-reach, max=reach).astype(kind)


def setup_inputs(seed: int = 0) -> dict:
    seeds = jax.random.split(jax.random.key(seed), 6)
    queries = draw_queries(jax.random.fold_in(seeds[5], 71), 0)
    keys = draw_keys(jax.random.fold_in(seeds[5], 71), 0)
    values = normal_values(seeds[2], (PACKED_TOKENS, KEY_VALUE_HEADS * HEAD_SIZE), 1.0, 6.0, ((0, 8), (1, 4)))
    doc_ids = draw_doc_ids(jax.random.fold_in(seeds[5], 71), 0)
    out_weight = normal_values(seeds[4], (QUERY_HEADS * HEAD_SIZE, D), (QUERY_HEADS * HEAD_SIZE // 64) ** -0.5, 1.0, ((0, 4),))
    return dict(queries=queries, keys=keys, values=values, doc_ids=doc_ids, out_weight=out_weight)


def reference(queries, keys, values, doc_ids, out_weight):
    query_group = QUERY_HEADS // KEY_VALUE_HEADS
    scale = 168.0 ** -0.5
    tok_doc = jnp.repeat(doc_ids, BLOCK)
    key_pos = jnp.arange(PACKED_TOKENS, dtype=jnp.int32)
    key_head_rows = keys.reshape(PACKED_TOKENS, KEY_VALUE_HEADS, HEAD_SIZE).astype(jnp.float32)
    value_head_rows = values.reshape(PACKED_TOKENS, KEY_VALUE_HEADS, HEAD_SIZE).astype(jnp.float32)
    token_rows = math.gcd(PACKED_TOKENS, 512)

    def one_block(start):
        mask_block = lax.dynamic_slice_in_dim(queries, start, token_rows, 0)
        mask_block = mask_block.reshape(token_rows, KEY_VALUE_HEADS, query_group, HEAD_SIZE).astype(jnp.float32)
        scores = jnp.einsum("qkgd,skd->kgqs", mask_block, key_head_rows) * scale
        q_pos = start + jnp.arange(token_rows, dtype=jnp.int32)
        q_doc = lax.dynamic_slice_in_dim(tok_doc, start, token_rows, 0)
        allowed = (q_doc[:, None] == tok_doc[None, :]) & (q_pos[:, None] >= key_pos[None, :])
        scores = jnp.where(allowed, scores, -1e30)
        peak = jnp.max(scores, axis=-1, keepdims=True)
        weights = jnp.exp(scores - peak)
        totals = jnp.sum(weights, axis=-1)
        rounded = weights.astype(jnp.bfloat16).astype(jnp.float32)
        summed = jnp.einsum("kgqs,skd->qkgd", rounded, value_head_rows)
        result = summed / jnp.transpose(totals, (2, 0, 1))[..., None]
        return result.reshape(token_rows, QUERY_HEADS * HEAD_SIZE).astype(jnp.bfloat16)

    starts = jnp.arange(PACKED_TOKENS // token_rows, dtype=jnp.int32) * token_rows
    attended = lax.map(one_block, starts).reshape(PACKED_TOKENS, QUERY_HEADS * HEAD_SIZE)
    return jnp.dot(attended, out_weight, preferred_element_type=jnp.float32).astype(jnp.bfloat16)
```

```python
import functools

import jax
import jax.numpy as jnp
from jax import lax
from jax.experimental import pallas as pl
from jax.experimental.pallas import tpu as pltpu
from jax.sharding import PartitionSpec as P

HEAD_SIZE = 128
BLOCK = 128
SCALE = 168.0 ** (-0.5)
LOG2E = 1.4426950408889634
NEG = -1e30


def hop(block, axis, pairs):
    return lax.ppermute(block, axis, pairs)


def gather_chunks(own, n_ctx):
    first = n_ctx * 3 // 4
    by_two = hop(own, "ctx", [(i, i + 2) for i in range(first - 2)])
    by_four = hop(own, "ctx", [(i, i + 4) for i in range(first - 4)])
    beside = hop(own, "ctx", [(i, i + 1) for i in range(0, n_ctx, 2)])
    swap_two = hop(by_two, "ctx", [(i, i ^ 1) for i in range(2, first)])
    swap_four = hop(by_four, "ctx", [(i, i ^ 1) for i in range(4, first)])
    return [beside, by_two, swap_two, by_four, swap_four]


def describe(position, place, doc_ids, n_ctx):
    first = n_ctx * 3 // 4
    in_first = position < first
    chunks = [
        (position, position >= 0),
        (position ^ 1, position % 2 == 1),
        (position - 2, in_first & (position >= 2)),
        ((position - 2) ^ 1, in_first & (position >= 2)),
        (position - 4, in_first & (position >= 4)),
        ((position - 4) ^ 1, in_first & (position >= 4)),
    ]
    numbers = [position, place]
    for source, there in chunks:
        numbers += [jnp.where(there, source, 0), there.astype(jnp.int32)]
    return jnp.concatenate([jnp.stack(numbers), doc_ids])


def attention_kernel(info, queries, *refs):
    chunks, (keep, send, attended) = refs[:-3], refs[-3:]
    position, place = info[0], info[1]
    docs = 2 + 2 * len(chunks)
    n_query, width = queries.shape
    kv_width = chunks[0].shape[1] // 2
    kv_heads = kv_width // HEAD_SIZE
    group = width // kv_width
    q_blocks = n_query // BLOCK
    factor = SCALE * LOG2E
    row = lax.broadcasted_iota(jnp.int32, (BLOCK, BLOCK), 0)
    col = lax.broadcasted_iota(jnp.int32, (BLOCK, BLOCK), 1)
    triangle = jnp.where(row >= col, 0.0, NEG)
    triangle = jnp.concatenate([triangle] * group, axis=0)
    for a in range(q_blocks):
        rows = slice(a * BLOCK, (a + 1) * BLOCK)
        doc = info[docs + position * q_blocks + a]
        for h in range(kv_heads):
            heads = [slice((h * group + g) * HEAD_SIZE, (h * group + g + 1) * HEAD_SIZE) for g in range(group)]
            q = jnp.concatenate([queries[rows, head] for head in heads], axis=0)
            scores = []
            for c, chunk in enumerate(chunks):
                count = (a + 1) * BLOCK if c == 0 else n_query
                k = chunk[:count, h * HEAD_SIZE : (h + 1) * HEAD_SIZE]
                s = lax.dot_general(q, k, (((1,), (1,)), ((), ())), preferred_element_type=jnp.float32)
                source, there = info[2 + 2 * c], info[3 + 2 * c]
                for b in range(count // BLOCK):
                    part = s[:, b * BLOCK : (b + 1) * BLOCK]
                    if c == 0 and b == a:
                        part = part + triangle
                    else:
                        seen = (info[docs + source * q_blocks + b] == doc) & (there == 1)
                        part = part + jnp.where(seen, 0.0, NEG)
                    scores.append(part)
            peak = functools.reduce(jnp.maximum, scores)
            peak = jnp.max(peak, axis=1, keepdims=True) * factor
            total = added = None
            for c, chunk in enumerate(chunks):
                count = (a + 1) * BLOCK if c == 0 else n_query
                parts = []
                for b in range(count // BLOCK):
                    w = jnp.exp2(scores.pop(0) * factor - peak)
                    total = w if total is None else total + w
                    parts.append(w.astype(jnp.bfloat16))
                w = jnp.concatenate(parts, axis=1) if len(parts) > 1 else parts[0]
                v = chunk[:count, kv_width + h * HEAD_SIZE : kv_width + (h + 1) * HEAD_SIZE]
                term = jnp.dot(w, v, preferred_element_type=jnp.float32)
                added = term if added is None else added + term
            total = jnp.sum(total, axis=1, keepdims=True)
            result = (added / total).astype(jnp.bfloat16)
            for g, head in enumerate(heads):
                attended[rows, head] = result[g * BLOCK : (g + 1) * BLOCK]
    part_out(place, attended, keep, send)


def part_out(place, attended, keep, send):
    share = keep.shape[0] // 2
    for i, chip in enumerate((place ^ 2, place)):
        at = slice(i * share, (i + 1) * share)
        keep[at, :] = attended[pl.ds(pl.multiple_of(chip * share, share), share), :]
        send[at, :] = attended[pl.ds(pl.multiple_of((chip ^ 1) * share, share), share), :]


def attention(info, queries, chunks):
    n_query, width = queries.shape
    vmem = pl.BlockSpec(memory_space=pltpu.VMEM)
    keys = len(chunks) * chunks[0].shape[0]
    half = jax.ShapeDtypeStruct((n_query // 2, width), jnp.bfloat16)
    return pl.pallas_call(
        attention_kernel,
        out_shape=(half, half),
        in_specs=[pl.BlockSpec(memory_space=pltpu.SMEM)] + [vmem] * (1 + len(chunks)),
        out_specs=(vmem, vmem),
        scratch_shapes=[pltpu.VMEM(queries.shape, jnp.bfloat16)],
        compiler_params=pltpu.CompilerParams(vmem_limit_bytes=32 * 1024 * 1024),
        cost_estimate=pl.CostEstimate(
            flops=4 * n_query * width * keys,
            bytes_accessed=2 * keys * width,
            transcendentals=n_query * keys * width // HEAD_SIZE,
        ),
        name="attention",
    )(info, queries, *chunks)


def project_kernel(left, right, weight_left, weight_right, out):
    total = jnp.dot(left[...], weight_left[...], preferred_element_type=jnp.float32)
    total += jnp.dot(right[...], weight_right[...], preferred_element_type=jnp.float32)
    out[...] = total.astype(out.dtype)


def project(left, right, weight_left, weight_right, half, start, count, tile, dtype):
    rows, depth = left.shape[0] // 2, left.shape[1]
    flat = pl.BlockSpec((rows, depth), lambda j: (half, 0))
    tall = pl.BlockSpec((depth, tile), lambda j: (0, start + j))
    return pl.pallas_call(
        project_kernel,
        grid=(count,),
        out_shape=jax.ShapeDtypeStruct((rows, count * tile), dtype),
        in_specs=[flat, flat, tall, tall],
        out_specs=pl.BlockSpec((rows, tile), lambda j: (0, j)),
        compiler_params=pltpu.CompilerParams(vmem_limit_bytes=16 * 1024 * 1024),
        cost_estimate=pl.CostEstimate(
            flops=4 * rows * depth * count * tile,
            bytes_accessed=4 * depth * count * tile,
            transcendentals=0,
        ),
        name="project",
    )(left, right, weight_left, weight_right)


def combine_kernel(mine, *refs):
    parts, out = refs[:-1], refs[-1]
    at = 0
    for part in parts:
        width = part.shape[1]
        total = mine[:, at : at + width].astype(jnp.float32) + part[...].astype(jnp.float32)
        out[:, at : at + width] = total.astype(out.dtype)
        at += width


def combine(mine, parts):
    vmem = pl.BlockSpec(memory_space=pltpu.VMEM)
    return pl.pallas_call(
        combine_kernel,
        out_shape=jax.ShapeDtypeStruct(mine.shape, jnp.bfloat16),
        in_specs=[vmem] * (1 + len(parts)),
        out_specs=vmem,
        compiler_params=pltpu.CompilerParams(vmem_limit_bytes=16 * 1024 * 1024),
        name="combine",
    )(mine, *parts)


def from_behind(block, axis, distance):
    devices = range(lax.axis_size(axis))
    route = [(i - distance, i) for i in devices if i - distance in devices]
    return lax.ppermute(block, axis, route)


def token_docs(doc_ids, start, count):
    blocks = (start + jnp.arange(count, dtype=jnp.int32)) // BLOCK
    table = blocks[:, None] == jnp.arange(doc_ids.shape[0], dtype=jnp.int32)[None, :]
    return jnp.sum(jnp.where(table, doc_ids[None, :], 0), axis=1)


def attend(carry, queries, q_docs, q_start, k_piece, v_piece, k_docs, k_start):
    peak, totals, accum = carry
    n_query = queries.shape[0]
    n_key = k_piece.shape[0]
    kv_heads = k_piece.shape[1] // HEAD_SIZE
    query_group = queries.shape[1] // k_piece.shape[1]
    q_heads = queries.reshape(n_query, kv_heads, query_group, HEAD_SIZE)
    k_heads = k_piece.reshape(n_key, kv_heads, HEAD_SIZE)
    v_heads = v_piece.reshape(n_key, kv_heads, HEAD_SIZE)
    scores = (
        jnp.einsum("qkgd,skd->kgqs", q_heads, k_heads, preferred_element_type=jnp.float32) * SCALE
    )
    q_pos = q_start + jnp.arange(n_query, dtype=jnp.int32)
    k_pos = k_start + jnp.arange(n_key, dtype=jnp.int32)
    allowed = (q_docs[:, None] == k_docs[None, :]) & (q_pos[:, None] >= k_pos[None, :])
    scores = jnp.where(allowed, scores, NEG)
    new_peak = jnp.maximum(peak, jnp.max(scores, axis=-1))
    shrink = jnp.exp(peak - new_peak)
    weights = jnp.exp(scores - new_peak[..., None])
    totals = totals * shrink + jnp.sum(weights, axis=-1)
    rounded = weights.astype(jnp.bfloat16)
    added = jnp.einsum("kgqs,skd->kgqd", rounded, v_heads, preferred_element_type=jnp.float32)
    accum = accum * shrink[..., None] + added
    return (new_peak, totals, accum)


def absorb_block(carry, queries, q_docs, q_start, k_piece, v_piece, k_start, doc_ids, flag):
    n_key = k_piece.shape[0]
    k_docs = token_docs(doc_ids, k_start, n_key)
    fresh = attend(carry, queries, q_docs, q_start, k_piece, v_piece, k_docs, k_start)
    return jax.tree.map(lambda new, old: jnp.where(flag, new, old), fresh, carry)


def ring_attention(queries, keys, values, doc_ids, n_ctx, position):
    n_query = queries.shape[0]
    q_start = position * n_query
    q_docs = token_docs(doc_ids, q_start, n_query)
    kv_heads = keys.shape[1] // HEAD_SIZE
    query_group = queries.shape[1] // keys.shape[1]
    carry = (
        jnp.full((kv_heads, query_group, n_query), NEG, jnp.float32),
        jnp.zeros((kv_heads, query_group, n_query), jnp.float32),
        jnp.zeros((kv_heads, query_group, n_query, HEAD_SIZE), jnp.float32),
    )
    always = jnp.array(True)
    carry = absorb_block(carry, queries, q_docs, q_start, keys, values, q_start, doc_ids, always)

    def turn_one(step, state):
        inner_state, moving = state
        moving = from_behind(moving, "ctx", 1)
        start = ((position - step) % n_ctx) * n_query
        inner_state = absorb_block(
            inner_state, queries, q_docs, q_start, moving[0], moving[1], start, doc_ids, always
        )
        return (inner_state, moving)

    _, totals, accum = lax.fori_loop(1, n_ctx, turn_one, (carry, jnp.stack((keys, values))))[0]
    result = accum / totals[..., None]
    return jnp.transpose(result, (2, 0, 1, 3)).reshape(queries.shape).astype(jnp.bfloat16)


def part_rows(attended, place):
    share = attended.shape[0] // 4
    rows = [lax.dynamic_slice_in_dim(attended, (place ^ flip) * share, share, 0) for flip in (2, 0, 3, 1)]
    return jnp.concatenate(rows[:2], axis=0), jnp.concatenate(rows[2:], axis=0)


def per_device(queries, keys, values, doc_ids, out_weight):
    n_ctx = lax.axis_size("ctx")
    heads = lax.axis_size("head")
    position = lax.axis_index("ctx")
    place = lax.axis_index("head")
    other_core = [(i, i ^ 1) for i in range(heads)]
    other_chip = [(i, i ^ 2) for i in range(heads)]

    if n_ctx == 8:
        own = jnp.concatenate([keys, values], axis=1)
        chunks = [own] + gather_chunks(own, n_ctx)
        info = describe(position, place, doc_ids, n_ctx)
        keep, send = attention(info, queries, chunks)
    else:
        attended = ring_attention(queries, keys, values, doc_ids, n_ctx, position)
        keep, send = part_rows(attended, place)
    other_weight = hop(out_weight, "head", other_core)
    theirs = hop(send, "head", other_core)

    columns = out_weight.shape[1]
    tile = next(t for t in (768, 512, 256, 128, columns) if columns % t == 0)
    tiles = columns // tile
    weights = (out_weight, other_weight)
    cuts = [0, tiles * 3 // 7, tiles]
    parts = []
    for start, end in zip(cuts[:-1], cuts[1:]):
        far = project(keep, theirs, *weights, 0, start, end - start, tile, jnp.bfloat16)
        parts.append(hop(far, "head", other_chip))
    near = project(keep, theirs, *weights, 1, 0, tiles, tile, jnp.float32)
    return combine(near, parts)


def solution(mesh):
    placed = (P("ctx", "head"), P("ctx", "head"), P("ctx", "head"), P(), P("head", None))
    return jax.shard_map(
        per_device, mesh=mesh, in_specs=placed, out_specs=P(("ctx", "head"), None), check_vma=False
    )
```

```python
import functools

import jax
import jax.numpy as jnp
from jax import lax
from jax.experimental import pallas as pl
from jax.experimental.pallas import tpu as pltpu
from jax.sharding import PartitionSpec as P

HEAD_SIZE = 128
BLOCK = 128
SCALE = 168.0 ** (-0.5)
LOG2E = 1.4426950408889634
NEG = -1e30
VMEM = pl.BlockSpec(memory_space=pltpu.VMEM)
SMEM = pl.BlockSpec(memory_space=pltpu.SMEM)
HBM = pl.BlockSpec(memory_space=pltpu.HBM)
LIMIT = pltpu.CompilerParams(vmem_limit_bytes=32 * 1024 * 1024)


def hop(block, axis, pairs):
    return lax.ppermute(block, axis, pairs)


def describe(position, place, doc_ids, n_ctx):
    first = n_ctx * 3 // 4
    in_first = position < first
    chunks = [
        (position, position >= 0),
        (position ^ 1, position % 2 == 1),
        (position - 2, in_first & (position >= 2)),
        (position - 4, in_first & (position >= 4)),
        ((position - 2) ^ 1, in_first & (position >= 2)),
        ((position - 4) ^ 1, in_first & (position >= 4)),
    ]
    numbers = [position, place]
    for source, there in chunks:
        numbers += [jnp.where(there, source, 0), there.astype(jnp.int32)]
    return jnp.concatenate([jnp.stack(numbers), doc_ids])


CHUNKS = 6


def score_blocks(info, q, a, h, chunks, numbers):
    docs = 2 + 2 * CHUNKS
    position = info[0]
    rows = q.shape[0]
    n_query = chunks[0][0].shape[0]
    q_blocks = n_query // BLOCK
    doc = info[docs + position * q_blocks + a]
    row = lax.broadcasted_iota(jnp.int32, (rows, BLOCK), 0) % BLOCK
    col = lax.broadcasted_iota(jnp.int32, (rows, BLOCK), 1)
    scores = []
    for (keys, _), c in zip(chunks, numbers):
        count = (a + 1) * BLOCK if c == 0 else n_query
        k = keys[:count, h * HEAD_SIZE : (h + 1) * HEAD_SIZE]
        s = lax.dot_general(q, k, (((1,), (1,)), ((), ())), preferred_element_type=jnp.float32)
        source, there = info[2 + 2 * c], info[3 + 2 * c]
        for b in range(count // BLOCK):
            part = s[:, b * BLOCK : (b + 1) * BLOCK]
            if c == 0 and b == a:
                part = jnp.where(row >= col, part, NEG)
            else:
                seen = (info[docs + source * q_blocks + b] == doc) & (there == 1)
                part = part + jnp.where(seen, 0.0, NEG)
            scores.append(part)
    return scores


def weigh(scores, peak, factor, a, h, chunks, numbers):
    n_query = chunks[0][0].shape[0]
    total = added = None
    scores = list(scores)
    for (_, values), c in zip(chunks, numbers):
        count = (a + 1) * BLOCK if c == 0 else n_query
        parts = []
        for b in range(count // BLOCK):
            w = jnp.exp2(scores.pop(0) * factor - peak)
            total = w if total is None else total + w
            parts.append(w.astype(jnp.bfloat16))
        w = jnp.concatenate(parts, axis=1) if len(parts) > 1 else parts[0]
        v = values[:count, h * HEAD_SIZE : (h + 1) * HEAD_SIZE]
        term = jnp.dot(w, v, preferred_element_type=jnp.float32)
        added = term if added is None else added + term
    return total, added


def head_slices(queries, keys, h):
    group = queries.shape[1] // keys.shape[1]
    return [slice((h * group + g) * HEAD_SIZE, (h * group + g + 1) * HEAD_SIZE) for g in range(group)]


def early_kernel(numbers, info, queries_in, keys_in, values_in, weight_in, *refs):
    pairs = 2 * len(numbers) - 2
    peaks, totals, sums, queries, weight, keys, values, sems = refs[pairs:]
    chunks = [(keys, values)] + list(zip(refs[0:pairs:2], refs[1:pairs:2]))
    places = ((queries_in, queries), (keys_in, keys), (values_in, values), (weight_in, weight))
    fetches = [pltpu.make_async_copy(a, b, sems.at[i]) for i, (a, b) in enumerate(places)]
    for fetch in fetches:
        fetch.start()
    for fetch in fetches[:3]:
        fetch.wait()
    n_query = queries.shape[0]
    factor = SCALE * LOG2E
    at = 0
    for a in range(n_query // BLOCK):
        for h in range(chunks[0][0].shape[1] // HEAD_SIZE):
            heads = head_slices(queries, chunks[0][0], h)
            q = jnp.concatenate([queries[a * BLOCK : (a + 1) * BLOCK, s] for s in heads], axis=0)
            scores = score_blocks(info, q, a, h, chunks, numbers)
            peak = functools.reduce(jnp.maximum, scores)
            peak = jnp.max(peak, axis=1, keepdims=True) * factor
            total, added = weigh(scores, peak, factor, a, h, chunks, numbers)
            rows = slice(at, at + q.shape[0])
            at += q.shape[0]
            peaks[rows, :] = jnp.broadcast_to(peak, (q.shape[0], HEAD_SIZE))
            totals[rows, :] = total
            sums[rows, :] = added
    fetches[3].wait()


def early_attention(info, queries, keys, values, weight, chunks, numbers):
    n_query, width = queries.shape
    rows = n_query * width // HEAD_SIZE
    state = pltpu.VMEM((rows, HEAD_SIZE), jnp.float32)
    count = len(numbers) * n_query
    return pl.pallas_call(
        functools.partial(early_kernel, numbers),
        out_shape=(
            state,
            state,
            state,
            pltpu.VMEM(queries.shape, queries.dtype),
            pltpu.VMEM(weight.shape, weight.dtype),
        ),
        in_specs=[SMEM, HBM, HBM, HBM, HBM] + [VMEM] * (2 * len(chunks)),
        out_specs=(VMEM,) * 5,
        scratch_shapes=[
            pltpu.VMEM(keys.shape, keys.dtype),
            pltpu.VMEM(values.shape, values.dtype),
            pltpu.SemaphoreType.DMA((4,)),
        ],
        compiler_params=LIMIT,
        cost_estimate=pl.CostEstimate(
            flops=4 * n_query * width * count,
            bytes_accessed=weight.size * 2,
            transcendentals=n_query * count * width // HEAD_SIZE,
        ),
        name="early",
    )(
        info,
        *[pltpu.with_memory_space_constraint(x, pltpu.HBM) for x in (queries, keys, values, weight)],
        *[x for pair in chunks for x in pair],
    )


def late_kernel(numbers, columns, info, queries, weight, peaks, totals, sums, *refs):
    pairs = 2 * len(numbers)
    chunks = list(zip(refs[0:pairs:2], refs[1:pairs:2]))
    far, near, mine, send, attended = refs[pairs:]
    n_query = queries.shape[0]
    factor = SCALE * LOG2E
    at = 0
    for a in range(n_query // BLOCK):
        for h in range(chunks[0][0].shape[1] // HEAD_SIZE):
            heads = head_slices(queries, chunks[0][0], h)
            q = jnp.concatenate([queries[a * BLOCK : (a + 1) * BLOCK, s] for s in heads], axis=0)
            scores = score_blocks(info, q, a, h, chunks, numbers)
            rows = slice(at, at + q.shape[0])
            at += q.shape[0]
            peak = functools.reduce(jnp.maximum, scores)
            before = peaks[rows, :]
            peak = jnp.maximum(before, jnp.max(peak, axis=1, keepdims=True) * factor)
            shrink = jnp.exp2(before - peak)
            total, added = weigh(scores, peak, factor, a, h, chunks, numbers)
            total = jnp.sum(total + totals[rows, :] * shrink, axis=1, keepdims=True)
            result = ((added + sums[rows, :] * shrink) / total).astype(jnp.bfloat16)
            for g, head in enumerate(heads):
                attended[a * BLOCK : (a + 1) * BLOCK, head] = result[g * BLOCK : (g + 1) * BLOCK]
    place = info[1]
    share = n_query // 4
    for i, owner in enumerate((place ^ 2, place ^ 3)):
        far[i * share : (i + 1) * share, :] = attended[pl.ds(pl.multiple_of(owner * share, share), share), :]
    for i, owner in enumerate((place, place ^ 1)):
        near[i * share : (i + 1) * share, :] = attended[pl.ds(pl.multiple_of(owner * share, share), share), :]
    project_columns(far, weight, mine, (send,), *columns)


def late_attention(info, queries, weight, state, chunks, numbers, columns):
    n_query, width = queries.shape
    keys = len(numbers) * n_query
    half = jax.ShapeDtypeStruct((n_query // 2, width), jnp.bfloat16)
    count = columns[1] - columns[0]
    return pl.pallas_call(
        functools.partial(late_kernel, numbers, columns),
        out_shape=(half, half) + project_shapes(n_query // 4, count),
        in_specs=[SMEM] + [VMEM] * (5 + 2 * len(numbers)),
        out_specs=(VMEM,) * 4,
        scratch_shapes=[pltpu.VMEM(queries.shape, jnp.bfloat16)],
        compiler_params=LIMIT,
        cost_estimate=pl.CostEstimate(
            flops=4 * n_query * width * keys + n_query * width * count,
            bytes_accessed=0,
            transcendentals=n_query * keys * width // HEAD_SIZE,
        ),
        name="late",
    )(info, queries, weight, *state, *[x for pair in chunks for x in pair])


def project_shapes(rows, count, sends=1):
    send = jax.ShapeDtypeStruct((rows, count // sends), jnp.bfloat16)
    return (jax.ShapeDtypeStruct((rows, count), jnp.float32),) + (send,) * sends


def project_columns(rows, weight, mine, sends, start, end):
    share = rows.shape[0] // 2
    width = sends[0].shape[1]
    for at in range(start, end, width):
        for left in range(at, at + width, 768):
            right = min(left + 768, at + width)
            product = jnp.dot(rows[...], weight[:, left:right], preferred_element_type=jnp.float32)
            mine[:, left - start : right - start] = product[:share]
            send = sends[(at - start) // width]
            send[:, left - at : right - at] = product[share:].astype(send.dtype)


def project_kernel(columns, rows, weight, mine, *sends):
    project_columns(rows, weight, mine, sends, *columns)


def project(rows, weight, columns, sends=1):
    count = columns[1] - columns[0]
    return pl.pallas_call(
        functools.partial(project_kernel, columns),
        out_shape=project_shapes(rows.shape[0] // 2, count, sends),
        in_specs=[VMEM, VMEM],
        out_specs=(VMEM,) * (1 + sends),
        compiler_params=LIMIT,
        cost_estimate=pl.CostEstimate(
            flops=2 * rows.shape[0] * rows.shape[1] * count, bytes_accessed=0, transcendentals=0
        ),
        name="project",
    )(rows, weight)


def add_kernel(mine, theirs, out):
    out[...] = (mine[...] + theirs[...].astype(jnp.float32)).astype(out.dtype)


def add_up(mine, theirs):
    return pl.pallas_call(
        add_kernel,
        out_shape=jax.ShapeDtypeStruct(theirs.shape, theirs.dtype),
        in_specs=[VMEM, VMEM],
        out_specs=VMEM,
        compiler_params=LIMIT,
        cost_estimate=pl.CostEstimate(flops=theirs.size, bytes_accessed=0, transcendentals=0),
        name="add_up",
    )(mine, theirs)


def combine_kernel(counts, mine, *refs):
    out = refs[-1]
    ends = []
    for part in (refs[: counts[0]], refs[counts[0] : -1]):
        at, pieces = 0, []
        for ref in part:
            pieces.append((at, at + ref.shape[1], ref))
            at += ref.shape[1]
        ends.append(pieces)
    for low, high, beside in ends[0]:
        for start, stop, across in ends[1]:
            left, right = max(low, start), min(high, stop)
            if left < right:
                total = mine[:, left:right] + beside[:, left - low : right - low].astype(jnp.float32)
                total += across[:, left - start : right - start].astype(jnp.float32)
                out[:, left:right] = total.astype(out.dtype)


def combine(mine, beside, across):
    return pl.pallas_call(
        functools.partial(combine_kernel, (len(beside), len(across))),
        out_shape=jax.ShapeDtypeStruct(mine.shape, across[0].dtype),
        in_specs=[VMEM] * (1 + len(beside) + len(across)),
        out_specs=VMEM,
        compiler_params=LIMIT,
        name="combine",
    )(mine, *beside, *across)


def from_behind(block, axis, distance):
    devices = range(lax.axis_size(axis))
    route = [(i - distance, i) for i in devices if i - distance in devices]
    return lax.ppermute(block, axis, route)


def token_docs(doc_ids, start, count):
    blocks = (start + jnp.arange(count, dtype=jnp.int32)) // BLOCK
    table = blocks[:, None] == jnp.arange(doc_ids.shape[0], dtype=jnp.int32)[None, :]
    return jnp.sum(jnp.where(table, doc_ids[None, :], 0), axis=1)


def attend(carry, queries, q_docs, q_start, k_piece, v_piece, k_docs, k_start):
    peak, totals, accum = carry
    n_query = queries.shape[0]
    n_key = k_piece.shape[0]
    kv_heads = k_piece.shape[1] // HEAD_SIZE
    query_group = queries.shape[1] // k_piece.shape[1]
    q_heads = queries.reshape(n_query, kv_heads, query_group, HEAD_SIZE)
    k_heads = k_piece.reshape(n_key, kv_heads, HEAD_SIZE)
    v_heads = v_piece.reshape(n_key, kv_heads, HEAD_SIZE)
    scores = (
        jnp.einsum("qkgd,skd->kgqs", q_heads, k_heads, preferred_element_type=jnp.float32) * SCALE
    )
    q_pos = q_start + jnp.arange(n_query, dtype=jnp.int32)
    k_pos = k_start + jnp.arange(n_key, dtype=jnp.int32)
    allowed = (q_docs[:, None] == k_docs[None, :]) & (q_pos[:, None] >= k_pos[None, :])
    scores = jnp.where(allowed, scores, NEG)
    new_peak = jnp.maximum(peak, jnp.max(scores, axis=-1))
    shrink = jnp.exp(peak - new_peak)
    weights = jnp.exp(scores - new_peak[..., None])
    totals = totals * shrink + jnp.sum(weights, axis=-1)
    rounded = weights.astype(jnp.bfloat16)
    added = jnp.einsum("kgqs,skd->kgqd", rounded, v_heads, preferred_element_type=jnp.float32)
    accum = accum * shrink[..., None] + added
    return (new_peak, totals, accum)


def absorb_block(carry, queries, q_docs, q_start, k_piece, v_piece, k_start, doc_ids, flag):
    n_key = k_piece.shape[0]
    k_docs = token_docs(doc_ids, k_start, n_key)
    fresh = attend(carry, queries, q_docs, q_start, k_piece, v_piece, k_docs, k_start)
    return jax.tree.map(lambda new, old: jnp.where(flag, new, old), fresh, carry)


def ring_attention(queries, keys, values, doc_ids, n_ctx, position):
    n_query = queries.shape[0]
    q_start = position * n_query
    q_docs = token_docs(doc_ids, q_start, n_query)
    kv_heads = keys.shape[1] // HEAD_SIZE
    query_group = queries.shape[1] // keys.shape[1]
    carry = (
        jnp.full((kv_heads, query_group, n_query), NEG, jnp.float32),
        jnp.zeros((kv_heads, query_group, n_query), jnp.float32),
        jnp.zeros((kv_heads, query_group, n_query, HEAD_SIZE), jnp.float32),
    )
    always = jnp.array(True)
    carry = absorb_block(carry, queries, q_docs, q_start, keys, values, q_start, doc_ids, always)

    def turn_one(step, state):
        inner_state, moving = state
        moving = from_behind(moving, "ctx", 1)
        start = ((position - step) % n_ctx) * n_query
        inner_state = absorb_block(
            inner_state, queries, q_docs, q_start, moving[0], moving[1], start, doc_ids, always
        )
        return (inner_state, moving)

    _, totals, accum = lax.fori_loop(1, n_ctx, turn_one, (carry, jnp.stack((keys, values))))[0]
    result = accum / totals[..., None]
    return jnp.transpose(result, (2, 0, 1, 3)).reshape(queries.shape).astype(jnp.bfloat16)


def part_rows(attended, place):
    share = attended.shape[0] // 4
    rows = [lax.dynamic_slice_in_dim(attended, (place ^ flip) * share, share, 0) for flip in (2, 3, 0, 1)]
    return jnp.concatenate(rows[:2], axis=0), jnp.concatenate(rows[2:], axis=0)


def per_device(queries, keys, values, doc_ids, out_weight):
    n_ctx = lax.axis_size("ctx")
    heads = lax.axis_size("head")
    position = lax.axis_index("ctx")
    place = lax.axis_index("head")
    other_core = [(i, i ^ 1) for i in range(heads)]
    other_chip = [(i, i ^ 2) for i in range(heads)]
    columns = out_weight.shape[1]
    cut = columns * 4 // 7 // BLOCK * BLOCK

    if n_ctx == 8:
        first = n_ctx * 3 // 4
        own = (keys, values)
        by_two = [hop(x, "ctx", [(i, i + 2) for i in range(first - 2)]) for x in own]
        by_four = [hop(x, "ctx", [(i, i + 4) for i in range(first - 4)]) for x in own]
        beside = [hop(x, "ctx", [(i, i + 1) for i in range(0, n_ctx, 2)]) for x in own]
        swap_two = [hop(x, "ctx", [(i, i ^ 1) for i in range(2, first)]) for x in by_two]
        swap_four = [hop(x, "ctx", [(i, i ^ 1) for i in range(4, first)]) for x in by_four]
        info = describe(position, place, doc_ids, n_ctx)
        *state, fetched, weight = early_attention(
            info, queries, keys, values, out_weight, [beside, by_two, by_four], (0, 1, 2, 3)
        )
        far, near, mine, send = late_attention(
            info, fetched, weight, state, [swap_two, swap_four], (4, 5), (0, cut)
        )
    else:
        weight = out_weight
        attended = ring_attention(queries, keys, values, doc_ids, n_ctx, position)
        far, near = part_rows(attended, place)
        mine, send = project(far, weight, (0, cut))
    theirs = hop(send, "head", other_core)
    later_mine, later_send = project(far, weight, (cut, columns))
    mine, later_mine = lax.optimization_barrier((mine, later_mine))
    first_sum = add_up(mine, theirs)
    first_part = hop(first_sum, "head", other_chip)
    later_theirs = hop(later_send, "head", other_core)
    later_mine, first_sum = lax.optimization_barrier((later_mine, first_sum))
    later_sum = add_up(later_mine, later_theirs)
    second_part = hop(later_sum, "head", other_chip)
    near, later_sum = lax.optimization_barrier((near, later_sum))
    mine, *sends = project(near, weight, (0, columns), 3)
    theirs = [hop(send, "head", other_core) for send in sends]
    return combine(mine, theirs, (first_part, second_part))


def solution(mesh):
    placed = (P("ctx", "head"), P("ctx", "head"), P("ctx", "head"), P(), P("head", None))
    return jax.shard_map(
        per_device, mesh=mesh, in_specs=placed, out_specs=P(("ctx", "head"), None), check_vma=False
    )
```

```python
import functools

import jax
import jax.numpy as jnp
from jax import lax
from jax.experimental import pallas as pl
from jax.experimental.pallas import tpu as pltpu
from jax.sharding import PartitionSpec as P

HEAD_SIZE = 128
BLOCK = 128
SCALE = 168.0 ** (-0.5)
LOG2E = 1.4426950408889634
NEG = -1e30
VMEM = pl.BlockSpec(memory_space=pltpu.VMEM)
SMEM = pl.BlockSpec(memory_space=pltpu.SMEM)
HBM = pl.BlockSpec(memory_space=pltpu.HBM)
LIMIT = pltpu.CompilerParams(vmem_limit_bytes=32 * 1024 * 1024)


def hop(block, axis, pairs):
    return lax.ppermute(block, axis, pairs)


def describe(position, place, doc_ids, n_ctx):
    first = n_ctx * 3 // 4
    in_first = position < first
    chunks = [
        (position, position >= 0),
        (position ^ 1, position % 2 == 1),
        (position - 2, in_first & (position >= 2)),
        (position - 4, in_first & (position >= 4)),
        ((position - 2) ^ 1, in_first & (position >= 2)),
        ((position - 4) ^ 1, in_first & (position >= 4)),
    ]
    numbers = [position, place]
    for source, there in chunks:
        numbers += [jnp.where(there, source, 0), there.astype(jnp.int32)]
    return jnp.concatenate([jnp.stack(numbers), doc_ids])


CHUNKS = 6


def score_blocks(info, q, a, h, chunks, numbers):
    docs = 2 + 2 * CHUNKS
    position = info[0]
    rows = q.shape[0]
    n_query = chunks[0][0].shape[0]
    q_blocks = n_query // BLOCK
    doc = info[docs + position * q_blocks + a]
    row = lax.broadcasted_iota(jnp.int32, (rows, BLOCK), 0) % BLOCK
    col = lax.broadcasted_iota(jnp.int32, (rows, BLOCK), 1)
    scores = []
    for (keys, _), c in zip(chunks, numbers):
        count = (a + 1) * BLOCK if c == 0 else n_query
        k = keys[:count, h * HEAD_SIZE : (h + 1) * HEAD_SIZE]
        s = lax.dot_general(q, k, (((1,), (1,)), ((), ())), preferred_element_type=jnp.float32)
        source, there = info[2 + 2 * c], info[3 + 2 * c]
        for b in range(count // BLOCK):
            part = s[:, b * BLOCK : (b + 1) * BLOCK]
            if c == 0 and b == a:
                part = jnp.where(row >= col, part, NEG)
            else:
                seen = (info[docs + source * q_blocks + b] == doc) & (there == 1)
                part = part + jnp.where(seen, 0.0, NEG)
            scores.append(part)
    return scores


def weigh(scores, peak, factor, a, h, chunks, numbers):
    n_query = chunks[0][0].shape[0]
    total = added = None
    scores = list(scores)
    for (_, values), c in zip(chunks, numbers):
        count = (a + 1) * BLOCK if c == 0 else n_query
        parts = []
        for b in range(count // BLOCK):
            w = jnp.exp2(scores.pop(0) * factor - peak)
            total = w if total is None else total + w
            parts.append(w.astype(jnp.bfloat16))
        w = jnp.concatenate(parts, axis=1) if len(parts) > 1 else parts[0]
        v = values[:count, h * HEAD_SIZE : (h + 1) * HEAD_SIZE]
        term = jnp.dot(w, v, preferred_element_type=jnp.float32)
        added = term if added is None else added + term
    return total, added


def head_slices(queries, keys, h):
    group = queries.shape[1] // keys.shape[1]
    return [slice((h * group + g) * HEAD_SIZE, (h * group + g + 1) * HEAD_SIZE) for g in range(group)]


def early_kernel(numbers, info, queries_in, keys_in, values_in, weight_in, *refs):
    pairs = 2 * len(numbers) - 2
    peaks, totals, sums, queries, weight, keys, values, sems = refs[pairs:]
    chunks = [(keys, values)] + list(zip(refs[0:pairs:2], refs[1:pairs:2]))
    places = ((queries_in, queries), (keys_in, keys), (values_in, values), (weight_in, weight))
    fetches = [pltpu.make_async_copy(a, b, sems.at[i]) for i, (a, b) in enumerate(places)]
    for fetch in fetches:
        fetch.start()
    for fetch in fetches[:3]:
        fetch.wait()
    n_query = queries.shape[0]
    factor = SCALE * LOG2E
    at = 0
    for a in range(n_query // BLOCK):
        for h in range(chunks[0][0].shape[1] // HEAD_SIZE):
            heads = head_slices(queries, chunks[0][0], h)
            q = jnp.concatenate([queries[a * BLOCK : (a + 1) * BLOCK, s] for s in heads], axis=0)
            scores = score_blocks(info, q, a, h, chunks, numbers)
            peak = functools.reduce(jnp.maximum, scores)
            peak = jnp.max(peak, axis=1, keepdims=True) * factor
            total, added = weigh(scores, peak, factor, a, h, chunks, numbers)
            rows = slice(at, at + q.shape[0])
            at += q.shape[0]
            peaks[rows, :] = jnp.broadcast_to(peak, (q.shape[0], HEAD_SIZE))
            totals[rows, :] = total
            sums[rows, :] = added
    fetches[3].wait()


def early_attention(info, queries, keys, values, weight, chunks, numbers):
    n_query, width = queries.shape
    rows = n_query * width // HEAD_SIZE
    state = pltpu.VMEM((rows, HEAD_SIZE), jnp.float32)
    count = len(numbers) * n_query
    return pl.pallas_call(
        functools.partial(early_kernel, numbers),
        out_shape=(
            state,
            state,
            state,
            pltpu.VMEM(queries.shape, queries.dtype),
            pltpu.VMEM(weight.shape, weight.dtype),
        ),
        in_specs=[SMEM, HBM, HBM, HBM, HBM] + [VMEM] * (2 * len(chunks)),
        out_specs=(VMEM,) * 5,
        scratch_shapes=[
            pltpu.VMEM(keys.shape, keys.dtype),
            pltpu.VMEM(values.shape, values.dtype),
            pltpu.SemaphoreType.DMA((4,)),
        ],
        compiler_params=LIMIT,
        cost_estimate=pl.CostEstimate(
            flops=4 * n_query * width * count,
            bytes_accessed=weight.size * 2,
            transcendentals=n_query * count * width // HEAD_SIZE,
        ),
        name="early",
    )(
        info,
        *[pltpu.with_memory_space_constraint(x, pltpu.HBM) for x in (queries, keys, values, weight)],
        *[x for pair in chunks for x in pair],
    )


def late_kernel(numbers, columns, info, queries, weight, peaks, totals, sums, *refs):
    pairs = 2 * len(numbers)
    chunks = list(zip(refs[0:pairs:2], refs[1:pairs:2]))
    far, near, mine, send, attended = refs[pairs:]
    n_query = queries.shape[0]
    factor = SCALE * LOG2E
    at = 0
    for a in range(n_query // BLOCK):
        for h in range(chunks[0][0].shape[1] // HEAD_SIZE):
            heads = head_slices(queries, chunks[0][0], h)
            q = jnp.concatenate([queries[a * BLOCK : (a + 1) * BLOCK, s] for s in heads], axis=0)
            scores = score_blocks(info, q, a, h, chunks, numbers)
            rows = slice(at, at + q.shape[0])
            at += q.shape[0]
            peak = functools.reduce(jnp.maximum, scores)
            before = peaks[rows, :]
            peak = jnp.maximum(before, jnp.max(peak, axis=1, keepdims=True) * factor)
            shrink = jnp.exp2(before - peak)
            total, added = weigh(scores, peak, factor, a, h, chunks, numbers)
            total = jnp.sum(total + totals[rows, :] * shrink, axis=1, keepdims=True)
            result = ((added + sums[rows, :] * shrink) / total).astype(jnp.bfloat16)
            for g, head in enumerate(heads):
                attended[a * BLOCK : (a + 1) * BLOCK, head] = result[g * BLOCK : (g + 1) * BLOCK]
    place = info[1]
    share = n_query // 4
    for i, owner in enumerate((place ^ 2, place ^ 3)):
        far[i * share : (i + 1) * share, :] = attended[pl.ds(pl.multiple_of(owner * share, share), share), :]
    for i, owner in enumerate((place, place ^ 1)):
        near[i * share : (i + 1) * share, :] = attended[pl.ds(pl.multiple_of(owner * share, share), share), :]
    project_columns(far, weight, mine, (send,), *columns)


def late_attention(info, queries, weight, state, chunks, numbers, columns):
    n_query, width = queries.shape
    keys = len(numbers) * n_query
    half = jax.ShapeDtypeStruct((n_query // 2, width), jnp.bfloat16)
    count = columns[1] - columns[0]
    return pl.pallas_call(
        functools.partial(late_kernel, numbers, columns),
        out_shape=(half, half) + project_shapes(n_query // 4, count),
        in_specs=[SMEM] + [VMEM] * (5 + 2 * len(numbers)),
        out_specs=(VMEM,) * 4,
        scratch_shapes=[pltpu.VMEM(queries.shape, jnp.bfloat16)],
        compiler_params=LIMIT,
        cost_estimate=pl.CostEstimate(
            flops=4 * n_query * width * keys + n_query * width * count,
            bytes_accessed=0,
            transcendentals=n_query * keys * width // HEAD_SIZE,
        ),
        name="late",
    )(info, queries, weight, *state, *[x for pair in chunks for x in pair])


def project_shapes(rows, count, sends=1):
    send = jax.ShapeDtypeStruct((rows, count // sends), jnp.bfloat16)
    return (jax.ShapeDtypeStruct((rows, count), jnp.float32),) + (send,) * sends


def project_columns(rows, weight, mine, sends, start, end):
    share = rows.shape[0] // 2
    width = sends[0].shape[1]
    for at in range(start, end, width):
        for left in range(at, at + width, 768):
            right = min(left + 768, at + width)
            product = jnp.dot(rows[...], weight[:, left:right], preferred_element_type=jnp.float32)
            mine[:, left - start : right - start] = product[:share]
            send = sends[(at - start) // width]
            send[:, left - at : right - at] = product[share:].astype(send.dtype)


def project_kernel(columns, rows, weight, mine, *sends):
    project_columns(rows, weight, mine, sends, *columns)


def project(rows, weight, columns, sends=1):
    count = columns[1] - columns[0]
    return pl.pallas_call(
        functools.partial(project_kernel, columns),
        out_shape=project_shapes(rows.shape[0] // 2, count, sends),
        in_specs=[VMEM, VMEM],
        out_specs=(VMEM,) * (1 + sends),
        compiler_params=LIMIT,
        cost_estimate=pl.CostEstimate(
            flops=2 * rows.shape[0] * rows.shape[1] * count, bytes_accessed=0, transcendentals=0
        ),
        name="project",
    )(rows, weight)


def add_kernel(mine, theirs, out):
    out[...] = (mine[...] + theirs[...].astype(jnp.float32)).astype(out.dtype)


def add_up(mine, theirs):
    return pl.pallas_call(
        add_kernel,
        out_shape=jax.ShapeDtypeStruct(theirs.shape, theirs.dtype),
        in_specs=[VMEM, VMEM],
        out_specs=VMEM,
        compiler_params=LIMIT,
        cost_estimate=pl.CostEstimate(flops=theirs.size, bytes_accessed=0, transcendentals=0),
        name="add_up",
    )(mine, theirs)


def combine_kernel(counts, mine, *refs):
    out = refs[-1]
    ends = []
    for part in (refs[: counts[0]], refs[counts[0] : -1]):
        at, pieces = 0, []
        for ref in part:
            pieces.append((at, at + ref.shape[1], ref))
            at += ref.shape[1]
        ends.append(pieces)
    for low, high, beside in ends[0]:
        for start, stop, across in ends[1]:
            left, right = max(low, start), min(high, stop)
            if left < right:
                total = mine[:, left:right] + beside[:, left - low : right - low].astype(jnp.float32)
                total += across[:, left - start : right - start].astype(jnp.float32)
                out[:, left:right] = total.astype(out.dtype)


def combine(mine, beside, across):
    return pl.pallas_call(
        functools.partial(combine_kernel, (len(beside), len(across))),
        out_shape=jax.ShapeDtypeStruct(mine.shape, across[0].dtype),
        in_specs=[VMEM] * (1 + len(beside) + len(across)),
        out_specs=VMEM,
        compiler_params=LIMIT,
        name="combine",
    )(mine, *beside, *across)


def from_behind(block, axis, distance):
    devices = range(lax.axis_size(axis))
    route = [(i - distance, i) for i in devices if i - distance in devices]
    return lax.ppermute(block, axis, route)


def token_docs(doc_ids, start, count):
    blocks = (start + jnp.arange(count, dtype=jnp.int32)) // BLOCK
    table = blocks[:, None] == jnp.arange(doc_ids.shape[0], dtype=jnp.int32)[None, :]
    return jnp.sum(jnp.where(table, doc_ids[None, :], 0), axis=1)


def attend(carry, queries, q_docs, q_start, k_piece, v_piece, k_docs, k_start):
    peak, totals, accum = carry
    n_query = queries.shape[0]
    n_key = k_piece.shape[0]
    kv_heads = k_piece.shape[1] // HEAD_SIZE
    query_group = queries.shape[1] // k_piece.shape[1]
    q_heads = queries.reshape(n_query, kv_heads, query_group, HEAD_SIZE)
    k_heads = k_piece.reshape(n_key, kv_heads, HEAD_SIZE)
    v_heads = v_piece.reshape(n_key, kv_heads, HEAD_SIZE)
    scores = (
        jnp.einsum("qkgd,skd->kgqs", q_heads, k_heads, preferred_element_type=jnp.float32) * SCALE
    )
    q_pos = q_start + jnp.arange(n_query, dtype=jnp.int32)
    k_pos = k_start + jnp.arange(n_key, dtype=jnp.int32)
    allowed = (q_docs[:, None] == k_docs[None, :]) & (q_pos[:, None] >= k_pos[None, :])
    scores = jnp.where(allowed, scores, NEG)
    new_peak = jnp.maximum(peak, jnp.max(scores, axis=-1))
    shrink = jnp.exp(peak - new_peak)
    weights = jnp.exp(scores - new_peak[..., None])
    totals = totals * shrink + jnp.sum(weights, axis=-1)
    rounded = weights.astype(jnp.bfloat16)
    added = jnp.einsum("kgqs,skd->kgqd", rounded, v_heads, preferred_element_type=jnp.float32)
    accum = accum * shrink[..., None] + added
    return (new_peak, totals, accum)


def absorb_block(carry, queries, q_docs, q_start, k_piece, v_piece, k_start, doc_ids, flag):
    n_key = k_piece.shape[0]
    k_docs = token_docs(doc_ids, k_start, n_key)
    fresh = attend(carry, queries, q_docs, q_start, k_piece, v_piece, k_docs, k_start)
    return jax.tree.map(lambda new, old: jnp.where(flag, new, old), fresh, carry)


def ring_attention(queries, keys, values, doc_ids, n_ctx, position):
    n_query = queries.shape[0]
    q_start = position * n_query
    q_docs = token_docs(doc_ids, q_start, n_query)
    kv_heads = keys.shape[1] // HEAD_SIZE
    query_group = queries.shape[1] // keys.shape[1]
    carry = (
        jnp.full((kv_heads, query_group, n_query), NEG, jnp.float32),
        jnp.zeros((kv_heads, query_group, n_query), jnp.float32),
        jnp.zeros((kv_heads, query_group, n_query, HEAD_SIZE), jnp.float32),
    )
    always = jnp.array(True)
    carry = absorb_block(carry, queries, q_docs, q_start, keys, values, q_start, doc_ids, always)

    def turn_one(step, state):
        inner_state, moving = state
        moving = from_behind(moving, "ctx", 1)
        start = ((position - step) % n_ctx) * n_query
        inner_state = absorb_block(
            inner_state, queries, q_docs, q_start, moving[0], moving[1], start, doc_ids, always
        )
        return (inner_state, moving)

    _, totals, accum = lax.fori_loop(1, n_ctx, turn_one, (carry, jnp.stack((keys, values))))[0]
    result = accum / totals[..., None]
    return jnp.transpose(result, (2, 0, 1, 3)).reshape(queries.shape).astype(jnp.bfloat16)


def part_rows(attended, place):
    share = attended.shape[0] // 4
    rows = [lax.dynamic_slice_in_dim(attended, (place ^ flip) * share, share, 0) for flip in (2, 3, 0, 1)]
    return jnp.concatenate(rows[:2], axis=0), jnp.concatenate(rows[2:], axis=0)


def per_device(queries, keys, values, doc_ids, out_weight):
    n_ctx = lax.axis_size("ctx")
    heads = lax.axis_size("head")
    position = lax.axis_index("ctx")
    place = lax.axis_index("head")
    other_core = [(i, i ^ 1) for i in range(heads)]
    other_chip = [(i, i ^ 2) for i in range(heads)]
    columns = out_weight.shape[1]
    cut = columns * 4 // 7 // BLOCK * BLOCK

    if n_ctx == 8:
        ahead = lambda far: [(i, (i + far) % n_ctx) for i in range(n_ctx)]
        across = [(i, i ^ 1) for i in range(n_ctx)]
        own = (keys, values)
        by_two = [hop(x, "ctx", ahead(2)) for x in own]
        by_four = [hop(x, "ctx", ahead(4)) for x in own]
        beside = [hop(x, "ctx", across) for x in own]
        swap_two = [hop(x, "ctx", across) for x in by_two]
        swap_four = [hop(x, "ctx", across) for x in by_four]
        info = describe(position, place, doc_ids, n_ctx)
        *state, fetched, weight = early_attention(
            info, queries, keys, values, out_weight, [beside, by_two, by_four], (0, 1, 2, 3)
        )
        far, near, mine, send = late_attention(
            info, fetched, weight, state, [swap_two, swap_four], (4, 5), (0, cut)
        )
    else:
        weight = out_weight
        attended = ring_attention(queries, keys, values, doc_ids, n_ctx, position)
        far, near = part_rows(attended, place)
        mine, send = project(far, weight, (0, cut))
    theirs = hop(send, "head", other_core)
    later_mine, later_send = project(far, weight, (cut, columns))
    mine, later_mine = lax.optimization_barrier((mine, later_mine))
    first_sum = add_up(mine, theirs)
    first_part = hop(first_sum, "head", other_chip)
    later_theirs = hop(later_send, "head", other_core)
    later_mine, first_sum = lax.optimization_barrier((later_mine, first_sum))
    later_sum = add_up(later_mine, later_theirs)
    second_part = hop(later_sum, "head", other_chip)
    near, later_sum = lax.optimization_barrier((near, later_sum))
    mine, *sends = project(near, weight, (0, columns), 3)
    theirs = [hop(send, "head", other_core) for send in sends]
    return combine(mine, theirs, (first_part, second_part))


def solution(mesh):
    placed = (P("ctx", "head"), P("ctx", "head"), P("ctx", "head"), P(), P("head", None))
    return jax.shard_map(
        per_device, mesh=mesh, in_specs=placed, out_specs=P(("ctx", "head"), None), check_vma=False
    )
```

```python
import functools

import jax
import jax.numpy as jnp
from jax import lax
from jax.experimental import pallas as pl
from jax.experimental.pallas import tpu as pltpu
from jax.sharding import PartitionSpec as P

HEAD_SIZE = 128
BLOCK = 128
SCALE = 168.0 ** (-0.5)
LOG2E = 1.4426950408889634
NEG = -1e30
VMEM = pl.BlockSpec(memory_space=pltpu.VMEM)
SMEM = pl.BlockSpec(memory_space=pltpu.SMEM)
HBM = pl.BlockSpec(memory_space=pltpu.HBM)
LIMIT = pltpu.CompilerParams(vmem_limit_bytes=32 * 1024 * 1024)


def hop(block, axis, pairs):
    return lax.ppermute(block, axis, pairs)


def describe(position, place, doc_ids, n_ctx):
    first = n_ctx * 3 // 4
    in_first = position < first
    chunks = [
        (position, position >= 0),
        (position ^ 1, position % 2 == 1),
        (position - 2, in_first & (position >= 2)),
        (position - 4, in_first & (position >= 4)),
        ((position - 2) ^ 1, in_first & (position >= 2)),
        ((position - 4) ^ 1, in_first & (position >= 4)),
    ]
    numbers = [position, place]
    for source, there in chunks:
        numbers += [jnp.where(there, source, 0), there.astype(jnp.int32)]
    return jnp.concatenate([jnp.stack(numbers), doc_ids])


CHUNKS = 6
BESIDE = ((0, 1), (2, 3), (4, 5), (6, 7))
BY_TWO = ((0, 2, 4), (1, 3, 5), (6, 7))
BY_FOUR = ((0, 4, 2), (1, 5, 3), (6, 7))


def after(x, state):
    return lax.optimization_barrier((x, state[0]))[0]


def cycles(rings):
    return [(ring[i], ring[(i + 1) % len(ring)]) for ring in rings for i in range(len(ring))]


def score_blocks(info, q, a, h, chunks, numbers):
    docs = 2 + 2 * CHUNKS
    position = info[0]
    rows = q.shape[0]
    n_query = chunks[0][0].shape[0]
    q_blocks = n_query // BLOCK
    doc = info[docs + position * q_blocks + a]
    row = lax.broadcasted_iota(jnp.int32, (rows, BLOCK), 0) % BLOCK
    col = lax.broadcasted_iota(jnp.int32, (rows, BLOCK), 1)
    scores = []
    for (keys, _), c in zip(chunks, numbers):
        count = (a + 1) * BLOCK if c == 0 else n_query
        k = keys[:count, h * HEAD_SIZE : (h + 1) * HEAD_SIZE]
        s = lax.dot_general(q, k, (((1,), (1,)), ((), ())), preferred_element_type=jnp.float32)
        source, there = info[2 + 2 * c], info[3 + 2 * c]
        for b in range(count // BLOCK):
            part = s[:, b * BLOCK : (b + 1) * BLOCK]
            if c == 0 and b == a:
                part = jnp.where(row >= col, part, NEG)
            else:
                seen = (info[docs + source * q_blocks + b] == doc) & (there == 1)
                part = part + jnp.where(seen, 0.0, NEG)
            scores.append(part)
    return scores


def weigh(scores, peak, factor, a, h, chunks, numbers):
    n_query = chunks[0][0].shape[0]
    total = added = None
    scores = list(scores)
    for (_, values), c in zip(chunks, numbers):
        count = (a + 1) * BLOCK if c == 0 else n_query
        parts = []
        for b in range(count // BLOCK):
            w = jnp.exp2(scores.pop(0) * factor - peak)
            total = w if total is None else total + w
            parts.append(w.astype(jnp.bfloat16))
        w = jnp.concatenate(parts, axis=1) if len(parts) > 1 else parts[0]
        v = values[:count, h * HEAD_SIZE : (h + 1) * HEAD_SIZE]
        term = jnp.dot(w, v, preferred_element_type=jnp.float32)
        added = term if added is None else added + term
    return total, added


def head_slices(queries, keys, h):
    group = queries.shape[1] // keys.shape[1]
    return [slice((h * group + g) * HEAD_SIZE, (h * group + g + 1) * HEAD_SIZE) for g in range(group)]


def absorb(numbers, info, queries, chunks, before, after):
    n_query = queries.shape[0]
    factor = SCALE * LOG2E
    at = 0
    for a in range(n_query // BLOCK):
        for h in range(chunks[0][0].shape[1] // HEAD_SIZE):
            heads = head_slices(queries, chunks[0][0], h)
            q = jnp.concatenate([queries[a * BLOCK : (a + 1) * BLOCK, s] for s in heads], axis=0)
            scores = score_blocks(info, q, a, h, chunks, numbers)
            rows = slice(at, at + q.shape[0])
            at += q.shape[0]
            peak = functools.reduce(jnp.maximum, scores)
            peak = jnp.max(peak, axis=1, keepdims=True) * factor
            if before is None:
                total, added = weigh(scores, peak, factor, a, h, chunks, numbers)
                peak = jnp.broadcast_to(peak, (q.shape[0], HEAD_SIZE))
            else:
                last = before[0][rows, :]
                peak = jnp.maximum(last, peak)
                shrink = jnp.exp2(last - peak)
                total, added = weigh(scores, peak, factor, a, h, chunks, numbers)
                total = total + before[1][rows, :] * shrink
                added = added + before[2][rows, :] * shrink
            after(a, heads, rows, peak, total, added)


def store_state(state):
    def after(a, heads, rows, *parts):
        for ref, part in zip(state, parts):
            ref[rows, :] = part

    return after


def pairs_of(refs):
    return list(zip(refs[0::2], refs[1::2]))


def first_kernel(numbers, info, queries_in, keys_in, values_in, weight_in, *refs):
    pairs = 2 * len(numbers) - 2
    *state, queries, weight, keys, values, sems = refs[pairs:]
    chunks = [(keys, values)] + pairs_of(refs[:pairs])
    places = ((queries_in, queries), (keys_in, keys), (values_in, values), (weight_in, weight))
    fetches = [pltpu.make_async_copy(a, b, sems.at[i]) for i, (a, b) in enumerate(places)]
    for fetch in fetches:
        fetch.start()
    for fetch in fetches[:3]:
        fetch.wait()
    absorb(numbers, info, queries, chunks, None, store_state(state))
    fetches[3].wait()


def next_kernel(numbers, info, queries, *refs):
    pairs = 2 * len(numbers)
    absorb(numbers, info, queries, pairs_of(refs[3 : 3 + pairs]), refs[:3], store_state(refs[3 + pairs :]))


def attend_cost(queries, numbers, fetched=0):
    n_query, width = queries.shape
    count = len(numbers) * n_query
    return pl.CostEstimate(
        flops=4 * n_query * width * count,
        bytes_accessed=fetched,
        transcendentals=n_query * count * width // HEAD_SIZE,
    )


def state_shapes(queries):
    rows = queries.size // HEAD_SIZE
    return (pltpu.VMEM((rows, HEAD_SIZE), jnp.float32),) * 3


def attend_first(info, queries, keys, values, weight, chunks, numbers):
    return pl.pallas_call(
        functools.partial(first_kernel, numbers),
        out_shape=state_shapes(queries)
        + (pltpu.VMEM(queries.shape, queries.dtype), pltpu.VMEM(weight.shape, weight.dtype)),
        in_specs=[SMEM, HBM, HBM, HBM, HBM] + [VMEM] * (2 * len(chunks)),
        out_specs=(VMEM,) * 5,
        scratch_shapes=[
            pltpu.VMEM(keys.shape, keys.dtype),
            pltpu.VMEM(values.shape, values.dtype),
            pltpu.SemaphoreType.DMA((4,)),
        ],
        compiler_params=LIMIT,
        cost_estimate=attend_cost(queries, numbers, 2 * weight.size),
        name="attend_first",
    )(
        info,
        *[pltpu.with_memory_space_constraint(x, pltpu.HBM) for x in (queries, keys, values, weight)],
        *[x for pair in chunks for x in pair],
    )


def attend_next(info, queries, state, chunks, numbers):
    return pl.pallas_call(
        functools.partial(next_kernel, numbers),
        out_shape=state_shapes(queries),
        in_specs=[SMEM] + [VMEM] * (4 + 2 * len(chunks)),
        out_specs=(VMEM,) * 3,
        compiler_params=LIMIT,
        cost_estimate=attend_cost(queries, numbers),
        name="attend_next",
    )(info, queries, *state, *[x for pair in chunks for x in pair])


def last_kernel(numbers, columns, info, queries, weight, *refs):
    pairs = 2 * len(numbers)
    chunks = pairs_of(refs[3 : 3 + pairs])
    far, near, mine, send, attended = refs[3 + pairs :]

    def after(a, heads, rows, peak, total, added):
        result = (added / jnp.sum(total, axis=1, keepdims=True)).astype(jnp.bfloat16)
        for g, head in enumerate(heads):
            attended[a * BLOCK : (a + 1) * BLOCK, head] = result[g * BLOCK : (g + 1) * BLOCK]

    absorb(numbers, info, queries, chunks, refs[:3], after)
    place = info[1]
    share = queries.shape[0] // 4
    for half, owners in ((far, (place ^ 2, place ^ 3)), (near, (place, place ^ 1))):
        for i, owner in enumerate(owners):
            source = pl.ds(pl.multiple_of(owner * share, share), share)
            half[i * share : (i + 1) * share, :] = attended[source, :]
    project_columns(far, weight, mine, (send,), *columns)


def attend_last(info, queries, weight, state, chunks, numbers, columns):
    n_query, width = queries.shape
    half = jax.ShapeDtypeStruct((n_query // 2, width), jnp.bfloat16)
    return pl.pallas_call(
        functools.partial(last_kernel, numbers, columns),
        out_shape=(half, half) + project_shapes(n_query // 4, columns[1] - columns[0]),
        in_specs=[SMEM] + [VMEM] * (5 + 2 * len(numbers)),
        out_specs=(VMEM,) * 4,
        scratch_shapes=[pltpu.VMEM(queries.shape, jnp.bfloat16)],
        compiler_params=LIMIT,
        cost_estimate=attend_cost(queries, numbers),
        name="attend_last",
    )(info, queries, weight, *state, *[x for pair in chunks for x in pair])


def project_shapes(rows, count, sends=1):
    send = jax.ShapeDtypeStruct((rows, count // sends), jnp.bfloat16)
    return (jax.ShapeDtypeStruct((rows, count), jnp.float32),) + (send,) * sends


def project_columns(rows, weight, mine, sends, start, end):
    share = rows.shape[0] // 2
    width = sends[0].shape[1]
    for at in range(start, end, width):
        for left in range(at, at + width, 768):
            right = min(left + 768, at + width)
            product = jnp.dot(rows[...], weight[:, left:right], preferred_element_type=jnp.float32)
            mine[:, left - start : right - start] = product[:share]
            send = sends[(at - start) // width]
            send[:, left - at : right - at] = product[share:].astype(send.dtype)


def project_kernel(columns, rows, weight, mine, *sends):
    project_columns(rows, weight, mine, sends, *columns)


def project(rows, weight, columns, sends=1):
    count = columns[1] - columns[0]
    return pl.pallas_call(
        functools.partial(project_kernel, columns),
        out_shape=project_shapes(rows.shape[0] // 2, count, sends),
        in_specs=[VMEM, VMEM],
        out_specs=(VMEM,) * (1 + sends),
        compiler_params=LIMIT,
        cost_estimate=pl.CostEstimate(
            flops=2 * rows.shape[0] * rows.shape[1] * count, bytes_accessed=0, transcendentals=0
        ),
        name="project",
    )(rows, weight)


def add_kernel(mine, theirs, out):
    out[...] = (mine[...] + theirs[...].astype(jnp.float32)).astype(out.dtype)


def add_up(mine, theirs):
    return pl.pallas_call(
        add_kernel,
        out_shape=jax.ShapeDtypeStruct(theirs.shape, theirs.dtype),
        in_specs=[VMEM, VMEM],
        out_specs=VMEM,
        compiler_params=LIMIT,
        cost_estimate=pl.CostEstimate(flops=theirs.size, bytes_accessed=0, transcendentals=0),
        name="add_up",
    )(mine, theirs)


def combine_kernel(counts, mine, *refs):
    out = refs[-1]
    ends = []
    for part in (refs[: counts[0]], refs[counts[0] : -1]):
        at, pieces = 0, []
        for ref in part:
            pieces.append((at, at + ref.shape[1], ref))
            at += ref.shape[1]
        ends.append(pieces)
    for low, high, beside in ends[0]:
        for start, stop, across in ends[1]:
            left, right = max(low, start), min(high, stop)
            if left < right:
                total = mine[:, left:right] + beside[:, left - low : right - low].astype(jnp.float32)
                total += across[:, left - start : right - start].astype(jnp.float32)
                out[:, left:right] = total.astype(out.dtype)


def combine(mine, beside, across):
    return pl.pallas_call(
        functools.partial(combine_kernel, (len(beside), len(across))),
        out_shape=jax.ShapeDtypeStruct(mine.shape, across[0].dtype),
        in_specs=[VMEM] * (1 + len(beside) + len(across)),
        out_specs=VMEM,
        compiler_params=LIMIT,
        name="combine",
    )(mine, *beside, *across)


def from_behind(block, axis, distance):
    devices = range(lax.axis_size(axis))
    route = [(i - distance, i) for i in devices if i - distance in devices]
    return lax.ppermute(block, axis, route)


def token_docs(doc_ids, start, count):
    blocks = (start + jnp.arange(count, dtype=jnp.int32)) // BLOCK
    table = blocks[:, None] == jnp.arange(doc_ids.shape[0], dtype=jnp.int32)[None, :]
    return jnp.sum(jnp.where(table, doc_ids[None, :], 0), axis=1)


def attend(carry, queries, q_docs, q_start, k_piece, v_piece, k_docs, k_start):
    peak, totals, accum = carry
    n_query = queries.shape[0]
    n_key = k_piece.shape[0]
    kv_heads = k_piece.shape[1] // HEAD_SIZE
    query_group = queries.shape[1] // k_piece.shape[1]
    q_heads = queries.reshape(n_query, kv_heads, query_group, HEAD_SIZE)
    k_heads = k_piece.reshape(n_key, kv_heads, HEAD_SIZE)
    v_heads = v_piece.reshape(n_key, kv_heads, HEAD_SIZE)
    scores = (
        jnp.einsum("qkgd,skd->kgqs", q_heads, k_heads, preferred_element_type=jnp.float32) * SCALE
    )
    q_pos = q_start + jnp.arange(n_query, dtype=jnp.int32)
    k_pos = k_start + jnp.arange(n_key, dtype=jnp.int32)
    allowed = (q_docs[:, None] == k_docs[None, :]) & (q_pos[:, None] >= k_pos[None, :])
    scores = jnp.where(allowed, scores, NEG)
    new_peak = jnp.maximum(peak, jnp.max(scores, axis=-1))
    shrink = jnp.exp(peak - new_peak)
    weights = jnp.exp(scores - new_peak[..., None])
    totals = totals * shrink + jnp.sum(weights, axis=-1)
    rounded = weights.astype(jnp.bfloat16)
    added = jnp.einsum("kgqs,skd->kgqd", rounded, v_heads, preferred_element_type=jnp.float32)
    accum = accum * shrink[..., None] + added
    return (new_peak, totals, accum)


def absorb_block(carry, queries, q_docs, q_start, k_piece, v_piece, k_start, doc_ids, flag):
    n_key = k_piece.shape[0]
    k_docs = token_docs(doc_ids, k_start, n_key)
    fresh = attend(carry, queries, q_docs, q_start, k_piece, v_piece, k_docs, k_start)
    return jax.tree.map(lambda new, old: jnp.where(flag, new, old), fresh, carry)


def ring_attention(queries, keys, values, doc_ids, n_ctx, position):
    n_query = queries.shape[0]
    q_start = position * n_query
    q_docs = token_docs(doc_ids, q_start, n_query)
    kv_heads = keys.shape[1] // HEAD_SIZE
    query_group = queries.shape[1] // keys.shape[1]
    carry = (
        jnp.full((kv_heads, query_group, n_query), NEG, jnp.float32),
        jnp.zeros((kv_heads, query_group, n_query), jnp.float32),
        jnp.zeros((kv_heads, query_group, n_query, HEAD_SIZE), jnp.float32),
    )
    always = jnp.array(True)
    carry = absorb_block(carry, queries, q_docs, q_start, keys, values, q_start, doc_ids, always)

    def turn_one(step, state):
        inner_state, moving = state
        moving = from_behind(moving, "ctx", 1)
        start = ((position - step) % n_ctx) * n_query
        inner_state = absorb_block(
            inner_state, queries, q_docs, q_start, moving[0], moving[1], start, doc_ids, always
        )
        return (inner_state, moving)

    _, totals, accum = lax.fori_loop(1, n_ctx, turn_one, (carry, jnp.stack((keys, values))))[0]
    result = accum / totals[..., None]
    return jnp.transpose(result, (2, 0, 1, 3)).reshape(queries.shape).astype(jnp.bfloat16)


def part_rows(attended, place):
    share = attended.shape[0] // 4
    rows = [lax.dynamic_slice_in_dim(attended, (place ^ flip) * share, share, 0) for flip in (2, 3, 0, 1)]
    return jnp.concatenate(rows[:2], axis=0), jnp.concatenate(rows[2:], axis=0)


def per_device(queries, keys, values, doc_ids, out_weight):
    n_ctx = lax.axis_size("ctx")
    heads = lax.axis_size("head")
    position = lax.axis_index("ctx")
    place = lax.axis_index("head")
    other_core = [(i, i ^ 1) for i in range(heads)]
    other_chip = [(i, i ^ 2) for i in range(heads)]
    columns = out_weight.shape[1]
    cut = columns * 4 // 7 // BLOCK * BLOCK

    if n_ctx == 8:
        by_two = [hop(x, "ctx", cycles(BY_TWO)) for x in (keys, values)]
        by_four = [hop(x, "ctx", cycles(BY_FOUR)) for x in (keys, values)]
        beside = [hop(x, "ctx", cycles(BESIDE)) for x in (keys, values)]
        info = describe(position, place, doc_ids, n_ctx)
        *state, fetched, weight = attend_first(
            info, queries, keys, values, out_weight, [beside], (0, 1)
        )
        by_two = [after(x, state) for x in by_two]
        swap_two = [hop(x, "ctx", cycles(BESIDE)) for x in by_two]
        state = attend_next(info, fetched, state, [by_two], (2,))
        by_four = [after(x, state) for x in by_four]
        swap_four = [hop(x, "ctx", cycles(BESIDE)) for x in by_four]
        state = attend_next(info, fetched, state, [by_four, swap_two], (3, 4))
        far, near, mine, send = attend_last(info, fetched, weight, state, [swap_four], (5,), (0, cut))
    else:
        weight = out_weight
        attended = ring_attention(queries, keys, values, doc_ids, n_ctx, position)
        far, near = part_rows(attended, place)
        mine, send = project(far, weight, (0, cut))
    theirs = hop(send, "head", other_core)
    later_mine, later_send = project(far, weight, (cut, columns))
    mine, later_mine = lax.optimization_barrier((mine, later_mine))
    first_sum = add_up(mine, theirs)
    first_part = hop(first_sum, "head", other_chip)
    later_theirs = hop(later_send, "head", other_core)
    later_mine, first_sum = lax.optimization_barrier((later_mine, first_sum))
    later_sum = add_up(later_mine, later_theirs)
    second_part = hop(later_sum, "head", other_chip)
    near, later_sum = lax.optimization_barrier((near, later_sum))
    mine, *sends = project(near, weight, (0, columns), 3)
    theirs = [hop(send, "head", other_core) for send in sends]
    return combine(mine, theirs, (first_part, second_part))


def solution(mesh):
    placed = (P("ctx", "head"), P("ctx", "head"), P("ctx", "head"), P(), P("head", None))
    return jax.shard_map(
        per_device, mesh=mesh, in_specs=placed, out_specs=P(("ctx", "head"), None), check_vma=False
    )
```

```python
import functools

import jax
import jax.numpy as jnp
from jax import lax
from jax.experimental import pallas as pl
from jax.experimental.pallas import tpu as pltpu
from jax.sharding import PartitionSpec as P

HEAD_SIZE = 128
BLOCK = 128
SCALE = 168.0 ** (-0.5)
LOG2E = 1.4426950408889634
NEG = -1e30
VMEM = pl.BlockSpec(memory_space=pltpu.VMEM)
SMEM = pl.BlockSpec(memory_space=pltpu.SMEM)
HBM = pl.BlockSpec(memory_space=pltpu.HBM)
LIMIT = pltpu.CompilerParams(vmem_limit_bytes=32 * 1024 * 1024)


def hop(block, axis, pairs):
    return lax.ppermute(block, axis, pairs)


def describe(position, place, doc_ids, n_ctx):
    first = n_ctx * 3 // 4
    in_first = position < first
    chunks = [
        (position, position >= 0),
        (position ^ 1, position % 2 == 1),
        (position - 2, in_first & (position >= 2)),
        (position - 4, in_first & (position >= 4)),
        ((position - 2) ^ 1, in_first & (position >= 2)),
        ((position - 4) ^ 1, in_first & (position >= 4)),
    ]
    numbers = [position, place]
    for source, there in chunks:
        numbers += [jnp.where(there, source, 0), there.astype(jnp.int32)]
    return jnp.concatenate([jnp.stack(numbers), doc_ids])


CHUNKS = 6
BESIDE = ((0, 1), (2, 3), (4, 5), (6, 7))
BY_TWO = ((0, 2, 4, 6), (1, 3, 5, 7))
BY_FOUR = ((0, 4, 6, 2), (1, 5, 7, 3))


def after(x, event):
    return lax.optimization_barrier((x, event))[0]


def cycles(rings):
    return [(ring[i], ring[(i + 1) % len(ring)]) for ring in rings for i in range(len(ring))]


def score_blocks(info, q, a, h, chunks, numbers):
    docs = 2 + 2 * CHUNKS
    position = info[0]
    rows = q.shape[0]
    n_query = chunks[0][0].shape[0]
    q_blocks = n_query // BLOCK
    doc = info[docs + position * q_blocks + a]
    row = lax.broadcasted_iota(jnp.int32, (rows, BLOCK), 0) % BLOCK
    col = lax.broadcasted_iota(jnp.int32, (rows, BLOCK), 1)
    scores = []
    for (keys, _), c in zip(chunks, numbers):
        count = (a + 1) * BLOCK if c == 0 else n_query
        k = keys[:count, h * HEAD_SIZE : (h + 1) * HEAD_SIZE]
        s = lax.dot_general(q, k, (((1,), (1,)), ((), ())), preferred_element_type=jnp.float32)
        source, there = info[2 + 2 * c], info[3 + 2 * c]
        for b in range(count // BLOCK):
            part = s[:, b * BLOCK : (b + 1) * BLOCK]
            if c == 0 and b == a:
                part = jnp.where(row >= col, part, NEG)
            else:
                seen = (info[docs + source * q_blocks + b] == doc) & (there == 1)
                part = part + jnp.where(seen, 0.0, NEG)
            scores.append(part)
    return scores


def weigh(scores, peak, factor, a, h, chunks, numbers):
    n_query = chunks[0][0].shape[0]
    total = added = None
    scores = list(scores)
    for (_, values), c in zip(chunks, numbers):
        count = (a + 1) * BLOCK if c == 0 else n_query
        parts = []
        for b in range(count // BLOCK):
            w = jnp.exp2(scores.pop(0) * factor - peak)
            total = w if total is None else total + w
            parts.append(w.astype(jnp.bfloat16))
        w = jnp.concatenate(parts, axis=1) if len(parts) > 1 else parts[0]
        v = values[:count, h * HEAD_SIZE : (h + 1) * HEAD_SIZE]
        term = jnp.dot(w, v, preferred_element_type=jnp.float32)
        added = term if added is None else added + term
    return total, added


def head_slices(queries, keys, h):
    group = queries.shape[1] // keys.shape[1]
    return [slice((h * group + g) * HEAD_SIZE, (h * group + g + 1) * HEAD_SIZE) for g in range(group)]


def absorb(numbers, info, queries, chunks, before, after):
    n_query = queries.shape[0]
    factor = SCALE * LOG2E
    at = 0
    for a in range(n_query // BLOCK):
        for h in range(chunks[0][0].shape[1] // HEAD_SIZE):
            heads = head_slices(queries, chunks[0][0], h)
            q = jnp.concatenate([queries[a * BLOCK : (a + 1) * BLOCK, s] for s in heads], axis=0)
            scores = score_blocks(info, q, a, h, chunks, numbers)
            rows = slice(at, at + q.shape[0])
            at += q.shape[0]
            peak = functools.reduce(jnp.maximum, scores)
            peak = jnp.max(peak, axis=1, keepdims=True) * factor
            if before is None:
                total, added = weigh(scores, peak, factor, a, h, chunks, numbers)
                peak = jnp.broadcast_to(peak, (q.shape[0], HEAD_SIZE))
            else:
                last = before[0][rows, :]
                peak = jnp.maximum(last, peak)
                shrink = jnp.exp2(last - peak)
                total, added = weigh(scores, peak, factor, a, h, chunks, numbers)
                total = total + before[1][rows, :] * shrink
                added = added + before[2][rows, :] * shrink
            after(a, heads, rows, peak, total, added)


def store_state(state):
    def after(a, heads, rows, *parts):
        for ref, part in zip(state, parts):
            ref[rows, :] = part

    return after


def pairs_of(refs):
    return list(zip(refs[0::2], refs[1::2]))


def first_kernel(numbers, cut, info, queries_in, keys_in, values_in, weight_in, *refs):
    *state, queries, weight, keys, values, sems = refs
    places = (
        (queries_in, queries),
        (keys_in, keys),
        (values_in, values),
        (weight_in.at[:, :cut], weight),
    )
    fetches = [pltpu.make_async_copy(a, b, sems.at[i]) for i, (a, b) in enumerate(places)]
    for fetch in fetches:
        fetch.start()
    for fetch in fetches[:3]:
        fetch.wait()
    absorb(numbers, info, queries, [(keys, values)], None, store_state(state))
    fetches[3].wait()


def next_kernel(numbers, cut, info, queries, *refs):
    if cut is not None:
        weight_in, *refs, weight, sem = refs
        fetch = pltpu.make_async_copy(weight_in.at[:, cut:], weight, sem)
        fetch.start()
    pairs = 2 * len(numbers)
    absorb(numbers, info, queries, pairs_of(refs[3 : 3 + pairs]), refs[:3], store_state(refs[3 + pairs :]))
    if cut is not None:
        fetch.wait()


def attend_cost(queries, numbers, fetched=0):
    n_query, width = queries.shape
    count = len(numbers) * n_query
    return pl.CostEstimate(
        flops=4 * n_query * width * count,
        bytes_accessed=fetched,
        transcendentals=n_query * count * width // HEAD_SIZE,
    )


def state_shapes(queries):
    rows = queries.size // HEAD_SIZE
    return (pltpu.VMEM((rows, HEAD_SIZE), jnp.float32),) * 3


def attend_first(info, queries, keys, values, weight, cut):
    part = pltpu.VMEM((weight.shape[0], cut), weight.dtype)
    return pl.pallas_call(
        functools.partial(first_kernel, (0,), cut),
        out_shape=state_shapes(queries) + (pltpu.VMEM(queries.shape, queries.dtype), part),
        in_specs=[SMEM, HBM, HBM, HBM, HBM],
        out_specs=(VMEM,) * 5,
        scratch_shapes=[
            pltpu.VMEM(keys.shape, keys.dtype),
            pltpu.VMEM(values.shape, values.dtype),
            pltpu.SemaphoreType.DMA((4,)),
        ],
        compiler_params=LIMIT,
        cost_estimate=attend_cost(queries, (0,), 2 * weight.size),
        name="attend_first",
    )(info, *[pltpu.with_memory_space_constraint(x, pltpu.HBM) for x in (queries, keys, values, weight)])


def attend_next(info, queries, state, chunks, numbers, weight=None, cut=None):
    fetched, shapes, scratch = [], state_shapes(queries), []
    if cut is not None:
        fetched = [pltpu.with_memory_space_constraint(weight, pltpu.HBM)]
        shapes += (pltpu.VMEM((weight.shape[0], weight.shape[1] - cut), weight.dtype),)
        scratch = [pltpu.SemaphoreType.DMA]
    return pl.pallas_call(
        functools.partial(next_kernel, numbers, cut),
        out_shape=shapes,
        in_specs=[SMEM, VMEM] + [HBM] * len(fetched) + [VMEM] * (3 + 2 * len(chunks)),
        out_specs=(VMEM,) * len(shapes),
        scratch_shapes=scratch,
        compiler_params=LIMIT,
        cost_estimate=attend_cost(queries, numbers),
        name="attend_next",
    )(info, queries, *fetched, *state, *[x for pair in chunks for x in pair])


def last_kernel(numbers, info, queries, weight, *refs):
    pairs = 2 * len(numbers)
    chunks = pairs_of(refs[3 : 3 + pairs])
    far, near, mine, send, attended = refs[3 + pairs :]

    def after(a, heads, rows, peak, total, added):
        result = (added / jnp.sum(total, axis=1, keepdims=True)).astype(jnp.bfloat16)
        for g, head in enumerate(heads):
            attended[a * BLOCK : (a + 1) * BLOCK, head] = result[g * BLOCK : (g + 1) * BLOCK]

    absorb(numbers, info, queries, chunks, refs[:3], after)
    place = info[1]
    share = queries.shape[0] // 4
    for half, owners in ((far, (place ^ 2, place ^ 3)), (near, (place, place ^ 1))):
        for i, owner in enumerate(owners):
            source = pl.ds(pl.multiple_of(owner * share, share), share)
            half[i * share : (i + 1) * share, :] = attended[source, :]
    project_columns(far, [weight], mine, (send,))


def attend_last(info, queries, weight, state, chunks, numbers):
    n_query, width = queries.shape
    half = jax.ShapeDtypeStruct((n_query // 2, width), jnp.bfloat16)
    return pl.pallas_call(
        functools.partial(last_kernel, numbers),
        out_shape=(half, half) + project_shapes(n_query // 4, weight.shape[1]),
        in_specs=[SMEM] + [VMEM] * (5 + 2 * len(numbers)),
        out_specs=(VMEM,) * 4,
        scratch_shapes=[pltpu.VMEM(queries.shape, jnp.bfloat16)],
        compiler_params=LIMIT,
        cost_estimate=attend_cost(queries, numbers),
        name="attend_last",
    )(info, queries, weight, *state, *[x for pair in chunks for x in pair])


def project_shapes(rows, count, sends=1):
    send = jax.ShapeDtypeStruct((rows, count // sends), jnp.bfloat16)
    return (jax.ShapeDtypeStruct((rows, count), jnp.float32),) + (send,) * sends


def project_columns(rows, weights, mine, sends):
    share = rows.shape[0] // 2
    width = sends[0].shape[1]
    ends = [0]
    for weight in weights:
        ends.append(ends[-1] + weight.shape[1])
    stops = sorted(set(ends) | {i * width for i in range(len(sends) + 1)} | set(range(0, ends[-1], 768)))
    for left, right in zip(stops[:-1], stops[1:]):
        i = max(i for i in range(len(weights)) if ends[i] <= left)
        columns = weights[i][:, left - ends[i] : right - ends[i]]
        product = jnp.dot(rows[...], columns, preferred_element_type=jnp.float32)
        mine[:, left:right] = product[:share]
        send, at = sends[left // width], left // width * width
        send[:, left - at : right - at] = product[share:].astype(send.dtype)


def project_kernel(count, rows, *refs):
    project_columns(rows, refs[:count], refs[count], refs[count + 1 :])


def project(rows, weights, sends=1):
    columns = sum(weight.shape[1] for weight in weights)
    return pl.pallas_call(
        functools.partial(project_kernel, len(weights)),
        out_shape=project_shapes(rows.shape[0] // 2, columns, sends),
        in_specs=[VMEM] * (1 + len(weights)),
        out_specs=(VMEM,) * (1 + sends),
        compiler_params=LIMIT,
        cost_estimate=pl.CostEstimate(
            flops=2 * rows.shape[0] * rows.shape[1] * columns, bytes_accessed=0, transcendentals=0
        ),
        name="project",
    )(rows, *weights)


def add_kernel(mine, theirs, out):
    out[...] = (mine[...] + theirs[...].astype(jnp.float32)).astype(out.dtype)


def add_up(mine, theirs):
    return pl.pallas_call(
        add_kernel,
        out_shape=jax.ShapeDtypeStruct(theirs.shape, theirs.dtype),
        in_specs=[VMEM, VMEM],
        out_specs=VMEM,
        compiler_params=LIMIT,
        cost_estimate=pl.CostEstimate(flops=theirs.size, bytes_accessed=0, transcendentals=0),
        name="add_up",
    )(mine, theirs)


def combine_kernel(counts, mine, *refs):
    out = refs[-1]
    ends = []
    for part in (refs[: counts[0]], refs[counts[0] : -1]):
        at, pieces = 0, []
        for ref in part:
            pieces.append((at, at + ref.shape[1], ref))
            at += ref.shape[1]
        ends.append(pieces)
    for low, high, beside in ends[0]:
        for start, stop, across in ends[1]:
            left, right = max(low, start), min(high, stop)
            if left < right:
                total = mine[:, left:right] + beside[:, left - low : right - low].astype(jnp.float32)
                total += across[:, left - start : right - start].astype(jnp.float32)
                out[:, left:right] = total.astype(out.dtype)


def combine(mine, beside, across):
    return pl.pallas_call(
        functools.partial(combine_kernel, (len(beside), len(across))),
        out_shape=jax.ShapeDtypeStruct(mine.shape, across[0].dtype),
        in_specs=[VMEM] * (1 + len(beside) + len(across)),
        out_specs=VMEM,
        compiler_params=LIMIT,
        name="combine",
    )(mine, *beside, *across)


def from_behind(block, axis, distance):
    devices = range(lax.axis_size(axis))
    route = [(i - distance, i) for i in devices if i - distance in devices]
    return lax.ppermute(block, axis, route)


def token_docs(doc_ids, start, count):
    blocks = (start + jnp.arange(count, dtype=jnp.int32)) // BLOCK
    table = blocks[:, None] == jnp.arange(doc_ids.shape[0], dtype=jnp.int32)[None, :]
    return jnp.sum(jnp.where(table, doc_ids[None, :], 0), axis=1)


def attend(carry, queries, q_docs, q_start, k_piece, v_piece, k_docs, k_start):
    peak, totals, accum = carry
    n_query = queries.shape[0]
    n_key = k_piece.shape[0]
    kv_heads = k_piece.shape[1] // HEAD_SIZE
    query_group = queries.shape[1] // k_piece.shape[1]
    q_heads = queries.reshape(n_query, kv_heads, query_group, HEAD_SIZE)
    k_heads = k_piece.reshape(n_key, kv_heads, HEAD_SIZE)
    v_heads = v_piece.reshape(n_key, kv_heads, HEAD_SIZE)
    scores = (
        jnp.einsum("qkgd,skd->kgqs", q_heads, k_heads, preferred_element_type=jnp.float32) * SCALE
    )
    q_pos = q_start + jnp.arange(n_query, dtype=jnp.int32)
    k_pos = k_start + jnp.arange(n_key, dtype=jnp.int32)
    allowed = (q_docs[:, None] == k_docs[None, :]) & (q_pos[:, None] >= k_pos[None, :])
    scores = jnp.where(allowed, scores, NEG)
    new_peak = jnp.maximum(peak, jnp.max(scores, axis=-1))
    shrink = jnp.exp(peak - new_peak)
    weights = jnp.exp(scores - new_peak[..., None])
    totals = totals * shrink + jnp.sum(weights, axis=-1)
    rounded = weights.astype(jnp.bfloat16)
    added = jnp.einsum("kgqs,skd->kgqd", rounded, v_heads, preferred_element_type=jnp.float32)
    accum = accum * shrink[..., None] + added
    return (new_peak, totals, accum)


def absorb_block(carry, queries, q_docs, q_start, k_piece, v_piece, k_start, doc_ids, flag):
    n_key = k_piece.shape[0]
    k_docs = token_docs(doc_ids, k_start, n_key)
    fresh = attend(carry, queries, q_docs, q_start, k_piece, v_piece, k_docs, k_start)
    return jax.tree.map(lambda new, old: jnp.where(flag, new, old), fresh, carry)


def ring_attention(queries, keys, values, doc_ids, n_ctx, position):
    n_query = queries.shape[0]
    q_start = position * n_query
    q_docs = token_docs(doc_ids, q_start, n_query)
    kv_heads = keys.shape[1] // HEAD_SIZE
    query_group = queries.shape[1] // keys.shape[1]
    carry = (
        jnp.full((kv_heads, query_group, n_query), NEG, jnp.float32),
        jnp.zeros((kv_heads, query_group, n_query), jnp.float32),
        jnp.zeros((kv_heads, query_group, n_query, HEAD_SIZE), jnp.float32),
    )
    always = jnp.array(True)
    carry = absorb_block(carry, queries, q_docs, q_start, keys, values, q_start, doc_ids, always)

    def turn_one(step, state):
        inner_state, moving = state
        moving = from_behind(moving, "ctx", 1)
        start = ((position - step) % n_ctx) * n_query
        inner_state = absorb_block(
            inner_state, queries, q_docs, q_start, moving[0], moving[1], start, doc_ids, always
        )
        return (inner_state, moving)

    _, totals, accum = lax.fori_loop(1, n_ctx, turn_one, (carry, jnp.stack((keys, values))))[0]
    result = accum / totals[..., None]
    return jnp.transpose(result, (2, 0, 1, 3)).reshape(queries.shape).astype(jnp.bfloat16)


def part_rows(attended, place):
    share = attended.shape[0] // 4
    rows = [lax.dynamic_slice_in_dim(attended, (place ^ flip) * share, share, 0) for flip in (2, 3, 0, 1)]
    return jnp.concatenate(rows[:2], axis=0), jnp.concatenate(rows[2:], axis=0)


def per_device(queries, keys, values, doc_ids, out_weight):
    n_ctx = lax.axis_size("ctx")
    heads = lax.axis_size("head")
    position = lax.axis_index("ctx")
    place = lax.axis_index("head")
    other_core = [(i, i ^ 1) for i in range(heads)]
    other_chip = [(i, i ^ 2) for i in range(heads)]
    columns = out_weight.shape[1]
    cut = columns * 4 // 7 // BLOCK * BLOCK

    if n_ctx == 8:
        info = describe(position, place, doc_ids, n_ctx)
        by_two = [hop(x, "ctx", cycles(BY_TWO)) for x in (keys, values)]
        beside = [hop(x, "ctx", cycles(BESIDE)) for x in (keys, values)]
        *state, fetched, weight_a = attend_first(info, queries, keys, values, out_weight, cut)
        later = [after(keys, state[0]), after(values, by_two[1])]
        by_four = [hop(x, "ctx", cycles(BY_FOUR)) for x in later]
        swap_two = [hop(x, "ctx", cycles(BESIDE)) for x in by_two]
        *state, weight_b = attend_next(
            info, fetched, state, [beside, by_two], (1, 2), out_weight, cut
        )
        swap_four = [
            hop(after(by_four[0], state[0]), "ctx", cycles(BESIDE)),
            hop(after(beside[1], by_two[1]), "ctx", cycles(BY_FOUR)),
        ]
        state = attend_next(info, fetched, state, [by_four, swap_two], (3, 4))
        far, near, mine, send = attend_last(info, fetched, weight_a, state, [swap_four], (5,))
    else:
        weight_a, weight_b = out_weight[:, :cut], out_weight[:, cut:]
        attended = ring_attention(queries, keys, values, doc_ids, n_ctx, position)
        far, near = part_rows(attended, place)
        mine, send = project(far, [weight_a])
    theirs = hop(send, "head", other_core)
    later_mine, later_send = project(far, [weight_b])
    mine, later_mine = lax.optimization_barrier((mine, later_mine))
    first_sum = add_up(mine, theirs)
    first_part = hop(first_sum, "head", other_chip)
    later_theirs = hop(later_send, "head", other_core)
    later_mine, first_sum = lax.optimization_barrier((later_mine, first_sum))
    later_sum = add_up(later_mine, later_theirs)
    second_part = hop(later_sum, "head", other_chip)
    near, later_sum = lax.optimization_barrier((near, later_sum))
    mine, *sends = project(near, [weight_a, weight_b], 3)
    theirs = [hop(send, "head", other_core) for send in sends]
    return combine(mine, theirs, (first_part, second_part))


def solution(mesh):
    placed = (P("ctx", "head"), P("ctx", "head"), P("ctx", "head"), P(), P("head", None))
    return jax.shard_map(
        per_device, mesh=mesh, in_specs=placed, out_specs=P(("ctx", "head"), None), check_vma=False
    )
```

```python
import functools

import jax
import jax.numpy as jnp
from jax import lax
from jax.experimental import pallas as pl
from jax.experimental.pallas import tpu as pltpu
from jax.sharding import PartitionSpec as P

HEAD_SIZE = 128
BLOCK = 128
SCALE = 168.0 ** (-0.5)
LOG2E = 1.4426950408889634
NEG = -1e30
VMEM = pl.BlockSpec(memory_space=pltpu.VMEM)
SMEM = pl.BlockSpec(memory_space=pltpu.SMEM)
HBM = pl.BlockSpec(memory_space=pltpu.HBM)
LIMIT = pltpu.CompilerParams(vmem_limit_bytes=32 * 1024 * 1024)


def hop(block, axis, pairs):
    return lax.ppermute(block, axis, pairs)


def chunk_source(number, position, n_ctx):
    first = n_ctx * 3 // 4
    in_first = position < first
    return (
        (position, None),
        (position ^ 1, position % 2 == 1),
        (position - 2, in_first & (position >= 2)),
        (position - 4, in_first & (position >= 4)),
        ((position - 2) ^ 1, in_first & (position >= 2)),
        ((position - 4) ^ 1, in_first & (position >= 4)),
    )[number]


BESIDE = ((0, 1), (2, 3), (4, 5), (6, 7))
BY_TWO = ((0, 2, 4, 6), (1, 3, 5, 7))
BY_FOUR = ((0, 4, 6, 2), (1, 5, 7, 3))


def after(x, event):
    return lax.optimization_barrier((x, event))[0]


def cycles(rings):
    return [(ring[i], ring[(i + 1) % len(ring)]) for ring in rings for i in range(len(ring))]


def score_blocks(docs, q, a, h, chunks, numbers):
    position = lax.axis_index("ctx")
    n_ctx = lax.axis_size("ctx")
    n_query = chunks[0][0].shape[0]
    q_blocks = n_query // BLOCK
    doc = docs[position * q_blocks + a]
    scores = []
    for (keys, _), c in zip(chunks, numbers):
        count = (a + 1) * BLOCK if c == 0 else n_query
        k = keys[:count, h * HEAD_SIZE : (h + 1) * HEAD_SIZE]
        s = lax.dot_general(q, k, (((1,), (1,)), ((), ())), preferred_element_type=jnp.float32)
        source, there = chunk_source(c, position, n_ctx)
        for b in range(count // BLOCK):
            part = s[:, b * BLOCK : (b + 1) * BLOCK]
            if c == 0 and b == a:
                row = lax.broadcasted_iota(jnp.int32, part.shape, 0) % BLOCK
                col = lax.broadcasted_iota(jnp.int32, part.shape, 1)
                part = jnp.where(row >= col, part, NEG)
            else:
                seen = docs[jnp.maximum(source, 0) * q_blocks + b] == doc
                if there is not None:
                    seen = seen & there
                part = part + jnp.where(seen, 0.0, NEG)
            scores.append(part)
    return scores


def weigh(scores, peak, factor, a, h, chunks, numbers):
    n_query = chunks[0][0].shape[0]
    total = added = None
    scores = list(scores)
    for (_, values), c in zip(chunks, numbers):
        count = (a + 1) * BLOCK if c == 0 else n_query
        parts = []
        for b in range(count // BLOCK):
            w = jnp.exp2(scores.pop(0) * factor - peak)
            total = w if total is None else total + w
            parts.append(w.astype(jnp.bfloat16))
        w = jnp.concatenate(parts, axis=1) if len(parts) > 1 else parts[0]
        v = values[:count, h * HEAD_SIZE : (h + 1) * HEAD_SIZE]
        term = jnp.dot(w, v, preferred_element_type=jnp.float32)
        added = term if added is None else added + term
    return total, added


def head_slices(queries, keys, h):
    group = queries.shape[1] // keys.shape[1]
    return [slice((h * group + g) * HEAD_SIZE, (h * group + g + 1) * HEAD_SIZE) for g in range(group)]


def absorb(numbers, docs, queries, chunks, before, after):
    n_query = queries.shape[0]
    factor = SCALE * LOG2E
    parts = []
    for a in range(n_query // BLOCK):
        for h in range(chunks[0][0].shape[1] // HEAD_SIZE):
            heads = head_slices(queries, chunks[0][0], h)
            size = len(heads) * BLOCK
            parts.append((a, h, heads, slice(len(parts) * size, (len(parts) + 1) * size)))
    scores = []
    for a, h, heads, _ in parts:
        q = jnp.concatenate([queries[a * BLOCK : (a + 1) * BLOCK, s] for s in heads], axis=0)
        scores.append(score_blocks(docs, q, a, h, chunks, numbers))
    peaks = [functools.reduce(jnp.maximum, s) for s in scores]
    peaks = [jnp.max(peak, axis=1, keepdims=True) * factor for peak in peaks]
    shrinks = None
    if before is None:
        peaks = [jnp.broadcast_to(peak, (peak.shape[0], HEAD_SIZE)) for peak in peaks]
    else:
        lasts = [before[0][rows, :] for _, _, _, rows in parts]
        peaks = [jnp.maximum(last, peak) for last, peak in zip(lasts, peaks)]
        shrinks = [jnp.exp2(last - peak) for last, peak in zip(lasts, peaks)]
    sums = [
        weigh(s, peak, factor, a, h, chunks, numbers)
        for s, peak, (a, h, _, _) in zip(scores, peaks, parts)
    ]
    for i, (a, h, heads, rows) in enumerate(parts):
        total, added = sums[i]
        if before is not None:
            total = total + before[1][rows, :] * shrinks[i]
            added = added + before[2][rows, :] * shrinks[i]
        sums[i] = (total, added)
    after(parts, peaks, sums)


def store_state(state):
    def after(parts, peaks, sums):
        for (_, _, _, rows), peak, (total, added) in zip(parts, peaks, sums):
            for ref, part in zip(state, (peak, total, added)):
                ref[rows, :] = part

    return after


def pairs_of(refs):
    return list(zip(refs[0::2], refs[1::2]))


def first_kernel(numbers, cut, docs, queries_in, keys_in, values_in, weight_in, *refs):
    *state, queries, weight, keys, values, sems = refs
    places = (
        (queries_in, queries),
        (keys_in, keys),
        (values_in, values),
        (weight_in.at[:, :cut], weight),
    )
    fetches = [pltpu.make_async_copy(a, b, sems.at[i]) for i, (a, b) in enumerate(places)]
    for fetch in fetches:
        fetch.start()
    for fetch in fetches[:3]:
        fetch.wait()
    absorb(numbers, docs, queries, [(keys, values)], None, store_state(state))
    fetches[3].wait()


def next_kernel(numbers, cut, docs, queries, *refs):
    if cut is not None:
        weight_in, *refs, weight, sem = refs
        fetch = pltpu.make_async_copy(weight_in.at[:, cut:], weight, sem)
        fetch.start()
    pairs = 2 * len(numbers)
    absorb(numbers, docs, queries, pairs_of(refs[3 : 3 + pairs]), refs[:3], store_state(refs[3 + pairs :]))
    if cut is not None:
        fetch.wait()


def attend_cost(queries, numbers, fetched=0):
    n_query, width = queries.shape
    count = len(numbers) * n_query
    return pl.CostEstimate(
        flops=4 * n_query * width * count,
        bytes_accessed=fetched,
        transcendentals=n_query * count * width // HEAD_SIZE,
    )


def state_shapes(queries):
    rows = queries.size // HEAD_SIZE
    return (pltpu.VMEM((rows, HEAD_SIZE), jnp.float32),) * 3


def attend_first(docs, queries, keys, values, weight, cut):
    part = pltpu.VMEM((weight.shape[0], cut), weight.dtype)
    return pl.pallas_call(
        functools.partial(first_kernel, (0,), cut),
        out_shape=state_shapes(queries) + (pltpu.VMEM(queries.shape, queries.dtype), part),
        in_specs=[SMEM, HBM, HBM, HBM, HBM],
        out_specs=(VMEM,) * 5,
        scratch_shapes=[
            pltpu.VMEM(keys.shape, keys.dtype),
            pltpu.VMEM(values.shape, values.dtype),
            pltpu.SemaphoreType.DMA((4,)),
        ],
        compiler_params=LIMIT,
        cost_estimate=attend_cost(queries, (0,), 2 * weight.size),
        name="attend_first",
    )(docs, *[pltpu.with_memory_space_constraint(x, pltpu.HBM) for x in (queries, keys, values, weight)])


def attend_next(docs, queries, state, chunks, numbers, weight=None, cut=None):
    fetched, shapes, scratch = [], state_shapes(queries), []
    if cut is not None:
        fetched = [pltpu.with_memory_space_constraint(weight, pltpu.HBM)]
        shapes += (pltpu.VMEM((weight.shape[0], weight.shape[1] - cut), weight.dtype),)
        scratch = [pltpu.SemaphoreType.DMA]
    return pl.pallas_call(
        functools.partial(next_kernel, numbers, cut),
        out_shape=shapes,
        in_specs=[SMEM, VMEM] + [HBM] * len(fetched) + [VMEM] * (3 + 2 * len(chunks)),
        out_specs=(VMEM,) * len(shapes),
        scratch_shapes=scratch,
        compiler_params=LIMIT,
        cost_estimate=attend_cost(queries, numbers),
        name="attend_next",
    )(docs, queries, *fetched, *state, *[x for pair in chunks for x in pair])


def last_kernel(numbers, docs, queries, weight, *refs):
    pairs = 2 * len(numbers)
    chunks = pairs_of(refs[3 : 3 + pairs])
    far, near, mine, send, attended = refs[3 + pairs :]

    def after(parts, peaks, sums):
        inverses = [1.0 / jnp.sum(total, axis=1, keepdims=True) for total, _ in sums]
        for (a, _, heads, _), inverse, (_, added) in zip(parts, inverses, sums):
            result = (added * inverse).astype(jnp.bfloat16)
            for g, head in enumerate(heads):
                attended[a * BLOCK : (a + 1) * BLOCK, head] = result[g * BLOCK : (g + 1) * BLOCK]

    absorb(numbers, docs, queries, chunks, refs[:3], after)
    place = lax.axis_index("head")
    share = queries.shape[0] // 4
    for half, owners in ((far, (place ^ 2, place ^ 3)), (near, (place, place ^ 1))):
        for i, owner in enumerate(owners):
            source = pl.ds(pl.multiple_of(owner * share, share), share)
            half[i * share : (i + 1) * share, :] = attended[source, :]
    project_columns(far, [weight], mine, (send,))


def attend_last(docs, queries, weight, state, chunks, numbers):
    n_query, width = queries.shape
    half = jax.ShapeDtypeStruct((n_query // 2, width), jnp.bfloat16)
    return pl.pallas_call(
        functools.partial(last_kernel, numbers),
        out_shape=(half, half) + project_shapes(n_query // 4, weight.shape[1]),
        in_specs=[SMEM] + [VMEM] * (5 + 2 * len(numbers)),
        out_specs=(VMEM,) * 4,
        scratch_shapes=[pltpu.VMEM(queries.shape, jnp.bfloat16)],
        compiler_params=LIMIT,
        cost_estimate=attend_cost(queries, numbers),
        name="attend_last",
    )(docs, queries, weight, *state, *[x for pair in chunks for x in pair])


def project_shapes(rows, count, sends=1):
    send = jax.ShapeDtypeStruct((rows, count // sends), jnp.bfloat16)
    return (jax.ShapeDtypeStruct((rows, count), jnp.float32),) + (send,) * sends


def project_columns(rows, weights, mine, sends):
    share = rows.shape[0] // 2
    width = sends[0].shape[1]
    ends = [0]
    for weight in weights:
        ends.append(ends[-1] + weight.shape[1])
    stops = sorted(set(ends) | {i * width for i in range(len(sends) + 1)} | set(range(0, ends[-1], 768)))
    for left, right in zip(stops[:-1], stops[1:]):
        i = max(i for i in range(len(weights)) if ends[i] <= left)
        columns = weights[i][:, left - ends[i] : right - ends[i]]
        product = jnp.dot(rows[...], columns, preferred_element_type=jnp.float32)
        mine[:, left:right] = product[:share]
        send, at = sends[left // width], left // width * width
        send[:, left - at : right - at] = product[share:].astype(send.dtype)


def project_kernel(count, rows, *refs):
    project_columns(rows, refs[:count], refs[count], refs[count + 1 :])


def project(rows, weights, sends=1):
    columns = sum(weight.shape[1] for weight in weights)
    return pl.pallas_call(
        functools.partial(project_kernel, len(weights)),
        out_shape=project_shapes(rows.shape[0] // 2, columns, sends),
        in_specs=[VMEM] * (1 + len(weights)),
        out_specs=(VMEM,) * (1 + sends),
        compiler_params=LIMIT,
        cost_estimate=pl.CostEstimate(
            flops=2 * rows.shape[0] * rows.shape[1] * columns, bytes_accessed=0, transcendentals=0
        ),
        name="project",
    )(rows, *weights)


def add_kernel(mine, theirs, out):
    out[...] = (mine[...] + theirs[...].astype(jnp.float32)).astype(out.dtype)


def add_up(mine, theirs):
    return pl.pallas_call(
        add_kernel,
        out_shape=jax.ShapeDtypeStruct(theirs.shape, theirs.dtype),
        in_specs=[VMEM, VMEM],
        out_specs=VMEM,
        compiler_params=LIMIT,
        cost_estimate=pl.CostEstimate(flops=theirs.size, bytes_accessed=0, transcendentals=0),
        name="add_up",
    )(mine, theirs)


def combine_kernel(at, mine, across, *refs):
    *beside, out, total, sem = refs
    width = across.shape[1]
    left = 0
    for part in beside[: len(beside) - (at > 0)]:
        low, high = max(left, at), min(left + part.shape[1], at + width)
        if low < high:
            piece = mine[:, low:high] + part[:, low - left : high - left].astype(jnp.float32)
            piece += across[:, low - at : high - at].astype(jnp.float32)
            total[:, low - at : high - at] = piece.astype(total.dtype)
        left += part.shape[1]
    copy = pltpu.make_async_copy(total, out.at[:, at : at + width], sem)
    copy.start()
    copy.wait()


def combine(mine, beside, across, at=0, out=None):
    outs = [] if out is None else [out]
    return pl.pallas_call(
        functools.partial(combine_kernel, at),
        out_shape=jax.ShapeDtypeStruct(mine.shape, across.dtype),
        in_specs=[VMEM] * (2 + len(beside)) + [HBM] * len(outs),
        out_specs=HBM,
        scratch_shapes=[pltpu.VMEM(across.shape, across.dtype), pltpu.SemaphoreType.DMA],
        input_output_aliases={2 + len(beside): 0} if outs else {},
        compiler_params=LIMIT,
        name="combine",
    )(mine, across, *beside, *outs)


def from_behind(block, axis, distance):
    devices = range(lax.axis_size(axis))
    route = [(i - distance, i) for i in devices if i - distance in devices]
    return lax.ppermute(block, axis, route)


def token_docs(doc_ids, start, count):
    blocks = (start + jnp.arange(count, dtype=jnp.int32)) // BLOCK
    table = blocks[:, None] == jnp.arange(doc_ids.shape[0], dtype=jnp.int32)[None, :]
    return jnp.sum(jnp.where(table, doc_ids[None, :], 0), axis=1)


def attend(carry, queries, q_docs, q_start, k_piece, v_piece, k_docs, k_start):
    peak, totals, accum = carry
    n_query = queries.shape[0]
    n_key = k_piece.shape[0]
    kv_heads = k_piece.shape[1] // HEAD_SIZE
    query_group = queries.shape[1] // k_piece.shape[1]
    q_heads = queries.reshape(n_query, kv_heads, query_group, HEAD_SIZE)
    k_heads = k_piece.reshape(n_key, kv_heads, HEAD_SIZE)
    v_heads = v_piece.reshape(n_key, kv_heads, HEAD_SIZE)
    scores = (
        jnp.einsum("qkgd,skd->kgqs", q_heads, k_heads, preferred_element_type=jnp.float32) * SCALE
    )
    q_pos = q_start + jnp.arange(n_query, dtype=jnp.int32)
    k_pos = k_start + jnp.arange(n_key, dtype=jnp.int32)
    allowed = (q_docs[:, None] == k_docs[None, :]) & (q_pos[:, None] >= k_pos[None, :])
    scores = jnp.where(allowed, scores, NEG)
    new_peak = jnp.maximum(peak, jnp.max(scores, axis=-1))
    shrink = jnp.exp(peak - new_peak)
    weights = jnp.exp(scores - new_peak[..., None])
    totals = totals * shrink + jnp.sum(weights, axis=-1)
    rounded = weights.astype(jnp.bfloat16)
    added = jnp.einsum("kgqs,skd->kgqd", rounded, v_heads, preferred_element_type=jnp.float32)
    accum = accum * shrink[..., None] + added
    return (new_peak, totals, accum)


def absorb_block(carry, queries, q_docs, q_start, k_piece, v_piece, k_start, doc_ids, flag):
    n_key = k_piece.shape[0]
    k_docs = token_docs(doc_ids, k_start, n_key)
    fresh = attend(carry, queries, q_docs, q_start, k_piece, v_piece, k_docs, k_start)
    return jax.tree.map(lambda new, old: jnp.where(flag, new, old), fresh, carry)


def ring_attention(queries, keys, values, doc_ids, n_ctx, position):
    n_query = queries.shape[0]
    q_start = position * n_query
    q_docs = token_docs(doc_ids, q_start, n_query)
    kv_heads = keys.shape[1] // HEAD_SIZE
    query_group = queries.shape[1] // keys.shape[1]
    carry = (
        jnp.full((kv_heads, query_group, n_query), NEG, jnp.float32),
        jnp.zeros((kv_heads, query_group, n_query), jnp.float32),
        jnp.zeros((kv_heads, query_group, n_query, HEAD_SIZE), jnp.float32),
    )
    always = jnp.array(True)
    carry = absorb_block(carry, queries, q_docs, q_start, keys, values, q_start, doc_ids, always)

    def turn_one(step, state):
        inner_state, moving = state
        moving = from_behind(moving, "ctx", 1)
        start = ((position - step) % n_ctx) * n_query
        inner_state = absorb_block(
            inner_state, queries, q_docs, q_start, moving[0], moving[1], start, doc_ids, always
        )
        return (inner_state, moving)

    _, totals, accum = lax.fori_loop(1, n_ctx, turn_one, (carry, jnp.stack((keys, values))))[0]
    result = accum / totals[..., None]
    return jnp.transpose(result, (2, 0, 1, 3)).reshape(queries.shape).astype(jnp.bfloat16)


def part_rows(attended, place):
    share = attended.shape[0] // 4
    rows = [lax.dynamic_slice_in_dim(attended, (place ^ flip) * share, share, 0) for flip in (2, 3, 0, 1)]
    return jnp.concatenate(rows[:2], axis=0), jnp.concatenate(rows[2:], axis=0)


def per_device(queries, keys, values, doc_ids, out_weight):
    n_ctx = lax.axis_size("ctx")
    heads = lax.axis_size("head")
    position = lax.axis_index("ctx")
    place = lax.axis_index("head")
    other_core = [(i, i ^ 1) for i in range(heads)]
    other_chip = [(i, i ^ 2) for i in range(heads)]
    columns = out_weight.shape[1]
    cut = columns * 4 // 7 // BLOCK * BLOCK

    if n_ctx == 8:
        by_two = [hop(x, "ctx", cycles(BY_TWO)) for x in (keys, values)]
        beside = [hop(x, "ctx", cycles(BESIDE)) for x in (keys, values)]
        *state, fetched, weight_a = attend_first(doc_ids, queries, keys, values, out_weight, cut)
        swap_two = [hop(after(x, state[0]), "ctx", cycles(BESIDE)) for x in by_two]
        four_keys = hop(keys, "ctx", cycles(BY_FOUR))
        four_values = hop(after(values, by_two[0]), "ctx", cycles(BY_FOUR))
        swap_four = [
            hop(four_keys, "ctx", cycles(BESIDE)),
            hop(after(beside[1], four_keys), "ctx", cycles(BY_FOUR)),
        ]
        *state, weight_b = attend_next(
            doc_ids,
            fetched,
            state,
            [beside, by_two, (four_keys, four_values), swap_two],
            (1, 2, 3, 4),
            out_weight,
            cut,
        )
        far, near, mine, send = attend_last(doc_ids, fetched, weight_a, state, [swap_four], (5,))
    else:
        weight_a, weight_b = out_weight[:, :cut], out_weight[:, cut:]
        attended = ring_attention(queries, keys, values, doc_ids, n_ctx, position)
        far, near = part_rows(attended, place)
        mine, send = project(far, [weight_a])
    theirs = hop(send, "head", other_core)
    later_mine, later_send = project(far, [weight_b])
    mine, later_mine = lax.optimization_barrier((mine, later_mine))
    first_sum = add_up(mine, theirs)
    first_part = hop(first_sum, "head", other_chip)
    later_theirs = hop(later_send, "head", other_core)
    later_mine, first_sum = lax.optimization_barrier((later_mine, first_sum))
    later_sum = add_up(later_mine, later_theirs)
    second_part = hop(later_sum, "head", other_chip)
    near, later_sum = lax.optimization_barrier((near, later_sum))
    mine, *sends = project(near, [weight_a, weight_b], 3)
    theirs = [hop(send, "head", other_core) for send in sends]
    out = combine(mine, theirs, first_part)
    return combine(mine, theirs, second_part, cut, out)


def solution(mesh):
    placed = (P("ctx", "head"), P("ctx", "head"), P("ctx", "head"), P(), P("head", None))
    return jax.shard_map(
        per_device, mesh=mesh, in_specs=placed, out_specs=P(("ctx", "head"), None), check_vma=False
    )
```

```python
import functools

import jax
import jax.numpy as jnp
from jax import lax
from jax.experimental import pallas as pl
from jax.experimental.pallas import tpu as pltpu
from jax.sharding import PartitionSpec as P

HEAD_SIZE = 128
BLOCK = 128
SCALE = 168.0 ** (-0.5)
LOG2E = 1.4426950408889634
NEG = -1e30
VMEM = pl.BlockSpec(memory_space=pltpu.VMEM)
SMEM = pl.BlockSpec(memory_space=pltpu.SMEM)
HBM = pl.BlockSpec(memory_space=pltpu.HBM)
LIMIT = pltpu.CompilerParams(vmem_limit_bytes=32 * 1024 * 1024)


def hop(block, axis, pairs):
    return lax.ppermute(block, axis, pairs)


def in_place(number, position, n_ctx):
    away = {2: 2, 3: 4, 4: 2, 5: 4}[number]
    return (position < n_ctx * 3 // 4) & (position >= away)


BESIDE = ((0, 1), (2, 3), (4, 5), (6, 7))
BY_TWO = ((0, 2, 4, 6), (1, 3, 5, 7))
BY_FOUR = ((0, 4, 6, 2), (1, 5, 7, 3))


def after(x, event):
    return lax.optimization_barrier((x, event))[0]


def cycles(rings):
    return [(ring[i], ring[(i + 1) % len(ring)]) for ring in rings for i in range(len(ring))]


def score_blocks(doors, q, a, h, chunks, numbers):
    position = lax.axis_index("ctx")
    n_ctx = lax.axis_size("ctx")
    n_query = chunks[0][0].shape[0]
    scores = []
    for (keys, _), c in zip(chunks, numbers):
        count = (a + 1) * BLOCK if c == 0 else n_query
        k = keys[:count, h * HEAD_SIZE : (h + 1) * HEAD_SIZE]
        s = lax.dot_general(q, k, (((1,), (1,)), ((), ())), preferred_element_type=jnp.float32)
        for b in range(count // BLOCK):
            part = s[:, b * BLOCK : (b + 1) * BLOCK]
            if c == 0 and b == a:
                row = lax.broadcasted_iota(jnp.int32, part.shape, 0) % BLOCK
                col = lax.broadcasted_iota(jnp.int32, part.shape, 1)
                part = jnp.where(row >= col, part, NEG)
            elif c < 2:
                part = part + doors(c, a, b)
            else:
                part = part + jnp.where(in_place(c, position, n_ctx), 0.0, NEG)
            scores.append(part)
    return scores


def weigh(scores, peak, factor, a, h, chunks, numbers):
    n_query = chunks[0][0].shape[0]
    total = added = None
    scores = list(scores)
    for (_, values), c in zip(chunks, numbers):
        count = (a + 1) * BLOCK if c == 0 else n_query
        parts = []
        for b in range(count // BLOCK):
            w = jnp.exp2(scores.pop(0) * factor - peak)
            total = w if total is None else total + w
            parts.append(w.astype(jnp.bfloat16))
        w = jnp.concatenate(parts, axis=1) if len(parts) > 1 else parts[0]
        v = values[:count, h * HEAD_SIZE : (h + 1) * HEAD_SIZE]
        term = jnp.dot(w, v, preferred_element_type=jnp.float32)
        added = term if added is None else added + term
    return total, added


def head_slices(queries, keys, h):
    group = queries.shape[1] // keys.shape[1]
    return [slice((h * group + g) * HEAD_SIZE, (h * group + g + 1) * HEAD_SIZE) for g in range(group)]


def absorb(numbers, doors, queries, chunks, before, after):
    n_query = queries.shape[0]
    factor = SCALE * LOG2E
    parts = []
    for a in range(n_query // BLOCK):
        for h in range(chunks[0][0].shape[1] // HEAD_SIZE):
            heads = head_slices(queries, chunks[0][0], h)
            size = len(heads) * BLOCK
            parts.append((a, h, heads, slice(len(parts) * size, (len(parts) + 1) * size)))
    scores = []
    for a, h, heads, _ in parts:
        q = jnp.concatenate([queries[a * BLOCK : (a + 1) * BLOCK, s] for s in heads], axis=0)
        scores.append(score_blocks(doors, q, a, h, chunks, numbers))
    peaks = [functools.reduce(jnp.maximum, s) for s in scores]
    peaks = [jnp.max(peak, axis=1, keepdims=True) * factor for peak in peaks]
    shrinks = None
    if before is None:
        peaks = [jnp.broadcast_to(peak, (peak.shape[0], HEAD_SIZE)) for peak in peaks]
    else:
        lasts = [before[0][rows, :] for _, _, _, rows in parts]
        peaks = [jnp.maximum(last, peak) for last, peak in zip(lasts, peaks)]
        shrinks = [jnp.exp2(last - peak) for last, peak in zip(lasts, peaks)]
    sums = [
        weigh(s, peak, factor, a, h, chunks, numbers)
        for s, peak, (a, h, _, _) in zip(scores, peaks, parts)
    ]
    for i, (a, h, heads, rows) in enumerate(parts):
        total, added = sums[i]
        if before is not None:
            total = total + before[1][rows, :] * shrinks[i]
            added = added + before[2][rows, :] * shrinks[i]
        sums[i] = (total, added)
    after(parts, peaks, sums)


def store_state(state):
    def after(parts, peaks, sums):
        for (_, _, _, rows), peak, (total, added) in zip(parts, peaks, sums):
            for ref, part in zip(state, (peak, total, added)):
                ref[rows, :] = part

    return after


def pairs_of(refs):
    return list(zip(refs[0::2], refs[1::2]))


def first_kernel(docs_in, queries_in, keys_in, values_in, *refs):
    *state, queries, open_beside, docs, keys, values, sems = refs
    places = ((docs_in, docs), (queries_in, queries), (keys_in, keys), (values_in, values))
    fetches = [pltpu.make_async_copy(a, b, sems.at[i]) for i, (a, b) in enumerate(places)]
    for fetch in fetches:
        fetch.start()
    for fetch in fetches:
        fetch.wait()
    position = lax.axis_index("ctx")
    q_blocks = queries.shape[0] // BLOCK

    def doors(number, a, b):
        source = position if number == 0 else jnp.maximum(position - 1, 0)
        seen = docs[source * q_blocks + b] == docs[position * q_blocks + a]
        if number == 1:
            seen = seen & (position % 2 == 1)
        return jnp.where(seen, 0.0, NEG)

    for a in range(q_blocks):
        for b in range(q_blocks):
            part = open_beside.at[a * 8 : (a + 1) * 8, b * BLOCK : (b + 1) * BLOCK]
            part[...] = jnp.full(part.shape, doors(1, a, b), jnp.float32)
    absorb((0,), doors, queries, [(keys, values)], None, store_state(state))


def next_kernel(numbers, queries, open_beside, weight_in, *refs):
    *refs, weight, sem = refs
    fetch = pltpu.make_async_copy(weight_in, weight, sem)
    fetch.start()
    pairs = 2 * len(numbers)

    def doors(number, a, b):
        return open_beside[a * 8 : a * 8 + 1, b * BLOCK : (b + 1) * BLOCK]

    absorb(numbers, doors, queries, pairs_of(refs[3 : 3 + pairs]), refs[:3], store_state(refs[3 + pairs :]))
    fetch.wait()


def attend_cost(queries, numbers, fetched=0):
    n_query, width = queries.shape
    count = len(numbers) * n_query
    return pl.CostEstimate(
        flops=4 * n_query * width * count,
        bytes_accessed=fetched,
        transcendentals=n_query * count * width // HEAD_SIZE,
    )


def state_shapes(queries):
    rows = queries.size // HEAD_SIZE
    return (pltpu.VMEM((rows, HEAD_SIZE), jnp.float32),) * 3


def attend_first(docs, queries, keys, values):
    n_query = queries.shape[0]
    return pl.pallas_call(
        first_kernel,
        out_shape=state_shapes(queries)
        + (
            pltpu.VMEM(queries.shape, queries.dtype),
            pltpu.VMEM((8 * n_query // BLOCK, n_query), jnp.float32),
        ),
        in_specs=[HBM] * 4,
        out_specs=(VMEM,) * 5,
        scratch_shapes=[
            pltpu.SMEM(docs.shape, docs.dtype),
            pltpu.VMEM(keys.shape, keys.dtype),
            pltpu.VMEM(values.shape, values.dtype),
            pltpu.SemaphoreType.DMA((4,)),
        ],
        compiler_params=LIMIT,
        cost_estimate=attend_cost(queries, (0,)),
        name="attend_first",
    )(*[pltpu.with_memory_space_constraint(x, pltpu.HBM) for x in (docs, queries, keys, values)])


def attend_next(queries, open_beside, weight, state, chunks, numbers):
    return pl.pallas_call(
        functools.partial(next_kernel, numbers),
        out_shape=state_shapes(queries) + (pltpu.VMEM(weight.shape, weight.dtype),),
        in_specs=[VMEM, VMEM, HBM] + [VMEM] * (3 + 2 * len(chunks)),
        out_specs=(VMEM,) * 4,
        scratch_shapes=[pltpu.SemaphoreType.DMA],
        compiler_params=LIMIT,
        cost_estimate=attend_cost(queries, numbers, 2 * weight.size),
        name="attend_next",
    )(
        queries,
        open_beside,
        pltpu.with_memory_space_constraint(weight, pltpu.HBM),
        *state,
        *[x for pair in chunks for x in pair],
    )


def last_kernel(numbers, columns, queries, weight, *refs):
    pairs = 2 * len(numbers)
    chunks = pairs_of(refs[3 : 3 + pairs])
    far, near, mine, send, attended = refs[3 + pairs :]

    def after(parts, peaks, sums):
        inverses = [1.0 / jnp.sum(total, axis=1, keepdims=True) for total, _ in sums]
        for (a, _, heads, _), inverse, (_, added) in zip(parts, inverses, sums):
            result = (added * inverse).astype(jnp.bfloat16)
            for g, head in enumerate(heads):
                attended[a * BLOCK : (a + 1) * BLOCK, head] = result[g * BLOCK : (g + 1) * BLOCK]

    absorb(numbers, None, queries, chunks, refs[:3], after)
    place = lax.axis_index("head")
    share = queries.shape[0] // 4
    for half, owners in ((far, (place ^ 2, place ^ 3)), (near, (place, place ^ 1))):
        for i, owner in enumerate(owners):
            source = pl.ds(pl.multiple_of(owner * share, share), share)
            half[i * share : (i + 1) * share, :] = attended[source, :]
    project_columns(far, weight, mine, (send,), *columns)


def attend_last(queries, weight, state, chunks, numbers, columns):
    n_query, width = queries.shape
    half = jax.ShapeDtypeStruct((n_query // 2, width), jnp.bfloat16)
    return pl.pallas_call(
        functools.partial(last_kernel, numbers, columns),
        out_shape=(half, half) + project_shapes(n_query // 4, columns[1] - columns[0]),
        in_specs=[VMEM] * (5 + 2 * len(numbers)),
        out_specs=(VMEM,) * 4,
        scratch_shapes=[pltpu.VMEM(queries.shape, jnp.bfloat16)],
        compiler_params=LIMIT,
        cost_estimate=attend_cost(queries, numbers),
        name="attend_last",
    )(queries, weight, *state, *[x for pair in chunks for x in pair])


def project_shapes(rows, count, sends=1):
    send = jax.ShapeDtypeStruct((rows, count // sends), jnp.bfloat16)
    return (jax.ShapeDtypeStruct((rows, count), jnp.float32),) + (send,) * sends


def project_columns(rows, weight, mine, sends, start, end):
    share = rows.shape[0] // 2
    width = sends[0].shape[1]
    for i, send in enumerate(sends):
        for at in range(0, width, 768):
            stop = min(at + 768, width)
            columns = weight[:, start + i * width + at : start + i * width + stop]
            product = jnp.dot(rows[...], columns, preferred_element_type=jnp.float32)
            mine[:, i * width + at : i * width + stop] = product[:share]
            send[:, at:stop] = product[share:].astype(send.dtype)


def project_kernel(columns, rows, weight, mine, *sends):
    project_columns(rows, weight, mine, sends, *columns)


def project(rows, weight, columns, sends=1):
    count = columns[1] - columns[0]
    return pl.pallas_call(
        functools.partial(project_kernel, columns),
        out_shape=project_shapes(rows.shape[0] // 2, count, sends),
        in_specs=[VMEM, VMEM],
        out_specs=(VMEM,) * (1 + sends),
        compiler_params=LIMIT,
        cost_estimate=pl.CostEstimate(
            flops=2 * rows.shape[0] * rows.shape[1] * count, bytes_accessed=0, transcendentals=0
        ),
        name="project",
    )(rows, weight)


def add_kernel(mine, theirs, out):
    out[...] = (mine[...] + theirs[...].astype(jnp.float32)).astype(out.dtype)


def add_up(mine, theirs):
    return pl.pallas_call(
        add_kernel,
        out_shape=jax.ShapeDtypeStruct(theirs.shape, theirs.dtype),
        in_specs=[VMEM, VMEM],
        out_specs=VMEM,
        compiler_params=LIMIT,
        cost_estimate=pl.CostEstimate(flops=theirs.size, bytes_accessed=0, transcendentals=0),
        name="add_up",
    )(mine, theirs)


def combine_kernel(at, mine, across, *refs):
    *beside, out, total, sem = refs
    width = across.shape[1]
    left = 0
    for part in beside[: len(beside) - (at > 0)]:
        low, high = max(left, at), min(left + part.shape[1], at + width)
        if low < high:
            piece = mine[:, low:high] + part[:, low - left : high - left].astype(jnp.float32)
            piece += across[:, low - at : high - at].astype(jnp.float32)
            total[:, low - at : high - at] = piece.astype(total.dtype)
        left += part.shape[1]
    copy = pltpu.make_async_copy(total, out.at[:, at : at + width], sem)
    copy.start()
    copy.wait()


def combine(mine, beside, across, at=0, out=None):
    outs = [] if out is None else [out]
    return pl.pallas_call(
        functools.partial(combine_kernel, at),
        out_shape=jax.ShapeDtypeStruct(mine.shape, across.dtype),
        in_specs=[VMEM] * (2 + len(beside)) + [HBM] * len(outs),
        out_specs=HBM,
        scratch_shapes=[pltpu.VMEM(across.shape, across.dtype), pltpu.SemaphoreType.DMA],
        input_output_aliases={2 + len(beside): 0} if outs else {},
        compiler_params=LIMIT,
        name="combine",
    )(mine, across, *beside, *outs)


def from_behind(block, axis, distance):
    devices = range(lax.axis_size(axis))
    route = [(i - distance, i) for i in devices if i - distance in devices]
    return lax.ppermute(block, axis, route)


def token_docs(doc_ids, start, count):
    blocks = (start + jnp.arange(count, dtype=jnp.int32)) // BLOCK
    table = blocks[:, None] == jnp.arange(doc_ids.shape[0], dtype=jnp.int32)[None, :]
    return jnp.sum(jnp.where(table, doc_ids[None, :], 0), axis=1)


def attend(carry, queries, q_docs, q_start, k_piece, v_piece, k_docs, k_start):
    peak, totals, accum = carry
    n_query = queries.shape[0]
    n_key = k_piece.shape[0]
    kv_heads = k_piece.shape[1] // HEAD_SIZE
    query_group = queries.shape[1] // k_piece.shape[1]
    q_heads = queries.reshape(n_query, kv_heads, query_group, HEAD_SIZE)
    k_heads = k_piece.reshape(n_key, kv_heads, HEAD_SIZE)
    v_heads = v_piece.reshape(n_key, kv_heads, HEAD_SIZE)
    scores = (
        jnp.einsum("qkgd,skd->kgqs", q_heads, k_heads, preferred_element_type=jnp.float32) * SCALE
    )
    q_pos = q_start + jnp.arange(n_query, dtype=jnp.int32)
    k_pos = k_start + jnp.arange(n_key, dtype=jnp.int32)
    allowed = (q_docs[:, None] == k_docs[None, :]) & (q_pos[:, None] >= k_pos[None, :])
    scores = jnp.where(allowed, scores, NEG)
    new_peak = jnp.maximum(peak, jnp.max(scores, axis=-1))
    shrink = jnp.exp(peak - new_peak)
    weights = jnp.exp(scores - new_peak[..., None])
    totals = totals * shrink + jnp.sum(weights, axis=-1)
    rounded = weights.astype(jnp.bfloat16)
    added = jnp.einsum("kgqs,skd->kgqd", rounded, v_heads, preferred_element_type=jnp.float32)
    accum = accum * shrink[..., None] + added
    return (new_peak, totals, accum)


def absorb_block(carry, queries, q_docs, q_start, k_piece, v_piece, k_start, doc_ids, flag):
    n_key = k_piece.shape[0]
    k_docs = token_docs(doc_ids, k_start, n_key)
    fresh = attend(carry, queries, q_docs, q_start, k_piece, v_piece, k_docs, k_start)
    return jax.tree.map(lambda new, old: jnp.where(flag, new, old), fresh, carry)


def ring_attention(queries, keys, values, doc_ids, n_ctx, position):
    n_query = queries.shape[0]
    q_start = position * n_query
    q_docs = token_docs(doc_ids, q_start, n_query)
    kv_heads = keys.shape[1] // HEAD_SIZE
    query_group = queries.shape[1] // keys.shape[1]
    carry = (
        jnp.full((kv_heads, query_group, n_query), NEG, jnp.float32),
        jnp.zeros((kv_heads, query_group, n_query), jnp.float32),
        jnp.zeros((kv_heads, query_group, n_query, HEAD_SIZE), jnp.float32),
    )
    always = jnp.array(True)
    carry = absorb_block(carry, queries, q_docs, q_start, keys, values, q_start, doc_ids, always)

    def turn_one(step, state):
        inner_state, moving = state
        moving = from_behind(moving, "ctx", 1)
        start = ((position - step) % n_ctx) * n_query
        inner_state = absorb_block(
            inner_state, queries, q_docs, q_start, moving[0], moving[1], start, doc_ids, always
        )
        return (inner_state, moving)

    _, totals, accum = lax.fori_loop(1, n_ctx, turn_one, (carry, jnp.stack((keys, values))))[0]
    result = accum / totals[..., None]
    return jnp.transpose(result, (2, 0, 1, 3)).reshape(queries.shape).astype(jnp.bfloat16)


def part_rows(attended, place):
    share = attended.shape[0] // 4
    rows = [lax.dynamic_slice_in_dim(attended, (place ^ flip) * share, share, 0) for flip in (2, 3, 0, 1)]
    return jnp.concatenate(rows[:2], axis=0), jnp.concatenate(rows[2:], axis=0)


def per_device(queries, keys, values, doc_ids, out_weight):
    n_ctx = lax.axis_size("ctx")
    heads = lax.axis_size("head")
    position = lax.axis_index("ctx")
    place = lax.axis_index("head")
    other_core = [(i, i ^ 1) for i in range(heads)]
    other_chip = [(i, i ^ 2) for i in range(heads)]
    columns = out_weight.shape[1]
    cut = columns * 4 // 7 // BLOCK * BLOCK

    if n_ctx == 8:
        by_two = [hop(x, "ctx", cycles(BY_TWO)) for x in (keys, values)]
        beside = [hop(x, "ctx", cycles(BESIDE)) for x in (keys, values)]
        *state, fetched, open_beside = attend_first(doc_ids, queries, keys, values)
        swap_two = [hop(after(x, state[0]), "ctx", cycles(BESIDE)) for x in by_two]
        four_keys = hop(after(after(keys, beside[0]), state[0]), "ctx", cycles(BY_FOUR))
        four_values = hop(after(values, by_two[0]), "ctx", cycles(BY_FOUR))
        swap_four = [
            hop(four_keys, "ctx", cycles(BESIDE)),
            hop(after(beside[1], four_keys), "ctx", cycles(BY_FOUR)),
        ]
        chunks = [beside, by_two, swap_two]
        *state, weight = attend_next(fetched, open_beside, out_weight, state, chunks, (1, 2, 4))
        chunks = [(four_keys, four_values), swap_four]
        far, near, mine, send = attend_last(fetched, weight, state, chunks, (3, 5), (0, cut))
    else:
        weight = out_weight
        attended = ring_attention(queries, keys, values, doc_ids, n_ctx, position)
        far, near = part_rows(attended, place)
        mine, send = project(far, weight, (0, cut))
    theirs = hop(send, "head", other_core)
    later_mine, later_send = project(far, weight, (cut, columns))
    mine, later_mine = lax.optimization_barrier((mine, later_mine))
    first_sum = add_up(mine, theirs)
    first_part = hop(first_sum, "head", other_chip)
    later_theirs = hop(later_send, "head", other_core)
    later_mine, first_sum = lax.optimization_barrier((later_mine, first_sum))
    later_sum = add_up(later_mine, later_theirs)
    second_part = hop(later_sum, "head", other_chip)
    near, later_sum = lax.optimization_barrier((near, later_sum))
    mine, *sends = project(near, weight, (0, columns), 3)
    theirs = [hop(send, "head", other_core) for send in sends]
    out = combine(mine, theirs, first_part)
    return combine(mine, theirs, second_part, cut, out)


def solution(mesh):
    placed = (P("ctx", "head"), P("ctx", "head"), P("ctx", "head"), P(), P("head", None))
    return jax.shard_map(
        per_device, mesh=mesh, in_specs=placed, out_specs=P(("ctx", "head"), None), check_vma=False
    )
```

```python
import functools

import jax
import jax.numpy as jnp
from jax import lax
from jax.experimental import pallas as pl
from jax.experimental.pallas import tpu as pltpu
from jax.sharding import PartitionSpec as P

HEAD_SIZE = 128
BLOCK = 128
SCALE = 168.0 ** (-0.5)
LOG2E = 1.4426950408889634
NEG = -1e30
VMEM = pl.BlockSpec(memory_space=pltpu.VMEM)
SMEM = pl.BlockSpec(memory_space=pltpu.SMEM)
HBM = pl.BlockSpec(memory_space=pltpu.HBM)
LIMIT = pltpu.CompilerParams(vmem_limit_bytes=32 * 1024 * 1024)


def hop(block, axis, pairs):
    return lax.ppermute(block, axis, pairs)


def in_place(number, position, n_ctx):
    away = {2: 2, 3: 4, 4: 2, 5: 4}[number]
    return (position < n_ctx * 3 // 4) & (position >= away)


BESIDE = ((0, 1), (2, 3), (4, 5), (6, 7))
BY_TWO = ((0, 2, 4), (1, 3, 5), (6,), (7,))
BY_FOUR = ((0, 4), (1, 5), (2,), (3,), (6,), (7,))


def after(x, event):
    return lax.optimization_barrier((x, event))[0]


def cycles(rings):
    return [(ring[i], ring[(i + 1) % len(ring)]) for ring in rings for i in range(len(ring))]


def score_blocks(doors, q, a, h, chunks, numbers):
    position = lax.axis_index("ctx")
    n_ctx = lax.axis_size("ctx")
    n_query = chunks[0][0].shape[0]
    scores = []
    for (keys, _), c in zip(chunks, numbers):
        count = (a + 1) * BLOCK if c == 0 else n_query
        k = keys[:count, h * HEAD_SIZE : (h + 1) * HEAD_SIZE]
        s = lax.dot_general(q, k, (((1,), (1,)), ((), ())), preferred_element_type=jnp.float32)
        for b in range(count // BLOCK):
            part = s[:, b * BLOCK : (b + 1) * BLOCK]
            if c == 0 and b == a:
                row = lax.broadcasted_iota(jnp.int32, part.shape, 0) % BLOCK
                col = lax.broadcasted_iota(jnp.int32, part.shape, 1)
                part = jnp.where(row >= col, part, NEG)
            elif c < 2:
                part = part + doors(c, a, b)
            else:
                part = part + jnp.where(in_place(c, position, n_ctx), 0.0, NEG)
            scores.append(part)
    return scores


def weigh(scores, peak, factor, a, h, chunks, numbers):
    n_query = chunks[0][0].shape[0]
    total = added = None
    scores = list(scores)
    for (_, values), c in zip(chunks, numbers):
        count = (a + 1) * BLOCK if c == 0 else n_query
        parts = []
        for b in range(count // BLOCK):
            w = jnp.exp2(scores.pop(0) * factor - peak)
            total = w if total is None else total + w
            parts.append(w.astype(jnp.bfloat16))
        w = jnp.concatenate(parts, axis=1) if len(parts) > 1 else parts[0]
        v = values[:count, h * HEAD_SIZE : (h + 1) * HEAD_SIZE]
        term = jnp.dot(w, v, preferred_element_type=jnp.float32)
        added = term if added is None else added + term
    return total, added


def head_slices(queries, keys, h):
    group = queries.shape[1] // keys.shape[1]
    return [slice((h * group + g) * HEAD_SIZE, (h * group + g + 1) * HEAD_SIZE) for g in range(group)]


def absorb(numbers, doors, queries, chunks, before, after):
    n_query = queries.shape[0]
    factor = SCALE * LOG2E
    parts = []
    for a in range(n_query // BLOCK):
        for h in range(chunks[0][0].shape[1] // HEAD_SIZE):
            heads = head_slices(queries, chunks[0][0], h)
            size = len(heads) * BLOCK
            parts.append((a, h, heads, slice(len(parts) * size, (len(parts) + 1) * size)))
    scores = []
    for a, h, heads, _ in parts:
        q = jnp.concatenate([queries[a * BLOCK : (a + 1) * BLOCK, s] for s in heads], axis=0)
        scores.append(score_blocks(doors, q, a, h, chunks, numbers))
    peaks = [functools.reduce(jnp.maximum, s) for s in scores]
    peaks = [jnp.max(peak, axis=1, keepdims=True) * factor for peak in peaks]
    shrinks = None
    if before is None:
        peaks = [jnp.broadcast_to(peak, (peak.shape[0], HEAD_SIZE)) for peak in peaks]
    else:
        lasts = [before[0][rows, :] for _, _, _, rows in parts]
        peaks = [jnp.maximum(last, peak) for last, peak in zip(lasts, peaks)]
        shrinks = [jnp.exp2(last - peak) for last, peak in zip(lasts, peaks)]
    sums = [
        weigh(s, peak, factor, a, h, chunks, numbers)
        for s, peak, (a, h, _, _) in zip(scores, peaks, parts)
    ]
    for i, (a, h, heads, rows) in enumerate(parts):
        total, added = sums[i]
        if before is not None:
            total = total + before[1][rows, :] * shrinks[i]
            added = added + before[2][rows, :] * shrinks[i]
        sums[i] = (total, added)
    after(parts, peaks, sums)


def store_state(state):
    def after(parts, peaks, sums):
        for (_, _, _, rows), peak, (total, added) in zip(parts, peaks, sums):
            for ref, part in zip(state, (peak, total, added)):
                ref[rows, :] = part

    return after


def pairs_of(refs):
    return list(zip(refs[0::2], refs[1::2]))


def first_kernel(docs_in, queries_in, keys_in, values_in, *refs):
    *state, queries, open_beside, docs, keys, values, sems = refs
    places = ((docs_in, docs), (queries_in, queries), (keys_in, keys), (values_in, values))
    fetches = [pltpu.make_async_copy(a, b, sems.at[i]) for i, (a, b) in enumerate(places)]
    for fetch in fetches:
        fetch.start()
    for fetch in fetches:
        fetch.wait()
    position = lax.axis_index("ctx")
    q_blocks = queries.shape[0] // BLOCK

    def doors(number, a, b):
        source = position if number == 0 else jnp.maximum(position - 1, 0)
        seen = docs[source * q_blocks + b] == docs[position * q_blocks + a]
        if number == 1:
            seen = seen & (position % 2 == 1)
        return jnp.where(seen, 0.0, NEG)

    for a in range(q_blocks):
        for b in range(q_blocks):
            part = open_beside.at[a * 8 : (a + 1) * 8, b * BLOCK : (b + 1) * BLOCK]
            part[...] = jnp.full(part.shape, doors(1, a, b), jnp.float32)
    absorb((0,), doors, queries, [(keys, values)], None, store_state(state))


def next_kernel(numbers, queries, open_beside, weight_in, *refs):
    *refs, weight, sem = refs
    fetch = pltpu.make_async_copy(weight_in, weight, sem)
    fetch.start()
    pairs = 2 * len(numbers)

    def doors(number, a, b):
        return open_beside[a * 8 : a * 8 + 1, b * BLOCK : (b + 1) * BLOCK]

    absorb(numbers, doors, queries, pairs_of(refs[3 : 3 + pairs]), refs[:3], store_state(refs[3 + pairs :]))
    fetch.wait()


def attend_cost(queries, numbers, fetched=0):
    n_query, width = queries.shape
    count = len(numbers) * n_query
    return pl.CostEstimate(
        flops=4 * n_query * width * count,
        bytes_accessed=fetched,
        transcendentals=n_query * count * width // HEAD_SIZE,
    )


def state_shapes(queries):
    rows = queries.size // HEAD_SIZE
    return (pltpu.VMEM((rows, HEAD_SIZE), jnp.float32),) * 3


def attend_first(docs, queries, keys, values):
    n_query = queries.shape[0]
    return pl.pallas_call(
        first_kernel,
        out_shape=state_shapes(queries)
        + (
            pltpu.VMEM(queries.shape, queries.dtype),
            pltpu.VMEM((8 * n_query // BLOCK, n_query), jnp.float32),
        ),
        in_specs=[HBM] * 4,
        out_specs=(VMEM,) * 5,
        scratch_shapes=[
            pltpu.SMEM(docs.shape, docs.dtype),
            pltpu.VMEM(keys.shape, keys.dtype),
            pltpu.VMEM(values.shape, values.dtype),
            pltpu.SemaphoreType.DMA((4,)),
        ],
        compiler_params=LIMIT,
        cost_estimate=attend_cost(queries, (0,)),
        name="attend_first",
    )(*[pltpu.with_memory_space_constraint(x, pltpu.HBM) for x in (docs, queries, keys, values)])


def attend_next(queries, open_beside, weight, state, chunks, numbers):
    return pl.pallas_call(
        functools.partial(next_kernel, numbers),
        out_shape=state_shapes(queries) + (pltpu.VMEM(weight.shape, weight.dtype),),
        in_specs=[VMEM, VMEM, HBM] + [VMEM] * (3 + 2 * len(chunks)),
        out_specs=(VMEM,) * 4,
        scratch_shapes=[pltpu.SemaphoreType.DMA],
        compiler_params=LIMIT,
        cost_estimate=attend_cost(queries, numbers, 2 * weight.size),
        name="attend_next",
    )(
        queries,
        open_beside,
        pltpu.with_memory_space_constraint(weight, pltpu.HBM),
        *state,
        *[x for pair in chunks for x in pair],
    )


def last_kernel(numbers, columns, queries, weight, *refs):
    pairs = 2 * len(numbers)
    chunks = pairs_of(refs[3 : 3 + pairs])
    far, near, mine, send, attended = refs[3 + pairs :]

    def after(parts, peaks, sums):
        inverses = [1.0 / jnp.sum(total, axis=1, keepdims=True) for total, _ in sums]
        for (a, _, heads, _), inverse, (_, added) in zip(parts, inverses, sums):
            result = (added * inverse).astype(jnp.bfloat16)
            for g, head in enumerate(heads):
                attended[a * BLOCK : (a + 1) * BLOCK, head] = result[g * BLOCK : (g + 1) * BLOCK]

    absorb(numbers, None, queries, chunks, refs[:3], after)
    place = lax.axis_index("head")
    share = queries.shape[0] // 4
    for half, owners in ((far, (place ^ 2, place ^ 3)), (near, (place, place ^ 1))):
        for i, owner in enumerate(owners):
            source = pl.ds(pl.multiple_of(owner * share, share), share)
            half[i * share : (i + 1) * share, :] = attended[source, :]
    project_columns(far, weight, mine, (send,), *columns)


def attend_last(queries, weight, state, chunks, numbers, columns):
    n_query, width = queries.shape
    half = jax.ShapeDtypeStruct((n_query // 2, width), jnp.bfloat16)
    return pl.pallas_call(
        functools.partial(last_kernel, numbers, columns),
        out_shape=(half, half) + project_shapes(n_query // 4, columns[1] - columns[0]),
        in_specs=[VMEM] * (5 + 2 * len(numbers)),
        out_specs=(VMEM,) * 4,
        scratch_shapes=[pltpu.VMEM(queries.shape, jnp.bfloat16)],
        compiler_params=LIMIT,
        cost_estimate=attend_cost(queries, numbers),
        name="attend_last",
    )(queries, weight, *state, *[x for pair in chunks for x in pair])


def project_shapes(rows, count, sends=1):
    send = jax.ShapeDtypeStruct((rows, count // sends), jnp.bfloat16)
    return (jax.ShapeDtypeStruct((rows, count), jnp.float32),) + (send,) * sends


def project_columns(rows, weight, mine, sends, start, end):
    share = rows.shape[0] // 2
    width = sends[0].shape[1]
    for i, send in enumerate(sends):
        for at in range(0, width, 768):
            stop = min(at + 768, width)
            columns = weight[:, start + i * width + at : start + i * width + stop]
            product = jnp.dot(rows[...], columns, preferred_element_type=jnp.float32)
            mine[:, i * width + at : i * width + stop] = product[:share]
            send[:, at:stop] = product[share:].astype(send.dtype)


def project_kernel(columns, rows, weight, mine, *sends):
    project_columns(rows, weight, mine, sends, *columns)


def project(rows, weight, columns, sends=1):
    count = columns[1] - columns[0]
    return pl.pallas_call(
        functools.partial(project_kernel, columns),
        out_shape=project_shapes(rows.shape[0] // 2, count, sends),
        in_specs=[VMEM, VMEM],
        out_specs=(VMEM,) * (1 + sends),
        compiler_params=LIMIT,
        cost_estimate=pl.CostEstimate(
            flops=2 * rows.shape[0] * rows.shape[1] * count, bytes_accessed=0, transcendentals=0
        ),
        name="project",
    )(rows, weight)


def add_kernel(mine, theirs, out):
    out[...] = (mine[...] + theirs[...].astype(jnp.float32)).astype(out.dtype)


def add_up(mine, theirs):
    return pl.pallas_call(
        add_kernel,
        out_shape=jax.ShapeDtypeStruct(theirs.shape, theirs.dtype),
        in_specs=[VMEM, VMEM],
        out_specs=VMEM,
        compiler_params=LIMIT,
        cost_estimate=pl.CostEstimate(flops=theirs.size, bytes_accessed=0, transcendentals=0),
        name="add_up",
    )(mine, theirs)


def combine_kernel(at, mine, across, *refs):
    *beside, out, total, sem = refs
    width = across.shape[1]
    left = 0
    for part in beside[: len(beside) - (at > 0)]:
        low, high = max(left, at), min(left + part.shape[1], at + width)
        if low < high:
            piece = mine[:, low:high] + part[:, low - left : high - left].astype(jnp.float32)
            piece += across[:, low - at : high - at].astype(jnp.float32)
            total[:, low - at : high - at] = piece.astype(total.dtype)
        left += part.shape[1]
    copy = pltpu.make_async_copy(total, out.at[:, at : at + width], sem)
    copy.start()
    copy.wait()


def combine(mine, beside, across, at=0, out=None):
    outs = [] if out is None else [out]
    return pl.pallas_call(
        functools.partial(combine_kernel, at),
        out_shape=jax.ShapeDtypeStruct(mine.shape, across.dtype),
        in_specs=[VMEM] * (2 + len(beside)) + [HBM] * len(outs),
        out_specs=HBM,
        scratch_shapes=[pltpu.VMEM(across.shape, across.dtype), pltpu.SemaphoreType.DMA],
        input_output_aliases={2 + len(beside): 0} if outs else {},
        compiler_params=LIMIT,
        name="combine",
    )(mine, across, *beside, *outs)


def from_behind(block, axis, distance):
    devices = range(lax.axis_size(axis))
    route = [(i - distance, i) for i in devices if i - distance in devices]
    return lax.ppermute(block, axis, route)


def token_docs(doc_ids, start, count):
    blocks = (start + jnp.arange(count, dtype=jnp.int32)) // BLOCK
    table = blocks[:, None] == jnp.arange(doc_ids.shape[0], dtype=jnp.int32)[None, :]
    return jnp.sum(jnp.where(table, doc_ids[None, :], 0), axis=1)


def attend(carry, queries, q_docs, q_start, k_piece, v_piece, k_docs, k_start):
    peak, totals, accum = carry
    n_query = queries.shape[0]
    n_key = k_piece.shape[0]
    kv_heads = k_piece.shape[1] // HEAD_SIZE
    query_group = queries.shape[1] // k_piece.shape[1]
    q_heads = queries.reshape(n_query, kv_heads, query_group, HEAD_SIZE)
    k_heads = k_piece.reshape(n_key, kv_heads, HEAD_SIZE)
    v_heads = v_piece.reshape(n_key, kv_heads, HEAD_SIZE)
    scores = (
        jnp.einsum("qkgd,skd->kgqs", q_heads, k_heads, preferred_element_type=jnp.float32) * SCALE
    )
    q_pos = q_start + jnp.arange(n_query, dtype=jnp.int32)
    k_pos = k_start + jnp.arange(n_key, dtype=jnp.int32)
    allowed = (q_docs[:, None] == k_docs[None, :]) & (q_pos[:, None] >= k_pos[None, :])
    scores = jnp.where(allowed, scores, NEG)
    new_peak = jnp.maximum(peak, jnp.max(scores, axis=-1))
    shrink = jnp.exp(peak - new_peak)
    weights = jnp.exp(scores - new_peak[..., None])
    totals = totals * shrink + jnp.sum(weights, axis=-1)
    rounded = weights.astype(jnp.bfloat16)
    added = jnp.einsum("kgqs,skd->kgqd", rounded, v_heads, preferred_element_type=jnp.float32)
    accum = accum * shrink[..., None] + added
    return (new_peak, totals, accum)


def absorb_block(carry, queries, q_docs, q_start, k_piece, v_piece, k_start, doc_ids, flag):
    n_key = k_piece.shape[0]
    k_docs = token_docs(doc_ids, k_start, n_key)
    fresh = attend(carry, queries, q_docs, q_start, k_piece, v_piece, k_docs, k_start)
    return jax.tree.map(lambda new, old: jnp.where(flag, new, old), fresh, carry)


def ring_attention(queries, keys, values, doc_ids, n_ctx, position):
    n_query = queries.shape[0]
    q_start = position * n_query
    q_docs = token_docs(doc_ids, q_start, n_query)
    kv_heads = keys.shape[1] // HEAD_SIZE
    query_group = queries.shape[1] // keys.shape[1]
    carry = (
        jnp.full((kv_heads, query_group, n_query), NEG, jnp.float32),
        jnp.zeros((kv_heads, query_group, n_query), jnp.float32),
        jnp.zeros((kv_heads, query_group, n_query, HEAD_SIZE), jnp.float32),
    )
    always = jnp.array(True)
    carry = absorb_block(carry, queries, q_docs, q_start, keys, values, q_start, doc_ids, always)

    def turn_one(step, state):
        inner_state, moving = state
        moving = from_behind(moving, "ctx", 1)
        start = ((position - step) % n_ctx) * n_query
        inner_state = absorb_block(
            inner_state, queries, q_docs, q_start, moving[0], moving[1], start, doc_ids, always
        )
        return (inner_state, moving)

    _, totals, accum = lax.fori_loop(1, n_ctx, turn_one, (carry, jnp.stack((keys, values))))[0]
    result = accum / totals[..., None]
    return jnp.transpose(result, (2, 0, 1, 3)).reshape(queries.shape).astype(jnp.bfloat16)


def part_rows(attended, place):
    share = attended.shape[0] // 4
    rows = [lax.dynamic_slice_in_dim(attended, (place ^ flip) * share, share, 0) for flip in (2, 3, 0, 1)]
    return jnp.concatenate(rows[:2], axis=0), jnp.concatenate(rows[2:], axis=0)


def per_device(queries, keys, values, doc_ids, out_weight):
    n_ctx = lax.axis_size("ctx")
    heads = lax.axis_size("head")
    position = lax.axis_index("ctx")
    place = lax.axis_index("head")
    other_core = [(i, i ^ 1) for i in range(heads)]
    other_chip = [(i, i ^ 2) for i in range(heads)]
    columns = out_weight.shape[1]
    cut = columns * 4 // 7 // BLOCK * BLOCK

    if n_ctx == 8:
        by_two = [hop(x, "ctx", cycles(BY_TWO)) for x in (keys, values)]
        beside = [hop(x, "ctx", cycles(BESIDE)) for x in (keys, values)]
        *state, fetched, open_beside = attend_first(doc_ids, queries, keys, values)
        swap_two = [hop(after(x, state[0]), "ctx", cycles(BESIDE)) for x in by_two]
        by_four = [after(after(x, beside[0]), state[0]) for x in (keys, values)]
        by_four = [hop(x, "ctx", cycles(BY_FOUR)) for x in by_four]
        beside_four = [hop(x, "ctx", cycles(BY_FOUR)) for x in beside]
        chunks = [beside, by_two, by_four]
        *state, weight = attend_next(fetched, open_beside, out_weight, state, chunks, (1, 2, 3))
        chunks = [swap_two, beside_four]
        far, near, mine, send = attend_last(fetched, weight, state, chunks, (4, 5), (0, cut))
    else:
        weight = out_weight
        attended = ring_attention(queries, keys, values, doc_ids, n_ctx, position)
        far, near = part_rows(attended, place)
        mine, send = project(far, weight, (0, cut))
    theirs = hop(send, "head", other_core)
    later_mine, later_send = project(far, weight, (cut, columns))
    mine, later_mine = lax.optimization_barrier((mine, later_mine))
    first_sum = add_up(mine, theirs)
    first_part = hop(first_sum, "head", other_chip)
    later_theirs = hop(later_send, "head", other_core)
    later_mine, first_sum = lax.optimization_barrier((later_mine, first_sum))
    later_sum = add_up(later_mine, later_theirs)
    second_part = hop(later_sum, "head", other_chip)
    near, later_sum = lax.optimization_barrier((near, later_sum))
    mine, *sends = project(near, weight, (0, columns), 3)
    theirs = [hop(send, "head", other_core) for send in sends]
    out = combine(mine, theirs, first_part)
    return combine(mine, theirs, second_part, cut, out)


def solution(mesh):
    placed = (P("ctx", "head"), P("ctx", "head"), P("ctx", "head"), P(), P("head", None))
    return jax.shard_map(
        per_device, mesh=mesh, in_specs=placed, out_specs=P(("ctx", "head"), None), check_vma=False
    )
```

```python
import functools

import jax
import jax.numpy as jnp
from jax import lax
from jax.experimental import pallas as pl
from jax.experimental.pallas import tpu as pltpu
from jax.sharding import PartitionSpec as P

HEAD_SIZE = 128
BLOCK = 128
SCALE = 168.0 ** (-0.5)
LOG2E = 1.4426950408889634
NEG = -1e30
VMEM = pl.BlockSpec(memory_space=pltpu.VMEM)
SMEM = pl.BlockSpec(memory_space=pltpu.SMEM)
HBM = pl.BlockSpec(memory_space=pltpu.HBM)
LIMIT = pltpu.CompilerParams(vmem_limit_bytes=32 * 1024 * 1024)


def hop(block, axis, pairs):
    return lax.ppermute(block, axis, pairs)


def in_place(number, position, n_ctx):
    away = {2: 2, 3: 4, 4: 2, 5: 4}[number]
    return (position < n_ctx * 3 // 4) & (position >= away)


BESIDE = ((0, 1), (2, 3), (4, 5), (6, 7))
BY_TWO = ((0, 2, 4, 6), (1, 3, 5, 7))
BY_FOUR = ((0, 4, 6, 2), (1, 5, 7, 3))


def after(x, event):
    return lax.optimization_barrier((x, event))[0]


def cycles(rings):
    return [(ring[i], ring[(i + 1) % len(ring)]) for ring in rings for i in range(len(ring))]


def score_blocks(doors, q, a, h, chunks, numbers):
    position = lax.axis_index("ctx")
    n_ctx = lax.axis_size("ctx")
    n_query = chunks[0][0].shape[0]
    scores = []
    for (keys, _), c in zip(chunks, numbers):
        count = (a + 1) * BLOCK if c == 0 else n_query
        k = keys[:count, h * HEAD_SIZE : (h + 1) * HEAD_SIZE]
        s = lax.dot_general(q, k, (((1,), (1,)), ((), ())), preferred_element_type=jnp.float32)
        for b in range(count // BLOCK):
            part = s[:, b * BLOCK : (b + 1) * BLOCK]
            if c == 0 and b == a:
                row = lax.broadcasted_iota(jnp.int32, part.shape, 0) % BLOCK
                col = lax.broadcasted_iota(jnp.int32, part.shape, 1)
                part = jnp.where(row >= col, part, NEG)
            elif c < 2:
                part = part + doors(c, a, b)
            else:
                part = part + jnp.where(in_place(c, position, n_ctx), 0.0, NEG)
            scores.append(part)
    return scores


def weigh(scores, peak, factor, a, h, chunks, numbers):
    n_query = chunks[0][0].shape[0]
    total = added = None
    scores = list(scores)
    for (_, values), c in zip(chunks, numbers):
        count = (a + 1) * BLOCK if c == 0 else n_query
        parts = []
        for b in range(count // BLOCK):
            w = jnp.exp2(scores.pop(0) * factor - peak)
            total = w if total is None else total + w
            parts.append(w.astype(jnp.bfloat16))
        w = jnp.concatenate(parts, axis=1) if len(parts) > 1 else parts[0]
        v = values[:count, h * HEAD_SIZE : (h + 1) * HEAD_SIZE]
        term = jnp.dot(w, v, preferred_element_type=jnp.float32)
        added = term if added is None else added + term
    return total, added


def head_slices(queries, keys, h):
    group = queries.shape[1] // keys.shape[1]
    return [slice((h * group + g) * HEAD_SIZE, (h * group + g + 1) * HEAD_SIZE) for g in range(group)]


def absorb(numbers, doors, queries, chunks, before, after):
    n_query = queries.shape[0]
    factor = SCALE * LOG2E
    parts = []
    for a in range(n_query // BLOCK):
        for h in range(chunks[0][0].shape[1] // HEAD_SIZE):
            heads = head_slices(queries, chunks[0][0], h)
            size = len(heads) * BLOCK
            parts.append((a, h, heads, slice(len(parts) * size, (len(parts) + 1) * size)))
    scores = []
    for a, h, heads, _ in parts:
        q = jnp.concatenate([queries[a * BLOCK : (a + 1) * BLOCK, s] for s in heads], axis=0)
        scores.append(score_blocks(doors, q, a, h, chunks, numbers))
    peaks = [functools.reduce(jnp.maximum, s) for s in scores]
    peaks = [jnp.max(peak, axis=1, keepdims=True) * factor for peak in peaks]
    shrinks = None
    if before is None:
        peaks = [jnp.broadcast_to(peak, (peak.shape[0], HEAD_SIZE)) for peak in peaks]
    else:
        lasts = [before[0][rows, :] for _, _, _, rows in parts]
        peaks = [jnp.maximum(last, peak) for last, peak in zip(lasts, peaks)]
        shrinks = [jnp.exp2(last - peak) for last, peak in zip(lasts, peaks)]
    sums = [
        weigh(s, peak, factor, a, h, chunks, numbers)
        for s, peak, (a, h, _, _) in zip(scores, peaks, parts)
    ]
    for i, (a, h, heads, rows) in enumerate(parts):
        total, added = sums[i]
        if before is not None:
            total = total + before[1][rows, :] * shrinks[i]
            added = added + before[2][rows, :] * shrinks[i]
        sums[i] = (total, added)
    after(parts, peaks, sums)


def store_state(state):
    def after(parts, peaks, sums):
        for (_, _, _, rows), peak, (total, added) in zip(parts, peaks, sums):
            for ref, part in zip(state, (peak, total, added)):
                ref[rows, :] = part

    return after


def pairs_of(refs):
    return list(zip(refs[0::2], refs[1::2]))


def first_kernel(docs_in, queries_in, keys_in, values_in, *refs):
    *state, queries, open_beside, docs, keys, values, sems = refs
    places = ((docs_in, docs), (queries_in, queries), (keys_in, keys), (values_in, values))
    fetches = [pltpu.make_async_copy(a, b, sems.at[i]) for i, (a, b) in enumerate(places)]
    for fetch in fetches:
        fetch.start()
    for fetch in fetches:
        fetch.wait()
    position = lax.axis_index("ctx")
    q_blocks = queries.shape[0] // BLOCK

    def doors(number, a, b):
        source = position if number == 0 else jnp.maximum(position - 1, 0)
        seen = docs[source * q_blocks + b] == docs[position * q_blocks + a]
        if number == 1:
            seen = seen & (position % 2 == 1)
        return jnp.where(seen, 0.0, NEG)

    for a in range(q_blocks):
        for b in range(q_blocks):
            part = open_beside.at[a * 8 : (a + 1) * 8, b * BLOCK : (b + 1) * BLOCK]
            part[...] = jnp.full(part.shape, doors(1, a, b), jnp.float32)
    absorb((0,), doors, queries, [(keys, values)], None, store_state(state))


def next_kernel(numbers, queries, open_beside, weight_in, *refs):
    *refs, weight, sem = refs
    fetch = pltpu.make_async_copy(weight_in, weight, sem)
    fetch.start()
    pairs = 2 * len(numbers)

    def doors(number, a, b):
        return open_beside[a * 8 : a * 8 + 1, b * BLOCK : (b + 1) * BLOCK]

    absorb(numbers, doors, queries, pairs_of(refs[3 : 3 + pairs]), refs[:3], store_state(refs[3 + pairs :]))
    fetch.wait()


def attend_cost(queries, numbers, fetched=0):
    n_query, width = queries.shape
    count = len(numbers) * n_query
    return pl.CostEstimate(
        flops=4 * n_query * width * count,
        bytes_accessed=fetched,
        transcendentals=n_query * count * width // HEAD_SIZE,
    )


def state_shapes(queries):
    rows = queries.size // HEAD_SIZE
    return (pltpu.VMEM((rows, HEAD_SIZE), jnp.float32),) * 3


def attend_first(docs, queries, keys, values):
    n_query = queries.shape[0]
    return pl.pallas_call(
        first_kernel,
        out_shape=state_shapes(queries)
        + (
            pltpu.VMEM(queries.shape, queries.dtype),
            pltpu.VMEM((8 * n_query // BLOCK, n_query), jnp.float32),
        ),
        in_specs=[HBM] * 4,
        out_specs=(VMEM,) * 5,
        scratch_shapes=[
            pltpu.SMEM(docs.shape, docs.dtype),
            pltpu.VMEM(keys.shape, keys.dtype),
            pltpu.VMEM(values.shape, values.dtype),
            pltpu.SemaphoreType.DMA((4,)),
        ],
        compiler_params=LIMIT,
        cost_estimate=attend_cost(queries, (0,)),
        name="attend_first",
    )(*[pltpu.with_memory_space_constraint(x, pltpu.HBM) for x in (docs, queries, keys, values)])


def attend_next(queries, open_beside, weight, state, chunks, numbers):
    return pl.pallas_call(
        functools.partial(next_kernel, numbers),
        out_shape=state_shapes(queries) + (pltpu.VMEM(weight.shape, weight.dtype),),
        in_specs=[VMEM, VMEM, HBM] + [VMEM] * (3 + 2 * len(chunks)),
        out_specs=(VMEM,) * 4,
        scratch_shapes=[pltpu.SemaphoreType.DMA],
        compiler_params=LIMIT,
        cost_estimate=attend_cost(queries, numbers, 2 * weight.size),
        name="attend_next",
    )(
        queries,
        open_beside,
        pltpu.with_memory_space_constraint(weight, pltpu.HBM),
        *state,
        *[x for pair in chunks for x in pair],
    )


def last_kernel(numbers, columns, queries, weight, *refs):
    pairs = 2 * len(numbers)
    chunks = pairs_of(refs[3 : 3 + pairs])
    far, near, mine, send, attended = refs[3 + pairs :]

    def after(parts, peaks, sums):
        inverses = [1.0 / jnp.sum(total, axis=1, keepdims=True) for total, _ in sums]
        for (a, _, heads, _), inverse, (_, added) in zip(parts, inverses, sums):
            result = (added * inverse).astype(jnp.bfloat16)
            for g, head in enumerate(heads):
                attended[a * BLOCK : (a + 1) * BLOCK, head] = result[g * BLOCK : (g + 1) * BLOCK]

    absorb(numbers, None, queries, chunks, refs[:3], after)
    place = lax.axis_index("head")
    share = queries.shape[0] // 4
    for half, owners in ((far, (place ^ 2, place ^ 3)), (near, (place, place ^ 1))):
        for i, owner in enumerate(owners):
            source = pl.ds(pl.multiple_of(owner * share, share), share)
            half[i * share : (i + 1) * share, :] = attended[source, :]
    project_columns(far, weight, mine, (send,), *columns)


def attend_last(queries, weight, state, chunks, numbers, columns):
    n_query, width = queries.shape
    half = jax.ShapeDtypeStruct((n_query // 2, width), jnp.bfloat16)
    return pl.pallas_call(
        functools.partial(last_kernel, numbers, columns),
        out_shape=(half, half) + project_shapes(n_query // 4, columns[1] - columns[0]),
        in_specs=[VMEM] * (5 + 2 * len(numbers)),
        out_specs=(VMEM,) * 4,
        scratch_shapes=[pltpu.VMEM(queries.shape, jnp.bfloat16)],
        compiler_params=LIMIT,
        cost_estimate=attend_cost(queries, numbers),
        name="attend_last",
    )(queries, weight, *state, *[x for pair in chunks for x in pair])


def project_shapes(rows, count, sends=1):
    send = jax.ShapeDtypeStruct((rows, count // sends), jnp.bfloat16)
    return (jax.ShapeDtypeStruct((rows, count), jnp.float32),) + (send,) * sends


def project_columns(rows, weight, mine, sends, start, end):
    share = rows.shape[0] // 2
    width = sends[0].shape[1]
    for i, send in enumerate(sends):
        for at in range(0, width, 768):
            stop = min(at + 768, width)
            columns = weight[:, start + i * width + at : start + i * width + stop]
            product = jnp.dot(rows[...], columns, preferred_element_type=jnp.float32)
            mine[:, i * width + at : i * width + stop] = product[:share]
            send[:, at:stop] = product[share:].astype(send.dtype)


def project_kernel(columns, rows, weight, mine, *sends):
    project_columns(rows, weight, mine, sends, *columns)


def project(rows, weight, columns, sends=1):
    count = columns[1] - columns[0]
    return pl.pallas_call(
        functools.partial(project_kernel, columns),
        out_shape=project_shapes(rows.shape[0] // 2, count, sends),
        in_specs=[VMEM, VMEM],
        out_specs=(VMEM,) * (1 + sends),
        compiler_params=LIMIT,
        cost_estimate=pl.CostEstimate(
            flops=2 * rows.shape[0] * rows.shape[1] * count, bytes_accessed=0, transcendentals=0
        ),
        name="project",
    )(rows, weight)


def add_kernel(mine, theirs, out):
    out[...] = (mine[...] + theirs[...].astype(jnp.float32)).astype(out.dtype)


def add_up(mine, theirs):
    return pl.pallas_call(
        add_kernel,
        out_shape=jax.ShapeDtypeStruct(theirs.shape, theirs.dtype),
        in_specs=[VMEM, VMEM],
        out_specs=VMEM,
        compiler_params=LIMIT,
        cost_estimate=pl.CostEstimate(flops=theirs.size, bytes_accessed=0, transcendentals=0),
        name="add_up",
    )(mine, theirs)


def combine_kernel(at, mine, across, *refs):
    *beside, out, total, sem = refs
    width = across.shape[1]
    left = 0
    for part in beside[: len(beside) - (at > 0)]:
        low, high = max(left, at), min(left + part.shape[1], at + width)
        if low < high:
            piece = mine[:, low:high] + part[:, low - left : high - left].astype(jnp.float32)
            piece += across[:, low - at : high - at].astype(jnp.float32)
            total[:, low - at : high - at] = piece.astype(total.dtype)
        left += part.shape[1]
    copy = pltpu.make_async_copy(total, out.at[:, at : at + width], sem)
    copy.start()
    copy.wait()


def combine(mine, beside, across, at=0, out=None):
    outs = [] if out is None else [out]
    return pl.pallas_call(
        functools.partial(combine_kernel, at),
        out_shape=jax.ShapeDtypeStruct(mine.shape, across.dtype),
        in_specs=[VMEM] * (2 + len(beside)) + [HBM] * len(outs),
        out_specs=HBM,
        scratch_shapes=[pltpu.VMEM(across.shape, across.dtype), pltpu.SemaphoreType.DMA],
        input_output_aliases={2 + len(beside): 0} if outs else {},
        compiler_params=LIMIT,
        name="combine",
    )(mine, across, *beside, *outs)


def from_behind(block, axis, distance):
    devices = range(lax.axis_size(axis))
    route = [(i - distance, i) for i in devices if i - distance in devices]
    return lax.ppermute(block, axis, route)


def token_docs(doc_ids, start, count):
    blocks = (start + jnp.arange(count, dtype=jnp.int32)) // BLOCK
    table = blocks[:, None] == jnp.arange(doc_ids.shape[0], dtype=jnp.int32)[None, :]
    return jnp.sum(jnp.where(table, doc_ids[None, :], 0), axis=1)


def attend(carry, queries, q_docs, q_start, k_piece, v_piece, k_docs, k_start):
    peak, totals, accum = carry
    n_query = queries.shape[0]
    n_key = k_piece.shape[0]
    kv_heads = k_piece.shape[1] // HEAD_SIZE
    query_group = queries.shape[1] // k_piece.shape[1]
    q_heads = queries.reshape(n_query, kv_heads, query_group, HEAD_SIZE)
    k_heads = k_piece.reshape(n_key, kv_heads, HEAD_SIZE)
    v_heads = v_piece.reshape(n_key, kv_heads, HEAD_SIZE)
    scores = (
        jnp.einsum("qkgd,skd->kgqs", q_heads, k_heads, preferred_element_type=jnp.float32) * SCALE
    )
    q_pos = q_start + jnp.arange(n_query, dtype=jnp.int32)
    k_pos = k_start + jnp.arange(n_key, dtype=jnp.int32)
    allowed = (q_docs[:, None] == k_docs[None, :]) & (q_pos[:, None] >= k_pos[None, :])
    scores = jnp.where(allowed, scores, NEG)
    new_peak = jnp.maximum(peak, jnp.max(scores, axis=-1))
    shrink = jnp.exp(peak - new_peak)
    weights = jnp.exp(scores - new_peak[..., None])
    totals = totals * shrink + jnp.sum(weights, axis=-1)
    rounded = weights.astype(jnp.bfloat16)
    added = jnp.einsum("kgqs,skd->kgqd", rounded, v_heads, preferred_element_type=jnp.float32)
    accum = accum * shrink[..., None] + added
    return (new_peak, totals, accum)


def absorb_block(carry, queries, q_docs, q_start, k_piece, v_piece, k_start, doc_ids, flag):
    n_key = k_piece.shape[0]
    k_docs = token_docs(doc_ids, k_start, n_key)
    fresh = attend(carry, queries, q_docs, q_start, k_piece, v_piece, k_docs, k_start)
    return jax.tree.map(lambda new, old: jnp.where(flag, new, old), fresh, carry)


def ring_attention(queries, keys, values, doc_ids, n_ctx, position):
    n_query = queries.shape[0]
    q_start = position * n_query
    q_docs = token_docs(doc_ids, q_start, n_query)
    kv_heads = keys.shape[1] // HEAD_SIZE
    query_group = queries.shape[1] // keys.shape[1]
    carry = (
        jnp.full((kv_heads, query_group, n_query), NEG, jnp.float32),
        jnp.zeros((kv_heads, query_group, n_query), jnp.float32),
        jnp.zeros((kv_heads, query_group, n_query, HEAD_SIZE), jnp.float32),
    )
    always = jnp.array(True)
    carry = absorb_block(carry, queries, q_docs, q_start, keys, values, q_start, doc_ids, always)

    def turn_one(step, state):
        inner_state, moving = state
        moving = from_behind(moving, "ctx", 1)
        start = ((position - step) % n_ctx) * n_query
        inner_state = absorb_block(
            inner_state, queries, q_docs, q_start, moving[0], moving[1], start, doc_ids, always
        )
        return (inner_state, moving)

    _, totals, accum = lax.fori_loop(1, n_ctx, turn_one, (carry, jnp.stack((keys, values))))[0]
    result = accum / totals[..., None]
    return jnp.transpose(result, (2, 0, 1, 3)).reshape(queries.shape).astype(jnp.bfloat16)


def part_rows(attended, place):
    share = attended.shape[0] // 4
    rows = [lax.dynamic_slice_in_dim(attended, (place ^ flip) * share, share, 0) for flip in (2, 3, 0, 1)]
    return jnp.concatenate(rows[:2], axis=0), jnp.concatenate(rows[2:], axis=0)


def per_device(queries, keys, values, doc_ids, out_weight):
    n_ctx = lax.axis_size("ctx")
    heads = lax.axis_size("head")
    position = lax.axis_index("ctx")
    place = lax.axis_index("head")
    other_core = [(i, i ^ 1) for i in range(heads)]
    other_chip = [(i, i ^ 2) for i in range(heads)]
    columns = out_weight.shape[1]
    cut = columns * 4 // 7 // BLOCK * BLOCK

    if n_ctx == 8:
        by_two = [hop(x, "ctx", cycles(BY_TWO)) for x in (keys, values)]
        beside = [hop(x, "ctx", cycles(BESIDE)) for x in (keys, values)]
        *state, fetched, open_beside = attend_first(doc_ids, queries, keys, values)
        swap_two = [hop(after(x, state[0]), "ctx", cycles(BESIDE)) for x in by_two]
        by_four = [after(after(x, beside[0]), state[0]) for x in (keys, values)]
        by_four = [hop(x, "ctx", cycles(BY_FOUR)) for x in by_four]
        beside_four = [hop(x, "ctx", cycles(BY_FOUR)) for x in beside]
        chunks = [beside, by_two, by_four]
        *state, weight = attend_next(fetched, open_beside, out_weight, state, chunks, (1, 2, 3))
        chunks = [swap_two, beside_four]
        far, near, mine, send = attend_last(fetched, weight, state, chunks, (4, 5), (0, cut))
    else:
        weight = out_weight
        attended = ring_attention(queries, keys, values, doc_ids, n_ctx, position)
        far, near = part_rows(attended, place)
        mine, send = project(far, weight, (0, cut))
    theirs = hop(send, "head", other_core)
    later_mine, later_send = project(far, weight, (cut, columns))
    mine, later_mine = lax.optimization_barrier((mine, later_mine))
    first_sum = add_up(mine, theirs)
    first_part = hop(first_sum, "head", other_chip)
    later_theirs = hop(later_send, "head", other_core)
    later_mine, first_sum = lax.optimization_barrier((later_mine, first_sum))
    later_sum = add_up(later_mine, later_theirs)
    second_part = hop(later_sum, "head", other_chip)
    near, later_sum = lax.optimization_barrier((near, later_sum))
    mine, *sends = project(near, weight, (0, columns), 3)
    theirs = [hop(send, "head", other_core) for send in sends]
    out = combine(mine, theirs, first_part)
    return combine(mine, theirs, second_part, cut, out)


def solution(mesh):
    placed = (P("ctx", "head"), P("ctx", "head"), P("ctx", "head"), P(), P("head", None))
    return jax.shard_map(
        per_device, mesh=mesh, in_specs=placed, out_specs=P(("ctx", "head"), None), check_vma=False
    )
```

```python
import functools

import jax
import jax.numpy as jnp
from jax import lax
from jax.experimental import pallas as pl
from jax.experimental.pallas import tpu as pltpu
from jax.sharding import PartitionSpec as P

HEAD_SIZE = 128
BLOCK = 128
SCALE = 168.0 ** (-0.5)
LOG2E = 1.4426950408889634
NEG = -1e30
VMEM = pl.BlockSpec(memory_space=pltpu.VMEM)
SMEM = pl.BlockSpec(memory_space=pltpu.SMEM)
HBM = pl.BlockSpec(memory_space=pltpu.HBM)
LIMIT = pltpu.CompilerParams(vmem_limit_bytes=32 * 1024 * 1024)


def hop(block, axis, pairs):
    return lax.ppermute(block, axis, pairs)


def in_place(number, position, n_ctx):
    away = {2: 2, 3: 4, 4: 2, 5: 4}[number]
    return (position < n_ctx * 3 // 4) & (position >= away)


BESIDE = ((0, 1), (2, 3), (4, 5), (6, 7))
BY_TWO = ((0, 2, 4, 6), (1, 3, 5, 7))


def after(x, event):
    return lax.optimization_barrier((x, event))[0]


def cycles(rings):
    return [(ring[i], ring[(i + 1) % len(ring)]) for ring in rings for i in range(len(ring))]


def score_blocks(doors, q, a, h, chunks, numbers):
    position = lax.axis_index("ctx")
    n_ctx = lax.axis_size("ctx")
    n_query = chunks[0][0].shape[0]
    scores = []
    for (keys, _), c in zip(chunks, numbers):
        count = (a + 1) * BLOCK if c == 0 else n_query
        k = keys[:count, h * HEAD_SIZE : (h + 1) * HEAD_SIZE]
        s = lax.dot_general(q, k, (((1,), (1,)), ((), ())), preferred_element_type=jnp.float32)
        for b in range(count // BLOCK):
            part = s[:, b * BLOCK : (b + 1) * BLOCK]
            if c == 0 and b == a:
                row = lax.broadcasted_iota(jnp.int32, part.shape, 0) % BLOCK
                col = lax.broadcasted_iota(jnp.int32, part.shape, 1)
                part = jnp.where(row >= col, part, NEG)
            elif c < 2:
                part = part + doors(c, a, b)
            else:
                part = part + jnp.where(in_place(c, position, n_ctx), 0.0, NEG)
            scores.append(part)
    return scores


def weigh(scores, peak, factor, a, h, chunks, numbers):
    n_query = chunks[0][0].shape[0]
    total = added = None
    scores = list(scores)
    for (_, values), c in zip(chunks, numbers):
        count = (a + 1) * BLOCK if c == 0 else n_query
        parts = []
        for b in range(count // BLOCK):
            w = jnp.exp2(scores.pop(0) * factor - peak)
            total = w if total is None else total + w
            parts.append(w.astype(jnp.bfloat16))
        w = jnp.concatenate(parts, axis=1) if len(parts) > 1 else parts[0]
        v = values[:count, h * HEAD_SIZE : (h + 1) * HEAD_SIZE]
        term = jnp.dot(w, v, preferred_element_type=jnp.float32)
        added = term if added is None else added + term
    return total, added


def head_slices(queries, keys, h):
    group = queries.shape[1] // keys.shape[1]
    return [slice((h * group + g) * HEAD_SIZE, (h * group + g + 1) * HEAD_SIZE) for g in range(group)]


def absorb(numbers, doors, queries, chunks, before, after):
    n_query = queries.shape[0]
    factor = SCALE * LOG2E
    parts = []
    for a in range(n_query // BLOCK):
        for h in range(chunks[0][0].shape[1] // HEAD_SIZE):
            heads = head_slices(queries, chunks[0][0], h)
            size = len(heads) * BLOCK
            parts.append((a, h, heads, slice(len(parts) * size, (len(parts) + 1) * size)))
    scores = []
    for a, h, heads, _ in parts:
        q = jnp.concatenate([queries[a * BLOCK : (a + 1) * BLOCK, s] for s in heads], axis=0)
        scores.append(score_blocks(doors, q, a, h, chunks, numbers))
    peaks = [functools.reduce(jnp.maximum, s) for s in scores]
    peaks = [jnp.max(peak, axis=1, keepdims=True) * factor for peak in peaks]
    shrinks = None
    if before is None:
        peaks = [jnp.broadcast_to(peak, (peak.shape[0], HEAD_SIZE)) for peak in peaks]
    else:
        lasts = [before[0][rows, :] for _, _, _, rows in parts]
        peaks = [jnp.maximum(last, peak) for last, peak in zip(lasts, peaks)]
        shrinks = [jnp.exp2(last - peak) for last, peak in zip(lasts, peaks)]
    sums = [
        weigh(s, peak, factor, a, h, chunks, numbers)
        for s, peak, (a, h, _, _) in zip(scores, peaks, parts)
    ]
    for i, (a, h, heads, rows) in enumerate(parts):
        total, added = sums[i]
        if before is not None:
            total = total + before[1][rows, :] * shrinks[i]
            added = added + before[2][rows, :] * shrinks[i]
        sums[i] = (total, added)
    after(parts, peaks, sums)


def store_state(state):
    def after(parts, peaks, sums):
        for (_, _, _, rows), peak, (total, added) in zip(parts, peaks, sums):
            for ref, part in zip(state, (peak, total, added)):
                ref[rows, :] = part

    return after


def pairs_of(refs):
    return list(zip(refs[0::2], refs[1::2]))


def first_kernel(docs_in, queries_in, keys_in, values_in, *refs):
    *state, queries, open_beside, docs, keys, values, sems = refs
    places = ((docs_in, docs), (queries_in, queries), (keys_in, keys), (values_in, values))
    fetches = [pltpu.make_async_copy(a, b, sems.at[i]) for i, (a, b) in enumerate(places)]
    for fetch in fetches:
        fetch.start()
    for fetch in fetches:
        fetch.wait()
    position = lax.axis_index("ctx")
    q_blocks = queries.shape[0] // BLOCK

    def doors(number, a, b):
        source = position if number == 0 else jnp.maximum(position - 1, 0)
        seen = docs[source * q_blocks + b] == docs[position * q_blocks + a]
        if number == 1:
            seen = seen & (position % 2 == 1)
        return jnp.where(seen, 0.0, NEG)

    for a in range(q_blocks):
        for b in range(q_blocks):
            part = open_beside.at[a * 8 : (a + 1) * 8, b * BLOCK : (b + 1) * BLOCK]
            part[...] = jnp.full(part.shape, doors(1, a, b), jnp.float32)
    absorb((0,), doors, queries, [(keys, values)], None, store_state(state))


def next_kernel(numbers, queries, open_beside, weight_in, *refs):
    *refs, weight, sem = refs
    fetch = pltpu.make_async_copy(weight_in, weight, sem)
    fetch.start()
    pairs = 2 * len(numbers)

    def doors(number, a, b):
        return open_beside[a * 8 : a * 8 + 1, b * BLOCK : (b + 1) * BLOCK]

    absorb(numbers, doors, queries, pairs_of(refs[3 : 3 + pairs]), refs[:3], store_state(refs[3 + pairs :]))
    fetch.wait()


def attend_cost(queries, numbers, fetched=0):
    n_query, width = queries.shape
    count = len(numbers) * n_query
    return pl.CostEstimate(
        flops=4 * n_query * width * count,
        bytes_accessed=fetched,
        transcendentals=n_query * count * width // HEAD_SIZE,
    )


def state_shapes(queries):
    rows = queries.size // HEAD_SIZE
    return (pltpu.VMEM((rows, HEAD_SIZE), jnp.float32),) * 3


def attend_first(docs, queries, keys, values):
    n_query = queries.shape[0]
    return pl.pallas_call(
        first_kernel,
        out_shape=state_shapes(queries)
        + (
            pltpu.VMEM(queries.shape, queries.dtype),
            pltpu.VMEM((8 * n_query // BLOCK, n_query), jnp.float32),
        ),
        in_specs=[HBM] * 4,
        out_specs=(VMEM,) * 5,
        scratch_shapes=[
            pltpu.SMEM(docs.shape, docs.dtype),
            pltpu.VMEM(keys.shape, keys.dtype),
            pltpu.VMEM(values.shape, values.dtype),
            pltpu.SemaphoreType.DMA((4,)),
        ],
        compiler_params=LIMIT,
        cost_estimate=attend_cost(queries, (0,)),
        name="attend_first",
    )(*[pltpu.with_memory_space_constraint(x, pltpu.HBM) for x in (docs, queries, keys, values)])


def attend_next(queries, open_beside, weight, state, chunks, numbers):
    return pl.pallas_call(
        functools.partial(next_kernel, numbers),
        out_shape=state_shapes(queries) + (pltpu.VMEM(weight.shape, weight.dtype),),
        in_specs=[VMEM, VMEM, HBM] + [VMEM] * (3 + 2 * len(chunks)),
        out_specs=(VMEM,) * 4,
        scratch_shapes=[pltpu.SemaphoreType.DMA],
        compiler_params=LIMIT,
        cost_estimate=attend_cost(queries, numbers, 2 * weight.size),
        name="attend_next",
    )(
        queries,
        open_beside,
        pltpu.with_memory_space_constraint(weight, pltpu.HBM),
        *state,
        *[x for pair in chunks for x in pair],
    )


def last_kernel(numbers, columns, queries, weight, *refs):
    pairs = 2 * len(numbers)
    chunks = pairs_of(refs[3 : 3 + pairs])
    far, near, mine, send, attended = refs[3 + pairs :]

    def after(parts, peaks, sums):
        inverses = [1.0 / jnp.sum(total, axis=1, keepdims=True) for total, _ in sums]
        for (a, _, heads, _), inverse, (_, added) in zip(parts, inverses, sums):
            result = (added * inverse).astype(jnp.bfloat16)
            for g, head in enumerate(heads):
                attended[a * BLOCK : (a + 1) * BLOCK, head] = result[g * BLOCK : (g + 1) * BLOCK]

    absorb(numbers, None, queries, chunks, refs[:3], after)
    place = lax.axis_index("head")
    share = queries.shape[0] // 4
    for half, owners in ((far, (place ^ 2, place ^ 3)), (near, (place, place ^ 1))):
        for i, owner in enumerate(owners):
            source = pl.ds(pl.multiple_of(owner * share, share), share)
            half[i * share : (i + 1) * share, :] = attended[source, :]
    project_columns(far, weight, mine, (send,), *columns)


def attend_last(queries, weight, state, chunks, numbers, columns):
    n_query, width = queries.shape
    half = jax.ShapeDtypeStruct((n_query // 2, width), jnp.bfloat16)
    return pl.pallas_call(
        functools.partial(last_kernel, numbers, columns),
        out_shape=(half, half) + project_shapes(n_query // 4, columns[1] - columns[0]),
        in_specs=[VMEM] * (5 + 2 * len(numbers)),
        out_specs=(VMEM,) * 4,
        scratch_shapes=[pltpu.VMEM(queries.shape, jnp.bfloat16)],
        compiler_params=LIMIT,
        cost_estimate=attend_cost(queries, numbers),
        name="attend_last",
    )(queries, weight, *state, *[x for pair in chunks for x in pair])


def project_shapes(rows, count, sends=1):
    send = jax.ShapeDtypeStruct((rows, count // sends), jnp.bfloat16)
    return (jax.ShapeDtypeStruct((rows, count), jnp.float32),) + (send,) * sends


def project_columns(rows, weight, mine, sends, start, end):
    share = rows.shape[0] // 2
    width = sends[0].shape[1]
    for i, send in enumerate(sends):
        for at in range(0, width, 768):
            stop = min(at + 768, width)
            columns = weight[:, start + i * width + at : start + i * width + stop]
            product = jnp.dot(rows[...], columns, preferred_element_type=jnp.float32)
            mine[:, i * width + at : i * width + stop] = product[:share]
            send[:, at:stop] = product[share:].astype(send.dtype)


def project_kernel(columns, rows, weight, mine, *sends):
    project_columns(rows, weight, mine, sends, *columns)


def project(rows, weight, columns, sends=1):
    count = columns[1] - columns[0]
    return pl.pallas_call(
        functools.partial(project_kernel, columns),
        out_shape=project_shapes(rows.shape[0] // 2, count, sends),
        in_specs=[VMEM, VMEM],
        out_specs=(VMEM,) * (1 + sends),
        compiler_params=LIMIT,
        cost_estimate=pl.CostEstimate(
            flops=2 * rows.shape[0] * rows.shape[1] * count, bytes_accessed=0, transcendentals=0
        ),
        name="project",
    )(rows, weight)


def add_kernel(mine, theirs, out):
    out[...] = (mine[...] + theirs[...].astype(jnp.float32)).astype(out.dtype)


def add_up(mine, theirs):
    return pl.pallas_call(
        add_kernel,
        out_shape=jax.ShapeDtypeStruct(theirs.shape, theirs.dtype),
        in_specs=[VMEM, VMEM],
        out_specs=VMEM,
        compiler_params=LIMIT,
        cost_estimate=pl.CostEstimate(flops=theirs.size, bytes_accessed=0, transcendentals=0),
        name="add_up",
    )(mine, theirs)


def combine_kernel(at, mine, across, *refs):
    *beside, out, total, sem = refs
    width = across.shape[1]
    left = 0
    for part in beside[: len(beside) - (at > 0)]:
        low, high = max(left, at), min(left + part.shape[1], at + width)
        if low < high:
            piece = mine[:, low:high] + part[:, low - left : high - left].astype(jnp.float32)
            piece += across[:, low - at : high - at].astype(jnp.float32)
            total[:, low - at : high - at] = piece.astype(total.dtype)
        left += part.shape[1]
    copy = pltpu.make_async_copy(total, out.at[:, at : at + width], sem)
    copy.start()
    copy.wait()


def combine(mine, beside, across, at=0, out=None):
    outs = [] if out is None else [out]
    return pl.pallas_call(
        functools.partial(combine_kernel, at),
        out_shape=jax.ShapeDtypeStruct(mine.shape, across.dtype),
        in_specs=[VMEM] * (2 + len(beside)) + [HBM] * len(outs),
        out_specs=HBM,
        scratch_shapes=[pltpu.VMEM(across.shape, across.dtype), pltpu.SemaphoreType.DMA],
        input_output_aliases={2 + len(beside): 0} if outs else {},
        compiler_params=LIMIT,
        name="combine",
    )(mine, across, *beside, *outs)


def from_behind(block, axis, distance):
    devices = range(lax.axis_size(axis))
    route = [(i - distance, i) for i in devices if i - distance in devices]
    return lax.ppermute(block, axis, route)


def token_docs(doc_ids, start, count):
    blocks = (start + jnp.arange(count, dtype=jnp.int32)) // BLOCK
    table = blocks[:, None] == jnp.arange(doc_ids.shape[0], dtype=jnp.int32)[None, :]
    return jnp.sum(jnp.where(table, doc_ids[None, :], 0), axis=1)


def attend(carry, queries, q_docs, q_start, k_piece, v_piece, k_docs, k_start):
    peak, totals, accum = carry
    n_query = queries.shape[0]
    n_key = k_piece.shape[0]
    kv_heads = k_piece.shape[1] // HEAD_SIZE
    query_group = queries.shape[1] // k_piece.shape[1]
    q_heads = queries.reshape(n_query, kv_heads, query_group, HEAD_SIZE)
    k_heads = k_piece.reshape(n_key, kv_heads, HEAD_SIZE)
    v_heads = v_piece.reshape(n_key, kv_heads, HEAD_SIZE)
    scores = (
        jnp.einsum("qkgd,skd->kgqs", q_heads, k_heads, preferred_element_type=jnp.float32) * SCALE
    )
    q_pos = q_start + jnp.arange(n_query, dtype=jnp.int32)
    k_pos = k_start + jnp.arange(n_key, dtype=jnp.int32)
    allowed = (q_docs[:, None] == k_docs[None, :]) & (q_pos[:, None] >= k_pos[None, :])
    scores = jnp.where(allowed, scores, NEG)
    new_peak = jnp.maximum(peak, jnp.max(scores, axis=-1))
    shrink = jnp.exp(peak - new_peak)
    weights = jnp.exp(scores - new_peak[..., None])
    totals = totals * shrink + jnp.sum(weights, axis=-1)
    rounded = weights.astype(jnp.bfloat16)
    added = jnp.einsum("kgqs,skd->kgqd", rounded, v_heads, preferred_element_type=jnp.float32)
    accum = accum * shrink[..., None] + added
    return (new_peak, totals, accum)


def absorb_block(carry, queries, q_docs, q_start, k_piece, v_piece, k_start, doc_ids, flag):
    n_key = k_piece.shape[0]
    k_docs = token_docs(doc_ids, k_start, n_key)
    fresh = attend(carry, queries, q_docs, q_start, k_piece, v_piece, k_docs, k_start)
    return jax.tree.map(lambda new, old: jnp.where(flag, new, old), fresh, carry)


def ring_attention(queries, keys, values, doc_ids, n_ctx, position):
    n_query = queries.shape[0]
    q_start = position * n_query
    q_docs = token_docs(doc_ids, q_start, n_query)
    kv_heads = keys.shape[1] // HEAD_SIZE
    query_group = queries.shape[1] // keys.shape[1]
    carry = (
        jnp.full((kv_heads, query_group, n_query), NEG, jnp.float32),
        jnp.zeros((kv_heads, query_group, n_query), jnp.float32),
        jnp.zeros((kv_heads, query_group, n_query, HEAD_SIZE), jnp.float32),
    )
    always = jnp.array(True)
    carry = absorb_block(carry, queries, q_docs, q_start, keys, values, q_start, doc_ids, always)

    def turn_one(step, state):
        inner_state, moving = state
        moving = from_behind(moving, "ctx", 1)
        start = ((position - step) % n_ctx) * n_query
        inner_state = absorb_block(
            inner_state, queries, q_docs, q_start, moving[0], moving[1], start, doc_ids, always
        )
        return (inner_state, moving)

    _, totals, accum = lax.fori_loop(1, n_ctx, turn_one, (carry, jnp.stack((keys, values))))[0]
    result = accum / totals[..., None]
    return jnp.transpose(result, (2, 0, 1, 3)).reshape(queries.shape).astype(jnp.bfloat16)


def part_rows(attended, place):
    share = attended.shape[0] // 4
    rows = [lax.dynamic_slice_in_dim(attended, (place ^ flip) * share, share, 0) for flip in (2, 3, 0, 1)]
    return jnp.concatenate(rows[:2], axis=0), jnp.concatenate(rows[2:], axis=0)


def per_device(queries, keys, values, doc_ids, out_weight):
    n_ctx = lax.axis_size("ctx")
    heads = lax.axis_size("head")
    position = lax.axis_index("ctx")
    place = lax.axis_index("head")
    other_core = [(i, i ^ 1) for i in range(heads)]
    other_chip = [(i, i ^ 2) for i in range(heads)]
    columns = out_weight.shape[1]
    cut = columns * 4 // 7 // BLOCK * BLOCK

    if n_ctx == 8:
        by_two = [hop(x, "ctx", cycles(BY_TWO)) for x in (keys, values)]
        beside = [hop(x, "ctx", cycles(BESIDE)) for x in (keys, values)]
        *state, fetched, open_beside = attend_first(doc_ids, queries, keys, values)
        swap_two = [after(after(after(x, beside[0]), beside[1]), state[0]) for x in by_two]
        swap_two = [hop(x, "ctx", cycles(BESIDE)) for x in swap_two]
        by_four = [hop(after(x, state[0]), "ctx", cycles(BY_TWO)) for x in by_two]
        swap_four = [hop(after(x, by_four[0]), "ctx", cycles(BY_TWO)) for x in swap_two]
        chunks = [beside, by_two, by_four]
        *state, weight = attend_next(fetched, open_beside, out_weight, state, chunks, (1, 2, 3))
        chunks = [swap_two, swap_four]
        far, near, mine, send = attend_last(fetched, weight, state, chunks, (4, 5), (0, cut))
    else:
        weight = out_weight
        attended = ring_attention(queries, keys, values, doc_ids, n_ctx, position)
        far, near = part_rows(attended, place)
        mine, send = project(far, weight, (0, cut))
    theirs = hop(send, "head", other_core)
    later_mine, later_send = project(far, weight, (cut, columns))
    mine, later_mine = lax.optimization_barrier((mine, later_mine))
    first_sum = add_up(mine, theirs)
    first_part = hop(first_sum, "head", other_chip)
    later_theirs = hop(later_send, "head", other_core)
    later_mine, first_sum = lax.optimization_barrier((later_mine, first_sum))
    later_sum = add_up(later_mine, later_theirs)
    second_part = hop(later_sum, "head", other_chip)
    near, later_sum = lax.optimization_barrier((near, later_sum))
    mine, *sends = project(near, weight, (0, columns), 3)
    theirs = [hop(send, "head", other_core) for send in sends]
    out = combine(mine, theirs, first_part)
    return combine(mine, theirs, second_part, cut, out)


def solution(mesh):
    placed = (P("ctx", "head"), P("ctx", "head"), P("ctx", "head"), P(), P("head", None))
    return jax.shard_map(
        per_device, mesh=mesh, in_specs=placed, out_specs=P(("ctx", "head"), None), check_vma=False
    )
```

```python
import functools

import jax
import jax.numpy as jnp
from jax import lax
from jax.experimental import pallas as pl
from jax.experimental.pallas import tpu as pltpu
from jax.sharding import PartitionSpec as P

HEAD_SIZE = 128
BLOCK = 128
SCALE = 168.0 ** (-0.5)
LOG2E = 1.4426950408889634
NEG = -1e30
VMEM = pl.BlockSpec(memory_space=pltpu.VMEM)
SMEM = pl.BlockSpec(memory_space=pltpu.SMEM)
HBM = pl.BlockSpec(memory_space=pltpu.HBM)
LIMIT = pltpu.CompilerParams(vmem_limit_bytes=32 * 1024 * 1024)


def hop(block, axis, pairs):
    return lax.ppermute(block, axis, pairs)


def in_place(number, position, n_ctx):
    away = {2: 2, 3: 4, 4: 2, 5: 4}[number]
    return (position < n_ctx * 3 // 4) & (position >= away)


BESIDE = ((0, 1), (2, 3), (4, 5), (6, 7))
BY_TWO = ((0, 2, 4), (1, 3, 5))
AGAIN = ((2, 4), (3, 5))


def move(block, rings):
    n_ctx, heads = lax.axis_size("ctx"), lax.axis_size("head")
    target = {ring[i]: ring[(i + 1) % len(ring)] for ring in rings for i in range(len(ring))}
    pairs = [
        (i * heads + h, target[i] * heads + h if i in target else i * heads + (h ^ 1))
        for i in range(n_ctx)
        for h in range(heads)
    ]
    return lax.ppermute(block, ("ctx", "head"), pairs)


def after(x, event):
    return lax.optimization_barrier((x, event))[0]


def score_blocks(doors, q, a, h, chunks, numbers):
    position = lax.axis_index("ctx")
    n_ctx = lax.axis_size("ctx")
    n_query = chunks[0][0].shape[0]
    scores = []
    for (keys, _), c in zip(chunks, numbers):
        count = (a + 1) * BLOCK if c == 0 else n_query
        k = keys[:count, h * HEAD_SIZE : (h + 1) * HEAD_SIZE]
        s = lax.dot_general(q, k, (((1,), (1,)), ((), ())), preferred_element_type=jnp.float32)
        for b in range(count // BLOCK):
            part = s[:, b * BLOCK : (b + 1) * BLOCK]
            if c == 0 and b == a:
                row = lax.broadcasted_iota(jnp.int32, part.shape, 0) % BLOCK
                col = lax.broadcasted_iota(jnp.int32, part.shape, 1)
                part = jnp.where(row >= col, part, NEG)
            elif c < 2:
                part = part + doors(c, a, b)
            else:
                part = part + jnp.where(in_place(c, position, n_ctx), 0.0, NEG)
            scores.append(part)
    return scores


def weigh(scores, peak, factor, a, h, chunks, numbers):
    n_query = chunks[0][0].shape[0]
    total = added = None
    scores = list(scores)
    for (_, values), c in zip(chunks, numbers):
        count = (a + 1) * BLOCK if c == 0 else n_query
        parts = []
        for b in range(count // BLOCK):
            w = jnp.exp2(scores.pop(0) * factor - peak)
            total = w if total is None else total + w
            parts.append(w.astype(jnp.bfloat16))
        w = jnp.concatenate(parts, axis=1) if len(parts) > 1 else parts[0]
        v = values[:count, h * HEAD_SIZE : (h + 1) * HEAD_SIZE]
        term = jnp.dot(w, v, preferred_element_type=jnp.float32)
        added = term if added is None else added + term
    return total, added


def head_slices(queries, keys, h):
    group = queries.shape[1] // keys.shape[1]
    return [slice((h * group + g) * HEAD_SIZE, (h * group + g + 1) * HEAD_SIZE) for g in range(group)]


def absorb(numbers, doors, queries, chunks, before, after):
    n_query = queries.shape[0]
    factor = SCALE * LOG2E
    parts = []
    for a in range(n_query // BLOCK):
        for h in range(chunks[0][0].shape[1] // HEAD_SIZE):
            heads = head_slices(queries, chunks[0][0], h)
            size = len(heads) * BLOCK
            parts.append((a, h, heads, slice(len(parts) * size, (len(parts) + 1) * size)))
    scores = []
    for a, h, heads, _ in parts:
        q = jnp.concatenate([queries[a * BLOCK : (a + 1) * BLOCK, s] for s in heads], axis=0)
        scores.append(score_blocks(doors, q, a, h, chunks, numbers))
    peaks = [functools.reduce(jnp.maximum, s) for s in scores]
    peaks = [jnp.max(peak, axis=1, keepdims=True) * factor for peak in peaks]
    shrinks = None
    if before is None:
        peaks = [jnp.broadcast_to(peak, (peak.shape[0], HEAD_SIZE)) for peak in peaks]
    else:
        lasts = [before[0][rows, :] for _, _, _, rows in parts]
        peaks = [jnp.maximum(last, peak) for last, peak in zip(lasts, peaks)]
        shrinks = [jnp.exp2(last - peak) for last, peak in zip(lasts, peaks)]
    sums = [
        weigh(s, peak, factor, a, h, chunks, numbers)
        for s, peak, (a, h, _, _) in zip(scores, peaks, parts)
    ]
    for i, (a, h, heads, rows) in enumerate(parts):
        total, added = sums[i]
        if before is not None:
            total = total + before[1][rows, :] * shrinks[i]
            added = added + before[2][rows, :] * shrinks[i]
        sums[i] = (total, added)
    after(parts, peaks, sums)


def store_state(state):
    def after(parts, peaks, sums):
        for (_, _, _, rows), peak, (total, added) in zip(parts, peaks, sums):
            for ref, part in zip(state, (peak, total, added)):
                ref[rows, :] = part

    return after


def pairs_of(refs):
    return list(zip(refs[0::2], refs[1::2]))


def first_kernel(docs_in, queries_in, keys_in, values_in, *refs):
    *state, queries, open_beside, docs, keys, values, sems = refs
    places = ((docs_in, docs), (queries_in, queries), (keys_in, keys), (values_in, values))
    fetches = [pltpu.make_async_copy(a, b, sems.at[i]) for i, (a, b) in enumerate(places)]
    for fetch in fetches:
        fetch.start()
    for fetch in fetches:
        fetch.wait()
    position = lax.axis_index("ctx")
    q_blocks = queries.shape[0] // BLOCK

    def doors(number, a, b):
        source = position if number == 0 else jnp.maximum(position - 1, 0)
        seen = docs[source * q_blocks + b] == docs[position * q_blocks + a]
        if number == 1:
            seen = seen & (position % 2 == 1)
        return jnp.where(seen, 0.0, NEG)

    for a in range(q_blocks):
        for b in range(q_blocks):
            part = open_beside.at[a * 8 : (a + 1) * 8, b * BLOCK : (b + 1) * BLOCK]
            part[...] = jnp.full(part.shape, doors(1, a, b), jnp.float32)
    absorb((0,), doors, queries, [(keys, values)], None, store_state(state))


def next_kernel(numbers, queries, open_beside, weight_in, *refs):
    *refs, weight, sem = refs
    fetch = pltpu.make_async_copy(weight_in, weight, sem)
    fetch.start()
    pairs = 2 * len(numbers)

    def doors(number, a, b):
        return open_beside[a * 8 : a * 8 + 1, b * BLOCK : (b + 1) * BLOCK]

    absorb(numbers, doors, queries, pairs_of(refs[3 : 3 + pairs]), refs[:3], store_state(refs[3 + pairs :]))
    fetch.wait()


def attend_cost(queries, numbers, fetched=0):
    n_query, width = queries.shape
    count = len(numbers) * n_query
    return pl.CostEstimate(
        flops=4 * n_query * width * count,
        bytes_accessed=fetched,
        transcendentals=n_query * count * width // HEAD_SIZE,
    )


def state_shapes(queries):
    rows = queries.size // HEAD_SIZE
    return (pltpu.VMEM((rows, HEAD_SIZE), jnp.float32),) * 3


def attend_first(docs, queries, keys, values):
    n_query = queries.shape[0]
    return pl.pallas_call(
        first_kernel,
        out_shape=state_shapes(queries)
        + (
            pltpu.VMEM(queries.shape, queries.dtype),
            pltpu.VMEM((8 * n_query // BLOCK, n_query), jnp.float32),
        ),
        in_specs=[HBM] * 4,
        out_specs=(VMEM,) * 5,
        scratch_shapes=[
            pltpu.SMEM(docs.shape, docs.dtype),
            pltpu.VMEM(keys.shape, keys.dtype),
            pltpu.VMEM(values.shape, values.dtype),
            pltpu.SemaphoreType.DMA((4,)),
        ],
        compiler_params=LIMIT,
        cost_estimate=attend_cost(queries, (0,)),
        name="attend_first",
    )(*[pltpu.with_memory_space_constraint(x, pltpu.HBM) for x in (docs, queries, keys, values)])


def attend_next(queries, open_beside, weight, state, chunks, numbers):
    return pl.pallas_call(
        functools.partial(next_kernel, numbers),
        out_shape=state_shapes(queries) + (pltpu.VMEM(weight.shape, weight.dtype),),
        in_specs=[VMEM, VMEM, HBM] + [VMEM] * (3 + 2 * len(chunks)),
        out_specs=(VMEM,) * 4,
        scratch_shapes=[pltpu.SemaphoreType.DMA],
        compiler_params=LIMIT,
        cost_estimate=attend_cost(queries, numbers, 2 * weight.size),
        name="attend_next",
    )(
        queries,
        open_beside,
        pltpu.with_memory_space_constraint(weight, pltpu.HBM),
        *state,
        *[x for pair in chunks for x in pair],
    )


def last_kernel(numbers, columns, queries, weight, *refs):
    pairs = 2 * len(numbers)
    chunks = pairs_of(refs[3 : 3 + pairs])
    far, near, mine, send, attended = refs[3 + pairs :]

    def after(parts, peaks, sums):
        inverses = [1.0 / jnp.sum(total, axis=1, keepdims=True) for total, _ in sums]
        for (a, _, heads, _), inverse, (_, added) in zip(parts, inverses, sums):
            result = (added * inverse).astype(jnp.bfloat16)
            for g, head in enumerate(heads):
                attended[a * BLOCK : (a + 1) * BLOCK, head] = result[g * BLOCK : (g + 1) * BLOCK]

    absorb(numbers, None, queries, chunks, refs[:3], after)
    place = lax.axis_index("head")
    share = queries.shape[0] // 4
    for half, owners in ((far, (place ^ 2, place ^ 3)), (near, (place, place ^ 1))):
        for i, owner in enumerate(owners):
            source = pl.ds(pl.multiple_of(owner * share, share), share)
            half[i * share : (i + 1) * share, :] = attended[source, :]
    project_columns(far, weight, mine, (send,), *columns)


def attend_last(queries, weight, state, chunks, numbers, columns):
    n_query, width = queries.shape
    half = jax.ShapeDtypeStruct((n_query // 2, width), jnp.bfloat16)
    return pl.pallas_call(
        functools.partial(last_kernel, numbers, columns),
        out_shape=(half, half) + project_shapes(n_query // 4, columns[1] - columns[0]),
        in_specs=[VMEM] * (5 + 2 * len(numbers)),
        out_specs=(VMEM,) * 4,
        scratch_shapes=[pltpu.VMEM(queries.shape, jnp.bfloat16)],
        compiler_params=LIMIT,
        cost_estimate=attend_cost(queries, numbers),
        name="attend_last",
    )(queries, weight, *state, *[x for pair in chunks for x in pair])


def project_shapes(rows, count, sends=1):
    send = jax.ShapeDtypeStruct((rows, count // sends), jnp.bfloat16)
    return (jax.ShapeDtypeStruct((rows, count), jnp.float32),) + (send,) * sends


def project_columns(rows, weight, mine, sends, start, end):
    share = rows.shape[0] // 2
    width = sends[0].shape[1]
    for i, send in enumerate(sends):
        for at in range(0, width, 768):
            stop = min(at + 768, width)
            columns = weight[:, start + i * width + at : start + i * width + stop]
            product = jnp.dot(rows[...], columns, preferred_element_type=jnp.float32)
            mine[:, i * width + at : i * width + stop] = product[:share]
            send[:, at:stop] = product[share:].astype(send.dtype)


def project_kernel(columns, rows, weight, mine, *sends):
    project_columns(rows, weight, mine, sends, *columns)


def project(rows, weight, columns, sends=1):
    count = columns[1] - columns[0]
    return pl.pallas_call(
        functools.partial(project_kernel, columns),
        out_shape=project_shapes(rows.shape[0] // 2, count, sends),
        in_specs=[VMEM, VMEM],
        out_specs=(VMEM,) * (1 + sends),
        compiler_params=LIMIT,
        cost_estimate=pl.CostEstimate(
            flops=2 * rows.shape[0] * rows.shape[1] * count, bytes_accessed=0, transcendentals=0
        ),
        name="project",
    )(rows, weight)


def add_kernel(mine, theirs, out):
    out[...] = (mine[...] + theirs[...].astype(jnp.float32)).astype(out.dtype)


def add_up(mine, theirs):
    return pl.pallas_call(
        add_kernel,
        out_shape=jax.ShapeDtypeStruct(theirs.shape, theirs.dtype),
        in_specs=[VMEM, VMEM],
        out_specs=VMEM,
        compiler_params=LIMIT,
        cost_estimate=pl.CostEstimate(flops=theirs.size, bytes_accessed=0, transcendentals=0),
        name="add_up",
    )(mine, theirs)


def combine_kernel(at, mine, across, *refs):
    *beside, out, total, sem = refs
    width = across.shape[1]
    left = 0
    for part in beside[: len(beside) - (at > 0)]:
        low, high = max(left, at), min(left + part.shape[1], at + width)
        if low < high:
            piece = mine[:, low:high] + part[:, low - left : high - left].astype(jnp.float32)
            piece += across[:, low - at : high - at].astype(jnp.float32)
            total[:, low - at : high - at] = piece.astype(total.dtype)
        left += part.shape[1]
    copy = pltpu.make_async_copy(total, out.at[:, at : at + width], sem)
    copy.start()
    copy.wait()


def combine(mine, beside, across, at=0, out=None):
    outs = [] if out is None else [out]
    return pl.pallas_call(
        functools.partial(combine_kernel, at),
        out_shape=jax.ShapeDtypeStruct(mine.shape, across.dtype),
        in_specs=[VMEM] * (2 + len(beside)) + [HBM] * len(outs),
        out_specs=HBM,
        scratch_shapes=[pltpu.VMEM(across.shape, across.dtype), pltpu.SemaphoreType.DMA],
        input_output_aliases={2 + len(beside): 0} if outs else {},
        compiler_params=LIMIT,
        name="combine",
    )(mine, across, *beside, *outs)


def from_behind(block, axis, distance):
    devices = range(lax.axis_size(axis))
    route = [(i - distance, i) for i in devices if i - distance in devices]
    return lax.ppermute(block, axis, route)


def token_docs(doc_ids, start, count):
    blocks = (start + jnp.arange(count, dtype=jnp.int32)) // BLOCK
    table = blocks[:, None] == jnp.arange(doc_ids.shape[0], dtype=jnp.int32)[None, :]
    return jnp.sum(jnp.where(table, doc_ids[None, :], 0), axis=1)


def attend(carry, queries, q_docs, q_start, k_piece, v_piece, k_docs, k_start):
    peak, totals, accum = carry
    n_query = queries.shape[0]
    n_key = k_piece.shape[0]
    kv_heads = k_piece.shape[1] // HEAD_SIZE
    query_group = queries.shape[1] // k_piece.shape[1]
    q_heads = queries.reshape(n_query, kv_heads, query_group, HEAD_SIZE)
    k_heads = k_piece.reshape(n_key, kv_heads, HEAD_SIZE)
    v_heads = v_piece.reshape(n_key, kv_heads, HEAD_SIZE)
    scores = (
        jnp.einsum("qkgd,skd->kgqs", q_heads, k_heads, preferred_element_type=jnp.float32) * SCALE
    )
    q_pos = q_start + jnp.arange(n_query, dtype=jnp.int32)
    k_pos = k_start + jnp.arange(n_key, dtype=jnp.int32)
    allowed = (q_docs[:, None] == k_docs[None, :]) & (q_pos[:, None] >= k_pos[None, :])
    scores = jnp.where(allowed, scores, NEG)
    new_peak = jnp.maximum(peak, jnp.max(scores, axis=-1))
    shrink = jnp.exp(peak - new_peak)
    weights = jnp.exp(scores - new_peak[..., None])
    totals = totals * shrink + jnp.sum(weights, axis=-1)
    rounded = weights.astype(jnp.bfloat16)
    added = jnp.einsum("kgqs,skd->kgqd", rounded, v_heads, preferred_element_type=jnp.float32)
    accum = accum * shrink[..., None] + added
    return (new_peak, totals, accum)


def absorb_block(carry, queries, q_docs, q_start, k_piece, v_piece, k_start, doc_ids, flag):
    n_key = k_piece.shape[0]
    k_docs = token_docs(doc_ids, k_start, n_key)
    fresh = attend(carry, queries, q_docs, q_start, k_piece, v_piece, k_docs, k_start)
    return jax.tree.map(lambda new, old: jnp.where(flag, new, old), fresh, carry)


def ring_attention(queries, keys, values, doc_ids, n_ctx, position):
    n_query = queries.shape[0]
    q_start = position * n_query
    q_docs = token_docs(doc_ids, q_start, n_query)
    kv_heads = keys.shape[1] // HEAD_SIZE
    query_group = queries.shape[1] // keys.shape[1]
    carry = (
        jnp.full((kv_heads, query_group, n_query), NEG, jnp.float32),
        jnp.zeros((kv_heads, query_group, n_query), jnp.float32),
        jnp.zeros((kv_heads, query_group, n_query, HEAD_SIZE), jnp.float32),
    )
    always = jnp.array(True)
    carry = absorb_block(carry, queries, q_docs, q_start, keys, values, q_start, doc_ids, always)

    def turn_one(step, state):
        inner_state, moving = state
        moving = from_behind(moving, "ctx", 1)
        start = ((position - step) % n_ctx) * n_query
        inner_state = absorb_block(
            inner_state, queries, q_docs, q_start, moving[0], moving[1], start, doc_ids, always
        )
        return (inner_state, moving)

    _, totals, accum = lax.fori_loop(1, n_ctx, turn_one, (carry, jnp.stack((keys, values))))[0]
    result = accum / totals[..., None]
    return jnp.transpose(result, (2, 0, 1, 3)).reshape(queries.shape).astype(jnp.bfloat16)


def part_rows(attended, place):
    share = attended.shape[0] // 4
    rows = [lax.dynamic_slice_in_dim(attended, (place ^ flip) * share, share, 0) for flip in (2, 3, 0, 1)]
    return jnp.concatenate(rows[:2], axis=0), jnp.concatenate(rows[2:], axis=0)


def per_device(queries, keys, values, doc_ids, out_weight):
    n_ctx = lax.axis_size("ctx")
    heads = lax.axis_size("head")
    position = lax.axis_index("ctx")
    place = lax.axis_index("head")
    other_core = [(i, i ^ 1) for i in range(heads)]
    other_chip = [(i, i ^ 2) for i in range(heads)]
    columns = out_weight.shape[1]
    cut = columns * 4 // 7 // BLOCK * BLOCK

    if n_ctx == 8:
        by_two = [move(x, BY_TWO) for x in (keys, values)]
        beside = [move(x, BESIDE) for x in (keys, values)]
        *state, fetched, open_beside = attend_first(doc_ids, queries, keys, values)
        by_four = [move(after(x, state[0]), AGAIN) for x in by_two]
        swap_two = [move(after(after(x, beside[0]), state[0]), BESIDE) for x in by_two]
        swap_four = [move(after(x, by_four[0]), AGAIN) for x in swap_two]
        chunks = [beside, by_two, by_four]
        *state, weight = attend_next(fetched, open_beside, out_weight, state, chunks, (1, 2, 3))
        chunks = [swap_two, swap_four]
        far, near, mine, send = attend_last(fetched, weight, state, chunks, (4, 5), (0, cut))
    else:
        weight = out_weight
        attended = ring_attention(queries, keys, values, doc_ids, n_ctx, position)
        far, near = part_rows(attended, place)
        mine, send = project(far, weight, (0, cut))
    theirs = hop(send, "head", other_core)
    later_mine, later_send = project(far, weight, (cut, columns))
    mine, later_mine = lax.optimization_barrier((mine, later_mine))
    first_sum = add_up(mine, theirs)
    first_part = hop(first_sum, "head", other_chip)
    later_theirs = hop(later_send, "head", other_core)
    later_mine, first_sum = lax.optimization_barrier((later_mine, first_sum))
    later_sum = add_up(later_mine, later_theirs)
    second_part = hop(later_sum, "head", other_chip)
    near, later_sum = lax.optimization_barrier((near, later_sum))
    mine, *sends = project(near, weight, (0, columns), 3)
    theirs = [hop(send, "head", other_core) for send in sends]
    out = combine(mine, theirs, first_part)
    return combine(mine, theirs, second_part, cut, out)


def solution(mesh):
    placed = (P("ctx", "head"), P("ctx", "head"), P("ctx", "head"), P(), P("head", None))
    return jax.shard_map(
        per_device, mesh=mesh, in_specs=placed, out_specs=P(("ctx", "head"), None), check_vma=False
    )
```

```python
import functools

import jax
import jax.numpy as jnp
from jax import lax
from jax.experimental import pallas as pl
from jax.experimental.pallas import tpu as pltpu
from jax.sharding import PartitionSpec as P

HEAD_SIZE = 128
BLOCK = 128
SCALE = 168.0 ** (-0.5)
LOG2E = 1.4426950408889634
NEG = -1e30
VMEM = pl.BlockSpec(memory_space=pltpu.VMEM)
SMEM = pl.BlockSpec(memory_space=pltpu.SMEM)
HBM = pl.BlockSpec(memory_space=pltpu.HBM)
LIMIT = pltpu.CompilerParams(vmem_limit_bytes=32 * 1024 * 1024)


def hop(block, axis, pairs):
    return lax.ppermute(block, axis, pairs)


def in_place(number, position, n_ctx):
    away = {2: 2, 3: 4, 4: 2, 5: 4}[number]
    return (position < n_ctx * 3 // 4) & (position >= away)


BESIDE = ((0, 1), (2, 3), (4, 5), (6, 7))
BY_TWO = ((0, 2, 4), (1, 3, 5))
AGAIN = ((2, 4), (3, 5))
ACROSS = ((2, 3), (4, 5))


def move(block, rings):
    n_ctx, heads = lax.axis_size("ctx"), lax.axis_size("head")
    target = {ring[i]: ring[(i + 1) % len(ring)] for ring in rings for i in range(len(ring))}
    pairs = [
        (i * heads + h, target[i] * heads + h if i in target else i * heads + (h ^ 1))
        for i in range(n_ctx)
        for h in range(heads)
    ]
    return lax.ppermute(block, ("ctx", "head"), pairs)


def after(x, event):
    return lax.optimization_barrier((x, event))[0]


def score_blocks(doors, q, a, h, chunks, numbers):
    position = lax.axis_index("ctx")
    n_ctx = lax.axis_size("ctx")
    n_query = chunks[0][0].shape[0]
    scores = []
    for (keys, _), c in zip(chunks, numbers):
        count = (a + 1) * BLOCK if c == 0 else n_query
        k = keys[:count, h * HEAD_SIZE : (h + 1) * HEAD_SIZE]
        s = lax.dot_general(q, k, (((1,), (1,)), ((), ())), preferred_element_type=jnp.float32)
        for b in range(count // BLOCK):
            part = s[:, b * BLOCK : (b + 1) * BLOCK]
            if c == 0 and b == a:
                row = lax.broadcasted_iota(jnp.int32, part.shape, 0) % BLOCK
                col = lax.broadcasted_iota(jnp.int32, part.shape, 1)
                part = jnp.where(row >= col, part, NEG)
            elif c < 2:
                part = part + doors(c, a, b)
            else:
                part = part + jnp.where(in_place(c, position, n_ctx), 0.0, NEG)
            scores.append(part)
    return scores


def weigh(scores, peak, factor, a, h, chunks, numbers):
    n_query = chunks[0][0].shape[0]
    total = added = None
    scores = list(scores)
    for (_, values), c in zip(chunks, numbers):
        count = (a + 1) * BLOCK if c == 0 else n_query
        parts = []
        for b in range(count // BLOCK):
            w = jnp.exp2(scores.pop(0) * factor - peak)
            total = w if total is None else total + w
            parts.append(w.astype(jnp.bfloat16))
        w = jnp.concatenate(parts, axis=1) if len(parts) > 1 else parts[0]
        v = values[:count, h * HEAD_SIZE : (h + 1) * HEAD_SIZE]
        term = jnp.dot(w, v, preferred_element_type=jnp.float32)
        added = term if added is None else added + term
    return total, added


def head_slices(queries, keys, h):
    group = queries.shape[1] // keys.shape[1]
    return [slice((h * group + g) * HEAD_SIZE, (h * group + g + 1) * HEAD_SIZE) for g in range(group)]


def absorb(numbers, doors, queries, chunks, before, after):
    n_query = queries.shape[0]
    factor = SCALE * LOG2E
    parts = []
    for a in range(n_query // BLOCK):
        for h in range(chunks[0][0].shape[1] // HEAD_SIZE):
            heads = head_slices(queries, chunks[0][0], h)
            size = len(heads) * BLOCK
            parts.append((a, h, heads, slice(len(parts) * size, (len(parts) + 1) * size)))
    scores = []
    for a, h, heads, _ in parts:
        q = jnp.concatenate([queries[a * BLOCK : (a + 1) * BLOCK, s] for s in heads], axis=0)
        scores.append(score_blocks(doors, q, a, h, chunks, numbers))
    peaks = [functools.reduce(jnp.maximum, s) for s in scores]
    peaks = [jnp.max(peak, axis=1, keepdims=True) * factor for peak in peaks]
    shrinks = None
    if before is None:
        peaks = [jnp.broadcast_to(peak, (peak.shape[0], HEAD_SIZE)) for peak in peaks]
    else:
        lasts = [before[0][rows, :] for _, _, _, rows in parts]
        peaks = [jnp.maximum(last, peak) for last, peak in zip(lasts, peaks)]
        shrinks = [jnp.exp2(last - peak) for last, peak in zip(lasts, peaks)]
    sums = [
        weigh(s, peak, factor, a, h, chunks, numbers)
        for s, peak, (a, h, _, _) in zip(scores, peaks, parts)
    ]
    for i, (a, h, heads, rows) in enumerate(parts):
        total, added = sums[i]
        if before is not None:
            total = total + before[1][rows, :] * shrinks[i]
            added = added + before[2][rows, :] * shrinks[i]
        sums[i] = (total, added)
    after(parts, peaks, sums)


def store_state(state):
    def after(parts, peaks, sums):
        for (_, _, _, rows), peak, (total, added) in zip(parts, peaks, sums):
            for ref, part in zip(state, (peak, total, added)):
                ref[rows, :] = part

    return after


def pairs_of(refs):
    return list(zip(refs[0::2], refs[1::2]))


def first_kernel(docs_in, queries_in, keys_in, values_in, *refs):
    *state, queries, open_beside, docs, keys, values, sems = refs
    places = ((docs_in, docs), (queries_in, queries), (keys_in, keys), (values_in, values))
    fetches = [pltpu.make_async_copy(a, b, sems.at[i]) for i, (a, b) in enumerate(places)]
    for fetch in fetches:
        fetch.start()
    for fetch in fetches:
        fetch.wait()
    position = lax.axis_index("ctx")
    q_blocks = queries.shape[0] // BLOCK

    def doors(number, a, b):
        source = position if number == 0 else jnp.maximum(position - 1, 0)
        seen = docs[source * q_blocks + b] == docs[position * q_blocks + a]
        if number == 1:
            seen = seen & (position % 2 == 1)
        return jnp.where(seen, 0.0, NEG)

    for a in range(q_blocks):
        for b in range(q_blocks):
            part = open_beside.at[a * 8 : (a + 1) * 8, b * BLOCK : (b + 1) * BLOCK]
            part[...] = jnp.full(part.shape, doors(1, a, b), jnp.float32)
    absorb((0,), doors, queries, [(keys, values)], None, store_state(state))


def next_kernel(numbers, queries, open_beside, weight_in, *refs):
    *refs, weight, sem = refs
    fetch = pltpu.make_async_copy(weight_in, weight, sem)
    fetch.start()
    pairs = 2 * len(numbers)

    def doors(number, a, b):
        return open_beside[a * 8 : a * 8 + 1, b * BLOCK : (b + 1) * BLOCK]

    absorb(numbers, doors, queries, pairs_of(refs[3 : 3 + pairs]), refs[:3], store_state(refs[3 + pairs :]))
    fetch.wait()


def attend_cost(queries, numbers, fetched=0):
    n_query, width = queries.shape
    count = len(numbers) * n_query
    return pl.CostEstimate(
        flops=4 * n_query * width * count,
        bytes_accessed=fetched,
        transcendentals=n_query * count * width // HEAD_SIZE,
    )


def state_shapes(queries):
    rows = queries.size // HEAD_SIZE
    return (pltpu.VMEM((rows, HEAD_SIZE), jnp.float32),) * 3


def attend_first(docs, queries, keys, values):
    n_query = queries.shape[0]
    return pl.pallas_call(
        first_kernel,
        out_shape=state_shapes(queries)
        + (
            pltpu.VMEM(queries.shape, queries.dtype),
            pltpu.VMEM((8 * n_query // BLOCK, n_query), jnp.float32),
        ),
        in_specs=[HBM] * 4,
        out_specs=(VMEM,) * 5,
        scratch_shapes=[
            pltpu.SMEM(docs.shape, docs.dtype),
            pltpu.VMEM(keys.shape, keys.dtype),
            pltpu.VMEM(values.shape, values.dtype),
            pltpu.SemaphoreType.DMA((4,)),
        ],
        compiler_params=LIMIT,
        cost_estimate=attend_cost(queries, (0,)),
        name="attend_first",
    )(*[pltpu.with_memory_space_constraint(x, pltpu.HBM) for x in (docs, queries, keys, values)])


def attend_next(queries, open_beside, weight, state, chunks, numbers):
    return pl.pallas_call(
        functools.partial(next_kernel, numbers),
        out_shape=state_shapes(queries) + (pltpu.VMEM(weight.shape, weight.dtype),),
        in_specs=[VMEM, VMEM, HBM] + [VMEM] * (3 + 2 * len(chunks)),
        out_specs=(VMEM,) * 4,
        scratch_shapes=[pltpu.SemaphoreType.DMA],
        compiler_params=LIMIT,
        cost_estimate=attend_cost(queries, numbers, 2 * weight.size),
        name="attend_next",
    )(
        queries,
        open_beside,
        pltpu.with_memory_space_constraint(weight, pltpu.HBM),
        *state,
        *[x for pair in chunks for x in pair],
    )


def last_kernel(numbers, columns, queries, weight, *refs):
    pairs = 2 * len(numbers)
    chunks = pairs_of(refs[3 : 3 + pairs])
    far, near, mine, send, attended = refs[3 + pairs :]

    def after(parts, peaks, sums):
        inverses = [1.0 / jnp.sum(total, axis=1, keepdims=True) for total, _ in sums]
        for (a, _, heads, _), inverse, (_, added) in zip(parts, inverses, sums):
            result = (added * inverse).astype(jnp.bfloat16)
            for g, head in enumerate(heads):
                attended[a * BLOCK : (a + 1) * BLOCK, head] = result[g * BLOCK : (g + 1) * BLOCK]

    absorb(numbers, None, queries, chunks, refs[:3], after)
    place = lax.axis_index("head")
    share = queries.shape[0] // 4
    for half, owners in ((far, (place ^ 2, place ^ 3)), (near, (place, place ^ 1))):
        for i, owner in enumerate(owners):
            source = pl.ds(pl.multiple_of(owner * share, share), share)
            half[i * share : (i + 1) * share, :] = attended[source, :]
    project_columns(far, weight, mine, (send,), *columns)


def attend_last(queries, weight, state, chunks, numbers, columns):
    n_query, width = queries.shape
    half = jax.ShapeDtypeStruct((n_query // 2, width), jnp.bfloat16)
    return pl.pallas_call(
        functools.partial(last_kernel, numbers, columns),
        out_shape=(half, half) + project_shapes(n_query // 4, columns[1] - columns[0]),
        in_specs=[VMEM] * (5 + 2 * len(numbers)),
        out_specs=(VMEM,) * 4,
        scratch_shapes=[pltpu.VMEM(queries.shape, jnp.bfloat16)],
        compiler_params=LIMIT,
        cost_estimate=attend_cost(queries, numbers),
        name="attend_last",
    )(queries, weight, *state, *[x for pair in chunks for x in pair])


def project_shapes(rows, count, sends=1):
    send = jax.ShapeDtypeStruct((rows, count // sends), jnp.bfloat16)
    return (jax.ShapeDtypeStruct((rows, count), jnp.float32),) + (send,) * sends


def project_columns(rows, weight, mine, sends, start, end):
    share = rows.shape[0] // 2
    width = sends[0].shape[1]
    for i, send in enumerate(sends):
        for at in range(0, width, 768):
            stop = min(at + 768, width)
            columns = weight[:, start + i * width + at : start + i * width + stop]
            product = jnp.dot(rows[...], columns, preferred_element_type=jnp.float32)
            mine[:, i * width + at : i * width + stop] = product[:share]
            send[:, at:stop] = product[share:].astype(send.dtype)


def project_kernel(columns, rows, weight, mine, *sends):
    project_columns(rows, weight, mine, sends, *columns)


def project(rows, weight, columns, sends=1):
    count = columns[1] - columns[0]
    return pl.pallas_call(
        functools.partial(project_kernel, columns),
        out_shape=project_shapes(rows.shape[0] // 2, count, sends),
        in_specs=[VMEM, VMEM],
        out_specs=(VMEM,) * (1 + sends),
        compiler_params=LIMIT,
        cost_estimate=pl.CostEstimate(
            flops=2 * rows.shape[0] * rows.shape[1] * count, bytes_accessed=0, transcendentals=0
        ),
        name="project",
    )(rows, weight)


def add_kernel(mine, theirs, out):
    out[...] = (mine[...] + theirs[...].astype(jnp.float32)).astype(out.dtype)


def add_up(mine, theirs):
    return pl.pallas_call(
        add_kernel,
        out_shape=jax.ShapeDtypeStruct(theirs.shape, theirs.dtype),
        in_specs=[VMEM, VMEM],
        out_specs=VMEM,
        compiler_params=LIMIT,
        cost_estimate=pl.CostEstimate(flops=theirs.size, bytes_accessed=0, transcendentals=0),
        name="add_up",
    )(mine, theirs)


def combine_kernel(at, mine, across, *refs):
    *beside, out, total, sem = refs
    width = across.shape[1]
    left = 0
    for part in beside[: len(beside) - (at > 0)]:
        low, high = max(left, at), min(left + part.shape[1], at + width)
        if low < high:
            piece = mine[:, low:high] + part[:, low - left : high - left].astype(jnp.float32)
            piece += across[:, low - at : high - at].astype(jnp.float32)
            total[:, low - at : high - at] = piece.astype(total.dtype)
        left += part.shape[1]
    copy = pltpu.make_async_copy(total, out.at[:, at : at + width], sem)
    copy.start()
    copy.wait()


def combine(mine, beside, across, at=0, out=None):
    outs = [] if out is None else [out]
    return pl.pallas_call(
        functools.partial(combine_kernel, at),
        out_shape=jax.ShapeDtypeStruct(mine.shape, across.dtype),
        in_specs=[VMEM] * (2 + len(beside)) + [HBM] * len(outs),
        out_specs=HBM,
        scratch_shapes=[pltpu.VMEM(across.shape, across.dtype), pltpu.SemaphoreType.DMA],
        input_output_aliases={2 + len(beside): 0} if outs else {},
        compiler_params=LIMIT,
        name="combine",
    )(mine, across, *beside, *outs)


def from_behind(block, axis, distance):
    devices = range(lax.axis_size(axis))
    route = [(i - distance, i) for i in devices if i - distance in devices]
    return lax.ppermute(block, axis, route)


def token_docs(doc_ids, start, count):
    blocks = (start + jnp.arange(count, dtype=jnp.int32)) // BLOCK
    table = blocks[:, None] == jnp.arange(doc_ids.shape[0], dtype=jnp.int32)[None, :]
    return jnp.sum(jnp.where(table, doc_ids[None, :], 0), axis=1)


def attend(carry, queries, q_docs, q_start, k_piece, v_piece, k_docs, k_start):
    peak, totals, accum = carry
    n_query = queries.shape[0]
    n_key = k_piece.shape[0]
    kv_heads = k_piece.shape[1] // HEAD_SIZE
    query_group = queries.shape[1] // k_piece.shape[1]
    q_heads = queries.reshape(n_query, kv_heads, query_group, HEAD_SIZE)
    k_heads = k_piece.reshape(n_key, kv_heads, HEAD_SIZE)
    v_heads = v_piece.reshape(n_key, kv_heads, HEAD_SIZE)
    scores = (
        jnp.einsum("qkgd,skd->kgqs", q_heads, k_heads, preferred_element_type=jnp.float32) * SCALE
    )
    q_pos = q_start + jnp.arange(n_query, dtype=jnp.int32)
    k_pos = k_start + jnp.arange(n_key, dtype=jnp.int32)
    allowed = (q_docs[:, None] == k_docs[None, :]) & (q_pos[:, None] >= k_pos[None, :])
    scores = jnp.where(allowed, scores, NEG)
    new_peak = jnp.maximum(peak, jnp.max(scores, axis=-1))
    shrink = jnp.exp(peak - new_peak)
    weights = jnp.exp(scores - new_peak[..., None])
    totals = totals * shrink + jnp.sum(weights, axis=-1)
    rounded = weights.astype(jnp.bfloat16)
    added = jnp.einsum("kgqs,skd->kgqd", rounded, v_heads, preferred_element_type=jnp.float32)
    accum = accum * shrink[..., None] + added
    return (new_peak, totals, accum)


def absorb_block(carry, queries, q_docs, q_start, k_piece, v_piece, k_start, doc_ids, flag):
    n_key = k_piece.shape[0]
    k_docs = token_docs(doc_ids, k_start, n_key)
    fresh = attend(carry, queries, q_docs, q_start, k_piece, v_piece, k_docs, k_start)
    return jax.tree.map(lambda new, old: jnp.where(flag, new, old), fresh, carry)


def ring_attention(queries, keys, values, doc_ids, n_ctx, position):
    n_query = queries.shape[0]
    q_start = position * n_query
    q_docs = token_docs(doc_ids, q_start, n_query)
    kv_heads = keys.shape[1] // HEAD_SIZE
    query_group = queries.shape[1] // keys.shape[1]
    carry = (
        jnp.full((kv_heads, query_group, n_query), NEG, jnp.float32),
        jnp.zeros((kv_heads, query_group, n_query), jnp.float32),
        jnp.zeros((kv_heads, query_group, n_query, HEAD_SIZE), jnp.float32),
    )
    always = jnp.array(True)
    carry = absorb_block(carry, queries, q_docs, q_start, keys, values, q_start, doc_ids, always)

    def turn_one(step, state):
        inner_state, moving = state
        moving = from_behind(moving, "ctx", 1)
        start = ((position - step) % n_ctx) * n_query
        inner_state = absorb_block(
            inner_state, queries, q_docs, q_start, moving[0], moving[1], start, doc_ids, always
        )
        return (inner_state, moving)

    _, totals, accum = lax.fori_loop(1, n_ctx, turn_one, (carry, jnp.stack((keys, values))))[0]
    result = accum / totals[..., None]
    return jnp.transpose(result, (2, 0, 1, 3)).reshape(queries.shape).astype(jnp.bfloat16)


def part_rows(attended, place):
    share = attended.shape[0] // 4
    rows = [lax.dynamic_slice_in_dim(attended, (place ^ flip) * share, share, 0) for flip in (2, 3, 0, 1)]
    return jnp.concatenate(rows[:2], axis=0), jnp.concatenate(rows[2:], axis=0)


def per_device(queries, keys, values, doc_ids, out_weight):
    n_ctx = lax.axis_size("ctx")
    heads = lax.axis_size("head")
    position = lax.axis_index("ctx")
    place = lax.axis_index("head")
    other_core = [(i, i ^ 1) for i in range(heads)]
    other_chip = [(i, i ^ 2) for i in range(heads)]
    columns = out_weight.shape[1]
    cut = columns * 4 // 7 // BLOCK * BLOCK

    if n_ctx == 8:
        by_two = [move(x, BY_TWO) for x in (keys, values)]
        beside = [move(x, BESIDE) for x in (keys, values)]
        *state, fetched, open_beside = attend_first(doc_ids, queries, keys, values)
        by_four = [move(after(x, state[0]), AGAIN) for x in by_two]
        swap_two = [
            move(after(after(by_two[0], beside[0]), state[0]), ACROSS),
            move(after(by_two[1], beside[1]), ACROSS),
        ]
        swap_four = [move(by_four[0], ACROSS), move(after(swap_two[1], by_four[0]), AGAIN)]
        chunks = [beside, by_two, by_four]
        *state, weight = attend_next(fetched, open_beside, out_weight, state, chunks, (1, 2, 3))
        chunks = [swap_two, swap_four]
        far, near, mine, send = attend_last(fetched, weight, state, chunks, (4, 5), (0, cut))
    else:
        weight = out_weight
        attended = ring_attention(queries, keys, values, doc_ids, n_ctx, position)
        far, near = part_rows(attended, place)
        mine, send = project(far, weight, (0, cut))
    theirs = hop(send, "head", other_core)
    later_mine, later_send = project(far, weight, (cut, columns))
    mine, later_mine = lax.optimization_barrier((mine, later_mine))
    first_sum = add_up(mine, theirs)
    first_part = hop(first_sum, "head", other_chip)
    later_theirs = hop(later_send, "head", other_core)
    later_mine, first_sum = lax.optimization_barrier((later_mine, first_sum))
    later_sum = add_up(later_mine, later_theirs)
    second_part = hop(later_sum, "head", other_chip)
    near, later_sum = lax.optimization_barrier((near, later_sum))
    mine, *sends = project(near, weight, (0, columns), 3)
    theirs = [hop(send, "head", other_core) for send in sends]
    out = combine(mine, theirs, first_part)
    return combine(mine, theirs, second_part, cut, out)


def solution(mesh):
    placed = (P("ctx", "head"), P("ctx", "head"), P("ctx", "head"), P(), P("head", None))
    return jax.shard_map(
        per_device, mesh=mesh, in_specs=placed, out_specs=P(("ctx", "head"), None), check_vma=False
    )
```

```python
import functools

import jax
import jax.numpy as jnp
from jax import lax
from jax.experimental import pallas as pl
from jax.experimental.pallas import tpu as pltpu
from jax.sharding import PartitionSpec as P

HEAD_SIZE = 128
BLOCK = 128
SCALE = 168.0 ** (-0.5)
LOG2E = 1.4426950408889634
NEG = -1e30
VMEM = pl.BlockSpec(memory_space=pltpu.VMEM)
SMEM = pl.BlockSpec(memory_space=pltpu.SMEM)
HBM = pl.BlockSpec(memory_space=pltpu.HBM)
LIMIT = pltpu.CompilerParams(vmem_limit_bytes=32 * 1024 * 1024)


def hop(block, axis, pairs):
    return lax.ppermute(block, axis, pairs)


def in_place(number, position, n_ctx):
    away = {2: 2, 3: 4, 4: 2, 5: 4}[number]
    return (position < n_ctx * 3 // 4) & (position >= away)


BESIDE = ((0, 1), (2, 3), (4, 5), (6, 7))
BY_TWO = ((0, 2, 4), (1, 3, 5))
AGAIN = ((2, 4), (3, 5))
ACROSS = ((2, 3), (4, 5))
LAST = ((4, 5),)


def move(block, rings):
    n_ctx, heads = lax.axis_size("ctx"), lax.axis_size("head")
    target = {ring[i]: ring[(i + 1) % len(ring)] for ring in rings for i in range(len(ring))}
    pairs = [
        (i * heads + h, target[i] * heads + h if i in target else i * heads + (h ^ 1))
        for i in range(n_ctx)
        for h in range(heads)
    ]
    return lax.ppermute(block, ("ctx", "head"), pairs)


def after(x, event):
    return lax.optimization_barrier((x, event))[0]


def score_blocks(doors, q, a, h, chunks, numbers):
    position = lax.axis_index("ctx")
    n_ctx = lax.axis_size("ctx")
    n_query = chunks[0][0].shape[0]
    scores = []
    for (keys, _), c in zip(chunks, numbers):
        count = (a + 1) * BLOCK if c == 0 else n_query
        k = keys[:count, h * HEAD_SIZE : (h + 1) * HEAD_SIZE]
        s = lax.dot_general(q, k, (((1,), (1,)), ((), ())), preferred_element_type=jnp.float32)
        for b in range(count // BLOCK):
            part = s[:, b * BLOCK : (b + 1) * BLOCK]
            if c == 0 and b == a:
                row = lax.broadcasted_iota(jnp.int32, part.shape, 0) % BLOCK
                col = lax.broadcasted_iota(jnp.int32, part.shape, 1)
                part = jnp.where(row >= col, part, NEG)
            elif c < 2:
                part = part + doors(c, a, b)
            else:
                part = part + jnp.where(in_place(c, position, n_ctx), 0.0, NEG)
            scores.append(part)
    return scores


def weigh(scores, peak, factor, a, h, chunks, numbers):
    n_query = chunks[0][0].shape[0]
    total = added = None
    scores = list(scores)
    for (_, values), c in zip(chunks, numbers):
        count = (a + 1) * BLOCK if c == 0 else n_query
        parts = []
        for b in range(count // BLOCK):
            w = jnp.exp2(scores.pop(0) * factor - peak)
            total = w if total is None else total + w
            parts.append(w.astype(jnp.bfloat16))
        w = jnp.concatenate(parts, axis=1) if len(parts) > 1 else parts[0]
        v = values[:count, h * HEAD_SIZE : (h + 1) * HEAD_SIZE]
        term = jnp.dot(w, v, preferred_element_type=jnp.float32)
        added = term if added is None else added + term
    return total, added


def head_slices(queries, keys, h):
    group = queries.shape[1] // keys.shape[1]
    return [slice((h * group + g) * HEAD_SIZE, (h * group + g + 1) * HEAD_SIZE) for g in range(group)]


def absorb(numbers, doors, queries, chunks, before, after):
    n_query = queries.shape[0]
    factor = SCALE * LOG2E
    parts = []
    for a in range(n_query // BLOCK):
        for h in range(chunks[0][0].shape[1] // HEAD_SIZE):
            heads = head_slices(queries, chunks[0][0], h)
            size = len(heads) * BLOCK
            parts.append((a, h, heads, slice(len(parts) * size, (len(parts) + 1) * size)))
    scores = []
    for a, h, heads, _ in parts:
        q = jnp.concatenate([queries[a * BLOCK : (a + 1) * BLOCK, s] for s in heads], axis=0)
        scores.append(score_blocks(doors, q, a, h, chunks, numbers))
    peaks = [functools.reduce(jnp.maximum, s) for s in scores]
    peaks = [jnp.max(peak, axis=1, keepdims=True) * factor for peak in peaks]
    shrinks = None
    if before is None:
        peaks = [jnp.broadcast_to(peak, (peak.shape[0], HEAD_SIZE)) for peak in peaks]
    else:
        lasts = [before[0][rows, :] for _, _, _, rows in parts]
        peaks = [jnp.maximum(last, peak) for last, peak in zip(lasts, peaks)]
        shrinks = [jnp.exp2(last - peak) for last, peak in zip(lasts, peaks)]
    sums = [
        weigh(s, peak, factor, a, h, chunks, numbers)
        for s, peak, (a, h, _, _) in zip(scores, peaks, parts)
    ]
    for i, (a, h, heads, rows) in enumerate(parts):
        total, added = sums[i]
        if before is not None:
            total = total + before[1][rows, :] * shrinks[i]
            added = added + before[2][rows, :] * shrinks[i]
        sums[i] = (total, added)
    after(parts, peaks, sums)


def store_state(state):
    def after(parts, peaks, sums):
        for (_, _, _, rows), peak, (total, added) in zip(parts, peaks, sums):
            for ref, part in zip(state, (peak, total, added)):
                ref[rows, :] = part

    return after


def pairs_of(refs):
    return list(zip(refs[0::2], refs[1::2]))


def first_kernel(docs_in, queries_in, keys_in, values_in, *refs):
    *state, queries, open_beside, docs, keys, values, sems = refs
    places = ((docs_in, docs), (queries_in, queries), (keys_in, keys), (values_in, values))
    fetches = [pltpu.make_async_copy(a, b, sems.at[i]) for i, (a, b) in enumerate(places)]
    for fetch in fetches:
        fetch.start()
    for fetch in fetches:
        fetch.wait()
    position = lax.axis_index("ctx")
    q_blocks = queries.shape[0] // BLOCK

    def doors(number, a, b):
        source = position if number == 0 else jnp.maximum(position - 1, 0)
        seen = docs[source * q_blocks + b] == docs[position * q_blocks + a]
        if number == 1:
            seen = seen & (position % 2 == 1)
        return jnp.where(seen, 0.0, NEG)

    for a in range(q_blocks):
        for b in range(q_blocks):
            part = open_beside.at[a * 8 : (a + 1) * 8, b * BLOCK : (b + 1) * BLOCK]
            part[...] = jnp.full(part.shape, doors(1, a, b), jnp.float32)
    absorb((0,), doors, queries, [(keys, values)], None, store_state(state))


def next_kernel(numbers, queries, open_beside, weight_in, *refs):
    *refs, weight, sem = refs
    fetch = pltpu.make_async_copy(weight_in, weight, sem)
    fetch.start()
    pairs = 2 * len(numbers)

    def doors(number, a, b):
        return open_beside[a * 8 : a * 8 + 1, b * BLOCK : (b + 1) * BLOCK]

    absorb(numbers, doors, queries, pairs_of(refs[3 : 3 + pairs]), refs[:3], store_state(refs[3 + pairs :]))
    fetch.wait()


def attend_cost(queries, numbers, fetched=0):
    n_query, width = queries.shape
    count = len(numbers) * n_query
    return pl.CostEstimate(
        flops=4 * n_query * width * count,
        bytes_accessed=fetched,
        transcendentals=n_query * count * width // HEAD_SIZE,
    )


def state_shapes(queries):
    rows = queries.size // HEAD_SIZE
    return (pltpu.VMEM((rows, HEAD_SIZE), jnp.float32),) * 3


def attend_first(docs, queries, keys, values):
    n_query = queries.shape[0]
    return pl.pallas_call(
        first_kernel,
        out_shape=state_shapes(queries)
        + (
            pltpu.VMEM(queries.shape, queries.dtype),
            pltpu.VMEM((8 * n_query // BLOCK, n_query), jnp.float32),
        ),
        in_specs=[HBM] * 4,
        out_specs=(VMEM,) * 5,
        scratch_shapes=[
            pltpu.SMEM(docs.shape, docs.dtype),
            pltpu.VMEM(keys.shape, keys.dtype),
            pltpu.VMEM(values.shape, values.dtype),
            pltpu.SemaphoreType.DMA((4,)),
        ],
        compiler_params=LIMIT,
        cost_estimate=attend_cost(queries, (0,)),
        name="attend_first",
    )(*[pltpu.with_memory_space_constraint(x, pltpu.HBM) for x in (docs, queries, keys, values)])


def attend_next(queries, open_beside, weight, state, chunks, numbers):
    return pl.pallas_call(
        functools.partial(next_kernel, numbers),
        out_shape=state_shapes(queries) + (pltpu.VMEM(weight.shape, weight.dtype),),
        in_specs=[VMEM, VMEM, HBM] + [VMEM] * (3 + 2 * len(chunks)),
        out_specs=(VMEM,) * 4,
        scratch_shapes=[pltpu.SemaphoreType.DMA],
        compiler_params=LIMIT,
        cost_estimate=attend_cost(queries, numbers, 2 * weight.size),
        name="attend_next",
    )(
        queries,
        open_beside,
        pltpu.with_memory_space_constraint(weight, pltpu.HBM),
        *state,
        *[x for pair in chunks for x in pair],
    )


def last_kernel(numbers, columns, queries, weight, *refs):
    pairs = 2 * len(numbers)
    chunks = pairs_of(refs[3 : 3 + pairs])
    far, near, mine, send, attended = refs[3 + pairs :]

    def after(parts, peaks, sums):
        inverses = [1.0 / jnp.sum(total, axis=1, keepdims=True) for total, _ in sums]
        for (a, _, heads, _), inverse, (_, added) in zip(parts, inverses, sums):
            result = (added * inverse).astype(jnp.bfloat16)
            for g, head in enumerate(heads):
                attended[a * BLOCK : (a + 1) * BLOCK, head] = result[g * BLOCK : (g + 1) * BLOCK]

    absorb(numbers, None, queries, chunks, refs[:3], after)
    place = lax.axis_index("head")
    share = queries.shape[0] // 4
    for half, owners in ((far, (place ^ 2, place ^ 3)), (near, (place, place ^ 1))):
        for i, owner in enumerate(owners):
            source = pl.ds(pl.multiple_of(owner * share, share), share)
            half[i * share : (i + 1) * share, :] = attended[source, :]
    project_columns(far, weight, mine, (send,), *columns)


def attend_last(queries, weight, state, chunks, numbers, columns):
    n_query, width = queries.shape
    half = jax.ShapeDtypeStruct((n_query // 2, width), jnp.bfloat16)
    return pl.pallas_call(
        functools.partial(last_kernel, numbers, columns),
        out_shape=(half, half) + project_shapes(n_query // 4, columns[1] - columns[0]),
        in_specs=[VMEM] * (5 + 2 * len(numbers)),
        out_specs=(VMEM,) * 4,
        scratch_shapes=[pltpu.VMEM(queries.shape, jnp.bfloat16)],
        compiler_params=LIMIT,
        cost_estimate=attend_cost(queries, numbers),
        name="attend_last",
    )(queries, weight, *state, *[x for pair in chunks for x in pair])


def project_shapes(rows, count, sends=1):
    send = jax.ShapeDtypeStruct((rows, count // sends), jnp.bfloat16)
    return (jax.ShapeDtypeStruct((rows, count), jnp.float32),) + (send,) * sends


def project_columns(rows, weight, mine, sends, start, end):
    share = rows.shape[0] // 2
    width = sends[0].shape[1]
    for i, send in enumerate(sends):
        for at in range(0, width, 768):
            stop = min(at + 768, width)
            columns = weight[:, start + i * width + at : start + i * width + stop]
            product = jnp.dot(rows[...], columns, preferred_element_type=jnp.float32)
            mine[:, i * width + at : i * width + stop] = product[:share]
            send[:, at:stop] = product[share:].astype(send.dtype)


def project_kernel(columns, rows, weight, mine, *sends):
    project_columns(rows, weight, mine, sends, *columns)


def project(rows, weight, columns, sends=1):
    count = columns[1] - columns[0]
    return pl.pallas_call(
        functools.partial(project_kernel, columns),
        out_shape=project_shapes(rows.shape[0] // 2, count, sends),
        in_specs=[VMEM, VMEM],
        out_specs=(VMEM,) * (1 + sends),
        compiler_params=LIMIT,
        cost_estimate=pl.CostEstimate(
            flops=2 * rows.shape[0] * rows.shape[1] * count, bytes_accessed=0, transcendentals=0
        ),
        name="project",
    )(rows, weight)


def add_kernel(mine, theirs, out):
    out[...] = (mine[...] + theirs[...].astype(jnp.float32)).astype(out.dtype)


def add_up(mine, theirs):
    return pl.pallas_call(
        add_kernel,
        out_shape=jax.ShapeDtypeStruct(theirs.shape, theirs.dtype),
        in_specs=[VMEM, VMEM],
        out_specs=VMEM,
        compiler_params=LIMIT,
        cost_estimate=pl.CostEstimate(flops=theirs.size, bytes_accessed=0, transcendentals=0),
        name="add_up",
    )(mine, theirs)


def combine_kernel(at, mine, across, *refs):
    *beside, out, total, sem = refs
    width = across.shape[1]
    left = 0
    for part in beside[: len(beside) - (at > 0)]:
        low, high = max(left, at), min(left + part.shape[1], at + width)
        if low < high:
            piece = mine[:, low:high] + part[:, low - left : high - left].astype(jnp.float32)
            piece += across[:, low - at : high - at].astype(jnp.float32)
            total[:, low - at : high - at] = piece.astype(total.dtype)
        left += part.shape[1]
    copy = pltpu.make_async_copy(total, out.at[:, at : at + width], sem)
    copy.start()
    copy.wait()


def combine(mine, beside, across, at=0, out=None):
    outs = [] if out is None else [out]
    return pl.pallas_call(
        functools.partial(combine_kernel, at),
        out_shape=jax.ShapeDtypeStruct(mine.shape, across.dtype),
        in_specs=[VMEM] * (2 + len(beside)) + [HBM] * len(outs),
        out_specs=HBM,
        scratch_shapes=[pltpu.VMEM(across.shape, across.dtype), pltpu.SemaphoreType.DMA],
        input_output_aliases={2 + len(beside): 0} if outs else {},
        compiler_params=LIMIT,
        name="combine",
    )(mine, across, *beside, *outs)


def from_behind(block, axis, distance):
    devices = range(lax.axis_size(axis))
    route = [(i - distance, i) for i in devices if i - distance in devices]
    return lax.ppermute(block, axis, route)


def token_docs(doc_ids, start, count):
    blocks = (start + jnp.arange(count, dtype=jnp.int32)) // BLOCK
    table = blocks[:, None] == jnp.arange(doc_ids.shape[0], dtype=jnp.int32)[None, :]
    return jnp.sum(jnp.where(table, doc_ids[None, :], 0), axis=1)


def attend(carry, queries, q_docs, q_start, k_piece, v_piece, k_docs, k_start):
    peak, totals, accum = carry
    n_query = queries.shape[0]
    n_key = k_piece.shape[0]
    kv_heads = k_piece.shape[1] // HEAD_SIZE
    query_group = queries.shape[1] // k_piece.shape[1]
    q_heads = queries.reshape(n_query, kv_heads, query_group, HEAD_SIZE)
    k_heads = k_piece.reshape(n_key, kv_heads, HEAD_SIZE)
    v_heads = v_piece.reshape(n_key, kv_heads, HEAD_SIZE)
    scores = (
        jnp.einsum("qkgd,skd->kgqs", q_heads, k_heads, preferred_element_type=jnp.float32) * SCALE
    )
    q_pos = q_start + jnp.arange(n_query, dtype=jnp.int32)
    k_pos = k_start + jnp.arange(n_key, dtype=jnp.int32)
    allowed = (q_docs[:, None] == k_docs[None, :]) & (q_pos[:, None] >= k_pos[None, :])
    scores = jnp.where(allowed, scores, NEG)
    new_peak = jnp.maximum(peak, jnp.max(scores, axis=-1))
    shrink = jnp.exp(peak - new_peak)
    weights = jnp.exp(scores - new_peak[..., None])
    totals = totals * shrink + jnp.sum(weights, axis=-1)
    rounded = weights.astype(jnp.bfloat16)
    added = jnp.einsum("kgqs,skd->kgqd", rounded, v_heads, preferred_element_type=jnp.float32)
    accum = accum * shrink[..., None] + added
    return (new_peak, totals, accum)


def absorb_block(carry, queries, q_docs, q_start, k_piece, v_piece, k_start, doc_ids, flag):
    n_key = k_piece.shape[0]
    k_docs = token_docs(doc_ids, k_start, n_key)
    fresh = attend(carry, queries, q_docs, q_start, k_piece, v_piece, k_docs, k_start)
    return jax.tree.map(lambda new, old: jnp.where(flag, new, old), fresh, carry)


def ring_attention(queries, keys, values, doc_ids, n_ctx, position):
    n_query = queries.shape[0]
    q_start = position * n_query
    q_docs = token_docs(doc_ids, q_start, n_query)
    kv_heads = keys.shape[1] // HEAD_SIZE
    query_group = queries.shape[1] // keys.shape[1]
    carry = (
        jnp.full((kv_heads, query_group, n_query), NEG, jnp.float32),
        jnp.zeros((kv_heads, query_group, n_query), jnp.float32),
        jnp.zeros((kv_heads, query_group, n_query, HEAD_SIZE), jnp.float32),
    )
    always = jnp.array(True)
    carry = absorb_block(carry, queries, q_docs, q_start, keys, values, q_start, doc_ids, always)

    def turn_one(step, state):
        inner_state, moving = state
        moving = from_behind(moving, "ctx", 1)
        start = ((position - step) % n_ctx) * n_query
        inner_state = absorb_block(
            inner_state, queries, q_docs, q_start, moving[0], moving[1], start, doc_ids, always
        )
        return (inner_state, moving)

    _, totals, accum = lax.fori_loop(1, n_ctx, turn_one, (carry, jnp.stack((keys, values))))[0]
    result = accum / totals[..., None]
    return jnp.transpose(result, (2, 0, 1, 3)).reshape(queries.shape).astype(jnp.bfloat16)


def part_rows(attended, place):
    share = attended.shape[0] // 4
    rows = [lax.dynamic_slice_in_dim(attended, (place ^ flip) * share, share, 0) for flip in (2, 3, 0, 1)]
    return jnp.concatenate(rows[:2], axis=0), jnp.concatenate(rows[2:], axis=0)


def per_device(queries, keys, values, doc_ids, out_weight):
    n_ctx = lax.axis_size("ctx")
    heads = lax.axis_size("head")
    position = lax.axis_index("ctx")
    place = lax.axis_index("head")
    other_core = [(i, i ^ 1) for i in range(heads)]
    other_chip = [(i, i ^ 2) for i in range(heads)]
    columns = out_weight.shape[1]
    cut = columns * 4 // 7 // BLOCK * BLOCK

    if n_ctx == 8:
        by_two = [move(x, BY_TWO) for x in (keys, values)]
        beside = [move(x, BESIDE) for x in (keys, values)]
        *state, fetched, open_beside = attend_first(doc_ids, queries, keys, values)
        by_four = [move(after(x, state[0]), AGAIN) for x in by_two]
        swap_two = [
            move(after(after(by_two[0], beside[0]), state[0]), ACROSS),
            move(after(by_two[1], beside[1]), ACROSS),
        ]
        swap_four = [move(after(swap_two[0], by_four[0]), AGAIN), move(by_four[1], LAST)]
        chunks = [beside, by_two, by_four]
        *state, weight = attend_next(fetched, open_beside, out_weight, state, chunks, (1, 2, 3))
        chunks = [swap_two, swap_four]
        far, near, mine, send = attend_last(fetched, weight, state, chunks, (4, 5), (0, cut))
    else:
        weight = out_weight
        attended = ring_attention(queries, keys, values, doc_ids, n_ctx, position)
        far, near = part_rows(attended, place)
        mine, send = project(far, weight, (0, cut))
    theirs = hop(send, "head", other_core)
    later_mine, later_send = project(far, weight, (cut, columns))
    mine, later_mine = lax.optimization_barrier((mine, later_mine))
    first_sum = add_up(mine, theirs)
    first_part = hop(first_sum, "head", other_chip)
    later_theirs = hop(later_send, "head", other_core)
    later_mine, first_sum = lax.optimization_barrier((later_mine, first_sum))
    later_sum = add_up(later_mine, later_theirs)
    second_part = hop(later_sum, "head", other_chip)
    near, later_sum = lax.optimization_barrier((near, later_sum))
    mine, *sends = project(near, weight, (0, columns), 3)
    theirs = [hop(send, "head", other_core) for send in sends]
    out = combine(mine, theirs, first_part)
    return combine(mine, theirs, second_part, cut, out)


def solution(mesh):
    placed = (P("ctx", "head"), P("ctx", "head"), P("ctx", "head"), P(), P("head", None))
    return jax.shard_map(
        per_device, mesh=mesh, in_specs=placed, out_specs=P(("ctx", "head"), None), check_vma=False
    )
```

```python
import functools

import jax
import jax.numpy as jnp
from jax import lax
from jax.experimental import pallas as pl
from jax.experimental.pallas import tpu as pltpu
from jax.sharding import PartitionSpec as P

HEAD_SIZE = 128
BLOCK = 128
SCALE = 168.0 ** (-0.5)
LOG2E = 1.4426950408889634
NEG = -1e30
VMEM = pl.BlockSpec(memory_space=pltpu.VMEM)
SMEM = pl.BlockSpec(memory_space=pltpu.SMEM)
HBM = pl.BlockSpec(memory_space=pltpu.HBM)
LIMIT = pltpu.CompilerParams(vmem_limit_bytes=32 * 1024 * 1024)


def hop(block, axis, pairs):
    return lax.ppermute(block, axis, pairs)


def in_place(number, position, n_ctx):
    away = {2: 2, 3: 4, 4: 2, 5: 4}[number]
    return (position < n_ctx * 3 // 4) & (position >= away)


BESIDE = ((0, 1), (2, 3), (4, 5), (6, 7))
BY_TWO = ((0, 2, 4), (1, 3, 5))
AGAIN = ((2, 4), (3, 5))
ACROSS = ((2, 3), (4, 5))
LAST = ((4, 5),)


def move(block, rings):
    n_ctx, heads = lax.axis_size("ctx"), lax.axis_size("head")
    target = {ring[i]: ring[(i + 1) % len(ring)] for ring in rings for i in range(len(ring))}
    pairs = [
        (i * heads + h, target[i] * heads + h if i in target else i * heads + (h ^ 1))
        for i in range(n_ctx)
        for h in range(heads)
    ]
    return lax.ppermute(block, ("ctx", "head"), pairs)


def after(x, event):
    return lax.optimization_barrier((x, event))[0]


def score_blocks(doors, q, a, h, chunks, numbers):
    position = lax.axis_index("ctx")
    n_ctx = lax.axis_size("ctx")
    n_query = chunks[0][0].shape[0]
    scores = []
    for (keys, _), c in zip(chunks, numbers):
        count = (a + 1) * BLOCK if c == 0 else n_query
        k = keys[:count, h * HEAD_SIZE : (h + 1) * HEAD_SIZE]
        s = lax.dot_general(q, k, (((1,), (1,)), ((), ())), preferred_element_type=jnp.float32)
        for b in range(count // BLOCK):
            part = s[:, b * BLOCK : (b + 1) * BLOCK]
            if c == 0 and b == a:
                row = lax.broadcasted_iota(jnp.int32, part.shape, 0) % BLOCK
                col = lax.broadcasted_iota(jnp.int32, part.shape, 1)
                part = jnp.where(row >= col, part, NEG)
            elif c < 2:
                part = part + doors(c, a, b)
            else:
                part = part + jnp.where(in_place(c, position, n_ctx), 0.0, NEG)
            scores.append(part)
    return scores


def weigh(scores, peak, factor, a, h, chunks, numbers):
    n_query = chunks[0][0].shape[0]
    total = added = None
    scores = list(scores)
    for (_, values), c in zip(chunks, numbers):
        count = (a + 1) * BLOCK if c == 0 else n_query
        parts = []
        for b in range(count // BLOCK):
            w = jnp.exp2(scores.pop(0) * factor - peak)
            total = w if total is None else total + w
            parts.append(w.astype(jnp.bfloat16))
        w = jnp.concatenate(parts, axis=1) if len(parts) > 1 else parts[0]
        v = values[:count, h * HEAD_SIZE : (h + 1) * HEAD_SIZE]
        term = jnp.dot(w, v, preferred_element_type=jnp.float32)
        added = term if added is None else added + term
    return total, added


def head_slices(queries, keys, h):
    group = queries.shape[1] // keys.shape[1]
    return [slice((h * group + g) * HEAD_SIZE, (h * group + g + 1) * HEAD_SIZE) for g in range(group)]


def absorb(numbers, doors, queries, chunks, before, after):
    n_query = queries.shape[0]
    factor = SCALE * LOG2E
    parts = []
    for a in range(n_query // BLOCK):
        for h in range(chunks[0][0].shape[1] // HEAD_SIZE):
            heads = head_slices(queries, chunks[0][0], h)
            size = len(heads) * BLOCK
            parts.append((a, h, heads, slice(len(parts) * size, (len(parts) + 1) * size)))
    scores = []
    for a, h, heads, _ in parts:
        q = jnp.concatenate([queries[a * BLOCK : (a + 1) * BLOCK, s] for s in heads], axis=0)
        scores.append(score_blocks(doors, q, a, h, chunks, numbers))
    peaks = [functools.reduce(jnp.maximum, s) for s in scores]
    peaks = [jnp.max(peak, axis=1, keepdims=True) * factor for peak in peaks]
    shrinks = None
    if before is None:
        peaks = [jnp.broadcast_to(peak, (peak.shape[0], HEAD_SIZE)) for peak in peaks]
    else:
        lasts = [before[0][rows, :] for _, _, _, rows in parts]
        peaks = [jnp.maximum(last, peak) for last, peak in zip(lasts, peaks)]
        shrinks = [jnp.exp2(last - peak) for last, peak in zip(lasts, peaks)]
    sums = [
        weigh(s, peak, factor, a, h, chunks, numbers)
        for s, peak, (a, h, _, _) in zip(scores, peaks, parts)
    ]
    for i, (a, h, heads, rows) in enumerate(parts):
        total, added = sums[i]
        if before is not None:
            total = total + before[1][rows, :] * shrinks[i]
            added = added + before[2][rows, :] * shrinks[i]
        sums[i] = (total, added)
    after(parts, peaks, sums)


def store_state(state):
    def after(parts, peaks, sums):
        for (_, _, _, rows), peak, (total, added) in zip(parts, peaks, sums):
            for ref, part in zip(state, (peak, total, added)):
                ref[rows, :] = part

    return after


def pairs_of(refs):
    return list(zip(refs[0::2], refs[1::2]))


def first_kernel(docs_in, queries_in, keys_in, values_in, *refs):
    *state, queries, open_beside, docs, keys, values, sems = refs
    places = ((docs_in, docs), (queries_in, queries), (keys_in, keys), (values_in, values))
    fetches = [pltpu.make_async_copy(a, b, sems.at[i]) for i, (a, b) in enumerate(places)]
    for fetch in fetches:
        fetch.start()
    for fetch in fetches:
        fetch.wait()
    position = lax.axis_index("ctx")
    q_blocks = queries.shape[0] // BLOCK

    def doors(number, a, b):
        source = position if number == 0 else jnp.maximum(position - 1, 0)
        seen = docs[source * q_blocks + b] == docs[position * q_blocks + a]
        if number == 1:
            seen = seen & (position % 2 == 1)
        return jnp.where(seen, 0.0, NEG)

    for a in range(q_blocks):
        for b in range(q_blocks):
            part = open_beside.at[a * 8 : (a + 1) * 8, b * BLOCK : (b + 1) * BLOCK]
            part[...] = jnp.full(part.shape, doors(1, a, b), jnp.float32)
    absorb((0,), doors, queries, [(keys, values)], None, store_state(state))


def next_kernel(numbers, queries, open_beside, weight_in, *refs):
    *refs, weight, sem = refs
    fetch = pltpu.make_async_copy(weight_in, weight, sem)
    fetch.start()
    pairs = 2 * len(numbers)

    def doors(number, a, b):
        return open_beside[a * 8 : a * 8 + 1, b * BLOCK : (b + 1) * BLOCK]

    absorb(numbers, doors, queries, pairs_of(refs[3 : 3 + pairs]), refs[:3], store_state(refs[3 + pairs :]))
    fetch.wait()


def attend_cost(queries, numbers, fetched=0):
    n_query, width = queries.shape
    count = len(numbers) * n_query
    return pl.CostEstimate(
        flops=4 * n_query * width * count,
        bytes_accessed=fetched,
        transcendentals=n_query * count * width // HEAD_SIZE,
    )


def state_shapes(queries):
    rows = queries.size // HEAD_SIZE
    return (pltpu.VMEM((rows, HEAD_SIZE), jnp.float32),) * 3


def attend_first(docs, queries, keys, values):
    n_query = queries.shape[0]
    return pl.pallas_call(
        first_kernel,
        out_shape=state_shapes(queries)
        + (
            pltpu.VMEM(queries.shape, queries.dtype),
            pltpu.VMEM((8 * n_query // BLOCK, n_query), jnp.float32),
        ),
        in_specs=[HBM] * 4,
        out_specs=(VMEM,) * 5,
        scratch_shapes=[
            pltpu.SMEM(docs.shape, docs.dtype),
            pltpu.VMEM(keys.shape, keys.dtype),
            pltpu.VMEM(values.shape, values.dtype),
            pltpu.SemaphoreType.DMA((4,)),
        ],
        compiler_params=LIMIT,
        cost_estimate=attend_cost(queries, (0,)),
        name="attend_first",
    )(*[pltpu.with_memory_space_constraint(x, pltpu.HBM) for x in (docs, queries, keys, values)])


def attend_next(queries, open_beside, weight, state, chunks, numbers):
    return pl.pallas_call(
        functools.partial(next_kernel, numbers),
        out_shape=state_shapes(queries) + (pltpu.VMEM(weight.shape, weight.dtype),),
        in_specs=[VMEM, VMEM, HBM] + [VMEM] * (3 + 2 * len(chunks)),
        out_specs=(VMEM,) * 4,
        scratch_shapes=[pltpu.SemaphoreType.DMA],
        compiler_params=LIMIT,
        cost_estimate=attend_cost(queries, numbers, 2 * weight.size),
        name="attend_next",
    )(
        queries,
        open_beside,
        pltpu.with_memory_space_constraint(weight, pltpu.HBM),
        *state,
        *[x for pair in chunks for x in pair],
    )


def last_kernel(numbers, columns, queries, weight, *refs):
    pairs = 2 * len(numbers)
    chunks = pairs_of(refs[3 : 3 + pairs])
    far, near, mine, send, attended = refs[3 + pairs :]

    def after(parts, peaks, sums):
        inverses = [1.0 / jnp.sum(total, axis=1, keepdims=True) for total, _ in sums]
        for (a, _, heads, _), inverse, (_, added) in zip(parts, inverses, sums):
            result = (added * inverse).astype(jnp.bfloat16)
            for g, head in enumerate(heads):
                attended[a * BLOCK : (a + 1) * BLOCK, head] = result[g * BLOCK : (g + 1) * BLOCK]

    absorb(numbers, None, queries, chunks, refs[:3], after)
    place = lax.axis_index("head")
    share = queries.shape[0] // 4
    for half, owners in ((far, (place ^ 2, place ^ 3)), (near, (place, place ^ 1))):
        for i, owner in enumerate(owners):
            source = pl.ds(pl.multiple_of(owner * share, share), share)
            half[i * share : (i + 1) * share, :] = attended[source, :]
    project_columns(far, weight, mine, (send,), *columns)


def attend_last(queries, weight, state, chunks, numbers, columns):
    n_query, width = queries.shape
    half = jax.ShapeDtypeStruct((n_query // 2, width), jnp.bfloat16)
    return pl.pallas_call(
        functools.partial(last_kernel, numbers, columns),
        out_shape=(half, half) + project_shapes(n_query // 4, columns[1] - columns[0]),
        in_specs=[VMEM] * (5 + 2 * len(numbers)),
        out_specs=(VMEM,) * 4,
        scratch_shapes=[pltpu.VMEM(queries.shape, jnp.bfloat16)],
        compiler_params=LIMIT,
        cost_estimate=attend_cost(queries, numbers),
        name="attend_last",
    )(queries, weight, *state, *[x for pair in chunks for x in pair])


def project_shapes(rows, count, sends=1):
    send = jax.ShapeDtypeStruct((rows, count // sends), jnp.bfloat16)
    return (jax.ShapeDtypeStruct((rows, count), jnp.float32),) + (send,) * sends


def project_columns(rows, weight, mine, sends, start, end):
    share = rows.shape[0] // 2
    width = sends[0].shape[1]
    for i, send in enumerate(sends):
        for at in range(0, width, 768):
            stop = min(at + 768, width)
            columns = weight[:, start + i * width + at : start + i * width + stop]
            product = jnp.dot(rows[...], columns, preferred_element_type=jnp.float32)
            mine[:, i * width + at : i * width + stop] = product[:share]
            send[:, at:stop] = product[share:].astype(send.dtype)


def project_kernel(columns, rows, weight, mine, *sends):
    project_columns(rows, weight, mine, sends, *columns)


def project(rows, weight, columns, sends=1):
    count = columns[1] - columns[0]
    return pl.pallas_call(
        functools.partial(project_kernel, columns),
        out_shape=project_shapes(rows.shape[0] // 2, count, sends),
        in_specs=[VMEM, VMEM],
        out_specs=(VMEM,) * (1 + sends),
        compiler_params=LIMIT,
        cost_estimate=pl.CostEstimate(
            flops=2 * rows.shape[0] * rows.shape[1] * count, bytes_accessed=0, transcendentals=0
        ),
        name="project",
    )(rows, weight)


def add_kernel(mine, theirs, out):
    out[...] = (mine[...] + theirs[...].astype(jnp.float32)).astype(out.dtype)


def add_up(mine, theirs):
    return pl.pallas_call(
        add_kernel,
        out_shape=jax.ShapeDtypeStruct(theirs.shape, theirs.dtype),
        in_specs=[VMEM, VMEM],
        out_specs=VMEM,
        compiler_params=LIMIT,
        cost_estimate=pl.CostEstimate(flops=theirs.size, bytes_accessed=0, transcendentals=0),
        name="add_up",
    )(mine, theirs)


def combine_kernel(at, mine, across, *refs):
    *beside, out, total, sem = refs
    width = across.shape[1]
    left = 0
    for part in beside[: len(beside) - (at > 0)]:
        low, high = max(left, at), min(left + part.shape[1], at + width)
        if low < high:
            piece = mine[:, low:high] + part[:, low - left : high - left].astype(jnp.float32)
            piece += across[:, low - at : high - at].astype(jnp.float32)
            total[:, low - at : high - at] = piece.astype(total.dtype)
        left += part.shape[1]
    copy = pltpu.make_async_copy(total, out.at[:, at : at + width], sem)
    copy.start()
    copy.wait()


def combine(mine, beside, across, at=0, out=None):
    outs = [] if out is None else [out]
    return pl.pallas_call(
        functools.partial(combine_kernel, at),
        out_shape=jax.ShapeDtypeStruct(mine.shape, across.dtype),
        in_specs=[VMEM] * (2 + len(beside)) + [HBM] * len(outs),
        out_specs=HBM,
        scratch_shapes=[pltpu.VMEM(across.shape, across.dtype), pltpu.SemaphoreType.DMA],
        input_output_aliases={2 + len(beside): 0} if outs else {},
        compiler_params=LIMIT,
        name="combine",
    )(mine, across, *beside, *outs)


def from_behind(block, axis, distance):
    devices = range(lax.axis_size(axis))
    route = [(i - distance, i) for i in devices if i - distance in devices]
    return lax.ppermute(block, axis, route)


def token_docs(doc_ids, start, count):
    blocks = (start + jnp.arange(count, dtype=jnp.int32)) // BLOCK
    table = blocks[:, None] == jnp.arange(doc_ids.shape[0], dtype=jnp.int32)[None, :]
    return jnp.sum(jnp.where(table, doc_ids[None, :], 0), axis=1)


def attend(carry, queries, q_docs, q_start, k_piece, v_piece, k_docs, k_start):
    peak, totals, accum = carry
    n_query = queries.shape[0]
    n_key = k_piece.shape[0]
    kv_heads = k_piece.shape[1] // HEAD_SIZE
    query_group = queries.shape[1] // k_piece.shape[1]
    q_heads = queries.reshape(n_query, kv_heads, query_group, HEAD_SIZE)
    k_heads = k_piece.reshape(n_key, kv_heads, HEAD_SIZE)
    v_heads = v_piece.reshape(n_key, kv_heads, HEAD_SIZE)
    scores = (
        jnp.einsum("qkgd,skd->kgqs", q_heads, k_heads, preferred_element_type=jnp.float32) * SCALE
    )
    q_pos = q_start + jnp.arange(n_query, dtype=jnp.int32)
    k_pos = k_start + jnp.arange(n_key, dtype=jnp.int32)
    allowed = (q_docs[:, None] == k_docs[None, :]) & (q_pos[:, None] >= k_pos[None, :])
    scores = jnp.where(allowed, scores, NEG)
    new_peak = jnp.maximum(peak, jnp.max(scores, axis=-1))
    shrink = jnp.exp(peak - new_peak)
    weights = jnp.exp(scores - new_peak[..., None])
    totals = totals * shrink + jnp.sum(weights, axis=-1)
    rounded = weights.astype(jnp.bfloat16)
    added = jnp.einsum("kgqs,skd->kgqd", rounded, v_heads, preferred_element_type=jnp.float32)
    accum = accum * shrink[..., None] + added
    return (new_peak, totals, accum)


def absorb_block(carry, queries, q_docs, q_start, k_piece, v_piece, k_start, doc_ids, flag):
    n_key = k_piece.shape[0]
    k_docs = token_docs(doc_ids, k_start, n_key)
    fresh = attend(carry, queries, q_docs, q_start, k_piece, v_piece, k_docs, k_start)
    return jax.tree.map(lambda new, old: jnp.where(flag, new, old), fresh, carry)


def ring_attention(queries, keys, values, doc_ids, n_ctx, position):
    n_query = queries.shape[0]
    q_start = position * n_query
    q_docs = token_docs(doc_ids, q_start, n_query)
    kv_heads = keys.shape[1] // HEAD_SIZE
    query_group = queries.shape[1] // keys.shape[1]
    carry = (
        jnp.full((kv_heads, query_group, n_query), NEG, jnp.float32),
        jnp.zeros((kv_heads, query_group, n_query), jnp.float32),
        jnp.zeros((kv_heads, query_group, n_query, HEAD_SIZE), jnp.float32),
    )
    always = jnp.array(True)
    carry = absorb_block(carry, queries, q_docs, q_start, keys, values, q_start, doc_ids, always)

    def turn_one(step, state):
        inner_state, moving = state
        moving = from_behind(moving, "ctx", 1)
        start = ((position - step) % n_ctx) * n_query
        inner_state = absorb_block(
            inner_state, queries, q_docs, q_start, moving[0], moving[1], start, doc_ids, always
        )
        return (inner_state, moving)

    _, totals, accum = lax.fori_loop(1, n_ctx, turn_one, (carry, jnp.stack((keys, values))))[0]
    result = accum / totals[..., None]
    return jnp.transpose(result, (2, 0, 1, 3)).reshape(queries.shape).astype(jnp.bfloat16)


def part_rows(attended, place):
    share = attended.shape[0] // 4
    rows = [lax.dynamic_slice_in_dim(attended, (place ^ flip) * share, share, 0) for flip in (2, 3, 0, 1)]
    return jnp.concatenate(rows[:2], axis=0), jnp.concatenate(rows[2:], axis=0)


def per_device(queries, keys, values, doc_ids, out_weight):
    n_ctx = lax.axis_size("ctx")
    heads = lax.axis_size("head")
    position = lax.axis_index("ctx")
    place = lax.axis_index("head")
    other_core = [(i, i ^ 1) for i in range(heads)]
    other_chip = [(i, i ^ 2) for i in range(heads)]
    columns = out_weight.shape[1]
    cut = columns * 4 // 7 // BLOCK * BLOCK

    if n_ctx == 8:
        by_two = [move(x, BY_TWO) for x in (keys, values)]
        beside = [move(x, BESIDE) for x in (keys, values)]
        *state, fetched, open_beside = attend_first(doc_ids, queries, keys, values)
        by_four = [
            move(after(after(by_two[0], state[0]), beside[0]), AGAIN),
            move(after(after(by_two[1], beside[1]), state[0]), AGAIN),
        ]
        swap_two = [
            move(after(by_two[0], state[0]), ACROSS),
            move(after(by_two[1], state[0]), ACROSS),
        ]
        swap_four = [move(after(by_four[0], swap_two[0]), LAST), move(swap_two[1], AGAIN)]
        chunks = [beside, by_two, by_four]
        *state, weight = attend_next(fetched, open_beside, out_weight, state, chunks, (1, 2, 3))
        chunks = [swap_two, swap_four]
        far, near, mine, send = attend_last(fetched, weight, state, chunks, (4, 5), (0, cut))
    else:
        weight = out_weight
        attended = ring_attention(queries, keys, values, doc_ids, n_ctx, position)
        far, near = part_rows(attended, place)
        mine, send = project(far, weight, (0, cut))
    theirs = hop(send, "head", other_core)
    later_mine, later_send = project(far, weight, (cut, columns))
    mine, later_mine = lax.optimization_barrier((mine, later_mine))
    first_sum = add_up(mine, theirs)
    first_part = hop(first_sum, "head", other_chip)
    later_theirs = hop(later_send, "head", other_core)
    later_mine, first_sum = lax.optimization_barrier((later_mine, first_sum))
    later_sum = add_up(later_mine, later_theirs)
    second_part = hop(later_sum, "head", other_chip)
    near, later_sum = lax.optimization_barrier((near, later_sum))
    mine, *sends = project(near, weight, (0, columns), 3)
    theirs = [hop(send, "head", other_core) for send in sends]
    out = combine(mine, theirs, first_part)
    return combine(mine, theirs, second_part, cut, out)


def solution(mesh):
    placed = (P("ctx", "head"), P("ctx", "head"), P("ctx", "head"), P(), P("head", None))
    return jax.shard_map(
        per_device, mesh=mesh, in_specs=placed, out_specs=P(("ctx", "head"), None), check_vma=False
    )
```

```python
import functools

import jax
import jax.numpy as jnp
from jax import lax
from jax.experimental import pallas as pl
from jax.experimental.pallas import tpu as pltpu
from jax.sharding import PartitionSpec as P

HEAD_SIZE = 128
BLOCK = 128
SCALE = 168.0 ** (-0.5)
LOG2E = 1.4426950408889634
NEG = -1e30
VMEM = pl.BlockSpec(memory_space=pltpu.VMEM)
SMEM = pl.BlockSpec(memory_space=pltpu.SMEM)
HBM = pl.BlockSpec(memory_space=pltpu.HBM)
LIMIT = pltpu.CompilerParams(vmem_limit_bytes=32 * 1024 * 1024)


def hop(block, axis, pairs):
    return lax.ppermute(block, axis, pairs)


def in_place(number, position, n_ctx):
    away = {2: 2, 3: 4, 4: 2, 5: 4}[number]
    return (position < n_ctx * 3 // 4) & (position >= away)


BESIDE = ((0, 1), (2, 3), (4, 5), (6, 7))
BY_TWO = ((0, 2, 4), (1, 3, 5))
AGAIN = ((2, 4), (3, 5))
ACROSS = ((2, 3), (4, 5))
LAST = ((4, 5),)
EARLY = (0, 1, 6, 7)
RELAY = ((0, 2), (1, 3), (4, 6), (5, 7))


def move(block, rings, crossing=()):
    n_ctx, heads = lax.axis_size("ctx"), lax.axis_size("head")
    target = {ring[i]: ring[(i + 1) % len(ring)] for ring in rings for i in range(len(ring))}
    pairs = []
    for i in range(n_ctx):
        flip = 0 if i in target else 2 if i in crossing else 1
        pairs += [(i * heads + h, target.get(i, i) * heads + (h ^ flip)) for h in range(heads)]
    return lax.ppermute(block, ("ctx", "head"), pairs)


def after(x, event):
    return lax.optimization_barrier((x, event))[0]


def score_blocks(doors, q, a, h, chunks, numbers):
    position = lax.axis_index("ctx")
    n_ctx = lax.axis_size("ctx")
    n_query = chunks[0][0].shape[0]
    scores = []
    for (keys, _), c in zip(chunks, numbers):
        count = (a + 1) * BLOCK if c == 0 else n_query
        k = keys[:count, h * HEAD_SIZE : (h + 1) * HEAD_SIZE]
        s = lax.dot_general(q, k, (((1,), (1,)), ((), ())), preferred_element_type=jnp.float32)
        for b in range(count // BLOCK):
            part = s[:, b * BLOCK : (b + 1) * BLOCK]
            if c == 0 and b == a:
                row = lax.broadcasted_iota(jnp.int32, part.shape, 0) % BLOCK
                col = lax.broadcasted_iota(jnp.int32, part.shape, 1)
                part = jnp.where(row >= col, part, NEG)
            elif c < 2:
                part = part + doors(c, a, b)
            else:
                part = part + jnp.where(in_place(c, position, n_ctx), 0.0, NEG)
            scores.append(part)
    return scores


def weigh(scores, peak, factor, a, h, chunks, numbers):
    n_query = chunks[0][0].shape[0]
    total = added = None
    scores = list(scores)
    for (_, values), c in zip(chunks, numbers):
        count = (a + 1) * BLOCK if c == 0 else n_query
        parts = []
        for b in range(count // BLOCK):
            w = jnp.exp2(scores.pop(0) * factor - peak)
            total = w if total is None else total + w
            parts.append(w.astype(jnp.bfloat16))
        w = jnp.concatenate(parts, axis=1) if len(parts) > 1 else parts[0]
        v = values[:count, h * HEAD_SIZE : (h + 1) * HEAD_SIZE]
        term = jnp.dot(w, v, preferred_element_type=jnp.float32)
        added = term if added is None else added + term
    return total, added


def head_slices(queries, keys, h):
    group = queries.shape[1] // keys.shape[1]
    return [slice((h * group + g) * HEAD_SIZE, (h * group + g + 1) * HEAD_SIZE) for g in range(group)]


def absorb(numbers, doors, queries, chunks, before, after):
    n_query = queries.shape[0]
    factor = SCALE * LOG2E
    parts = []
    for a in range(n_query // BLOCK):
        for h in range(chunks[0][0].shape[1] // HEAD_SIZE):
            heads = head_slices(queries, chunks[0][0], h)
            size = len(heads) * BLOCK
            parts.append((a, h, heads, slice(len(parts) * size, (len(parts) + 1) * size)))
    scores = []
    for a, h, heads, _ in parts:
        q = jnp.concatenate([queries[a * BLOCK : (a + 1) * BLOCK, s] for s in heads], axis=0)
        scores.append(score_blocks(doors, q, a, h, chunks, numbers))
    peaks = [functools.reduce(jnp.maximum, s) for s in scores]
    peaks = [jnp.max(peak, axis=1, keepdims=True) * factor for peak in peaks]
    shrinks = None
    if before is None:
        peaks = [jnp.broadcast_to(peak, (peak.shape[0], HEAD_SIZE)) for peak in peaks]
    else:
        lasts = [before[0][rows, :] for _, _, _, rows in parts]
        peaks = [jnp.maximum(last, peak) for last, peak in zip(lasts, peaks)]
        shrinks = [jnp.exp2(last - peak) for last, peak in zip(lasts, peaks)]
    sums = [
        weigh(s, peak, factor, a, h, chunks, numbers)
        for s, peak, (a, h, _, _) in zip(scores, peaks, parts)
    ]
    for i, (a, h, heads, rows) in enumerate(parts):
        total, added = sums[i]
        if before is not None:
            total = total + before[1][rows, :] * shrinks[i]
            added = added + before[2][rows, :] * shrinks[i]
        sums[i] = (total, added)
    after(parts, peaks, sums)


def store_state(state):
    def after(parts, peaks, sums):
        for (_, _, _, rows), peak, (total, added) in zip(parts, peaks, sums):
            for ref, part in zip(state, (peak, total, added)):
                ref[rows, :] = part

    return after


def pairs_of(refs):
    return list(zip(refs[0::2], refs[1::2]))


def first_kernel(docs_in, queries_in, keys_in, values_in, *refs):
    *state, queries, open_beside, docs, keys, values, sems = refs
    places = ((docs_in, docs), (queries_in, queries), (keys_in, keys), (values_in, values))
    fetches = [pltpu.make_async_copy(a, b, sems.at[i]) for i, (a, b) in enumerate(places)]
    for fetch in fetches:
        fetch.start()
    for fetch in fetches:
        fetch.wait()
    position = lax.axis_index("ctx")
    q_blocks = queries.shape[0] // BLOCK

    def doors(number, a, b):
        source = position if number == 0 else jnp.maximum(position - 1, 0)
        seen = docs[source * q_blocks + b] == docs[position * q_blocks + a]
        if number == 1:
            seen = seen & (position % 2 == 1)
        return jnp.where(seen, 0.0, NEG)

    for a in range(q_blocks):
        for b in range(q_blocks):
            part = open_beside.at[a * 8 : (a + 1) * 8, b * BLOCK : (b + 1) * BLOCK]
            part[...] = jnp.full(part.shape, doors(1, a, b), jnp.float32)
    absorb((0,), doors, queries, [(keys, values)], None, store_state(state))


def next_kernel(numbers, queries, open_beside, weight_in, *refs):
    *refs, weight, sem = refs
    fetch = pltpu.make_async_copy(weight_in, weight, sem)
    fetch.start()
    pairs = 2 * len(numbers)

    def doors(number, a, b):
        return open_beside[a * 8 : a * 8 + 1, b * BLOCK : (b + 1) * BLOCK]

    absorb(numbers, doors, queries, pairs_of(refs[3 : 3 + pairs]), refs[:3], store_state(refs[3 + pairs :]))
    fetch.wait()


def attend_cost(queries, numbers, fetched=0):
    n_query, width = queries.shape
    count = len(numbers) * n_query
    return pl.CostEstimate(
        flops=4 * n_query * width * count,
        bytes_accessed=fetched,
        transcendentals=n_query * count * width // HEAD_SIZE,
    )


def state_shapes(queries):
    rows = queries.size // HEAD_SIZE
    return (pltpu.VMEM((rows, HEAD_SIZE), jnp.float32),) * 3


def attend_first(docs, queries, keys, values):
    n_query = queries.shape[0]
    return pl.pallas_call(
        first_kernel,
        out_shape=state_shapes(queries)
        + (
            pltpu.VMEM(queries.shape, queries.dtype),
            pltpu.VMEM((8 * n_query // BLOCK, n_query), jnp.float32),
        ),
        in_specs=[HBM] * 4,
        out_specs=(VMEM,) * 5,
        scratch_shapes=[
            pltpu.SMEM(docs.shape, docs.dtype),
            pltpu.VMEM(keys.shape, keys.dtype),
            pltpu.VMEM(values.shape, values.dtype),
            pltpu.SemaphoreType.DMA((4,)),
        ],
        compiler_params=LIMIT,
        cost_estimate=attend_cost(queries, (0,)),
        name="attend_first",
    )(*[pltpu.with_memory_space_constraint(x, pltpu.HBM) for x in (docs, queries, keys, values)])


def attend_next(queries, open_beside, weight, state, chunks, numbers):
    return pl.pallas_call(
        functools.partial(next_kernel, numbers),
        out_shape=state_shapes(queries) + (pltpu.VMEM(weight.shape, weight.dtype),),
        in_specs=[VMEM, VMEM, HBM] + [VMEM] * (3 + 2 * len(chunks)),
        out_specs=(VMEM,) * 4,
        scratch_shapes=[pltpu.SemaphoreType.DMA],
        compiler_params=LIMIT,
        cost_estimate=attend_cost(queries, numbers, 2 * weight.size),
        name="attend_next",
    )(
        queries,
        open_beside,
        pltpu.with_memory_space_constraint(weight, pltpu.HBM),
        *state,
        *[x for pair in chunks for x in pair],
    )


def last_kernel(numbers, columns, queries, weight, *refs):
    pairs = 2 * len(numbers)
    chunks = pairs_of(refs[3 : 3 + pairs])
    far, near, mine, send, attended = refs[3 + pairs :]

    def after(parts, peaks, sums):
        inverses = [1.0 / jnp.sum(total, axis=1, keepdims=True) for total, _ in sums]
        for (a, _, heads, _), inverse, (_, added) in zip(parts, inverses, sums):
            result = (added * inverse).astype(jnp.bfloat16)
            for g, head in enumerate(heads):
                attended[a * BLOCK : (a + 1) * BLOCK, head] = result[g * BLOCK : (g + 1) * BLOCK]

    absorb(numbers, None, queries, chunks, refs[:3], after)
    place = lax.axis_index("head")
    share = queries.shape[0] // 4
    for half, owners in ((far, (place ^ 2, place ^ 3)), (near, (place, place ^ 1))):
        for i, owner in enumerate(owners):
            source = pl.ds(pl.multiple_of(owner * share, share), share)
            half[i * share : (i + 1) * share, :] = attended[source, :]
    project_columns(far, weight, mine, (send,), *columns)


def attend_last(queries, weight, state, chunks, numbers, columns):
    n_query, width = queries.shape
    half = jax.ShapeDtypeStruct((n_query // 2, width), jnp.bfloat16)
    return pl.pallas_call(
        functools.partial(last_kernel, numbers, columns),
        out_shape=(half, half) + project_shapes(n_query // 4, columns[1] - columns[0]),
        in_specs=[VMEM] * (5 + 2 * len(numbers)),
        out_specs=(VMEM,) * 4,
        scratch_shapes=[pltpu.VMEM(queries.shape, jnp.bfloat16)],
        compiler_params=LIMIT,
        cost_estimate=attend_cost(queries, numbers),
        name="attend_last",
    )(queries, weight, *state, *[x for pair in chunks for x in pair])


def project_shapes(rows, count, sends=1):
    send = jax.ShapeDtypeStruct((rows, count // sends), jnp.bfloat16)
    return (jax.ShapeDtypeStruct((rows, count), jnp.float32),) + (send,) * sends


def project_columns(rows, weight, mine, sends, start, end):
    share = rows.shape[0] // 2
    width = sends[0].shape[1]
    for i, send in enumerate(sends):
        for at in range(0, width, 768):
            stop = min(at + 768, width)
            columns = weight[:, start + i * width + at : start + i * width + stop]
            product = jnp.dot(rows[...], columns, preferred_element_type=jnp.float32)
            mine[:, i * width + at : i * width + stop] = product[:share]
            send[:, at:stop] = product[share:].astype(send.dtype)


def project_kernel(columns, rows, weight, mine, *sends):
    project_columns(rows, weight, mine, sends, *columns)


def project(rows, weight, columns, sends=1):
    count = columns[1] - columns[0]
    return pl.pallas_call(
        functools.partial(project_kernel, columns),
        out_shape=project_shapes(rows.shape[0] // 2, count, sends),
        in_specs=[VMEM, VMEM],
        out_specs=(VMEM,) * (1 + sends),
        compiler_params=LIMIT,
        cost_estimate=pl.CostEstimate(
            flops=2 * rows.shape[0] * rows.shape[1] * count, bytes_accessed=0, transcendentals=0
        ),
        name="project",
    )(rows, weight)


def add_kernel(mine, theirs, *outs):
    at = 0
    for out in outs:
        columns = slice(at, at + out.shape[1])
        at += out.shape[1]
        out[...] = (mine[:, columns] + theirs[:, columns].astype(jnp.float32)).astype(out.dtype)


def add_up(mine, theirs, widths):
    return pl.pallas_call(
        add_kernel,
        out_shape=[jax.ShapeDtypeStruct((mine.shape[0], width), theirs.dtype) for width in widths],
        in_specs=[VMEM, VMEM],
        out_specs=[VMEM] * len(widths),
        compiler_params=LIMIT,
        cost_estimate=pl.CostEstimate(flops=theirs.size, bytes_accessed=0, transcendentals=0),
        name="add_up",
    )(mine, theirs)


def combine_kernel(cuts, counts, mine, *refs):
    across, refs = refs[: sum(counts)], refs[sum(counts) :]
    beside, (out, *totals, sems) = refs[: len(refs) - len(cuts) - 2], refs[len(refs) - len(cuts) - 2 :]
    copies = []
    for i, (at, total) in enumerate(zip(cuts, totals)):
        options = across[sum(counts[:i]) : sum(counts[: i + 1])]
        width = options[0].shape[1]
        left = 0
        for part in beside:
            low, high = max(left, at), min(left + part.shape[1], at + width)
            if low < high:
                piece = mine[:, low:high] + part[:, low - left : high - left].astype(jnp.float32)
                there = options[0][:, low - at : high - at].astype(jnp.float32)
                if len(options) == 2:
                    position = lax.axis_index("ctx")
                    early = functools.reduce(jnp.logical_or, [position == i for i in EARLY])
                    relayed = options[1][:, low - at : high - at].astype(jnp.float32)
                    there = jnp.where(early, there, relayed)
                total[:, low - at : high - at] = (piece + there).astype(total.dtype)
            left += part.shape[1]
        copies.append(pltpu.make_async_copy(total, out.at[:, at : at + width], sems.at[i]))
        copies[-1].start()
    for copy in copies:
        copy.wait()


def combine(mine, beside, across, cuts, out=None):
    outs = [] if out is None else [out]
    across = [x if isinstance(x, tuple) else (x,) for x in across]
    arrays = [x for options in across for x in options]
    counts = [len(options) for options in across]
    inputs = 1 + len(arrays) + len(beside)

    def kernel(*refs):
        combine_kernel(cuts, counts, *refs[:inputs], *refs[inputs + len(outs) :])

    return pl.pallas_call(
        kernel,
        out_shape=jax.ShapeDtypeStruct(mine.shape, jnp.bfloat16),
        in_specs=[VMEM] * inputs + [HBM] * len(outs),
        out_specs=HBM,
        scratch_shapes=[pltpu.VMEM(options[0].shape, jnp.bfloat16) for options in across]
        + [pltpu.SemaphoreType.DMA((len(cuts),))],
        input_output_aliases={inputs: 0} if outs else {},
        compiler_params=LIMIT,
        name="combine",
    )(mine, *arrays, *beside, *outs)


def from_behind(block, axis, distance):
    devices = range(lax.axis_size(axis))
    route = [(i - distance, i) for i in devices if i - distance in devices]
    return lax.ppermute(block, axis, route)


def token_docs(doc_ids, start, count):
    blocks = (start + jnp.arange(count, dtype=jnp.int32)) // BLOCK
    table = blocks[:, None] == jnp.arange(doc_ids.shape[0], dtype=jnp.int32)[None, :]
    return jnp.sum(jnp.where(table, doc_ids[None, :], 0), axis=1)


def attend(carry, queries, q_docs, q_start, k_piece, v_piece, k_docs, k_start):
    peak, totals, accum = carry
    n_query = queries.shape[0]
    n_key = k_piece.shape[0]
    kv_heads = k_piece.shape[1] // HEAD_SIZE
    query_group = queries.shape[1] // k_piece.shape[1]
    q_heads = queries.reshape(n_query, kv_heads, query_group, HEAD_SIZE)
    k_heads = k_piece.reshape(n_key, kv_heads, HEAD_SIZE)
    v_heads = v_piece.reshape(n_key, kv_heads, HEAD_SIZE)
    scores = (
        jnp.einsum("qkgd,skd->kgqs", q_heads, k_heads, preferred_element_type=jnp.float32) * SCALE
    )
    q_pos = q_start + jnp.arange(n_query, dtype=jnp.int32)
    k_pos = k_start + jnp.arange(n_key, dtype=jnp.int32)
    allowed = (q_docs[:, None] == k_docs[None, :]) & (q_pos[:, None] >= k_pos[None, :])
    scores = jnp.where(allowed, scores, NEG)
    new_peak = jnp.maximum(peak, jnp.max(scores, axis=-1))
    shrink = jnp.exp(peak - new_peak)
    weights = jnp.exp(scores - new_peak[..., None])
    totals = totals * shrink + jnp.sum(weights, axis=-1)
    rounded = weights.astype(jnp.bfloat16)
    added = jnp.einsum("kgqs,skd->kgqd", rounded, v_heads, preferred_element_type=jnp.float32)
    accum = accum * shrink[..., None] + added
    return (new_peak, totals, accum)


def absorb_block(carry, queries, q_docs, q_start, k_piece, v_piece, k_start, doc_ids, flag):
    n_key = k_piece.shape[0]
    k_docs = token_docs(doc_ids, k_start, n_key)
    fresh = attend(carry, queries, q_docs, q_start, k_piece, v_piece, k_docs, k_start)
    return jax.tree.map(lambda new, old: jnp.where(flag, new, old), fresh, carry)


def ring_attention(queries, keys, values, doc_ids, n_ctx, position):
    n_query = queries.shape[0]
    q_start = position * n_query
    q_docs = token_docs(doc_ids, q_start, n_query)
    kv_heads = keys.shape[1] // HEAD_SIZE
    query_group = queries.shape[1] // keys.shape[1]
    carry = (
        jnp.full((kv_heads, query_group, n_query), NEG, jnp.float32),
        jnp.zeros((kv_heads, query_group, n_query), jnp.float32),
        jnp.zeros((kv_heads, query_group, n_query, HEAD_SIZE), jnp.float32),
    )
    always = jnp.array(True)
    carry = absorb_block(carry, queries, q_docs, q_start, keys, values, q_start, doc_ids, always)

    def turn_one(step, state):
        inner_state, moving = state
        moving = from_behind(moving, "ctx", 1)
        start = ((position - step) % n_ctx) * n_query
        inner_state = absorb_block(
            inner_state, queries, q_docs, q_start, moving[0], moving[1], start, doc_ids, always
        )
        return (inner_state, moving)

    _, totals, accum = lax.fori_loop(1, n_ctx, turn_one, (carry, jnp.stack((keys, values))))[0]
    result = accum / totals[..., None]
    return jnp.transpose(result, (2, 0, 1, 3)).reshape(queries.shape).astype(jnp.bfloat16)


def part_rows(attended, place):
    share = attended.shape[0] // 4
    rows = [lax.dynamic_slice_in_dim(attended, (place ^ flip) * share, share, 0) for flip in (2, 3, 0, 1)]
    return jnp.concatenate(rows[:2], axis=0), jnp.concatenate(rows[2:], axis=0)


def per_device(queries, keys, values, doc_ids, out_weight):
    n_ctx = lax.axis_size("ctx")
    heads = lax.axis_size("head")
    position = lax.axis_index("ctx")
    place = lax.axis_index("head")
    other_core = [(i, i ^ 1) for i in range(heads)]
    other_chip = [(i, i ^ 2) for i in range(heads)]
    columns = out_weight.shape[1]
    relay = columns // 8 // BLOCK * BLOCK
    cuts = [0, columns * 2 // 7 // BLOCK * BLOCK, columns * 2 // 7 // BLOCK * BLOCK + relay]

    if n_ctx == 8:
        by_two = [move(x, BY_TWO) for x in (keys, values)]
        beside = [move(x, BESIDE) for x in (keys, values)]
        *state, fetched, open_beside = attend_first(doc_ids, queries, keys, values)
        by_four = [move(after(x, state[0]), AGAIN) for x in by_two]
        swap_two = [
            move(after(after(by_two[0], beside[0]), state[0]), ACROSS),
            move(after(by_two[1], beside[1]), ACROSS),
        ]
        swap_four = [move(after(swap_two[0], by_four[0]), AGAIN), move(by_four[1], LAST)]
        chunks = [beside, by_two, by_four]
        *state, weight = attend_next(fetched, open_beside, out_weight, state, chunks, (1, 2, 3))
        chunks = [swap_two, swap_four]
        far, near, mine, send = attend_last(fetched, weight, state, chunks, (4, 5), (0, cuts[2]))
    else:
        weight = out_weight
        attended = ring_attention(queries, keys, values, doc_ids, n_ctx, position)
        far, near = part_rows(attended, place)
        mine, send = project(far, weight, (0, cuts[2]))
    theirs = hop(send, "head", other_core)
    later_mine, later_send = project(far, weight, (cuts[2], columns))
    first_sum, relay_sum = add_up(mine, theirs, [cuts[1], cuts[2] - cuts[1]])
    first_part = hop(first_sum, "head", other_chip)
    later_theirs = hop(after(later_send, relay_sum), "head", other_core)
    later_mine = after(later_mine, first_sum)
    (later_sum,) = add_up(later_mine, later_theirs, [columns - cuts[2]])
    later_part = hop(later_sum, "head", other_chip)
    mine, *sends = project(after(near, later_sum), weight, (0, columns), 4)
    theirs = [hop(send, "head", other_core) for send in sends]
    if n_ctx == 8:
        direct = move(relay_sum, (), EARLY)
        arrived = move(after(relay_sum, mine), RELAY)
        relay_part = (direct, move(move(after(after(arrived, first_part), direct), (), EARLY), RELAY))
    else:
        relay_part = hop(relay_sum, "head", other_chip)
    out = combine(mine, theirs, [first_part], [0])
    return combine(mine, theirs, [later_part, relay_part], [cuts[2], cuts[1]], out)


def solution(mesh):
    placed = (P("ctx", "head"), P("ctx", "head"), P("ctx", "head"), P(), P("head", None))
    return jax.shard_map(
        per_device, mesh=mesh, in_specs=placed, out_specs=P(("ctx", "head"), None), check_vma=False
    )
```

```python
import functools

import jax
import jax.numpy as jnp
from jax import lax
from jax.experimental import pallas as pl
from jax.experimental.pallas import tpu as pltpu
from jax.sharding import PartitionSpec as P

HEAD_SIZE = 128
BLOCK = 128
SCALE = 168.0 ** (-0.5)
LOG2E = 1.4426950408889634
NEG = -1e30
VMEM = pl.BlockSpec(memory_space=pltpu.VMEM)
SMEM = pl.BlockSpec(memory_space=pltpu.SMEM)
HBM = pl.BlockSpec(memory_space=pltpu.HBM)
LIMIT = pltpu.CompilerParams(vmem_limit_bytes=32 * 1024 * 1024)


def hop(block, axis, pairs):
    return lax.ppermute(block, axis, pairs)


def in_place(number, position, n_ctx):
    away = {2: 2, 3: 4, 4: 2, 5: 4}[number]
    return (position < n_ctx * 3 // 4) & (position >= away)


BESIDE = ((0, 1), (2, 3), (4, 5), (6, 7))
BY_TWO = ((0, 2, 4), (1, 3, 5))
AGAIN = ((2, 4), (3, 5))
ACROSS = ((2, 3), (4, 5))
LAST = ((4, 5),)
LATE = (4, 5)
RELAY = ((4, 6), (5, 7))


def move(block, rings, crossing=()):
    n_ctx, heads = lax.axis_size("ctx"), lax.axis_size("head")
    target = {ring[i]: ring[(i + 1) % len(ring)] for ring in rings for i in range(len(ring))}
    pairs = []
    for i in range(n_ctx):
        flip = 0 if i in target else 2 if i in crossing else 1
        pairs += [(i * heads + h, target.get(i, i) * heads + (h ^ flip)) for h in range(heads)]
    return lax.ppermute(block, ("ctx", "head"), pairs)


def after(x, event):
    return lax.optimization_barrier((x, event))[0]


def score_blocks(doors, q, a, h, chunks, numbers):
    position = lax.axis_index("ctx")
    n_ctx = lax.axis_size("ctx")
    n_query = chunks[0][0].shape[0]
    scores = []
    for (keys, _), c in zip(chunks, numbers):
        count = (a + 1) * BLOCK if c == 0 else n_query
        k = keys[:count, h * HEAD_SIZE : (h + 1) * HEAD_SIZE]
        s = lax.dot_general(q, k, (((1,), (1,)), ((), ())), preferred_element_type=jnp.float32)
        for b in range(count // BLOCK):
            part = s[:, b * BLOCK : (b + 1) * BLOCK]
            if c == 0 and b == a:
                row = lax.broadcasted_iota(jnp.int32, part.shape, 0) % BLOCK
                col = lax.broadcasted_iota(jnp.int32, part.shape, 1)
                part = jnp.where(row >= col, part, NEG)
            elif c < 2:
                part = part + doors(c, a, b)
            else:
                part = part + jnp.where(in_place(c, position, n_ctx), 0.0, NEG)
            scores.append(part)
    return scores


def weigh(scores, peak, factor, a, h, chunks, numbers):
    n_query = chunks[0][0].shape[0]
    total = added = None
    scores = list(scores)
    for (_, values), c in zip(chunks, numbers):
        count = (a + 1) * BLOCK if c == 0 else n_query
        parts = []
        for b in range(count // BLOCK):
            w = jnp.exp2(scores.pop(0) * factor - peak)
            total = w if total is None else total + w
            parts.append(w.astype(jnp.bfloat16))
        w = jnp.concatenate(parts, axis=1) if len(parts) > 1 else parts[0]
        v = values[:count, h * HEAD_SIZE : (h + 1) * HEAD_SIZE]
        term = jnp.dot(w, v, preferred_element_type=jnp.float32)
        added = term if added is None else added + term
    return total, added


def head_slices(queries, keys, h):
    group = queries.shape[1] // keys.shape[1]
    return [slice((h * group + g) * HEAD_SIZE, (h * group + g + 1) * HEAD_SIZE) for g in range(group)]


def absorb(numbers, doors, queries, chunks, before, after):
    n_query = queries.shape[0]
    factor = SCALE * LOG2E
    parts = []
    for a in range(n_query // BLOCK):
        for h in range(chunks[0][0].shape[1] // HEAD_SIZE):
            heads = head_slices(queries, chunks[0][0], h)
            size = len(heads) * BLOCK
            parts.append((a, h, heads, slice(len(parts) * size, (len(parts) + 1) * size)))
    scores = []
    for a, h, heads, _ in parts:
        q = jnp.concatenate([queries[a * BLOCK : (a + 1) * BLOCK, s] for s in heads], axis=0)
        scores.append(score_blocks(doors, q, a, h, chunks, numbers))
    peaks = [functools.reduce(jnp.maximum, s) for s in scores]
    peaks = [jnp.max(peak, axis=1, keepdims=True) * factor for peak in peaks]
    shrinks = None
    if before is None:
        peaks = [jnp.broadcast_to(peak, (peak.shape[0], HEAD_SIZE)) for peak in peaks]
    else:
        lasts = [before[0][rows, :] for _, _, _, rows in parts]
        peaks = [jnp.maximum(last, peak) for last, peak in zip(lasts, peaks)]
        shrinks = [jnp.exp2(last - peak) for last, peak in zip(lasts, peaks)]
    sums = [
        weigh(s, peak, factor, a, h, chunks, numbers)
        for s, peak, (a, h, _, _) in zip(scores, peaks, parts)
    ]
    for i, (a, h, heads, rows) in enumerate(parts):
        total, added = sums[i]
        if before is not None:
            total = total + before[1][rows, :] * shrinks[i]
            added = added + before[2][rows, :] * shrinks[i]
        sums[i] = (total, added)
    after(parts, peaks, sums)


def store_state(state):
    def after(parts, peaks, sums):
        for (_, _, _, rows), peak, (total, added) in zip(parts, peaks, sums):
            for ref, part in zip(state, (peak, total, added)):
                ref[rows, :] = part

    return after


def pairs_of(refs):
    return list(zip(refs[0::2], refs[1::2]))


def first_kernel(docs_in, queries_in, keys_in, values_in, *refs):
    *state, queries, open_beside, docs, keys, values, sems = refs
    places = ((docs_in, docs), (queries_in, queries), (keys_in, keys), (values_in, values))
    fetches = [pltpu.make_async_copy(a, b, sems.at[i]) for i, (a, b) in enumerate(places)]
    for fetch in fetches:
        fetch.start()
    for fetch in fetches:
        fetch.wait()
    position = lax.axis_index("ctx")
    q_blocks = queries.shape[0] // BLOCK

    def doors(number, a, b):
        source = position if number == 0 else jnp.maximum(position - 1, 0)
        seen = docs[source * q_blocks + b] == docs[position * q_blocks + a]
        if number == 1:
            seen = seen & (position % 2 == 1)
        return jnp.where(seen, 0.0, NEG)

    for a in range(q_blocks):
        for b in range(q_blocks):
            part = open_beside.at[a * 8 : (a + 1) * 8, b * BLOCK : (b + 1) * BLOCK]
            part[...] = jnp.full(part.shape, doors(1, a, b), jnp.float32)
    absorb((0,), doors, queries, [(keys, values)], None, store_state(state))


def next_kernel(numbers, queries, open_beside, weight_in, *refs):
    *refs, weight, sem = refs
    fetch = pltpu.make_async_copy(weight_in, weight, sem)
    fetch.start()
    pairs = 2 * len(numbers)

    def doors(number, a, b):
        return open_beside[a * 8 : a * 8 + 1, b * BLOCK : (b + 1) * BLOCK]

    absorb(numbers, doors, queries, pairs_of(refs[3 : 3 + pairs]), refs[:3], store_state(refs[3 + pairs :]))
    fetch.wait()


def attend_cost(queries, numbers, fetched=0):
    n_query, width = queries.shape
    count = len(numbers) * n_query
    return pl.CostEstimate(
        flops=4 * n_query * width * count,
        bytes_accessed=fetched,
        transcendentals=n_query * count * width // HEAD_SIZE,
    )


def state_shapes(queries):
    rows = queries.size // HEAD_SIZE
    return (pltpu.VMEM((rows, HEAD_SIZE), jnp.float32),) * 3


def attend_first(docs, queries, keys, values):
    n_query = queries.shape[0]
    return pl.pallas_call(
        first_kernel,
        out_shape=state_shapes(queries)
        + (
            pltpu.VMEM(queries.shape, queries.dtype),
            pltpu.VMEM((8 * n_query // BLOCK, n_query), jnp.float32),
        ),
        in_specs=[HBM] * 4,
        out_specs=(VMEM,) * 5,
        scratch_shapes=[
            pltpu.SMEM(docs.shape, docs.dtype),
            pltpu.VMEM(keys.shape, keys.dtype),
            pltpu.VMEM(values.shape, values.dtype),
            pltpu.SemaphoreType.DMA((4,)),
        ],
        compiler_params=LIMIT,
        cost_estimate=attend_cost(queries, (0,)),
        name="attend_first",
    )(*[pltpu.with_memory_space_constraint(x, pltpu.HBM) for x in (docs, queries, keys, values)])


def attend_next(queries, open_beside, weight, state, chunks, numbers):
    return pl.pallas_call(
        functools.partial(next_kernel, numbers),
        out_shape=state_shapes(queries) + (pltpu.VMEM(weight.shape, weight.dtype),),
        in_specs=[VMEM, VMEM, HBM] + [VMEM] * (3 + 2 * len(chunks)),
        out_specs=(VMEM,) * 4,
        scratch_shapes=[pltpu.SemaphoreType.DMA],
        compiler_params=LIMIT,
        cost_estimate=attend_cost(queries, numbers, 2 * weight.size),
        name="attend_next",
    )(
        queries,
        open_beside,
        pltpu.with_memory_space_constraint(weight, pltpu.HBM),
        *state,
        *[x for pair in chunks for x in pair],
    )


def last_kernel(numbers, columns, queries, weight, *refs):
    pairs = 2 * len(numbers)
    chunks = pairs_of(refs[3 : 3 + pairs])
    far, near, mine, send, attended = refs[3 + pairs :]

    def after(parts, peaks, sums):
        inverses = [1.0 / jnp.sum(total, axis=1, keepdims=True) for total, _ in sums]
        for (a, _, heads, _), inverse, (_, added) in zip(parts, inverses, sums):
            result = (added * inverse).astype(jnp.bfloat16)
            for g, head in enumerate(heads):
                attended[a * BLOCK : (a + 1) * BLOCK, head] = result[g * BLOCK : (g + 1) * BLOCK]

    absorb(numbers, None, queries, chunks, refs[:3], after)
    place = lax.axis_index("head")
    share = queries.shape[0] // 4
    for half, owners in ((far, (place ^ 2, place ^ 3)), (near, (place, place ^ 1))):
        for i, owner in enumerate(owners):
            source = pl.ds(pl.multiple_of(owner * share, share), share)
            half[i * share : (i + 1) * share, :] = attended[source, :]
    project_columns(far, weight, mine, (send,), *columns)


def attend_last(queries, weight, state, chunks, numbers, columns):
    n_query, width = queries.shape
    half = jax.ShapeDtypeStruct((n_query // 2, width), jnp.bfloat16)
    return pl.pallas_call(
        functools.partial(last_kernel, numbers, columns),
        out_shape=(half, half) + project_shapes(n_query // 4, columns[1] - columns[0]),
        in_specs=[VMEM] * (5 + 2 * len(numbers)),
        out_specs=(VMEM,) * 4,
        scratch_shapes=[pltpu.VMEM(queries.shape, jnp.bfloat16)],
        compiler_params=LIMIT,
        cost_estimate=attend_cost(queries, numbers),
        name="attend_last",
    )(queries, weight, *state, *[x for pair in chunks for x in pair])


def project_shapes(rows, count, sends=1):
    send = jax.ShapeDtypeStruct((rows, count // sends), jnp.bfloat16)
    return (jax.ShapeDtypeStruct((rows, count), jnp.float32),) + (send,) * sends


def project_columns(rows, weight, mine, sends, start, end):
    share = rows.shape[0] // 2
    width = sends[0].shape[1]
    for i, send in enumerate(sends):
        for at in range(0, width, 768):
            stop = min(at + 768, width)
            columns = weight[:, start + i * width + at : start + i * width + stop]
            product = jnp.dot(rows[...], columns, preferred_element_type=jnp.float32)
            mine[:, i * width + at : i * width + stop] = product[:share]
            send[:, at:stop] = product[share:].astype(send.dtype)


def project_kernel(columns, rows, weight, mine, *sends):
    project_columns(rows, weight, mine, sends, *columns)


def project(rows, weight, columns, sends=1):
    count = columns[1] - columns[0]
    return pl.pallas_call(
        functools.partial(project_kernel, columns),
        out_shape=project_shapes(rows.shape[0] // 2, count, sends),
        in_specs=[VMEM, VMEM],
        out_specs=(VMEM,) * (1 + sends),
        compiler_params=LIMIT,
        cost_estimate=pl.CostEstimate(
            flops=2 * rows.shape[0] * rows.shape[1] * count, bytes_accessed=0, transcendentals=0
        ),
        name="project",
    )(rows, weight)


def add_kernel(mine, theirs, *outs):
    at = 0
    for out in outs:
        columns = slice(at, at + out.shape[1])
        at += out.shape[1]
        out[...] = (mine[:, columns] + theirs[:, columns].astype(jnp.float32)).astype(out.dtype)


def add_up(mine, theirs, widths):
    return pl.pallas_call(
        add_kernel,
        out_shape=[jax.ShapeDtypeStruct((mine.shape[0], width), theirs.dtype) for width in widths],
        in_specs=[VMEM, VMEM],
        out_specs=[VMEM] * len(widths),
        compiler_params=LIMIT,
        cost_estimate=pl.CostEstimate(flops=theirs.size, bytes_accessed=0, transcendentals=0),
        name="add_up",
    )(mine, theirs)


def combine_kernel(cuts, counts, mine, *refs):
    across, refs = refs[: sum(counts)], refs[sum(counts) :]
    beside, (out, *totals, sems) = refs[: len(refs) - len(cuts) - 2], refs[len(refs) - len(cuts) - 2 :]
    copies = []
    for i, (at, total) in enumerate(zip(cuts, totals)):
        options = across[sum(counts[:i]) : sum(counts[: i + 1])]
        width = options[0].shape[1]
        left = 0
        for part in beside:
            low, high = max(left, at), min(left + part.shape[1], at + width)
            if low < high:
                piece = mine[:, low:high] + part[:, low - left : high - left].astype(jnp.float32)
                there = options[0][:, low - at : high - at].astype(jnp.float32)
                if len(options) == 2:
                    position = lax.axis_index("ctx")
                    late = functools.reduce(jnp.logical_or, [position == i for i in LATE])
                    relayed = options[1][:, low - at : high - at].astype(jnp.float32)
                    there = jnp.where(late, relayed, there)
                total[:, low - at : high - at] = (piece + there).astype(total.dtype)
            left += part.shape[1]
        copies.append(pltpu.make_async_copy(total, out.at[:, at : at + width], sems.at[i]))
        copies[-1].start()
    for copy in copies:
        copy.wait()


def combine(mine, beside, across, cuts, out=None):
    outs = [] if out is None else [out]
    across = [x if isinstance(x, tuple) else (x,) for x in across]
    arrays = [x for options in across for x in options]
    counts = [len(options) for options in across]
    inputs = 1 + len(arrays) + len(beside)

    def kernel(*refs):
        combine_kernel(cuts, counts, *refs[:inputs], *refs[inputs + len(outs) :])

    return pl.pallas_call(
        kernel,
        out_shape=jax.ShapeDtypeStruct(mine.shape, jnp.bfloat16),
        in_specs=[VMEM] * inputs + [HBM] * len(outs),
        out_specs=HBM,
        scratch_shapes=[pltpu.VMEM(options[0].shape, jnp.bfloat16) for options in across]
        + [pltpu.SemaphoreType.DMA((len(cuts),))],
        input_output_aliases={inputs: 0} if outs else {},
        compiler_params=LIMIT,
        name="combine",
    )(mine, *arrays, *beside, *outs)


def from_behind(block, axis, distance):
    devices = range(lax.axis_size(axis))
    route = [(i - distance, i) for i in devices if i - distance in devices]
    return lax.ppermute(block, axis, route)


def token_docs(doc_ids, start, count):
    blocks = (start + jnp.arange(count, dtype=jnp.int32)) // BLOCK
    table = blocks[:, None] == jnp.arange(doc_ids.shape[0], dtype=jnp.int32)[None, :]
    return jnp.sum(jnp.where(table, doc_ids[None, :], 0), axis=1)


def attend(carry, queries, q_docs, q_start, k_piece, v_piece, k_docs, k_start):
    peak, totals, accum = carry
    n_query = queries.shape[0]
    n_key = k_piece.shape[0]
    kv_heads = k_piece.shape[1] // HEAD_SIZE
    query_group = queries.shape[1] // k_piece.shape[1]
    q_heads = queries.reshape(n_query, kv_heads, query_group, HEAD_SIZE)
    k_heads = k_piece.reshape(n_key, kv_heads, HEAD_SIZE)
    v_heads = v_piece.reshape(n_key, kv_heads, HEAD_SIZE)
    scores = (
        jnp.einsum("qkgd,skd->kgqs", q_heads, k_heads, preferred_element_type=jnp.float32) * SCALE
    )
    q_pos = q_start + jnp.arange(n_query, dtype=jnp.int32)
    k_pos = k_start + jnp.arange(n_key, dtype=jnp.int32)
    allowed = (q_docs[:, None] == k_docs[None, :]) & (q_pos[:, None] >= k_pos[None, :])
    scores = jnp.where(allowed, scores, NEG)
    new_peak = jnp.maximum(peak, jnp.max(scores, axis=-1))
    shrink = jnp.exp(peak - new_peak)
    weights = jnp.exp(scores - new_peak[..., None])
    totals = totals * shrink + jnp.sum(weights, axis=-1)
    rounded = weights.astype(jnp.bfloat16)
    added = jnp.einsum("kgqs,skd->kgqd", rounded, v_heads, preferred_element_type=jnp.float32)
    accum = accum * shrink[..., None] + added
    return (new_peak, totals, accum)


def absorb_block(carry, queries, q_docs, q_start, k_piece, v_piece, k_start, doc_ids, flag):
    n_key = k_piece.shape[0]
    k_docs = token_docs(doc_ids, k_start, n_key)
    fresh = attend(carry, queries, q_docs, q_start, k_piece, v_piece, k_docs, k_start)
    return jax.tree.map(lambda new, old: jnp.where(flag, new, old), fresh, carry)


def ring_attention(queries, keys, values, doc_ids, n_ctx, position):
    n_query = queries.shape[0]
    q_start = position * n_query
    q_docs = token_docs(doc_ids, q_start, n_query)
    kv_heads = keys.shape[1] // HEAD_SIZE
    query_group = queries.shape[1] // keys.shape[1]
    carry = (
        jnp.full((kv_heads, query_group, n_query), NEG, jnp.float32),
        jnp.zeros((kv_heads, query_group, n_query), jnp.float32),
        jnp.zeros((kv_heads, query_group, n_query, HEAD_SIZE), jnp.float32),
    )
    always = jnp.array(True)
    carry = absorb_block(carry, queries, q_docs, q_start, keys, values, q_start, doc_ids, always)

    def turn_one(step, state):
        inner_state, moving = state
        moving = from_behind(moving, "ctx", 1)
        start = ((position - step) % n_ctx) * n_query
        inner_state = absorb_block(
            inner_state, queries, q_docs, q_start, moving[0], moving[1], start, doc_ids, always
        )
        return (inner_state, moving)

    _, totals, accum = lax.fori_loop(1, n_ctx, turn_one, (carry, jnp.stack((keys, values))))[0]
    result = accum / totals[..., None]
    return jnp.transpose(result, (2, 0, 1, 3)).reshape(queries.shape).astype(jnp.bfloat16)


def part_rows(attended, place):
    share = attended.shape[0] // 4
    rows = [lax.dynamic_slice_in_dim(attended, (place ^ flip) * share, share, 0) for flip in (2, 3, 0, 1)]
    return jnp.concatenate(rows[:2], axis=0), jnp.concatenate(rows[2:], axis=0)


def per_device(queries, keys, values, doc_ids, out_weight):
    n_ctx = lax.axis_size("ctx")
    heads = lax.axis_size("head")
    position = lax.axis_index("ctx")
    place = lax.axis_index("head")
    other_core = [(i, i ^ 1) for i in range(heads)]
    other_chip = [(i, i ^ 2) for i in range(heads)]
    columns = out_weight.shape[1]
    relay = columns // 8 // BLOCK * BLOCK
    cuts = [0, columns * 2 // 7 // BLOCK * BLOCK, columns * 2 // 7 // BLOCK * BLOCK + relay]

    if n_ctx == 8:
        by_two = [move(x, BY_TWO) for x in (keys, values)]
        beside = [move(x, BESIDE) for x in (keys, values)]
        *state, fetched, open_beside = attend_first(doc_ids, queries, keys, values)
        by_four = [move(after(x, state[0]), AGAIN) for x in by_two]
        swap_two = [
            move(after(after(by_two[0], beside[0]), state[0]), ACROSS),
            move(after(by_two[1], beside[1]), ACROSS),
        ]
        swap_four = [move(after(swap_two[0], by_four[0]), AGAIN), move(by_four[1], LAST)]
        chunks = [beside, by_two, by_four]
        *state, weight = attend_next(fetched, open_beside, out_weight, state, chunks, (1, 2, 3))
        chunks = [swap_two, swap_four]
        far, near, mine, send = attend_last(fetched, weight, state, chunks, (4, 5), (0, cuts[2]))
    else:
        weight = out_weight
        attended = ring_attention(queries, keys, values, doc_ids, n_ctx, position)
        far, near = part_rows(attended, place)
        mine, send = project(far, weight, (0, cuts[2]))
    theirs = hop(send, "head", other_core)
    later_mine, later_send = project(far, weight, (cuts[2], columns))
    first_sum, relay_sum = add_up(mine, theirs, [cuts[1], cuts[2] - cuts[1]])
    first_part = hop(first_sum, "head", other_chip)
    later_theirs = hop(after(later_send, relay_sum), "head", other_core)
    later_mine = after(later_mine, first_sum)
    (later_sum,) = add_up(later_mine, later_theirs, [columns - cuts[2]])
    later_part = hop(later_sum, "head", other_chip)
    mine, *sends = project(after(near, later_sum), weight, (0, columns), 3)
    theirs = [hop(send, "head", other_core) for send in sends]
    if n_ctx == 8:
        direct = move(relay_sum, (), [i for i in range(n_ctx) if i not in LATE])
        arrived = move(after(relay_sum, mine), RELAY)
        relay_part = (direct, move(move(after(arrived, first_part), (), [ring[1] for ring in RELAY]), RELAY))
    else:
        relay_part = hop(relay_sum, "head", other_chip)
    out = combine(mine, theirs, [first_part], [0])
    return combine(mine, theirs, [later_part, relay_part], [cuts[2], cuts[1]], out)


def solution(mesh):
    placed = (P("ctx", "head"), P("ctx", "head"), P("ctx", "head"), P(), P("head", None))
    return jax.shard_map(
        per_device, mesh=mesh, in_specs=placed, out_specs=P(("ctx", "head"), None), check_vma=False
    )
```

```python
import functools

import jax
import jax.numpy as jnp
from jax import lax
from jax.experimental import pallas as pl
from jax.experimental.pallas import tpu as pltpu
from jax.sharding import PartitionSpec as P

HEAD_SIZE = 128
BLOCK = 128
SCALE = 168.0 ** (-0.5)
LOG2E = 1.4426950408889634
NEG = -1e30
VMEM = pl.BlockSpec(memory_space=pltpu.VMEM)
SMEM = pl.BlockSpec(memory_space=pltpu.SMEM)
HBM = pl.BlockSpec(memory_space=pltpu.HBM)
LIMIT = pltpu.CompilerParams(vmem_limit_bytes=32 * 1024 * 1024)


def hop(block, axis, pairs):
    return lax.ppermute(block, axis, pairs)


def in_place(number, position, n_ctx):
    away = {2: 2, 3: 4, 4: 2, 5: 4}[number]
    return (position < n_ctx * 3 // 4) & (position >= away)


BESIDE = ((0, 1), (2, 3), (4, 5), (6, 7))
BY_TWO = ((0, 2, 4), (1, 3, 5))
AGAIN = ((2, 4), (3, 5))
ACROSS = ((2, 3), (4, 5))
LAST = ((4, 5),)
LATE = (4, 5)
RELAY = ((4, 6), (5, 7))


def move(block, rings, crossing=()):
    n_ctx, heads = lax.axis_size("ctx"), lax.axis_size("head")
    target = {ring[i]: ring[(i + 1) % len(ring)] for ring in rings for i in range(len(ring))}
    pairs = []
    for i in range(n_ctx):
        flip = 0 if i in target else 2 if i in crossing else 1
        pairs += [(i * heads + h, target.get(i, i) * heads + (h ^ flip)) for h in range(heads)]
    return lax.ppermute(block, ("ctx", "head"), pairs)


def after(x, event):
    return lax.optimization_barrier((x, event))[0]


def score_blocks(doors, q, a, h, chunks, numbers):
    position = lax.axis_index("ctx")
    n_ctx = lax.axis_size("ctx")
    n_query = chunks[0][0].shape[0]
    scores = []
    for (keys, _), c in zip(chunks, numbers):
        count = (a + 1) * BLOCK if c == 0 else n_query
        k = keys[:count, h * HEAD_SIZE : (h + 1) * HEAD_SIZE]
        s = lax.dot_general(q, k, (((1,), (1,)), ((), ())), preferred_element_type=jnp.float32)
        for b in range(count // BLOCK):
            part = s[:, b * BLOCK : (b + 1) * BLOCK]
            if c == 0 and b == a:
                row = lax.broadcasted_iota(jnp.int32, part.shape, 0) % BLOCK
                col = lax.broadcasted_iota(jnp.int32, part.shape, 1)
                part = jnp.where(row >= col, part, NEG)
            elif c < 2:
                part = part + doors(c, a, b)
            else:
                part = part + jnp.where(in_place(c, position, n_ctx), 0.0, NEG)
            scores.append(part)
    return scores


def weigh(scores, peak, factor, a, h, chunks, numbers):
    n_query = chunks[0][0].shape[0]
    total = added = None
    scores = list(scores)
    for (_, values), c in zip(chunks, numbers):
        count = (a + 1) * BLOCK if c == 0 else n_query
        parts = []
        for b in range(count // BLOCK):
            w = jnp.exp2(scores.pop(0) * factor - peak)
            total = w if total is None else total + w
            parts.append(w.astype(jnp.bfloat16))
        w = jnp.concatenate(parts, axis=1) if len(parts) > 1 else parts[0]
        v = values[:count, h * HEAD_SIZE : (h + 1) * HEAD_SIZE]
        term = jnp.dot(w, v, preferred_element_type=jnp.float32)
        added = term if added is None else added + term
    return total, added


def head_slices(queries, keys, h):
    group = queries.shape[1] // keys.shape[1]
    return [slice((h * group + g) * HEAD_SIZE, (h * group + g + 1) * HEAD_SIZE) for g in range(group)]


def absorb(numbers, doors, queries, chunks, before, after):
    n_query = queries.shape[0]
    factor = SCALE * LOG2E
    parts = []
    for a in range(n_query // BLOCK):
        for h in range(chunks[0][0].shape[1] // HEAD_SIZE):
            heads = head_slices(queries, chunks[0][0], h)
            size = len(heads) * BLOCK
            parts.append((a, h, heads, slice(len(parts) * size, (len(parts) + 1) * size)))
    scores = []
    for a, h, heads, _ in parts:
        q = jnp.concatenate([queries[a * BLOCK : (a + 1) * BLOCK, s] for s in heads], axis=0)
        scores.append(score_blocks(doors, q, a, h, chunks, numbers))
    peaks = [functools.reduce(jnp.maximum, s) for s in scores]
    peaks = [jnp.max(peak, axis=1, keepdims=True) * factor for peak in peaks]
    shrinks = None
    if before is None:
        peaks = [jnp.broadcast_to(peak, (peak.shape[0], HEAD_SIZE)) for peak in peaks]
    else:
        lasts = [before[0][rows, :] for _, _, _, rows in parts]
        peaks = [jnp.maximum(last, peak) for last, peak in zip(lasts, peaks)]
        shrinks = [jnp.exp2(last - peak) for last, peak in zip(lasts, peaks)]
    sums = [
        weigh(s, peak, factor, a, h, chunks, numbers)
        for s, peak, (a, h, _, _) in zip(scores, peaks, parts)
    ]
    for i, (a, h, heads, rows) in enumerate(parts):
        total, added = sums[i]
        if before is not None:
            total = total + before[1][rows, :] * shrinks[i]
            added = added + before[2][rows, :] * shrinks[i]
        sums[i] = (total, added)
    after(parts, peaks, sums)


def store_state(state):
    def after(parts, peaks, sums):
        for (_, _, _, rows), peak, (total, added) in zip(parts, peaks, sums):
            for ref, part in zip(state, (peak, total, added)):
                ref[rows, :] = part

    return after


def pairs_of(refs):
    return list(zip(refs[0::2], refs[1::2]))


def first_kernel(docs_in, queries_in, keys_in, values_in, *refs):
    *state, queries, open_beside, docs, keys, values, sems = refs
    places = ((docs_in, docs), (queries_in, queries), (keys_in, keys), (values_in, values))
    fetches = [pltpu.make_async_copy(a, b, sems.at[i]) for i, (a, b) in enumerate(places)]
    for fetch in fetches:
        fetch.start()
    for fetch in fetches:
        fetch.wait()
    position = lax.axis_index("ctx")
    q_blocks = queries.shape[0] // BLOCK

    def doors(number, a, b):
        source = position if number == 0 else jnp.maximum(position - 1, 0)
        seen = docs[source * q_blocks + b] == docs[position * q_blocks + a]
        if number == 1:
            seen = seen & (position % 2 == 1)
        return jnp.where(seen, 0.0, NEG)

    for a in range(q_blocks):
        for b in range(q_blocks):
            part = open_beside.at[a * 8 : (a + 1) * 8, b * BLOCK : (b + 1) * BLOCK]
            part[...] = jnp.full(part.shape, doors(1, a, b), jnp.float32)
    absorb((0,), doors, queries, [(keys, values)], None, store_state(state))


def next_kernel(numbers, queries, open_beside, weight_in, *refs):
    *refs, weight, sem = refs
    fetch = pltpu.make_async_copy(weight_in, weight, sem)
    fetch.start()
    pairs = 2 * len(numbers)

    def doors(number, a, b):
        return open_beside[a * 8 : a * 8 + 1, b * BLOCK : (b + 1) * BLOCK]

    absorb(numbers, doors, queries, pairs_of(refs[3 : 3 + pairs]), refs[:3], store_state(refs[3 + pairs :]))
    fetch.wait()


def attend_cost(queries, numbers, fetched=0):
    n_query, width = queries.shape
    count = len(numbers) * n_query
    return pl.CostEstimate(
        flops=4 * n_query * width * count,
        bytes_accessed=fetched,
        transcendentals=n_query * count * width // HEAD_SIZE,
    )


def state_shapes(queries):
    rows = queries.size // HEAD_SIZE
    return (pltpu.VMEM((rows, HEAD_SIZE), jnp.float32),) * 3


def attend_first(docs, queries, keys, values):
    n_query = queries.shape[0]
    return pl.pallas_call(
        first_kernel,
        out_shape=state_shapes(queries)
        + (
            pltpu.VMEM(queries.shape, queries.dtype),
            pltpu.VMEM((8 * n_query // BLOCK, n_query), jnp.float32),
        ),
        in_specs=[HBM] * 4,
        out_specs=(VMEM,) * 5,
        scratch_shapes=[
            pltpu.SMEM(docs.shape, docs.dtype),
            pltpu.VMEM(keys.shape, keys.dtype),
            pltpu.VMEM(values.shape, values.dtype),
            pltpu.SemaphoreType.DMA((4,)),
        ],
        compiler_params=LIMIT,
        cost_estimate=attend_cost(queries, (0,)),
        name="attend_first",
    )(*[pltpu.with_memory_space_constraint(x, pltpu.HBM) for x in (docs, queries, keys, values)])


def attend_next(queries, open_beside, weight, state, chunks, numbers):
    return pl.pallas_call(
        functools.partial(next_kernel, numbers),
        out_shape=state_shapes(queries) + (pltpu.VMEM(weight.shape, weight.dtype),),
        in_specs=[VMEM, VMEM, HBM] + [VMEM] * (3 + 2 * len(chunks)),
        out_specs=(VMEM,) * 4,
        scratch_shapes=[pltpu.SemaphoreType.DMA],
        compiler_params=LIMIT,
        cost_estimate=attend_cost(queries, numbers, 2 * weight.size),
        name="attend_next",
    )(
        queries,
        open_beside,
        pltpu.with_memory_space_constraint(weight, pltpu.HBM),
        *state,
        *[x for pair in chunks for x in pair],
    )


def last_kernel(numbers, columns, queries, weight, *refs):
    pairs = 2 * len(numbers)
    chunks = pairs_of(refs[3 : 3 + pairs])
    far, near, mine, send, attended = refs[3 + pairs :]

    def after(parts, peaks, sums):
        inverses = [1.0 / jnp.sum(total, axis=1, keepdims=True) for total, _ in sums]
        for (a, _, heads, _), inverse, (_, added) in zip(parts, inverses, sums):
            result = (added * inverse).astype(jnp.bfloat16)
            for g, head in enumerate(heads):
                attended[a * BLOCK : (a + 1) * BLOCK, head] = result[g * BLOCK : (g + 1) * BLOCK]

    absorb(numbers, None, queries, chunks, refs[:3], after)
    place = lax.axis_index("head")
    share = queries.shape[0] // 4
    for half, owners in ((far, (place ^ 2, place ^ 3)), (near, (place, place ^ 1))):
        for i, owner in enumerate(owners):
            source = pl.ds(pl.multiple_of(owner * share, share), share)
            half[i * share : (i + 1) * share, :] = attended[source, :]
    project_columns(far, weight, mine, (send,), *columns)


def attend_last(queries, weight, state, chunks, numbers, columns):
    n_query, width = queries.shape
    half = jax.ShapeDtypeStruct((n_query // 2, width), jnp.bfloat16)
    return pl.pallas_call(
        functools.partial(last_kernel, numbers, columns),
        out_shape=(half, half) + project_shapes(n_query // 4, columns[1] - columns[0]),
        in_specs=[VMEM] * (5 + 2 * len(numbers)),
        out_specs=(VMEM,) * 4,
        scratch_shapes=[pltpu.VMEM(queries.shape, jnp.bfloat16)],
        compiler_params=LIMIT,
        cost_estimate=attend_cost(queries, numbers),
        name="attend_last",
    )(queries, weight, *state, *[x for pair in chunks for x in pair])


def project_shapes(rows, count, sends=1):
    send = jax.ShapeDtypeStruct((rows, count // sends), jnp.bfloat16)
    return (jax.ShapeDtypeStruct((rows, count), jnp.float32),) + (send,) * sends


def project_columns(rows, weight, mine, sends, start, end):
    share = rows.shape[0] // 2
    width = sends[0].shape[1]
    for i, send in enumerate(sends):
        for at in range(0, width, 768):
            stop = min(at + 768, width)
            columns = weight[:, start + i * width + at : start + i * width + stop]
            product = jnp.dot(rows[...], columns, preferred_element_type=jnp.float32)
            mine[:, i * width + at : i * width + stop] = product[:share]
            send[:, at:stop] = product[share:].astype(send.dtype)


def project_kernel(columns, rows, weight, mine, *sends):
    project_columns(rows, weight, mine, sends, *columns)


def project(rows, weight, columns, sends=1):
    count = columns[1] - columns[0]
    return pl.pallas_call(
        functools.partial(project_kernel, columns),
        out_shape=project_shapes(rows.shape[0] // 2, count, sends),
        in_specs=[VMEM, VMEM],
        out_specs=(VMEM,) * (1 + sends),
        compiler_params=LIMIT,
        cost_estimate=pl.CostEstimate(
            flops=2 * rows.shape[0] * rows.shape[1] * count, bytes_accessed=0, transcendentals=0
        ),
        name="project",
    )(rows, weight)


def add_kernel(mine, theirs, *outs):
    at = 0
    for out in outs:
        columns = slice(at, at + out.shape[1])
        at += out.shape[1]
        out[...] = (mine[:, columns] + theirs[:, columns].astype(jnp.float32)).astype(out.dtype)


def add_up(mine, theirs, widths):
    return pl.pallas_call(
        add_kernel,
        out_shape=[jax.ShapeDtypeStruct((mine.shape[0], width), theirs.dtype) for width in widths],
        in_specs=[VMEM, VMEM],
        out_specs=[VMEM] * len(widths),
        compiler_params=LIMIT,
        cost_estimate=pl.CostEstimate(flops=theirs.size, bytes_accessed=0, transcendentals=0),
        name="add_up",
    )(mine, theirs)


def combine_kernel(cuts, counts, mine, *refs):
    across, refs = refs[: sum(counts)], refs[sum(counts) :]
    beside, (out, *totals, sems) = refs[: len(refs) - len(cuts) - 2], refs[len(refs) - len(cuts) - 2 :]
    copies = []
    for i, (at, total) in enumerate(zip(cuts, totals)):
        options = across[sum(counts[:i]) : sum(counts[: i + 1])]
        width = options[0].shape[1]
        left = 0
        for part in beside:
            low, high = max(left, at), min(left + part.shape[1], at + width)
            if low < high:
                piece = mine[:, low:high] + part[:, low - left : high - left].astype(jnp.float32)
                there = options[0][:, low - at : high - at].astype(jnp.float32)
                if len(options) == 2:
                    position = lax.axis_index("ctx")
                    late = functools.reduce(jnp.logical_or, [position == i for i in LATE])
                    relayed = options[1][:, low - at : high - at].astype(jnp.float32)
                    there = jnp.where(late, relayed, there)
                total[:, low - at : high - at] = (piece + there).astype(total.dtype)
            left += part.shape[1]
        copies.append(pltpu.make_async_copy(total, out.at[:, at : at + width], sems.at[i]))
        copies[-1].start()
    for copy in copies:
        copy.wait()


def combine(mine, beside, across, cuts, out=None):
    outs = [] if out is None else [out]
    across = [x if isinstance(x, tuple) else (x,) for x in across]
    arrays = [x for options in across for x in options]
    counts = [len(options) for options in across]
    inputs = 1 + len(arrays) + len(beside)

    def kernel(*refs):
        combine_kernel(cuts, counts, *refs[:inputs], *refs[inputs + len(outs) :])

    return pl.pallas_call(
        kernel,
        out_shape=jax.ShapeDtypeStruct(mine.shape, jnp.bfloat16),
        in_specs=[VMEM] * inputs + [HBM] * len(outs),
        out_specs=HBM,
        scratch_shapes=[pltpu.VMEM(options[0].shape, jnp.bfloat16) for options in across]
        + [pltpu.SemaphoreType.DMA((len(cuts),))],
        input_output_aliases={inputs: 0} if outs else {},
        compiler_params=LIMIT,
        name="combine",
    )(mine, *arrays, *beside, *outs)


def from_behind(block, axis, distance):
    devices = range(lax.axis_size(axis))
    route = [(i - distance, i) for i in devices if i - distance in devices]
    return lax.ppermute(block, axis, route)


def token_docs(doc_ids, start, count):
    blocks = (start + jnp.arange(count, dtype=jnp.int32)) // BLOCK
    table = blocks[:, None] == jnp.arange(doc_ids.shape[0], dtype=jnp.int32)[None, :]
    return jnp.sum(jnp.where(table, doc_ids[None, :], 0), axis=1)


def attend(carry, queries, q_docs, q_start, k_piece, v_piece, k_docs, k_start):
    peak, totals, accum = carry
    n_query = queries.shape[0]
    n_key = k_piece.shape[0]
    kv_heads = k_piece.shape[1] // HEAD_SIZE
    query_group = queries.shape[1] // k_piece.shape[1]
    q_heads = queries.reshape(n_query, kv_heads, query_group, HEAD_SIZE)
    k_heads = k_piece.reshape(n_key, kv_heads, HEAD_SIZE)
    v_heads = v_piece.reshape(n_key, kv_heads, HEAD_SIZE)
    scores = (
        jnp.einsum("qkgd,skd->kgqs", q_heads, k_heads, preferred_element_type=jnp.float32) * SCALE
    )
    q_pos = q_start + jnp.arange(n_query, dtype=jnp.int32)
    k_pos = k_start + jnp.arange(n_key, dtype=jnp.int32)
    allowed = (q_docs[:, None] == k_docs[None, :]) & (q_pos[:, None] >= k_pos[None, :])
    scores = jnp.where(allowed, scores, NEG)
    new_peak = jnp.maximum(peak, jnp.max(scores, axis=-1))
    shrink = jnp.exp(peak - new_peak)
    weights = jnp.exp(scores - new_peak[..., None])
    totals = totals * shrink + jnp.sum(weights, axis=-1)
    rounded = weights.astype(jnp.bfloat16)
    added = jnp.einsum("kgqs,skd->kgqd", rounded, v_heads, preferred_element_type=jnp.float32)
    accum = accum * shrink[..., None] + added
    return (new_peak, totals, accum)


def absorb_block(carry, queries, q_docs, q_start, k_piece, v_piece, k_start, doc_ids, flag):
    n_key = k_piece.shape[0]
    k_docs = token_docs(doc_ids, k_start, n_key)
    fresh = attend(carry, queries, q_docs, q_start, k_piece, v_piece, k_docs, k_start)
    return jax.tree.map(lambda new, old: jnp.where(flag, new, old), fresh, carry)


def ring_attention(queries, keys, values, doc_ids, n_ctx, position):
    n_query = queries.shape[0]
    q_start = position * n_query
    q_docs = token_docs(doc_ids, q_start, n_query)
    kv_heads = keys.shape[1] // HEAD_SIZE
    query_group = queries.shape[1] // keys.shape[1]
    carry = (
        jnp.full((kv_heads, query_group, n_query), NEG, jnp.float32),
        jnp.zeros((kv_heads, query_group, n_query), jnp.float32),
        jnp.zeros((kv_heads, query_group, n_query, HEAD_SIZE), jnp.float32),
    )
    always = jnp.array(True)
    carry = absorb_block(carry, queries, q_docs, q_start, keys, values, q_start, doc_ids, always)

    def turn_one(step, state):
        inner_state, moving = state
        moving = from_behind(moving, "ctx", 1)
        start = ((position - step) % n_ctx) * n_query
        inner_state = absorb_block(
            inner_state, queries, q_docs, q_start, moving[0], moving[1], start, doc_ids, always
        )
        return (inner_state, moving)

    _, totals, accum = lax.fori_loop(1, n_ctx, turn_one, (carry, jnp.stack((keys, values))))[0]
    result = accum / totals[..., None]
    return jnp.transpose(result, (2, 0, 1, 3)).reshape(queries.shape).astype(jnp.bfloat16)


def part_rows(attended, place):
    share = attended.shape[0] // 4
    rows = [lax.dynamic_slice_in_dim(attended, (place ^ flip) * share, share, 0) for flip in (2, 3, 0, 1)]
    return jnp.concatenate(rows[:2], axis=0), jnp.concatenate(rows[2:], axis=0)


def per_device(queries, keys, values, doc_ids, out_weight):
    n_ctx = lax.axis_size("ctx")
    heads = lax.axis_size("head")
    position = lax.axis_index("ctx")
    place = lax.axis_index("head")
    other_core = [(i, i ^ 1) for i in range(heads)]
    other_chip = [(i, i ^ 2) for i in range(heads)]
    columns = out_weight.shape[1]
    relay = columns // 8 // BLOCK * BLOCK
    cuts = [0, columns * 2 // 7 // BLOCK * BLOCK, columns * 2 // 7 // BLOCK * BLOCK + relay]

    if n_ctx == 8:
        by_two = [move(x, BY_TWO) for x in (keys, values)]
        beside = [move(x, BESIDE) for x in (keys, values)]
        *state, fetched, open_beside = attend_first(doc_ids, queries, keys, values)
        by_four = [move(after(x, state[0]), AGAIN) for x in by_two]
        swap_two = [
            move(after(after(by_two[0], beside[0]), state[0]), ACROSS),
            move(after(by_two[1], beside[1]), ACROSS),
        ]
        swap_four = [move(after(swap_two[0], by_four[0]), AGAIN), move(by_four[1], LAST)]
        chunks = [beside, by_two, by_four]
        *state, weight = attend_next(fetched, open_beside, out_weight, state, chunks, (1, 2, 3))
        chunks = [swap_two, swap_four]
        far, near, mine, send = attend_last(fetched, weight, state, chunks, (4, 5), (0, cuts[2]))
    else:
        weight = out_weight
        attended = ring_attention(queries, keys, values, doc_ids, n_ctx, position)
        far, near = part_rows(attended, place)
        mine, send = project(far, weight, (0, cuts[2]))
    theirs = hop(send, "head", other_core)
    later_mine, later_send = project(far, weight, (cuts[2], columns))
    first_sum, relay_sum = add_up(mine, theirs, [cuts[1], cuts[2] - cuts[1]])
    first_part = hop(first_sum, "head", other_chip)
    later_theirs = hop(after(later_send, relay_sum), "head", other_core)
    later_mine = after(later_mine, first_sum)
    (later_sum,) = add_up(later_mine, later_theirs, [columns - cuts[2]])
    later_part = hop(later_sum, "head", other_chip)
    mine, *sends = project(after(near, later_sum), weight, (0, columns), 2)
    theirs = [hop(send, "head", other_core) for send in sends]
    if n_ctx == 8:
        arrived = move(after(relay_sum, mine), RELAY)
        direct = move(relay_sum, (), [i for i in range(n_ctx) if i not in LATE])
        relayed = move(after(arrived, first_part), (), [ring[1] for ring in RELAY])
        relay_part = (direct, move(after(relayed, direct), RELAY))
    else:
        relay_part = hop(relay_sum, "head", other_chip)
    out = combine(mine, theirs, [first_part], [0])
    return combine(mine, theirs, [later_part, relay_part], [cuts[2], cuts[1]], out)


def solution(mesh):
    placed = (P("ctx", "head"), P("ctx", "head"), P("ctx", "head"), P(), P("head", None))
    return jax.shard_map(
        per_device, mesh=mesh, in_specs=placed, out_specs=P(("ctx", "head"), None), check_vma=False
    )
```

```python
import functools

import jax
import jax.numpy as jnp
from jax import lax
from jax.experimental import pallas as pl
from jax.experimental.pallas import tpu as pltpu
from jax.sharding import PartitionSpec as P

HEAD_SIZE = 128
BLOCK = 128
SCALE = 168.0 ** (-0.5)
LOG2E = 1.4426950408889634
NEG = -1e30
VMEM = pl.BlockSpec(memory_space=pltpu.VMEM)
SMEM = pl.BlockSpec(memory_space=pltpu.SMEM)
HBM = pl.BlockSpec(memory_space=pltpu.HBM)
LIMIT = pltpu.CompilerParams(vmem_limit_bytes=32 * 1024 * 1024)


def hop(block, axis, pairs):
    return lax.ppermute(block, axis, pairs)


def in_place(number, position, n_ctx):
    away = {2: 2, 3: 4, 4: 2, 5: 4}[number]
    return (position < n_ctx * 3 // 4) & (position >= away)


BESIDE = ((0, 1), (2, 3), (4, 5), (6, 7))
BY_TWO = ((0, 2, 4), (1, 3, 5))
AGAIN = ((2, 4), (3, 5))
ACROSS = ((2, 3), (4, 5))
LAST = ((4, 5),)
LATE = (4, 5)
RELAY = ((4, 6), (5, 7))


def move(block, rings, crossing=()):
    n_ctx, heads = lax.axis_size("ctx"), lax.axis_size("head")
    target = {ring[i]: ring[(i + 1) % len(ring)] for ring in rings for i in range(len(ring))}
    pairs = []
    for i in range(n_ctx):
        flip = 0 if i in target else 2 if i in crossing else 1
        pairs += [(i * heads + h, target.get(i, i) * heads + (h ^ flip)) for h in range(heads)]
    return lax.ppermute(block, ("ctx", "head"), pairs)


def after(x, event):
    return lax.optimization_barrier((x, event))[0]


def score_blocks(doors, q, a, h, chunks, numbers):
    position = lax.axis_index("ctx")
    n_ctx = lax.axis_size("ctx")
    n_query = chunks[0][0].shape[0]
    scores = []
    for (keys, _), c in zip(chunks, numbers):
        count = (a + 1) * BLOCK if c == 0 else n_query
        k = keys[:count, h * HEAD_SIZE : (h + 1) * HEAD_SIZE]
        s = lax.dot_general(q, k, (((1,), (1,)), ((), ())), preferred_element_type=jnp.float32)
        for b in range(count // BLOCK):
            part = s[:, b * BLOCK : (b + 1) * BLOCK]
            if c == 0 and b == a:
                row = lax.broadcasted_iota(jnp.int32, part.shape, 0) % BLOCK
                col = lax.broadcasted_iota(jnp.int32, part.shape, 1)
                part = jnp.where(row >= col, part, NEG)
            elif c < 2:
                part = part + doors(c, a, b)
            else:
                part = part + jnp.where(in_place(c, position, n_ctx), 0.0, NEG)
            scores.append(part)
    return scores


def weigh(scores, peak, factor, a, h, chunks, numbers):
    n_query = chunks[0][0].shape[0]
    total = added = None
    scores = list(scores)
    for (_, values), c in zip(chunks, numbers):
        count = (a + 1) * BLOCK if c == 0 else n_query
        parts = []
        for b in range(count // BLOCK):
            w = jnp.exp2(scores.pop(0) * factor - peak)
            total = w if total is None else total + w
            parts.append(w.astype(jnp.bfloat16))
        w = jnp.concatenate(parts, axis=1) if len(parts) > 1 else parts[0]
        v = values[:count, h * HEAD_SIZE : (h + 1) * HEAD_SIZE]
        term = jnp.dot(w, v, preferred_element_type=jnp.float32)
        added = term if added is None else added + term
    return total, added


def head_slices(queries, keys, h):
    group = queries.shape[1] // keys.shape[1]
    return [slice((h * group + g) * HEAD_SIZE, (h * group + g + 1) * HEAD_SIZE) for g in range(group)]


def absorb(numbers, doors, queries, chunks, before, after):
    n_query = queries.shape[0]
    factor = SCALE * LOG2E
    parts = []
    for a in range(n_query // BLOCK):
        for h in range(chunks[0][0].shape[1] // HEAD_SIZE):
            heads = head_slices(queries, chunks[0][0], h)
            size = len(heads) * BLOCK
            parts.append((a, h, heads, slice(len(parts) * size, (len(parts) + 1) * size)))
    scores = []
    for a, h, heads, _ in parts:
        q = jnp.concatenate([queries[a * BLOCK : (a + 1) * BLOCK, s] for s in heads], axis=0)
        scores.append(score_blocks(doors, q, a, h, chunks, numbers))
    peaks = [functools.reduce(jnp.maximum, s) for s in scores]
    peaks = [jnp.max(peak, axis=1, keepdims=True) * factor for peak in peaks]
    shrinks = None
    if before is None:
        peaks = [jnp.broadcast_to(peak, (peak.shape[0], HEAD_SIZE)) for peak in peaks]
    else:
        lasts = [before[0][rows, :] for _, _, _, rows in parts]
        peaks = [jnp.maximum(last, peak) for last, peak in zip(lasts, peaks)]
        shrinks = [jnp.exp2(last - peak) for last, peak in zip(lasts, peaks)]
    sums = [
        weigh(s, peak, factor, a, h, chunks, numbers)
        for s, peak, (a, h, _, _) in zip(scores, peaks, parts)
    ]
    for i, (a, h, heads, rows) in enumerate(parts):
        total, added = sums[i]
        if before is not None:
            total = total + before[1][rows, :] * shrinks[i]
            added = added + before[2][rows, :] * shrinks[i]
        sums[i] = (total, added)
    after(parts, peaks, sums)


def store_state(state):
    def after(parts, peaks, sums):
        for (_, _, _, rows), peak, (total, added) in zip(parts, peaks, sums):
            for ref, part in zip(state, (peak, total, added)):
                ref[rows, :] = part

    return after


def pairs_of(refs):
    return list(zip(refs[0::2], refs[1::2]))


def first_kernel(docs_in, queries_in, keys_in, values_in, *refs):
    *state, queries, open_beside, docs, keys, values, sems = refs
    places = ((docs_in, docs), (queries_in, queries), (keys_in, keys), (values_in, values))
    fetches = [pltpu.make_async_copy(a, b, sems.at[i]) for i, (a, b) in enumerate(places)]
    for fetch in fetches:
        fetch.start()
    for fetch in fetches:
        fetch.wait()
    position = lax.axis_index("ctx")
    q_blocks = queries.shape[0] // BLOCK

    def doors(number, a, b):
        source = position if number == 0 else jnp.maximum(position - 1, 0)
        seen = docs[source * q_blocks + b] == docs[position * q_blocks + a]
        if number == 1:
            seen = seen & (position % 2 == 1)
        return jnp.where(seen, 0.0, NEG)

    for a in range(q_blocks):
        for b in range(q_blocks):
            part = open_beside.at[a * 8 : (a + 1) * 8, b * BLOCK : (b + 1) * BLOCK]
            part[...] = jnp.full(part.shape, doors(1, a, b), jnp.float32)
    absorb((0,), doors, queries, [(keys, values)], None, store_state(state))


def next_kernel(numbers, queries, open_beside, weight_in, *refs):
    *refs, weight, sem = refs
    fetch = pltpu.make_async_copy(weight_in, weight, sem)
    fetch.start()
    pairs = 2 * len(numbers)

    def doors(number, a, b):
        return open_beside[a * 8 : a * 8 + 1, b * BLOCK : (b + 1) * BLOCK]

    absorb(numbers, doors, queries, pairs_of(refs[3 : 3 + pairs]), refs[:3], store_state(refs[3 + pairs :]))
    fetch.wait()


def attend_cost(queries, numbers, fetched=0):
    n_query, width = queries.shape
    count = len(numbers) * n_query
    return pl.CostEstimate(
        flops=4 * n_query * width * count,
        bytes_accessed=fetched,
        transcendentals=n_query * count * width // HEAD_SIZE,
    )


def state_shapes(queries):
    rows = queries.size // HEAD_SIZE
    return (pltpu.VMEM((rows, HEAD_SIZE), jnp.float32),) * 3


def attend_first(docs, queries, keys, values):
    n_query = queries.shape[0]
    return pl.pallas_call(
        first_kernel,
        out_shape=state_shapes(queries)
        + (
            pltpu.VMEM(queries.shape, queries.dtype),
            pltpu.VMEM((8 * n_query // BLOCK, n_query), jnp.float32),
        ),
        in_specs=[HBM] * 4,
        out_specs=(VMEM,) * 5,
        scratch_shapes=[
            pltpu.SMEM(docs.shape, docs.dtype),
            pltpu.VMEM(keys.shape, keys.dtype),
            pltpu.VMEM(values.shape, values.dtype),
            pltpu.SemaphoreType.DMA((4,)),
        ],
        compiler_params=LIMIT,
        cost_estimate=attend_cost(queries, (0,)),
        name="attend_first",
    )(*[pltpu.with_memory_space_constraint(x, pltpu.HBM) for x in (docs, queries, keys, values)])


def attend_next(queries, open_beside, weight, state, chunks, numbers):
    return pl.pallas_call(
        functools.partial(next_kernel, numbers),
        out_shape=state_shapes(queries) + (pltpu.VMEM(weight.shape, weight.dtype),),
        in_specs=[VMEM, VMEM, HBM] + [VMEM] * (3 + 2 * len(chunks)),
        out_specs=(VMEM,) * 4,
        scratch_shapes=[pltpu.SemaphoreType.DMA],
        compiler_params=LIMIT,
        cost_estimate=attend_cost(queries, numbers, 2 * weight.size),
        name="attend_next",
    )(
        queries,
        open_beside,
        pltpu.with_memory_space_constraint(weight, pltpu.HBM),
        *state,
        *[x for pair in chunks for x in pair],
    )


def last_kernel(numbers, columns, queries, weight, *refs):
    pairs = 2 * len(numbers)
    chunks = pairs_of(refs[3 : 3 + pairs])
    far, near, mine, send, attended = refs[3 + pairs :]

    def after(parts, peaks, sums):
        inverses = [1.0 / jnp.sum(total, axis=1, keepdims=True) for total, _ in sums]
        for (a, _, heads, _), inverse, (_, added) in zip(parts, inverses, sums):
            result = (added * inverse).astype(jnp.bfloat16)
            for g, head in enumerate(heads):
                attended[a * BLOCK : (a + 1) * BLOCK, head] = result[g * BLOCK : (g + 1) * BLOCK]

    absorb(numbers, None, queries, chunks, refs[:3], after)
    place = lax.axis_index("head")
    share = queries.shape[0] // 4
    for half, owners in ((far, (place ^ 2, place ^ 3)), (near, (place, place ^ 1))):
        for i, owner in enumerate(owners):
            source = pl.ds(pl.multiple_of(owner * share, share), share)
            half[i * share : (i + 1) * share, :] = attended[source, :]
    project_columns(far, weight, mine, (send,), *columns)


def attend_last(queries, weight, state, chunks, numbers, columns):
    n_query, width = queries.shape
    half = jax.ShapeDtypeStruct((n_query // 2, width), jnp.bfloat16)
    return pl.pallas_call(
        functools.partial(last_kernel, numbers, columns),
        out_shape=(half, half) + project_shapes(n_query // 4, columns[1] - columns[0]),
        in_specs=[VMEM] * (5 + 2 * len(numbers)),
        out_specs=(VMEM,) * 4,
        scratch_shapes=[pltpu.VMEM(queries.shape, jnp.bfloat16)],
        compiler_params=LIMIT,
        cost_estimate=attend_cost(queries, numbers),
        name="attend_last",
    )(queries, weight, *state, *[x for pair in chunks for x in pair])


def project_shapes(rows, count, sends=1):
    send = jax.ShapeDtypeStruct((rows, count // sends), jnp.bfloat16)
    return (jax.ShapeDtypeStruct((rows, count), jnp.float32),) + (send,) * sends


def project_columns(rows, weight, mine, sends, start, end):
    share = rows.shape[0] // 2
    width = sends[0].shape[1]
    for i, send in enumerate(sends):
        for at in range(0, width, 768):
            stop = min(at + 768, width)
            columns = weight[:, start + i * width + at : start + i * width + stop]
            product = jnp.dot(rows[...], columns, preferred_element_type=jnp.float32)
            mine[:, i * width + at : i * width + stop] = product[:share]
            send[:, at:stop] = product[share:].astype(send.dtype)


def project_kernel(columns, rows, weight, mine, *sends):
    project_columns(rows, weight, mine, sends, *columns)


def project(rows, weight, columns, sends=1):
    count = columns[1] - columns[0]
    return pl.pallas_call(
        functools.partial(project_kernel, columns),
        out_shape=project_shapes(rows.shape[0] // 2, count, sends),
        in_specs=[VMEM, VMEM],
        out_specs=(VMEM,) * (1 + sends),
        compiler_params=LIMIT,
        cost_estimate=pl.CostEstimate(
            flops=2 * rows.shape[0] * rows.shape[1] * count, bytes_accessed=0, transcendentals=0
        ),
        name="project",
    )(rows, weight)


def add_kernel(mine, theirs, *outs):
    at = 0
    for out in outs:
        columns = slice(at, at + out.shape[1])
        at += out.shape[1]
        out[...] = (mine[:, columns] + theirs[:, columns].astype(jnp.float32)).astype(out.dtype)


def add_up(mine, theirs, widths):
    return pl.pallas_call(
        add_kernel,
        out_shape=[jax.ShapeDtypeStruct((mine.shape[0], width), theirs.dtype) for width in widths],
        in_specs=[VMEM, VMEM],
        out_specs=[VMEM] * len(widths),
        compiler_params=LIMIT,
        cost_estimate=pl.CostEstimate(flops=theirs.size, bytes_accessed=0, transcendentals=0),
        name="add_up",
    )(mine, theirs)


def combine_kernel(cuts, counts, mine, *refs):
    across, refs = refs[: sum(counts)], refs[sum(counts) :]
    beside, (out, *totals, sems) = refs[: len(refs) - len(cuts) - 2], refs[len(refs) - len(cuts) - 2 :]
    copies = []
    for i, (at, total) in enumerate(zip(cuts, totals)):
        options = across[sum(counts[:i]) : sum(counts[: i + 1])]
        width = options[0].shape[1]
        left = 0
        for part in beside:
            low, high = max(left, at), min(left + part.shape[1], at + width)
            if low < high:
                piece = mine[:, low:high] + part[:, low - left : high - left].astype(jnp.float32)
                there = options[0][:, low - at : high - at].astype(jnp.float32)
                if len(options) == 2:
                    position = lax.axis_index("ctx")
                    late = functools.reduce(jnp.logical_or, [position == i for i in LATE])
                    relayed = options[1][:, low - at : high - at].astype(jnp.float32)
                    there = jnp.where(late, relayed, there)
                total[:, low - at : high - at] = (piece + there).astype(total.dtype)
            left += part.shape[1]
        copies.append(pltpu.make_async_copy(total, out.at[:, at : at + width], sems.at[i]))
        copies[-1].start()
    for copy in copies:
        copy.wait()


def combine(mine, beside, across, cuts, out=None):
    outs = [] if out is None else [out]
    across = [x if isinstance(x, tuple) else (x,) for x in across]
    arrays = [x for options in across for x in options]
    counts = [len(options) for options in across]
    inputs = 1 + len(arrays) + len(beside)

    def kernel(*refs):
        combine_kernel(cuts, counts, *refs[:inputs], *refs[inputs + len(outs) :])

    return pl.pallas_call(
        kernel,
        out_shape=jax.ShapeDtypeStruct(mine.shape, jnp.bfloat16),
        in_specs=[VMEM] * inputs + [HBM] * len(outs),
        out_specs=HBM,
        scratch_shapes=[pltpu.VMEM(options[0].shape, jnp.bfloat16) for options in across]
        + [pltpu.SemaphoreType.DMA((len(cuts),))],
        input_output_aliases={inputs: 0} if outs else {},
        compiler_params=LIMIT,
        name="combine",
    )(mine, *arrays, *beside, *outs)


def from_behind(block, axis, distance):
    devices = range(lax.axis_size(axis))
    route = [(i - distance, i) for i in devices if i - distance in devices]
    return lax.ppermute(block, axis, route)


def token_docs(doc_ids, start, count):
    blocks = (start + jnp.arange(count, dtype=jnp.int32)) // BLOCK
    table = blocks[:, None] == jnp.arange(doc_ids.shape[0], dtype=jnp.int32)[None, :]
    return jnp.sum(jnp.where(table, doc_ids[None, :], 0), axis=1)


def attend(carry, queries, q_docs, q_start, k_piece, v_piece, k_docs, k_start):
    peak, totals, accum = carry
    n_query = queries.shape[0]
    n_key = k_piece.shape[0]
    kv_heads = k_piece.shape[1] // HEAD_SIZE
    query_group = queries.shape[1] // k_piece.shape[1]
    q_heads = queries.reshape(n_query, kv_heads, query_group, HEAD_SIZE)
    k_heads = k_piece.reshape(n_key, kv_heads, HEAD_SIZE)
    v_heads = v_piece.reshape(n_key, kv_heads, HEAD_SIZE)
    scores = (
        jnp.einsum("qkgd,skd->kgqs", q_heads, k_heads, preferred_element_type=jnp.float32) * SCALE
    )
    q_pos = q_start + jnp.arange(n_query, dtype=jnp.int32)
    k_pos = k_start + jnp.arange(n_key, dtype=jnp.int32)
    allowed = (q_docs[:, None] == k_docs[None, :]) & (q_pos[:, None] >= k_pos[None, :])
    scores = jnp.where(allowed, scores, NEG)
    new_peak = jnp.maximum(peak, jnp.max(scores, axis=-1))
    shrink = jnp.exp(peak - new_peak)
    weights = jnp.exp(scores - new_peak[..., None])
    totals = totals * shrink + jnp.sum(weights, axis=-1)
    rounded = weights.astype(jnp.bfloat16)
    added = jnp.einsum("kgqs,skd->kgqd", rounded, v_heads, preferred_element_type=jnp.float32)
    accum = accum * shrink[..., None] + added
    return (new_peak, totals, accum)


def absorb_block(carry, queries, q_docs, q_start, k_piece, v_piece, k_start, doc_ids, flag):
    n_key = k_piece.shape[0]
    k_docs = token_docs(doc_ids, k_start, n_key)
    fresh = attend(carry, queries, q_docs, q_start, k_piece, v_piece, k_docs, k_start)
    return jax.tree.map(lambda new, old: jnp.where(flag, new, old), fresh, carry)


def ring_attention(queries, keys, values, doc_ids, n_ctx, position):
    n_query = queries.shape[0]
    q_start = position * n_query
    q_docs = token_docs(doc_ids, q_start, n_query)
    kv_heads = keys.shape[1] // HEAD_SIZE
    query_group = queries.shape[1] // keys.shape[1]
    carry = (
        jnp.full((kv_heads, query_group, n_query), NEG, jnp.float32),
        jnp.zeros((kv_heads, query_group, n_query), jnp.float32),
        jnp.zeros((kv_heads, query_group, n_query, HEAD_SIZE), jnp.float32),
    )
    always = jnp.array(True)
    carry = absorb_block(carry, queries, q_docs, q_start, keys, values, q_start, doc_ids, always)

    def turn_one(step, state):
        inner_state, moving = state
        moving = from_behind(moving, "ctx", 1)
        start = ((position - step) % n_ctx) * n_query
        inner_state = absorb_block(
            inner_state, queries, q_docs, q_start, moving[0], moving[1], start, doc_ids, always
        )
        return (inner_state, moving)

    _, totals, accum = lax.fori_loop(1, n_ctx, turn_one, (carry, jnp.stack((keys, values))))[0]
    result = accum / totals[..., None]
    return jnp.transpose(result, (2, 0, 1, 3)).reshape(queries.shape).astype(jnp.bfloat16)


def part_rows(attended, place):
    share = attended.shape[0] // 4
    rows = [lax.dynamic_slice_in_dim(attended, (place ^ flip) * share, share, 0) for flip in (2, 3, 0, 1)]
    return jnp.concatenate(rows[:2], axis=0), jnp.concatenate(rows[2:], axis=0)


def per_device(queries, keys, values, doc_ids, out_weight):
    n_ctx = lax.axis_size("ctx")
    heads = lax.axis_size("head")
    position = lax.axis_index("ctx")
    place = lax.axis_index("head")
    other_core = [(i, i ^ 1) for i in range(heads)]
    other_chip = [(i, i ^ 2) for i in range(heads)]
    columns = out_weight.shape[1]
    relay = columns // 10 // BLOCK * BLOCK
    early_columns = columns * 3 // 7 // BLOCK * BLOCK - BLOCK
    cuts = [0, early_columns - relay, early_columns]

    if n_ctx == 8:
        by_two = [move(x, BY_TWO) for x in (keys, values)]
        beside = [move(x, BESIDE) for x in (keys, values)]
        *state, fetched, open_beside = attend_first(doc_ids, queries, keys, values)
        by_four = [move(after(x, state[0]), AGAIN) for x in by_two]
        swap_two = [
            move(after(after(by_two[0], beside[0]), state[0]), ACROSS),
            move(after(by_two[1], beside[1]), ACROSS),
        ]
        swap_four = [move(after(swap_two[0], by_four[0]), AGAIN), move(by_four[1], LAST)]
        chunks = [beside, by_two, by_four]
        *state, weight = attend_next(fetched, open_beside, out_weight, state, chunks, (1, 2, 3))
        chunks = [swap_two, swap_four]
        far, near, mine, send = attend_last(fetched, weight, state, chunks, (4, 5), (0, cuts[2]))
    else:
        weight = out_weight
        attended = ring_attention(queries, keys, values, doc_ids, n_ctx, position)
        far, near = part_rows(attended, place)
        mine, send = project(far, weight, (0, cuts[2]))
    theirs = hop(send, "head", other_core)
    later_mine, later_send = project(far, weight, (cuts[2], columns))
    first_sum, relay_sum = add_up(mine, theirs, [cuts[1], cuts[2] - cuts[1]])
    first_part = hop(first_sum, "head", other_chip)
    later_theirs = hop(after(later_send, relay_sum), "head", other_core)
    later_mine = after(later_mine, first_sum)
    (later_sum,) = add_up(later_mine, later_theirs, [columns - cuts[2]])
    later_part = hop(later_sum, "head", other_chip)
    mine, *sends = project(after(near, later_sum), weight, (0, columns), 2)
    theirs = [hop(send, "head", other_core) for send in sends]
    if n_ctx == 8:
        direct = move(relay_sum, (), [i for i in range(n_ctx) if i not in LATE])
        arrived = move(after(relay_sum, mine), RELAY)
        relay_part = (direct, move(move(after(arrived, first_part), (), [ring[1] for ring in RELAY]), RELAY))
    else:
        relay_part = hop(relay_sum, "head", other_chip)
    out = combine(mine, theirs, [first_part], [0])
    return combine(mine, theirs, [later_part, relay_part], [cuts[2], cuts[1]], out)


def solution(mesh):
    placed = (P("ctx", "head"), P("ctx", "head"), P("ctx", "head"), P(), P("head", None))
    return jax.shard_map(
        per_device, mesh=mesh, in_specs=placed, out_specs=P(("ctx", "head"), None), check_vma=False
    )
```

```python
import functools

import jax
import jax.numpy as jnp
from jax import lax
from jax.experimental import pallas as pl
from jax.experimental.pallas import tpu as pltpu
from jax.sharding import PartitionSpec as P

HEAD_SIZE = 128
BLOCK = 128
SCALE = 168.0 ** (-0.5)
LOG2E = 1.4426950408889634
NEG = -1e30
VMEM = pl.BlockSpec(memory_space=pltpu.VMEM)
SMEM = pl.BlockSpec(memory_space=pltpu.SMEM)
HBM = pl.BlockSpec(memory_space=pltpu.HBM)
SPAN = 1024
LIMIT = pltpu.CompilerParams(vmem_limit_bytes=32 * 1024 * 1024)


def hop(block, axis, pairs):
    return lax.ppermute(block, axis, pairs)


def in_place(number, position, n_ctx):
    away = {2: 2, 3: 4, 4: 2, 5: 4}[number]
    return (position < n_ctx * 3 // 4) & (position >= away)


BESIDE = ((0, 1), (2, 3), (4, 5), (6, 7))
BY_TWO = ((0, 2, 4), (1, 3, 5))
AGAIN = ((2, 4), (3, 5))
ACROSS = ((2, 3), (4, 5))
LAST = ((4, 5),)
LATE = (4, 5)
RELAY = ((4, 6), (5, 7))


def move(block, rings, crossing=()):
    n_ctx, heads = lax.axis_size("ctx"), lax.axis_size("head")
    target = {ring[i]: ring[(i + 1) % len(ring)] for ring in rings for i in range(len(ring))}
    pairs = []
    for i in range(n_ctx):
        flip = 0 if i in target else 2 if i in crossing else 1
        pairs += [(i * heads + h, target.get(i, i) * heads + (h ^ flip)) for h in range(heads)]
    return lax.ppermute(block, ("ctx", "head"), pairs)


def after(x, event):
    return lax.optimization_barrier((x, event))[0]


def score_blocks(doors, q, a, h, chunks, numbers):
    position = lax.axis_index("ctx")
    n_ctx = lax.axis_size("ctx")
    n_query = chunks[0][0].shape[0]
    scores = []
    for (keys, _), c in zip(chunks, numbers):
        count = (a + 1) * BLOCK if c == 0 else n_query
        k = keys[:count, h * HEAD_SIZE : (h + 1) * HEAD_SIZE]
        s = lax.dot_general(q, k, (((1,), (1,)), ((), ())), preferred_element_type=jnp.float32)
        for b in range(count // BLOCK):
            part = s[:, b * BLOCK : (b + 1) * BLOCK]
            if c == 0 and b == a:
                row = lax.broadcasted_iota(jnp.int32, part.shape, 0) % BLOCK
                col = lax.broadcasted_iota(jnp.int32, part.shape, 1)
                part = jnp.where(row >= col, part, NEG)
            elif c < 2:
                part = part + doors(c, a, b)
            else:
                part = part + jnp.where(in_place(c, position, n_ctx), 0.0, NEG)
            scores.append(part)
    return scores


def weigh(scores, peak, factor, a, h, chunks, numbers):
    n_query = chunks[0][0].shape[0]
    total = added = None
    scores = list(scores)
    for (_, values), c in zip(chunks, numbers):
        count = (a + 1) * BLOCK if c == 0 else n_query
        parts = []
        for b in range(count // BLOCK):
            w = jnp.exp2(scores.pop(0) * factor - peak)
            total = w if total is None else total + w
            parts.append(w.astype(jnp.bfloat16))
        w = jnp.concatenate(parts, axis=1) if len(parts) > 1 else parts[0]
        v = values[:count, h * HEAD_SIZE : (h + 1) * HEAD_SIZE]
        term = jnp.dot(w, v, preferred_element_type=jnp.float32)
        added = term if added is None else added + term
    return total, added


def head_slices(queries, keys, h):
    group = queries.shape[1] // keys.shape[1]
    return [slice((h * group + g) * HEAD_SIZE, (h * group + g + 1) * HEAD_SIZE) for g in range(group)]


def absorb(numbers, doors, queries, chunks, before, after):
    n_query = queries.shape[0]
    factor = SCALE * LOG2E
    parts = []
    for a in range(n_query // BLOCK):
        for h in range(chunks[0][0].shape[1] // HEAD_SIZE):
            heads = head_slices(queries, chunks[0][0], h)
            size = len(heads) * BLOCK
            parts.append((a, h, heads, slice(len(parts) * size, (len(parts) + 1) * size)))
    scores = []
    for a, h, heads, _ in parts:
        q = jnp.concatenate([queries[a * BLOCK : (a + 1) * BLOCK, s] for s in heads], axis=0)
        scores.append(score_blocks(doors, q, a, h, chunks, numbers))
    peaks = [functools.reduce(jnp.maximum, s) for s in scores]
    peaks = [jnp.max(peak, axis=1, keepdims=True) * factor for peak in peaks]
    shrinks = None
    if before is None:
        peaks = [jnp.broadcast_to(peak, (peak.shape[0], HEAD_SIZE)) for peak in peaks]
    else:
        lasts = [before[0][rows, :] for _, _, _, rows in parts]
        peaks = [jnp.maximum(last, peak) for last, peak in zip(lasts, peaks)]
        shrinks = [jnp.exp2(last - peak) for last, peak in zip(lasts, peaks)]
    sums = [
        weigh(s, peak, factor, a, h, chunks, numbers)
        for s, peak, (a, h, _, _) in zip(scores, peaks, parts)
    ]
    for i, (a, h, heads, rows) in enumerate(parts):
        total, added = sums[i]
        if before is not None:
            total = total + before[1][rows, :] * shrinks[i]
            added = added + before[2][rows, :] * shrinks[i]
        sums[i] = (total, added)
    after(parts, peaks, sums)


def store_state(state):
    def after(parts, peaks, sums):
        for (_, _, _, rows), peak, (total, added) in zip(parts, peaks, sums):
            for ref, part in zip(state, (peak, total, added)):
                ref[rows, :] = part

    return after


def pairs_of(refs):
    return list(zip(refs[0::2], refs[1::2]))


def first_kernel(docs_in, queries_in, keys_in, values_in, *refs):
    *state, queries, open_beside, docs, keys, values, sems = refs
    places = ((docs_in, docs), (queries_in, queries), (keys_in, keys), (values_in, values))
    fetches = [pltpu.make_async_copy(a, b, sems.at[i]) for i, (a, b) in enumerate(places)]
    for fetch in fetches:
        fetch.start()
    for fetch in fetches:
        fetch.wait()
    position = lax.axis_index("ctx")
    q_blocks = queries.shape[0] // BLOCK

    def doors(number, a, b):
        source = position if number == 0 else jnp.maximum(position - 1, 0)
        seen = docs[source * q_blocks + b] == docs[position * q_blocks + a]
        if number == 1:
            seen = seen & (position % 2 == 1)
        return jnp.where(seen, 0.0, NEG)

    for a in range(q_blocks):
        for b in range(q_blocks):
            part = open_beside.at[a * 8 : (a + 1) * 8, b * BLOCK : (b + 1) * BLOCK]
            part[...] = jnp.full(part.shape, doors(1, a, b), jnp.float32)
    absorb((0,), doors, queries, [(keys, values)], None, store_state(state))


def next_kernel(numbers, queries, open_beside, weight_in, *refs):
    *refs, weight, sem = refs
    fetch = pltpu.make_async_copy(weight_in, weight, sem)
    fetch.start()
    pairs = 2 * len(numbers)

    def doors(number, a, b):
        return open_beside[a * 8 : a * 8 + 1, b * BLOCK : (b + 1) * BLOCK]

    absorb(numbers, doors, queries, pairs_of(refs[3 : 3 + pairs]), refs[:3], store_state(refs[3 + pairs :]))
    fetch.wait()


def attend_cost(queries, numbers, fetched=0):
    n_query, width = queries.shape
    count = len(numbers) * n_query
    return pl.CostEstimate(
        flops=4 * n_query * width * count,
        bytes_accessed=fetched,
        transcendentals=n_query * count * width // HEAD_SIZE,
    )


def state_shapes(queries):
    rows = queries.size // HEAD_SIZE
    return (pltpu.VMEM((rows, HEAD_SIZE), jnp.float32),) * 3


def attend_first(docs, queries, keys, values):
    n_query = queries.shape[0]
    return pl.pallas_call(
        first_kernel,
        out_shape=state_shapes(queries)
        + (
            pltpu.VMEM(queries.shape, queries.dtype),
            pltpu.VMEM((8 * n_query // BLOCK, n_query), jnp.float32),
        ),
        in_specs=[HBM] * 4,
        out_specs=(VMEM,) * 5,
        scratch_shapes=[
            pltpu.SMEM(docs.shape, docs.dtype),
            pltpu.VMEM(keys.shape, keys.dtype),
            pltpu.VMEM(values.shape, values.dtype),
            pltpu.SemaphoreType.DMA((4,)),
        ],
        compiler_params=LIMIT,
        cost_estimate=attend_cost(queries, (0,)),
        name="attend_first",
    )(*[pltpu.with_memory_space_constraint(x, pltpu.HBM) for x in (docs, queries, keys, values)])


def attend_next(queries, open_beside, weight, state, chunks, numbers):
    return pl.pallas_call(
        functools.partial(next_kernel, numbers),
        out_shape=state_shapes(queries) + (pltpu.VMEM(weight.shape, weight.dtype),),
        in_specs=[VMEM, VMEM, HBM] + [VMEM] * (3 + 2 * len(chunks)),
        out_specs=(VMEM,) * 4,
        scratch_shapes=[pltpu.SemaphoreType.DMA],
        compiler_params=LIMIT,
        cost_estimate=attend_cost(queries, numbers, 2 * weight.size),
        name="attend_next",
    )(
        queries,
        open_beside,
        pltpu.with_memory_space_constraint(weight, pltpu.HBM),
        *state,
        *[x for pair in chunks for x in pair],
    )


def last_kernel(numbers, columns, queries, weight, *refs):
    pairs = 2 * len(numbers)
    chunks = pairs_of(refs[3 : 3 + pairs])
    far, near, mine, send, attended = refs[3 + pairs :]

    def after(parts, peaks, sums):
        inverses = [1.0 / jnp.sum(total, axis=1, keepdims=True) for total, _ in sums]
        for (a, _, heads, _), inverse, (_, added) in zip(parts, inverses, sums):
            result = (added * inverse).astype(jnp.bfloat16)
            for g, head in enumerate(heads):
                attended[a * BLOCK : (a + 1) * BLOCK, head] = result[g * BLOCK : (g + 1) * BLOCK]

    absorb(numbers, None, queries, chunks, refs[:3], after)
    place = lax.axis_index("head")
    share = queries.shape[0] // 4
    for half, owners in ((far, (place ^ 2, place ^ 3)), (near, (place, place ^ 1))):
        for i, owner in enumerate(owners):
            source = pl.ds(pl.multiple_of(owner * share, share), share)
            half[i * share : (i + 1) * share, :] = attended[source, :]
    project_columns(far, weight, mine, (send,), *columns)


def attend_last(queries, weight, state, chunks, numbers, columns):
    n_query, width = queries.shape
    half = jax.ShapeDtypeStruct((n_query // 2, width), jnp.bfloat16)
    return pl.pallas_call(
        functools.partial(last_kernel, numbers, columns),
        out_shape=(half, half) + project_shapes(n_query // 4, columns[1] - columns[0]),
        in_specs=[VMEM] * (5 + 2 * len(numbers)),
        out_specs=(VMEM,) * 4,
        scratch_shapes=[pltpu.VMEM(queries.shape, jnp.bfloat16)],
        compiler_params=LIMIT,
        cost_estimate=attend_cost(queries, numbers),
        name="attend_last",
    )(queries, weight, *state, *[x for pair in chunks for x in pair])


def project_shapes(rows, count, sends=1):
    send = jax.ShapeDtypeStruct((rows, count // sends), jnp.bfloat16)
    return (jax.ShapeDtypeStruct((rows, count), jnp.float32),) + (send,) * sends


def project_columns(rows, weight, mine, sends, start, end):
    share = rows.shape[0] // 2
    width = sends[0].shape[1]
    for i, send in enumerate(sends):
        for at in range(0, width, 768):
            stop = min(at + 768, width)
            columns = weight[:, start + i * width + at : start + i * width + stop]
            product = jnp.dot(rows[...], columns, preferred_element_type=jnp.float32)
            mine[:, i * width + at : i * width + stop] = product[:share]
            send[:, at:stop] = product[share:].astype(send.dtype)


def project_kernel(columns, rows, weight, mine, *sends):
    project_columns(rows, weight, mine, sends, *columns)


def project(rows, weight, columns, sends=1):
    count = columns[1] - columns[0]
    return pl.pallas_call(
        functools.partial(project_kernel, columns),
        out_shape=project_shapes(rows.shape[0] // 2, count, sends),
        in_specs=[VMEM, VMEM],
        out_specs=(VMEM,) * (1 + sends),
        compiler_params=LIMIT,
        cost_estimate=pl.CostEstimate(
            flops=2 * rows.shape[0] * rows.shape[1] * count, bytes_accessed=0, transcendentals=0
        ),
        name="project",
    )(rows, weight)


def add_kernel(mine, theirs, *outs):
    at = 0
    for out in outs:
        columns = slice(at, at + out.shape[1])
        at += out.shape[1]
        out[...] = (mine[:, columns] + theirs[:, columns].astype(jnp.float32)).astype(out.dtype)


def add_up(mine, theirs, widths):
    return pl.pallas_call(
        add_kernel,
        out_shape=[jax.ShapeDtypeStruct((mine.shape[0], width), theirs.dtype) for width in widths],
        in_specs=[VMEM, VMEM],
        out_specs=[VMEM] * len(widths),
        compiler_params=LIMIT,
        cost_estimate=pl.CostEstimate(flops=theirs.size, bytes_accessed=0, transcendentals=0),
        name="add_up",
    )(mine, theirs)


def combine_kernel(cuts, counts, mine, *refs):
    across, refs = refs[: sum(counts)], refs[sum(counts) :]
    beside, (out, *totals, sems) = refs[: len(refs) - len(cuts) - 2], refs[len(refs) - len(cuts) - 2 :]
    copies = []
    for i, (at, total) in enumerate(zip(cuts, totals)):
        options = across[sum(counts[:i]) : sum(counts[: i + 1])]
        end = at + options[0].shape[1]
        stops = {at, end} | set(range(0, mine.shape[1], SPAN))
        for part in range(len(beside)):
            stops.add(part * beside[0].shape[1])
        stops = sorted(x for x in stops if at <= x <= end)
        for low, high in zip(stops[:-1], stops[1:]):
            part, left = beside[low // beside[0].shape[1]], low // beside[0].shape[1] * beside[0].shape[1]
            columns = slice(low - at, high - at)
            piece = mine[:, low:high] + part[:, low - left : high - left].astype(jnp.float32)
            there = options[0][:, columns].astype(jnp.float32)
            if len(options) == 2:
                position = lax.axis_index("ctx")
                late = functools.reduce(jnp.logical_or, [position == i for i in LATE])
                there = jnp.where(late, options[1][:, columns].astype(jnp.float32), there)
            total[:, columns] = (piece + there).astype(total.dtype)
            copies.append(
                pltpu.make_async_copy(total.at[:, columns], out.at[:, low:high], sems.at[len(copies)])
            )
            copies[-1].start()
    for copy in copies:
        copy.wait()


def combine(mine, beside, across, cuts, out=None):
    outs = [] if out is None else [out]
    across = [x if isinstance(x, tuple) else (x,) for x in across]
    arrays = [x for options in across for x in options]
    counts = [len(options) for options in across]
    inputs = 1 + len(arrays) + len(beside)

    def kernel(*refs):
        combine_kernel(cuts, counts, *refs[:inputs], *refs[inputs + len(outs) :])

    return pl.pallas_call(
        kernel,
        out_shape=jax.ShapeDtypeStruct(mine.shape, jnp.bfloat16),
        in_specs=[VMEM] * inputs + [HBM] * len(outs),
        out_specs=HBM,
        scratch_shapes=[pltpu.VMEM(options[0].shape, jnp.bfloat16) for options in across]
        + [pltpu.SemaphoreType.DMA((len(cuts) * (2 + len(beside) + mine.shape[1] // SPAN),))],
        input_output_aliases={inputs: 0} if outs else {},
        compiler_params=LIMIT,
        name="combine",
    )(mine, *arrays, *beside, *outs)


def from_behind(block, axis, distance):
    devices = range(lax.axis_size(axis))
    route = [(i - distance, i) for i in devices if i - distance in devices]
    return lax.ppermute(block, axis, route)


def token_docs(doc_ids, start, count):
    blocks = (start + jnp.arange(count, dtype=jnp.int32)) // BLOCK
    table = blocks[:, None] == jnp.arange(doc_ids.shape[0], dtype=jnp.int32)[None, :]
    return jnp.sum(jnp.where(table, doc_ids[None, :], 0), axis=1)


def attend(carry, queries, q_docs, q_start, k_piece, v_piece, k_docs, k_start):
    peak, totals, accum = carry
    n_query = queries.shape[0]
    n_key = k_piece.shape[0]
    kv_heads = k_piece.shape[1] // HEAD_SIZE
    query_group = queries.shape[1] // k_piece.shape[1]
    q_heads = queries.reshape(n_query, kv_heads, query_group, HEAD_SIZE)
    k_heads = k_piece.reshape(n_key, kv_heads, HEAD_SIZE)
    v_heads = v_piece.reshape(n_key, kv_heads, HEAD_SIZE)
    scores = (
        jnp.einsum("qkgd,skd->kgqs", q_heads, k_heads, preferred_element_type=jnp.float32) * SCALE
    )
    q_pos = q_start + jnp.arange(n_query, dtype=jnp.int32)
    k_pos = k_start + jnp.arange(n_key, dtype=jnp.int32)
    allowed = (q_docs[:, None] == k_docs[None, :]) & (q_pos[:, None] >= k_pos[None, :])
    scores = jnp.where(allowed, scores, NEG)
    new_peak = jnp.maximum(peak, jnp.max(scores, axis=-1))
    shrink = jnp.exp(peak - new_peak)
    weights = jnp.exp(scores - new_peak[..., None])
    totals = totals * shrink + jnp.sum(weights, axis=-1)
    rounded = weights.astype(jnp.bfloat16)
    added = jnp.einsum("kgqs,skd->kgqd", rounded, v_heads, preferred_element_type=jnp.float32)
    accum = accum * shrink[..., None] + added
    return (new_peak, totals, accum)


def absorb_block(carry, queries, q_docs, q_start, k_piece, v_piece, k_start, doc_ids, flag):
    n_key = k_piece.shape[0]
    k_docs = token_docs(doc_ids, k_start, n_key)
    fresh = attend(carry, queries, q_docs, q_start, k_piece, v_piece, k_docs, k_start)
    return jax.tree.map(lambda new, old: jnp.where(flag, new, old), fresh, carry)


def ring_attention(queries, keys, values, doc_ids, n_ctx, position):
    n_query = queries.shape[0]
    q_start = position * n_query
    q_docs = token_docs(doc_ids, q_start, n_query)
    kv_heads = keys.shape[1] // HEAD_SIZE
    query_group = queries.shape[1] // keys.shape[1]
    carry = (
        jnp.full((kv_heads, query_group, n_query), NEG, jnp.float32),
        jnp.zeros((kv_heads, query_group, n_query), jnp.float32),
        jnp.zeros((kv_heads, query_group, n_query, HEAD_SIZE), jnp.float32),
    )
    always = jnp.array(True)
    carry = absorb_block(carry, queries, q_docs, q_start, keys, values, q_start, doc_ids, always)

    def turn_one(step, state):
        inner_state, moving = state
        moving = from_behind(moving, "ctx", 1)
        start = ((position - step) % n_ctx) * n_query
        inner_state = absorb_block(
            inner_state, queries, q_docs, q_start, moving[0], moving[1], start, doc_ids, always
        )
        return (inner_state, moving)

    _, totals, accum = lax.fori_loop(1, n_ctx, turn_one, (carry, jnp.stack((keys, values))))[0]
    result = accum / totals[..., None]
    return jnp.transpose(result, (2, 0, 1, 3)).reshape(queries.shape).astype(jnp.bfloat16)


def part_rows(attended, place):
    share = attended.shape[0] // 4
    rows = [lax.dynamic_slice_in_dim(attended, (place ^ flip) * share, share, 0) for flip in (2, 3, 0, 1)]
    return jnp.concatenate(rows[:2], axis=0), jnp.concatenate(rows[2:], axis=0)


def per_device(queries, keys, values, doc_ids, out_weight):
    n_ctx = lax.axis_size("ctx")
    heads = lax.axis_size("head")
    position = lax.axis_index("ctx")
    place = lax.axis_index("head")
    other_core = [(i, i ^ 1) for i in range(heads)]
    other_chip = [(i, i ^ 2) for i in range(heads)]
    columns = out_weight.shape[1]
    relay = columns // 10 // BLOCK * BLOCK
    early_columns = columns * 3 // 7 // BLOCK * BLOCK - BLOCK
    cuts = [0, early_columns - relay, early_columns]

    if n_ctx == 8:
        by_two = [move(x, BY_TWO) for x in (keys, values)]
        beside = [move(x, BESIDE) for x in (keys, values)]
        *state, fetched, open_beside = attend_first(doc_ids, queries, keys, values)
        by_four = [move(after(x, state[0]), AGAIN) for x in by_two]
        swap_two = [
            move(after(after(by_two[0], beside[0]), state[0]), ACROSS),
            move(after(by_two[1], beside[1]), ACROSS),
        ]
        swap_four = [move(after(swap_two[0], by_four[0]), AGAIN), move(by_four[1], LAST)]
        chunks = [beside, by_two, by_four]
        *state, weight = attend_next(fetched, open_beside, out_weight, state, chunks, (1, 2, 3))
        chunks = [swap_two, swap_four]
        far, near, mine, send = attend_last(fetched, weight, state, chunks, (4, 5), (0, cuts[2]))
    else:
        weight = out_weight
        attended = ring_attention(queries, keys, values, doc_ids, n_ctx, position)
        far, near = part_rows(attended, place)
        mine, send = project(far, weight, (0, cuts[2]))
    theirs = hop(send, "head", other_core)
    later_mine, later_send = project(far, weight, (cuts[2], columns))
    first_sum, relay_sum = add_up(mine, theirs, [cuts[1], cuts[2] - cuts[1]])
    first_part = hop(first_sum, "head", other_chip)
    later_theirs = hop(after(later_send, relay_sum), "head", other_core)
    later_mine = after(later_mine, first_sum)
    (later_sum,) = add_up(later_mine, later_theirs, [columns - cuts[2]])
    later_part = hop(later_sum, "head", other_chip)
    mine, *sends = project(after(near, later_sum), weight, (0, columns), 2)
    theirs = [hop(send, "head", other_core) for send in sends]
    if n_ctx == 8:
        direct = move(relay_sum, (), [i for i in range(n_ctx) if i not in LATE])
        arrived = move(after(relay_sum, mine), RELAY)
        relay_part = (direct, move(move(after(arrived, first_part), (), [ring[1] for ring in RELAY]), RELAY))
    else:
        relay_part = hop(relay_sum, "head", other_chip)
    out = combine(mine, theirs, [first_part], [0])
    return combine(mine, theirs, [later_part, relay_part], [cuts[2], cuts[1]], out)


def solution(mesh):
    placed = (P("ctx", "head"), P("ctx", "head"), P("ctx", "head"), P(), P("head", None))
    return jax.shard_map(
        per_device, mesh=mesh, in_specs=placed, out_specs=P(("ctx", "head"), None), check_vma=False
    )
```

```python
import functools

import jax
import jax.numpy as jnp
from jax import lax
from jax.experimental import pallas as pl
from jax.experimental.pallas import tpu as pltpu
from jax.sharding import PartitionSpec as P

HEAD_SIZE = 128
BLOCK = 128
SCALE = 168.0 ** (-0.5)
LOG2E = 1.4426950408889634
NEG = -1e30
VMEM = pl.BlockSpec(memory_space=pltpu.VMEM)
SMEM = pl.BlockSpec(memory_space=pltpu.SMEM)
HBM = pl.BlockSpec(memory_space=pltpu.HBM)
LIMIT = pltpu.CompilerParams(vmem_limit_bytes=32 * 1024 * 1024)


def hop(block, axis, pairs):
    return lax.ppermute(block, axis, pairs)


def in_place(number, position, n_ctx):
    away = {2: 2, 3: 4, 4: 2, 5: 4}[number]
    return (position < n_ctx * 3 // 4) & (position >= away)


BESIDE = ((0, 1), (2, 3), (4, 5), (6, 7))
BY_TWO = ((0, 2, 4), (1, 3, 5))
AGAIN = ((2, 4), (3, 5))
ACROSS = ((2, 3), (4, 5))
LAST = ((4, 5),)
LATE = (4, 5)
RELAY = ((4, 6), (5, 7))


def move(block, rings, crossing=()):
    n_ctx, heads = lax.axis_size("ctx"), lax.axis_size("head")
    target = {ring[i]: ring[(i + 1) % len(ring)] for ring in rings for i in range(len(ring))}
    pairs = []
    for i in range(n_ctx):
        flip = 0 if i in target else 2 if i in crossing else 1
        pairs += [(i * heads + h, target.get(i, i) * heads + (h ^ flip)) for h in range(heads)]
    return lax.ppermute(block, ("ctx", "head"), pairs)


def after(x, event):
    return lax.optimization_barrier((x, event))[0]


def score_blocks(doors, q, a, h, chunks, numbers):
    position = lax.axis_index("ctx")
    n_ctx = lax.axis_size("ctx")
    n_query = chunks[0][0].shape[0]
    scores = []
    for (keys, _), c in zip(chunks, numbers):
        count = (a + 1) * BLOCK if c == 0 else n_query
        k = keys[:count, h * HEAD_SIZE : (h + 1) * HEAD_SIZE]
        s = lax.dot_general(q, k, (((1,), (1,)), ((), ())), preferred_element_type=jnp.float32)
        for b in range(count // BLOCK):
            part = s[:, b * BLOCK : (b + 1) * BLOCK]
            if c == 0 and b == a:
                row = lax.broadcasted_iota(jnp.int32, part.shape, 0) % BLOCK
                col = lax.broadcasted_iota(jnp.int32, part.shape, 1)
                part = jnp.where(row >= col, part, NEG)
            elif c < 2:
                part = part + doors(c, a, b)
            else:
                part = part + jnp.where(in_place(c, position, n_ctx), 0.0, NEG)
            scores.append(part)
    return scores


def weigh(scores, peak, factor, a, h, chunks, numbers):
    n_query = chunks[0][0].shape[0]
    total = added = None
    scores = list(scores)
    for (_, values), c in zip(chunks, numbers):
        count = (a + 1) * BLOCK if c == 0 else n_query
        parts = []
        for b in range(count // BLOCK):
            w = jnp.exp2(scores.pop(0) * factor - peak)
            total = w if total is None else total + w
            parts.append(w.astype(jnp.bfloat16))
        w = jnp.concatenate(parts, axis=1) if len(parts) > 1 else parts[0]
        v = values[:count, h * HEAD_SIZE : (h + 1) * HEAD_SIZE]
        term = jnp.dot(w, v, preferred_element_type=jnp.float32)
        added = term if added is None else added + term
    return total, added


def head_slices(queries, keys, h):
    group = queries.shape[1] // keys.shape[1]
    return [slice((h * group + g) * HEAD_SIZE, (h * group + g + 1) * HEAD_SIZE) for g in range(group)]


def absorb(numbers, doors, queries, chunks, before, after):
    n_query = queries.shape[0]
    factor = SCALE * LOG2E
    parts = []
    for a in range(n_query // BLOCK):
        for h in range(chunks[0][0].shape[1] // HEAD_SIZE):
            heads = head_slices(queries, chunks[0][0], h)
            size = len(heads) * BLOCK
            parts.append((a, h, heads, slice(len(parts) * size, (len(parts) + 1) * size)))
    scores = []
    for a, h, heads, _ in parts:
        q = jnp.concatenate([queries[a * BLOCK : (a + 1) * BLOCK, s] for s in heads], axis=0)
        scores.append(score_blocks(doors, q, a, h, chunks, numbers))
    peaks = [functools.reduce(jnp.maximum, s) for s in scores]
    peaks = [jnp.max(peak, axis=1, keepdims=True) * factor for peak in peaks]
    shrinks = None
    if before is None:
        peaks = [jnp.broadcast_to(peak, (peak.shape[0], HEAD_SIZE)) for peak in peaks]
    else:
        lasts = [before[0][rows, :] for _, _, _, rows in parts]
        peaks = [jnp.maximum(last, peak) for last, peak in zip(lasts, peaks)]
        shrinks = [jnp.exp2(last - peak) for last, peak in zip(lasts, peaks)]
    sums = [
        weigh(s, peak, factor, a, h, chunks, numbers)
        for s, peak, (a, h, _, _) in zip(scores, peaks, parts)
    ]
    for i, (a, h, heads, rows) in enumerate(parts):
        total, added = sums[i]
        if before is not None:
            total = total + before[1][rows, :] * shrinks[i]
            added = added + before[2][rows, :] * shrinks[i]
        sums[i] = (total, added)
    after(parts, peaks, sums)


def store_state(state):
    def after(parts, peaks, sums):
        for (_, _, _, rows), peak, (total, added) in zip(parts, peaks, sums):
            for ref, part in zip(state, (peak, total, added)):
                ref[rows, :] = part

    return after


def pairs_of(refs):
    return list(zip(refs[0::2], refs[1::2]))


def first_kernel(split, docs_in, queries_in, keys_in, values_in, weight_in, *refs):
    *state, queries, open_beside, weight, docs, keys, values, sems = refs
    places = (
        (docs_in, docs),
        (queries_in, queries),
        (keys_in, keys),
        (values_in, values),
        (weight_in.at[:, :split], weight.at[:, :split]),
    )
    fetches = [pltpu.make_async_copy(a, b, sems.at[i]) for i, (a, b) in enumerate(places)]
    for fetch in fetches:
        fetch.start()
    for fetch in fetches[:4]:
        fetch.wait()
    position = lax.axis_index("ctx")
    q_blocks = queries.shape[0] // BLOCK

    def doors(number, a, b):
        source = position if number == 0 else jnp.maximum(position - 1, 0)
        seen = docs[source * q_blocks + b] == docs[position * q_blocks + a]
        if number == 1:
            seen = seen & (position % 2 == 1)
        return jnp.where(seen, 0.0, NEG)

    for a in range(q_blocks):
        for b in range(q_blocks):
            part = open_beside.at[a * 8 : (a + 1) * 8, b * BLOCK : (b + 1) * BLOCK]
            part[...] = jnp.full(part.shape, doors(1, a, b), jnp.float32)
    absorb((0,), doors, queries, [(keys, values)], None, store_state(state))
    fetches[4].wait()


def next_kernel(numbers, split, queries, open_beside, weight_in, _, *refs):
    *refs, weight, sem = refs
    fetch = pltpu.make_async_copy(weight_in.at[:, split:], weight.at[:, split:], sem)
    fetch.start()
    pairs = 2 * len(numbers)

    def doors(number, a, b):
        return open_beside[a * 8 : a * 8 + 1, b * BLOCK : (b + 1) * BLOCK]

    absorb(numbers, doors, queries, pairs_of(refs[3 : 3 + pairs]), refs[:3], store_state(refs[3 + pairs :]))
    fetch.wait()


def attend_cost(queries, numbers, fetched=0):
    n_query, width = queries.shape
    count = len(numbers) * n_query
    return pl.CostEstimate(
        flops=4 * n_query * width * count,
        bytes_accessed=fetched,
        transcendentals=n_query * count * width // HEAD_SIZE,
    )


def state_shapes(queries):
    rows = queries.size // HEAD_SIZE
    return (pltpu.VMEM((rows, HEAD_SIZE), jnp.float32),) * 3


def attend_first(docs, queries, keys, values, weight, split):
    n_query = queries.shape[0]
    return pl.pallas_call(
        functools.partial(first_kernel, split),
        out_shape=state_shapes(queries)
        + (
            pltpu.VMEM(queries.shape, queries.dtype),
            pltpu.VMEM((8 * n_query // BLOCK, n_query), jnp.float32),
            pltpu.VMEM(weight.shape, weight.dtype),
        ),
        in_specs=[HBM] * 5,
        out_specs=(VMEM,) * 6,
        scratch_shapes=[
            pltpu.SMEM(docs.shape, docs.dtype),
            pltpu.VMEM(keys.shape, keys.dtype),
            pltpu.VMEM(values.shape, values.dtype),
            pltpu.SemaphoreType.DMA((5,)),
        ],
        compiler_params=LIMIT,
        cost_estimate=attend_cost(queries, (0,)),
        name="attend_first",
    )(*[pltpu.with_memory_space_constraint(x, pltpu.HBM) for x in (docs, queries, keys, values, weight)])


def attend_next(queries, open_beside, weight, part, split, state, chunks, numbers):
    return pl.pallas_call(
        functools.partial(next_kernel, numbers, split),
        out_shape=state_shapes(queries) + (pltpu.VMEM(weight.shape, weight.dtype),),
        in_specs=[VMEM, VMEM, HBM] + [VMEM] * (4 + 2 * len(chunks)),
        out_specs=(VMEM,) * 4,
        input_output_aliases={3: 3},
        scratch_shapes=[pltpu.SemaphoreType.DMA],
        compiler_params=LIMIT,
        cost_estimate=attend_cost(queries, numbers, 2 * weight.size),
        name="attend_next",
    )(
        queries,
        open_beside,
        pltpu.with_memory_space_constraint(weight, pltpu.HBM),
        part,
        *state,
        *[x for pair in chunks for x in pair],
    )


def middle_kernel(numbers, queries, *refs):
    pairs = 2 * len(numbers)
    absorb(numbers, None, queries, pairs_of(refs[3 : 3 + pairs]), refs[:3], store_state(refs[3 + pairs :]))


def attend_middle(queries, state, chunks, numbers):
    return pl.pallas_call(
        functools.partial(middle_kernel, numbers),
        out_shape=state_shapes(queries),
        in_specs=[VMEM] * (4 + 2 * len(chunks)),
        out_specs=(VMEM,) * 3,
        compiler_params=LIMIT,
        cost_estimate=attend_cost(queries, numbers),
        name="attend_middle",
    )(queries, *state, *[x for pair in chunks for x in pair])


def last_kernel(numbers, columns, queries, weight, *refs):
    pairs = 2 * len(numbers)
    chunks = pairs_of(refs[3 : 3 + pairs])
    far, near, mine, send, attended = refs[3 + pairs :]

    def after(parts, peaks, sums):
        inverses = [1.0 / jnp.sum(total, axis=1, keepdims=True) for total, _ in sums]
        for (a, _, heads, _), inverse, (_, added) in zip(parts, inverses, sums):
            result = (added * inverse).astype(jnp.bfloat16)
            for g, head in enumerate(heads):
                attended[a * BLOCK : (a + 1) * BLOCK, head] = result[g * BLOCK : (g + 1) * BLOCK]

    absorb(numbers, None, queries, chunks, refs[:3], after)
    place = lax.axis_index("head")
    share = queries.shape[0] // 4
    for half, owners in ((far, (place ^ 2, place ^ 3)), (near, (place, place ^ 1))):
        for i, owner in enumerate(owners):
            source = pl.ds(pl.multiple_of(owner * share, share), share)
            half[i * share : (i + 1) * share, :] = attended[source, :]
    project_columns(far, weight, mine, (send,), *columns)


def attend_last(queries, weight, state, chunks, numbers, columns):
    n_query, width = queries.shape
    half = jax.ShapeDtypeStruct((n_query // 2, width), jnp.bfloat16)
    return pl.pallas_call(
        functools.partial(last_kernel, numbers, columns),
        out_shape=(half, half) + project_shapes(n_query // 4, columns[1] - columns[0]),
        in_specs=[VMEM] * (5 + 2 * len(numbers)),
        out_specs=(VMEM,) * 4,
        scratch_shapes=[pltpu.VMEM(queries.shape, jnp.bfloat16)],
        compiler_params=LIMIT,
        cost_estimate=attend_cost(queries, numbers),
        name="attend_last",
    )(queries, weight, *state, *[x for pair in chunks for x in pair])


def project_shapes(rows, count, sends=1):
    send = jax.ShapeDtypeStruct((rows, count // sends), jnp.bfloat16)
    return (jax.ShapeDtypeStruct((rows, count), jnp.float32),) + (send,) * sends


def project_columns(rows, weight, mine, sends, start, end):
    share = rows.shape[0] // 2
    width = sends[0].shape[1]
    for i, send in enumerate(sends):
        for at in range(0, width, 768):
            stop = min(at + 768, width)
            columns = weight[:, start + i * width + at : start + i * width + stop]
            product = jnp.dot(rows[...], columns, preferred_element_type=jnp.float32)
            mine[:, i * width + at : i * width + stop] = product[:share]
            send[:, at:stop] = product[share:].astype(send.dtype)


def project_kernel(columns, rows, weight, mine, *sends):
    project_columns(rows, weight, mine, sends, *columns)


def project(rows, weight, columns, sends=1):
    count = columns[1] - columns[0]
    return pl.pallas_call(
        functools.partial(project_kernel, columns),
        out_shape=project_shapes(rows.shape[0] // 2, count, sends),
        in_specs=[VMEM, VMEM],
        out_specs=(VMEM,) * (1 + sends),
        compiler_params=LIMIT,
        cost_estimate=pl.CostEstimate(
            flops=2 * rows.shape[0] * rows.shape[1] * count, bytes_accessed=0, transcendentals=0
        ),
        name="project",
    )(rows, weight)


def add_kernel(mine, theirs, *outs):
    at = 0
    for out in outs:
        columns = slice(at, at + out.shape[1])
        at += out.shape[1]
        out[...] = (mine[:, columns] + theirs[:, columns].astype(jnp.float32)).astype(out.dtype)


def add_up(mine, theirs, widths):
    return pl.pallas_call(
        add_kernel,
        out_shape=[jax.ShapeDtypeStruct((mine.shape[0], width), theirs.dtype) for width in widths],
        in_specs=[VMEM, VMEM],
        out_specs=[VMEM] * len(widths),
        compiler_params=LIMIT,
        cost_estimate=pl.CostEstimate(flops=theirs.size, bytes_accessed=0, transcendentals=0),
        name="add_up",
    )(mine, theirs)


def combine_kernel(cuts, counts, mine, *refs):
    across, refs = refs[: sum(counts)], refs[sum(counts) :]
    beside, (out, *totals, sems) = refs[: len(refs) - len(cuts) - 2], refs[len(refs) - len(cuts) - 2 :]
    copies = []
    for i, (at, total) in enumerate(zip(cuts, totals)):
        options = across[sum(counts[:i]) : sum(counts[: i + 1])]
        width = options[0].shape[1]
        left = 0
        for part in beside:
            low, high = max(left, at), min(left + part.shape[1], at + width)
            if low < high:
                piece = mine[:, low:high] + part[:, low - left : high - left].astype(jnp.float32)
                there = options[0][:, low - at : high - at].astype(jnp.float32)
                if len(options) == 2:
                    position = lax.axis_index("ctx")
                    late = functools.reduce(jnp.logical_or, [position == i for i in LATE])
                    relayed = options[1][:, low - at : high - at].astype(jnp.float32)
                    there = jnp.where(late, relayed, there)
                total[:, low - at : high - at] = (piece + there).astype(total.dtype)
            left += part.shape[1]
        copies.append(pltpu.make_async_copy(total, out.at[:, at : at + width], sems.at[i]))
        copies[-1].start()
    for copy in copies:
        copy.wait()


def combine(mine, beside, across, cuts, out=None):
    outs = [] if out is None else [out]
    across = [x if isinstance(x, tuple) else (x,) for x in across]
    arrays = [x for options in across for x in options]
    counts = [len(options) for options in across]
    inputs = 1 + len(arrays) + len(beside)

    def kernel(*refs):
        combine_kernel(cuts, counts, *refs[:inputs], *refs[inputs + len(outs) :])

    return pl.pallas_call(
        kernel,
        out_shape=jax.ShapeDtypeStruct(mine.shape, jnp.bfloat16),
        in_specs=[VMEM] * inputs + [HBM] * len(outs),
        out_specs=HBM,
        scratch_shapes=[pltpu.VMEM(options[0].shape, jnp.bfloat16) for options in across]
        + [pltpu.SemaphoreType.DMA((len(cuts),))],
        input_output_aliases={inputs: 0} if outs else {},
        compiler_params=LIMIT,
        name="combine",
    )(mine, *arrays, *beside, *outs)


def from_behind(block, axis, distance):
    devices = range(lax.axis_size(axis))
    route = [(i - distance, i) for i in devices if i - distance in devices]
    return lax.ppermute(block, axis, route)


def token_docs(doc_ids, start, count):
    blocks = (start + jnp.arange(count, dtype=jnp.int32)) // BLOCK
    table = blocks[:, None] == jnp.arange(doc_ids.shape[0], dtype=jnp.int32)[None, :]
    return jnp.sum(jnp.where(table, doc_ids[None, :], 0), axis=1)


def attend(carry, queries, q_docs, q_start, k_piece, v_piece, k_docs, k_start):
    peak, totals, accum = carry
    n_query = queries.shape[0]
    n_key = k_piece.shape[0]
    kv_heads = k_piece.shape[1] // HEAD_SIZE
    query_group = queries.shape[1] // k_piece.shape[1]
    q_heads = queries.reshape(n_query, kv_heads, query_group, HEAD_SIZE)
    k_heads = k_piece.reshape(n_key, kv_heads, HEAD_SIZE)
    v_heads = v_piece.reshape(n_key, kv_heads, HEAD_SIZE)
    scores = (
        jnp.einsum("qkgd,skd->kgqs", q_heads, k_heads, preferred_element_type=jnp.float32) * SCALE
    )
    q_pos = q_start + jnp.arange(n_query, dtype=jnp.int32)
    k_pos = k_start + jnp.arange(n_key, dtype=jnp.int32)
    allowed = (q_docs[:, None] == k_docs[None, :]) & (q_pos[:, None] >= k_pos[None, :])
    scores = jnp.where(allowed, scores, NEG)
    new_peak = jnp.maximum(peak, jnp.max(scores, axis=-1))
    shrink = jnp.exp(peak - new_peak)
    weights = jnp.exp(scores - new_peak[..., None])
    totals = totals * shrink + jnp.sum(weights, axis=-1)
    rounded = weights.astype(jnp.bfloat16)
    added = jnp.einsum("kgqs,skd->kgqd", rounded, v_heads, preferred_element_type=jnp.float32)
    accum = accum * shrink[..., None] + added
    return (new_peak, totals, accum)


def absorb_block(carry, queries, q_docs, q_start, k_piece, v_piece, k_start, doc_ids, flag):
    n_key = k_piece.shape[0]
    k_docs = token_docs(doc_ids, k_start, n_key)
    fresh = attend(carry, queries, q_docs, q_start, k_piece, v_piece, k_docs, k_start)
    return jax.tree.map(lambda new, old: jnp.where(flag, new, old), fresh, carry)


def ring_attention(queries, keys, values, doc_ids, n_ctx, position):
    n_query = queries.shape[0]
    q_start = position * n_query
    q_docs = token_docs(doc_ids, q_start, n_query)
    kv_heads = keys.shape[1] // HEAD_SIZE
    query_group = queries.shape[1] // keys.shape[1]
    carry = (
        jnp.full((kv_heads, query_group, n_query), NEG, jnp.float32),
        jnp.zeros((kv_heads, query_group, n_query), jnp.float32),
        jnp.zeros((kv_heads, query_group, n_query, HEAD_SIZE), jnp.float32),
    )
    always = jnp.array(True)
    carry = absorb_block(carry, queries, q_docs, q_start, keys, values, q_start, doc_ids, always)

    def turn_one(step, state):
        inner_state, moving = state
        moving = from_behind(moving, "ctx", 1)
        start = ((position - step) % n_ctx) * n_query
        inner_state = absorb_block(
            inner_state, queries, q_docs, q_start, moving[0], moving[1], start, doc_ids, always
        )
        return (inner_state, moving)

    _, totals, accum = lax.fori_loop(1, n_ctx, turn_one, (carry, jnp.stack((keys, values))))[0]
    result = accum / totals[..., None]
    return jnp.transpose(result, (2, 0, 1, 3)).reshape(queries.shape).astype(jnp.bfloat16)


def part_rows(attended, place):
    share = attended.shape[0] // 4
    rows = [lax.dynamic_slice_in_dim(attended, (place ^ flip) * share, share, 0) for flip in (2, 3, 0, 1)]
    return jnp.concatenate(rows[:2], axis=0), jnp.concatenate(rows[2:], axis=0)


def per_device(queries, keys, values, doc_ids, out_weight):
    n_ctx = lax.axis_size("ctx")
    heads = lax.axis_size("head")
    position = lax.axis_index("ctx")
    place = lax.axis_index("head")
    other_core = [(i, i ^ 1) for i in range(heads)]
    other_chip = [(i, i ^ 2) for i in range(heads)]
    columns = out_weight.shape[1]
    relay = columns // 10 // BLOCK * BLOCK
    early_columns = columns * 3 // 7 // BLOCK * BLOCK - BLOCK
    cuts = [0, early_columns - relay, early_columns]

    if n_ctx == 8:
        by_two = [move(x, BY_TWO) for x in (keys, values)]
        beside = [move(x, BESIDE) for x in (keys, values)]
        split = columns // 3 // BLOCK * BLOCK
        *state, fetched, open_beside, part = attend_first(
            doc_ids, queries, keys, values, out_weight, split
        )
        by_four = [move(after(x, state[0]), AGAIN) for x in by_two]
        swap_two = [
            move(after(after(by_two[0], beside[0]), state[0]), ACROSS),
            move(after(by_two[1], beside[1]), ACROSS),
        ]
        swap_four = [move(after(swap_two[0], by_four[0]), AGAIN), move(by_four[1], LAST)]
        chunks = [beside, by_two, by_four]
        *state, weight = attend_next(
            fetched, open_beside, out_weight, part, split, state, chunks, (1, 2, 3)
        )
        state = attend_middle(fetched, state, [swap_two], (4,))
        chunks = [swap_four]
        far, near, mine, send = attend_last(fetched, weight, state, chunks, (5,), (0, cuts[2]))
    else:
        weight = out_weight
        attended = ring_attention(queries, keys, values, doc_ids, n_ctx, position)
        far, near = part_rows(attended, place)
        mine, send = project(far, weight, (0, cuts[2]))
    theirs = hop(send, "head", other_core)
    later_mine, later_send = project(far, weight, (cuts[2], columns))
    first_sum, relay_sum = add_up(mine, theirs, [cuts[1], cuts[2] - cuts[1]])
    first_part = hop(first_sum, "head", other_chip)
    later_theirs = hop(after(later_send, relay_sum), "head", other_core)
    later_mine = after(later_mine, first_sum)
    (later_sum,) = add_up(later_mine, later_theirs, [columns - cuts[2]])
    later_part = hop(later_sum, "head", other_chip)
    mine, *sends = project(after(near, later_sum), weight, (0, columns), 2)
    theirs = [hop(send, "head", other_core) for send in sends]
    if n_ctx == 8:
        direct = move(relay_sum, (), [i for i in range(n_ctx) if i not in LATE])
        arrived = move(after(relay_sum, mine), RELAY)
        relay_part = (direct, move(move(after(arrived, first_part), (), [ring[1] for ring in RELAY]), RELAY))
    else:
        relay_part = hop(relay_sum, "head", other_chip)
    out = combine(mine, theirs, [first_part], [0])
    return combine(mine, theirs, [later_part, relay_part], [cuts[2], cuts[1]], out)


def solution(mesh):
    placed = (P("ctx", "head"), P("ctx", "head"), P("ctx", "head"), P(), P("head", None))
    return jax.shard_map(
        per_device, mesh=mesh, in_specs=placed, out_specs=P(("ctx", "head"), None), check_vma=False
    )
```

```python
import functools

import jax
import jax.numpy as jnp
from jax import lax
from jax.experimental import pallas as pl
from jax.experimental.pallas import tpu as pltpu
from jax.sharding import PartitionSpec as P

HEAD_SIZE = 128
BLOCK = 128
SCALE = 168.0 ** (-0.5)
LOG2E = 1.4426950408889634
NEG = -1e30
VMEM = pl.BlockSpec(memory_space=pltpu.VMEM)
SMEM = pl.BlockSpec(memory_space=pltpu.SMEM)
HBM = pl.BlockSpec(memory_space=pltpu.HBM)
LIMIT = pltpu.CompilerParams(vmem_limit_bytes=32 * 1024 * 1024)


def hop(block, axis, pairs):
    return lax.ppermute(block, axis, pairs)


def in_place(number, position, n_ctx):
    away = {2: 2, 3: 4, 4: 2, 5: 4}[number]
    return (position < n_ctx * 3 // 4) & (position >= away)


BESIDE = ((0, 1), (2, 3), (4, 5), (6, 7))
BY_TWO = ((0, 2, 4), (1, 3, 5))
AGAIN = ((2, 4), (3, 5))
ACROSS = ((2, 3), (4, 5))
LAST = ((4, 5),)
LATE = (4, 5)
RELAY = ((4, 6), (5, 7))


def move(block, rings, crossing=()):
    n_ctx, heads = lax.axis_size("ctx"), lax.axis_size("head")
    target = {ring[i]: ring[(i + 1) % len(ring)] for ring in rings for i in range(len(ring))}
    pairs = []
    for i in range(n_ctx):
        flip = 0 if i in target else 2 if i in crossing else 1
        pairs += [(i * heads + h, target.get(i, i) * heads + (h ^ flip)) for h in range(heads)]
    return lax.ppermute(block, ("ctx", "head"), pairs)


def after(x, event):
    return lax.optimization_barrier((x, event))[0]


def score_blocks(doors, q, a, h, chunks, numbers):
    position = lax.axis_index("ctx")
    n_ctx = lax.axis_size("ctx")
    n_query = chunks[0][0].shape[0]
    scores = []
    for (keys, _), c in zip(chunks, numbers):
        count = (a + 1) * BLOCK if c == 0 else n_query
        k = keys[:count, h * HEAD_SIZE : (h + 1) * HEAD_SIZE]
        s = lax.dot_general(q, k, (((1,), (1,)), ((), ())), preferred_element_type=jnp.float32)
        for b in range(count // BLOCK):
            part = s[:, b * BLOCK : (b + 1) * BLOCK]
            if c == 0 and b == a:
                row = lax.broadcasted_iota(jnp.int32, part.shape, 0) % BLOCK
                col = lax.broadcasted_iota(jnp.int32, part.shape, 1)
                part = jnp.where(row >= col, part, NEG)
            elif c < 2:
                part = part + doors(c, a, b)
            else:
                part = part + jnp.where(in_place(c, position, n_ctx), 0.0, NEG)
            scores.append(part)
    return scores


def weigh(scores, peak, factor, a, h, chunks, numbers):
    n_query = chunks[0][0].shape[0]
    total = added = None
    scores = list(scores)
    for (_, values), c in zip(chunks, numbers):
        count = (a + 1) * BLOCK if c == 0 else n_query
        parts = []
        for b in range(count // BLOCK):
            w = jnp.exp2(scores.pop(0) * factor - peak)
            total = w if total is None else total + w
            parts.append(w.astype(jnp.bfloat16))
        w = jnp.concatenate(parts, axis=1) if len(parts) > 1 else parts[0]
        v = values[:count, h * HEAD_SIZE : (h + 1) * HEAD_SIZE]
        term = jnp.dot(w, v, preferred_element_type=jnp.float32)
        added = term if added is None else added + term
    return total, added


def head_slices(queries, keys, h):
    group = queries.shape[1] // keys.shape[1]
    return [slice((h * group + g) * HEAD_SIZE, (h * group + g + 1) * HEAD_SIZE) for g in range(group)]


def absorb(numbers, doors, queries, chunks, before, after):
    n_query = queries.shape[0]
    factor = SCALE * LOG2E
    parts = []
    for a in range(n_query // BLOCK):
        for h in range(chunks[0][0].shape[1] // HEAD_SIZE):
            heads = head_slices(queries, chunks[0][0], h)
            size = len(heads) * BLOCK
            parts.append((a, h, heads, slice(len(parts) * size, (len(parts) + 1) * size)))
    scores = []
    for a, h, heads, _ in parts:
        q = jnp.concatenate([queries[a * BLOCK : (a + 1) * BLOCK, s] for s in heads], axis=0)
        scores.append(score_blocks(doors, q, a, h, chunks, numbers))
    peaks = [functools.reduce(jnp.maximum, s) for s in scores]
    peaks = [jnp.max(peak, axis=1, keepdims=True) * factor for peak in peaks]
    shrinks = None
    if before is None:
        peaks = [jnp.broadcast_to(peak, (peak.shape[0], HEAD_SIZE)) for peak in peaks]
    else:
        lasts = [before[0][rows, :] for _, _, _, rows in parts]
        peaks = [jnp.maximum(last, peak) for last, peak in zip(lasts, peaks)]
        shrinks = [jnp.exp2(last - peak) for last, peak in zip(lasts, peaks)]
    sums = [
        weigh(s, peak, factor, a, h, chunks, numbers)
        for s, peak, (a, h, _, _) in zip(scores, peaks, parts)
    ]
    for i, (a, h, heads, rows) in enumerate(parts):
        total, added = sums[i]
        if before is not None:
            total = total + before[1][rows, :] * shrinks[i]
            added = added + before[2][rows, :] * shrinks[i]
        sums[i] = (total, added)
    after(parts, peaks, sums)


def store_state(state):
    def after(parts, peaks, sums):
        for (_, _, _, rows), peak, (total, added) in zip(parts, peaks, sums):
            for ref, part in zip(state, (peak, total, added)):
                ref[rows, :] = part

    return after


def pairs_of(refs):
    return list(zip(refs[0::2], refs[1::2]))


def first_kernel(split, docs_in, queries_in, keys_in, values_in, weight_in, *refs):
    *state, queries, open_beside, weight, docs, keys, values, sems = refs
    places = (
        (docs_in, docs),
        (queries_in, queries),
        (keys_in, keys),
        (values_in, values),
        (weight_in.at[:, :split], weight.at[:, :split]),
    )
    fetches = [pltpu.make_async_copy(a, b, sems.at[i]) for i, (a, b) in enumerate(places)]
    for fetch in fetches:
        fetch.start()
    for fetch in fetches[:4]:
        fetch.wait()
    position = lax.axis_index("ctx")
    q_blocks = queries.shape[0] // BLOCK

    def doors(number, a, b):
        source = position if number == 0 else jnp.maximum(position - 1, 0)
        seen = docs[source * q_blocks + b] == docs[position * q_blocks + a]
        if number == 1:
            seen = seen & (position % 2 == 1)
        return jnp.where(seen, 0.0, NEG)

    for a in range(q_blocks):
        for b in range(q_blocks):
            part = open_beside.at[a * 8 : (a + 1) * 8, b * BLOCK : (b + 1) * BLOCK]
            part[...] = jnp.full(part.shape, doors(1, a, b), jnp.float32)
    absorb((0,), doors, queries, [(keys, values)], None, store_state(state))
    fetches[4].wait()


def next_kernel(numbers, split, queries, open_beside, weight_in, _, *refs):
    *refs, weight, sem = refs
    fetch = pltpu.make_async_copy(weight_in.at[:, split:], weight.at[:, split:], sem)
    fetch.start()
    pairs = 2 * len(numbers)

    def doors(number, a, b):
        return open_beside[a * 8 : a * 8 + 1, b * BLOCK : (b + 1) * BLOCK]

    absorb(numbers, doors, queries, pairs_of(refs[3 : 3 + pairs]), refs[:3], store_state(refs[3 + pairs :]))
    fetch.wait()


def attend_cost(queries, numbers, fetched=0):
    n_query, width = queries.shape
    count = len(numbers) * n_query
    return pl.CostEstimate(
        flops=4 * n_query * width * count,
        bytes_accessed=fetched,
        transcendentals=n_query * count * width // HEAD_SIZE,
    )


def state_shapes(queries):
    rows = queries.size // HEAD_SIZE
    return (pltpu.VMEM((rows, HEAD_SIZE), jnp.float32),) * 3


def attend_first(docs, queries, keys, values, weight, split):
    n_query = queries.shape[0]
    return pl.pallas_call(
        functools.partial(first_kernel, split),
        out_shape=state_shapes(queries)
        + (
            pltpu.VMEM(queries.shape, queries.dtype),
            pltpu.VMEM((8 * n_query // BLOCK, n_query), jnp.float32),
            pltpu.VMEM(weight.shape, weight.dtype),
        ),
        in_specs=[HBM] * 5,
        out_specs=(VMEM,) * 6,
        scratch_shapes=[
            pltpu.SMEM(docs.shape, docs.dtype),
            pltpu.VMEM(keys.shape, keys.dtype),
            pltpu.VMEM(values.shape, values.dtype),
            pltpu.SemaphoreType.DMA((5,)),
        ],
        compiler_params=LIMIT,
        cost_estimate=attend_cost(queries, (0,)),
        name="attend_first",
    )(*[pltpu.with_memory_space_constraint(x, pltpu.HBM) for x in (docs, queries, keys, values, weight)])


def attend_next(queries, open_beside, weight, part, split, state, chunks, numbers):
    return pl.pallas_call(
        functools.partial(next_kernel, numbers, split),
        out_shape=state_shapes(queries) + (pltpu.VMEM(weight.shape, weight.dtype),),
        in_specs=[VMEM, VMEM, HBM] + [VMEM] * (4 + 2 * len(chunks)),
        out_specs=(VMEM,) * 4,
        input_output_aliases={3: 3},
        scratch_shapes=[pltpu.SemaphoreType.DMA],
        compiler_params=LIMIT,
        cost_estimate=attend_cost(queries, numbers, 2 * weight.size),
        name="attend_next",
    )(
        queries,
        open_beside,
        pltpu.with_memory_space_constraint(weight, pltpu.HBM),
        part,
        *state,
        *[x for pair in chunks for x in pair],
    )


def middle_kernel(numbers, queries, *refs):
    pairs = 2 * len(numbers)
    absorb(numbers, None, queries, pairs_of(refs[3 : 3 + pairs]), refs[:3], store_state(refs[3 + pairs :]))


def attend_middle(queries, state, chunks, numbers):
    return pl.pallas_call(
        functools.partial(middle_kernel, numbers),
        out_shape=state_shapes(queries),
        in_specs=[VMEM] * (4 + 2 * len(chunks)),
        out_specs=(VMEM,) * 3,
        compiler_params=LIMIT,
        cost_estimate=attend_cost(queries, numbers),
        name="attend_middle",
    )(queries, *state, *[x for pair in chunks for x in pair])


def last_kernel(numbers, columns, queries, weight, *refs):
    pairs = 2 * len(numbers)
    chunks = pairs_of(refs[3 : 3 + pairs])
    far, near, mine, send, attended = refs[3 + pairs :]

    def after(parts, peaks, sums):
        inverses = [1.0 / jnp.sum(total, axis=1, keepdims=True) for total, _ in sums]
        for (a, _, heads, _), inverse, (_, added) in zip(parts, inverses, sums):
            result = (added * inverse).astype(jnp.bfloat16)
            for g, head in enumerate(heads):
                attended[a * BLOCK : (a + 1) * BLOCK, head] = result[g * BLOCK : (g + 1) * BLOCK]

    absorb(numbers, None, queries, chunks, refs[:3], after)
    place = lax.axis_index("head")
    share = queries.shape[0] // 4
    for half, owners in ((far, (place ^ 2, place ^ 3)), (near, (place, place ^ 1))):
        for i, owner in enumerate(owners):
            source = pl.ds(pl.multiple_of(owner * share, share), share)
            half[i * share : (i + 1) * share, :] = attended[source, :]
    project_columns(far, weight, mine, (send,), *columns)


def attend_last(queries, weight, state, chunks, numbers, columns):
    n_query, width = queries.shape
    half = jax.ShapeDtypeStruct((n_query // 2, width), jnp.bfloat16)
    return pl.pallas_call(
        functools.partial(last_kernel, numbers, columns),
        out_shape=(half, half) + project_shapes(n_query // 4, columns[1] - columns[0]),
        in_specs=[VMEM] * (5 + 2 * len(numbers)),
        out_specs=(VMEM,) * 4,
        scratch_shapes=[pltpu.VMEM(queries.shape, jnp.bfloat16)],
        compiler_params=LIMIT,
        cost_estimate=attend_cost(queries, numbers),
        name="attend_last",
    )(queries, weight, *state, *[x for pair in chunks for x in pair])


def project_shapes(rows, count, sends=1):
    send = jax.ShapeDtypeStruct((rows, count // sends), jnp.bfloat16)
    return (jax.ShapeDtypeStruct((rows, count), jnp.float32),) + (send,) * sends


def project_columns(rows, weight, mine, sends, start, end):
    share = rows.shape[0] // 2
    width = sends[0].shape[1]
    for i, send in enumerate(sends):
        for at in range(0, width, 768):
            stop = min(at + 768, width)
            columns = weight[:, start + i * width + at : start + i * width + stop]
            product = jnp.dot(rows[...], columns, preferred_element_type=jnp.float32)
            mine[:, i * width + at : i * width + stop] = product[:share]
            send[:, at:stop] = product[share:].astype(send.dtype)


def project_kernel(columns, rows, weight, mine, *sends):
    project_columns(rows, weight, mine, sends, *columns)


def project(rows, weight, columns, sends=1):
    count = columns[1] - columns[0]
    return pl.pallas_call(
        functools.partial(project_kernel, columns),
        out_shape=project_shapes(rows.shape[0] // 2, count, sends),
        in_specs=[VMEM, VMEM],
        out_specs=(VMEM,) * (1 + sends),
        compiler_params=LIMIT,
        cost_estimate=pl.CostEstimate(
            flops=2 * rows.shape[0] * rows.shape[1] * count, bytes_accessed=0, transcendentals=0
        ),
        name="project",
    )(rows, weight)


def add_kernel(mine, theirs, *outs):
    at = 0
    for out in outs:
        columns = slice(at, at + out.shape[1])
        at += out.shape[1]
        out[...] = (mine[:, columns] + theirs[:, columns].astype(jnp.float32)).astype(out.dtype)


def add_up(mine, theirs, widths):
    return pl.pallas_call(
        add_kernel,
        out_shape=[jax.ShapeDtypeStruct((mine.shape[0], width), theirs.dtype) for width in widths],
        in_specs=[VMEM, VMEM],
        out_specs=[VMEM] * len(widths),
        compiler_params=LIMIT,
        cost_estimate=pl.CostEstimate(flops=theirs.size, bytes_accessed=0, transcendentals=0),
        name="add_up",
    )(mine, theirs)


def combine_kernel(cuts, counts, mine, *refs):
    across, refs = refs[: sum(counts)], refs[sum(counts) :]
    beside, (out, *totals, sems) = refs[: len(refs) - len(cuts) - 2], refs[len(refs) - len(cuts) - 2 :]
    copies = []
    for i, (at, total) in enumerate(zip(cuts, totals)):
        options = across[sum(counts[:i]) : sum(counts[: i + 1])]
        width = options[0].shape[1]
        left = 0
        for part in beside:
            low, high = max(left, at), min(left + part.shape[1], at + width)
            if low < high:
                piece = mine[:, low:high] + part[:, low - left : high - left].astype(jnp.float32)
                there = options[0][:, low - at : high - at].astype(jnp.float32)
                if len(options) == 2:
                    position = lax.axis_index("ctx")
                    late = functools.reduce(jnp.logical_or, [position == i for i in LATE])
                    relayed = options[1][:, low - at : high - at].astype(jnp.float32)
                    there = jnp.where(late, relayed, there)
                total[:, low - at : high - at] = (piece + there).astype(total.dtype)
            left += part.shape[1]
        copies.append(pltpu.make_async_copy(total, out.at[:, at : at + width], sems.at[i]))
        copies[-1].start()
    for copy in copies:
        copy.wait()


def combine(mine, beside, across, cuts, out=None):
    outs = [] if out is None else [out]
    across = [x if isinstance(x, tuple) else (x,) for x in across]
    arrays = [x for options in across for x in options]
    counts = [len(options) for options in across]
    inputs = 1 + len(arrays) + len(beside)

    def kernel(*refs):
        combine_kernel(cuts, counts, *refs[:inputs], *refs[inputs + len(outs) :])

    return pl.pallas_call(
        kernel,
        out_shape=jax.ShapeDtypeStruct(mine.shape, jnp.bfloat16),
        in_specs=[VMEM] * inputs + [HBM] * len(outs),
        out_specs=HBM,
        scratch_shapes=[pltpu.VMEM(options[0].shape, jnp.bfloat16) for options in across]
        + [pltpu.SemaphoreType.DMA((len(cuts),))],
        input_output_aliases={inputs: 0} if outs else {},
        compiler_params=LIMIT,
        name="combine",
    )(mine, *arrays, *beside, *outs)


def from_behind(block, axis, distance):
    devices = range(lax.axis_size(axis))
    route = [(i - distance, i) for i in devices if i - distance in devices]
    return lax.ppermute(block, axis, route)


def token_docs(doc_ids, start, count):
    blocks = (start + jnp.arange(count, dtype=jnp.int32)) // BLOCK
    table = blocks[:, None] == jnp.arange(doc_ids.shape[0], dtype=jnp.int32)[None, :]
    return jnp.sum(jnp.where(table, doc_ids[None, :], 0), axis=1)


def attend(carry, queries, q_docs, q_start, k_piece, v_piece, k_docs, k_start):
    peak, totals, accum = carry
    n_query = queries.shape[0]
    n_key = k_piece.shape[0]
    kv_heads = k_piece.shape[1] // HEAD_SIZE
    query_group = queries.shape[1] // k_piece.shape[1]
    q_heads = queries.reshape(n_query, kv_heads, query_group, HEAD_SIZE)
    k_heads = k_piece.reshape(n_key, kv_heads, HEAD_SIZE)
    v_heads = v_piece.reshape(n_key, kv_heads, HEAD_SIZE)
    scores = (
        jnp.einsum("qkgd,skd->kgqs", q_heads, k_heads, preferred_element_type=jnp.float32) * SCALE
    )
    q_pos = q_start + jnp.arange(n_query, dtype=jnp.int32)
    k_pos = k_start + jnp.arange(n_key, dtype=jnp.int32)
    allowed = (q_docs[:, None] == k_docs[None, :]) & (q_pos[:, None] >= k_pos[None, :])
    scores = jnp.where(allowed, scores, NEG)
    new_peak = jnp.maximum(peak, jnp.max(scores, axis=-1))
    shrink = jnp.exp(peak - new_peak)
    weights = jnp.exp(scores - new_peak[..., None])
    totals = totals * shrink + jnp.sum(weights, axis=-1)
    rounded = weights.astype(jnp.bfloat16)
    added = jnp.einsum("kgqs,skd->kgqd", rounded, v_heads, preferred_element_type=jnp.float32)
    accum = accum * shrink[..., None] + added
    return (new_peak, totals, accum)


def absorb_block(carry, queries, q_docs, q_start, k_piece, v_piece, k_start, doc_ids, flag):
    n_key = k_piece.shape[0]
    k_docs = token_docs(doc_ids, k_start, n_key)
    fresh = attend(carry, queries, q_docs, q_start, k_piece, v_piece, k_docs, k_start)
    return jax.tree.map(lambda new, old: jnp.where(flag, new, old), fresh, carry)


def ring_attention(queries, keys, values, doc_ids, n_ctx, position):
    n_query = queries.shape[0]
    q_start = position * n_query
    q_docs = token_docs(doc_ids, q_start, n_query)
    kv_heads = keys.shape[1] // HEAD_SIZE
    query_group = queries.shape[1] // keys.shape[1]
    carry = (
        jnp.full((kv_heads, query_group, n_query), NEG, jnp.float32),
        jnp.zeros((kv_heads, query_group, n_query), jnp.float32),
        jnp.zeros((kv_heads, query_group, n_query, HEAD_SIZE), jnp.float32),
    )
    always = jnp.array(True)
    carry = absorb_block(carry, queries, q_docs, q_start, keys, values, q_start, doc_ids, always)

    def turn_one(step, state):
        inner_state, moving = state
        moving = from_behind(moving, "ctx", 1)
        start = ((position - step) % n_ctx) * n_query
        inner_state = absorb_block(
            inner_state, queries, q_docs, q_start, moving[0], moving[1], start, doc_ids, always
        )
        return (inner_state, moving)

    _, totals, accum = lax.fori_loop(1, n_ctx, turn_one, (carry, jnp.stack((keys, values))))[0]
    result = accum / totals[..., None]
    return jnp.transpose(result, (2, 0, 1, 3)).reshape(queries.shape).astype(jnp.bfloat16)


def part_rows(attended, place):
    share = attended.shape[0] // 4
    rows = [lax.dynamic_slice_in_dim(attended, (place ^ flip) * share, share, 0) for flip in (2, 3, 0, 1)]
    return jnp.concatenate(rows[:2], axis=0), jnp.concatenate(rows[2:], axis=0)


def per_device(queries, keys, values, doc_ids, out_weight):
    n_ctx = lax.axis_size("ctx")
    heads = lax.axis_size("head")
    position = lax.axis_index("ctx")
    place = lax.axis_index("head")
    other_core = [(i, i ^ 1) for i in range(heads)]
    other_chip = [(i, i ^ 2) for i in range(heads)]
    columns = out_weight.shape[1]
    relay = columns // 10 // BLOCK * BLOCK
    early_columns = columns * 3 // 7 // BLOCK * BLOCK - BLOCK
    cuts = [0, early_columns - relay, early_columns]

    if n_ctx == 8:
        by_two = [move(x, BY_TWO) for x in (keys, values)]
        beside = [move(x, BESIDE) for x in (keys, values)]
        split = columns // 3 // BLOCK * BLOCK
        *state, fetched, open_beside, part = attend_first(
            doc_ids, queries, keys, values, out_weight, split
        )
        by_four = [move(after(x, state[0]), AGAIN) for x in by_two]
        swap_two = [
            move(after(after(by_two[0], beside[0]), state[0]), ACROSS),
            move(after(by_two[1], beside[1]), ACROSS),
        ]
        swap_four = [move(after(swap_two[0], by_four[0]), AGAIN), move(by_four[1], LAST)]
        chunks = [beside, by_two, by_four]
        *state, weight = attend_next(
            fetched, open_beside, out_weight, part, split, state, chunks, (1, 2, 3)
        )
        state = attend_middle(fetched, state, [swap_two], (4,))
        chunks = [swap_four]
        far, near, mine, send = attend_last(fetched, weight, state, chunks, (5,), (0, cuts[1]))
    else:
        weight = out_weight
        attended = ring_attention(queries, keys, values, doc_ids, n_ctx, position)
        far, near = part_rows(attended, place)
        mine, send = project(far, weight, (0, cuts[1]))
    theirs = hop(send, "head", other_core)
    later_mine, later_send = project(far, weight, (cuts[1], columns))
    (first_sum,) = add_up(mine, theirs, [cuts[1]])
    first_part = hop(first_sum, "head", other_chip)
    later_theirs = hop(after(later_send, first_sum), "head", other_core)
    later_mine = after(later_mine, first_sum)
    relay_sum, later_sum = add_up(later_mine, later_theirs, [cuts[2] - cuts[1], columns - cuts[2]])
    later_part = hop(later_sum, "head", other_chip)
    mine, *sends = project(after(near, later_sum), weight, (0, columns), 2)
    theirs = [hop(send, "head", other_core) for send in sends]
    if n_ctx == 8:
        direct = move(relay_sum, (), [i for i in range(n_ctx) if i not in LATE])
        arrived = move(after(relay_sum, mine), RELAY)
        relay_part = (direct, move(move(after(arrived, first_part), (), [ring[1] for ring in RELAY]), RELAY))
    else:
        relay_part = hop(relay_sum, "head", other_chip)
    out = combine(mine, theirs, [first_part], [0])
    return combine(mine, theirs, [later_part, relay_part], [cuts[2], cuts[1]], out)


def solution(mesh):
    placed = (P("ctx", "head"), P("ctx", "head"), P("ctx", "head"), P(), P("head", None))
    return jax.shard_map(
        per_device, mesh=mesh, in_specs=placed, out_specs=P(("ctx", "head"), None), check_vma=False
    )
```

```python
import functools

import jax
import jax.numpy as jnp
from jax import lax
from jax.experimental import pallas as pl
from jax.experimental.pallas import tpu as pltpu
from jax.sharding import PartitionSpec as P

HEAD_SIZE = 128
BLOCK = 128
SCALE = 168.0 ** (-0.5)
LOG2E = 1.4426950408889634
NEG = -1e30
VMEM = pl.BlockSpec(memory_space=pltpu.VMEM)
SMEM = pl.BlockSpec(memory_space=pltpu.SMEM)
HBM = pl.BlockSpec(memory_space=pltpu.HBM)
LIMIT = pltpu.CompilerParams(vmem_limit_bytes=32 * 1024 * 1024)


def hop(block, axis, pairs):
    return lax.ppermute(block, axis, pairs)


def in_place(number, position, n_ctx):
    away = {2: 2, 3: 4, 4: 2, 5: 4}[number]
    return (position < n_ctx * 3 // 4) & (position >= away)


BESIDE = ((0, 1), (2, 3), (4, 5), (6, 7))
BY_TWO = ((0, 2, 4), (1, 3, 5))
AGAIN = ((2, 4), (3, 5))
ACROSS = ((2, 3), (4, 5))
LAST = ((4, 5),)
LATE = (4, 5)
RELAY = ((4, 6), (5, 7))


def move(block, rings, crossing=()):
    n_ctx, heads = lax.axis_size("ctx"), lax.axis_size("head")
    target = {ring[i]: ring[(i + 1) % len(ring)] for ring in rings for i in range(len(ring))}
    pairs = []
    for i in range(n_ctx):
        flip = 0 if i in target else 2 if i in crossing else 1
        pairs += [(i * heads + h, target.get(i, i) * heads + (h ^ flip)) for h in range(heads)]
    return lax.ppermute(block, ("ctx", "head"), pairs)


def after(x, event):
    return lax.optimization_barrier((x, event))[0]


def score_blocks(doors, q, a, h, chunks, numbers):
    position = lax.axis_index("ctx")
    n_ctx = lax.axis_size("ctx")
    n_query = chunks[0][0].shape[0]
    scores = []
    for (keys, _), c in zip(chunks, numbers):
        count = (a + 1) * BLOCK if c == 0 else n_query
        k = keys[:count, h * HEAD_SIZE : (h + 1) * HEAD_SIZE]
        s = lax.dot_general(q, k, (((1,), (1,)), ((), ())), preferred_element_type=jnp.float32)
        for b in range(count // BLOCK):
            part = s[:, b * BLOCK : (b + 1) * BLOCK]
            if c == 0 and b == a:
                row = lax.broadcasted_iota(jnp.int32, part.shape, 0) % BLOCK
                col = lax.broadcasted_iota(jnp.int32, part.shape, 1)
                part = jnp.where(row >= col, part, NEG)
            elif c < 2:
                part = part + doors(c, a, b)
            else:
                part = part + jnp.where(in_place(c, position, n_ctx), 0.0, NEG)
            scores.append(part)
    return scores


def weigh(scores, peak, factor, a, h, chunks, numbers):
    n_query = chunks[0][0].shape[0]
    total = added = None
    scores = list(scores)
    for (_, values), c in zip(chunks, numbers):
        count = (a + 1) * BLOCK if c == 0 else n_query
        parts = []
        for b in range(count // BLOCK):
            w = jnp.exp2(scores.pop(0) * factor - peak)
            total = w if total is None else total + w
            parts.append(w.astype(jnp.bfloat16))
        w = jnp.concatenate(parts, axis=1) if len(parts) > 1 else parts[0]
        v = values[:count, h * HEAD_SIZE : (h + 1) * HEAD_SIZE]
        term = jnp.dot(w, v, preferred_element_type=jnp.float32)
        added = term if added is None else added + term
    return total, added


def head_slices(queries, keys, h):
    group = queries.shape[1] // keys.shape[1]
    return [slice((h * group + g) * HEAD_SIZE, (h * group + g + 1) * HEAD_SIZE) for g in range(group)]


def absorb(numbers, doors, queries, chunks, before, after):
    n_query = queries.shape[0]
    factor = SCALE * LOG2E
    parts = []
    for a in range(n_query // BLOCK):
        for h in range(chunks[0][0].shape[1] // HEAD_SIZE):
            heads = head_slices(queries, chunks[0][0], h)
            size = len(heads) * BLOCK
            parts.append((a, h, heads, slice(len(parts) * size, (len(parts) + 1) * size)))
    scores = []
    for a, h, heads, _ in parts:
        q = jnp.concatenate([queries[a * BLOCK : (a + 1) * BLOCK, s] for s in heads], axis=0)
        scores.append(score_blocks(doors, q, a, h, chunks, numbers))
    peaks = [functools.reduce(jnp.maximum, s) for s in scores]
    peaks = [jnp.max(peak, axis=1, keepdims=True) * factor for peak in peaks]
    shrinks = None
    if before is None:
        peaks = [jnp.broadcast_to(peak, (peak.shape[0], HEAD_SIZE)) for peak in peaks]
    else:
        lasts = [before[0][rows, :] for _, _, _, rows in parts]
        peaks = [jnp.maximum(last, peak) for last, peak in zip(lasts, peaks)]
        shrinks = [jnp.exp2(last - peak) for last, peak in zip(lasts, peaks)]
    sums = [
        weigh(s, peak, factor, a, h, chunks, numbers)
        for s, peak, (a, h, _, _) in zip(scores, peaks, parts)
    ]
    for i, (a, h, heads, rows) in enumerate(parts):
        total, added = sums[i]
        if before is not None:
            total = total + before[1][rows, :] * shrinks[i]
            added = added + before[2][rows, :] * shrinks[i]
        sums[i] = (total, added)
    after(parts, peaks, sums)


def store_state(state):
    def after(parts, peaks, sums):
        for (_, _, _, rows), peak, (total, added) in zip(parts, peaks, sums):
            for ref, part in zip(state, (peak, total, added)):
                ref[rows, :] = part

    return after


def pairs_of(refs):
    return list(zip(refs[0::2], refs[1::2]))


def first_kernel(split, docs_in, queries_in, keys_in, values_in, weight_in, *refs):
    *state, queries, open_beside, weight, docs, keys, values, sems = refs
    places = (
        (docs_in, docs),
        (queries_in, queries),
        (keys_in, keys),
        (values_in, values),
        (weight_in.at[:, :split], weight.at[:, :split]),
    )
    fetches = [pltpu.make_async_copy(a, b, sems.at[i]) for i, (a, b) in enumerate(places)]
    for fetch in fetches:
        fetch.start()
    for fetch in fetches[:4]:
        fetch.wait()
    position = lax.axis_index("ctx")
    q_blocks = queries.shape[0] // BLOCK

    def doors(number, a, b):
        source = position if number == 0 else jnp.maximum(position - 1, 0)
        seen = docs[source * q_blocks + b] == docs[position * q_blocks + a]
        if number == 1:
            seen = seen & (position % 2 == 1)
        return jnp.where(seen, 0.0, NEG)

    for a in range(q_blocks):
        for b in range(q_blocks):
            part = open_beside.at[a * 8 : (a + 1) * 8, b * BLOCK : (b + 1) * BLOCK]
            part[...] = jnp.full(part.shape, doors(1, a, b), jnp.float32)
    absorb((0,), doors, queries, [(keys, values)], None, store_state(state))
    fetches[4].wait()


def next_kernel(numbers, split, queries, open_beside, weight_in, _, *refs):
    *refs, weight, sem = refs
    fetch = pltpu.make_async_copy(weight_in.at[:, split:], weight.at[:, split:], sem)
    fetch.start()
    pairs = 2 * len(numbers)

    def doors(number, a, b):
        return open_beside[a * 8 : a * 8 + 1, b * BLOCK : (b + 1) * BLOCK]

    absorb(numbers, doors, queries, pairs_of(refs[3 : 3 + pairs]), refs[:3], store_state(refs[3 + pairs :]))
    fetch.wait()


def attend_cost(queries, numbers, fetched=0):
    n_query, width = queries.shape
    count = len(numbers) * n_query
    return pl.CostEstimate(
        flops=4 * n_query * width * count,
        bytes_accessed=fetched,
        transcendentals=n_query * count * width // HEAD_SIZE,
    )


def state_shapes(queries):
    rows = queries.size // HEAD_SIZE
    return (pltpu.VMEM((rows, HEAD_SIZE), jnp.float32),) * 3


def attend_first(docs, queries, keys, values, weight, split):
    n_query = queries.shape[0]
    return pl.pallas_call(
        functools.partial(first_kernel, split),
        out_shape=state_shapes(queries)
        + (
            pltpu.VMEM(queries.shape, queries.dtype),
            pltpu.VMEM((8 * n_query // BLOCK, n_query), jnp.float32),
            pltpu.VMEM(weight.shape, weight.dtype),
        ),
        in_specs=[HBM] * 5,
        out_specs=(VMEM,) * 6,
        scratch_shapes=[
            pltpu.SMEM(docs.shape, docs.dtype),
            pltpu.VMEM(keys.shape, keys.dtype),
            pltpu.VMEM(values.shape, values.dtype),
            pltpu.SemaphoreType.DMA((5,)),
        ],
        compiler_params=LIMIT,
        cost_estimate=attend_cost(queries, (0,)),
        name="attend_first",
    )(*[pltpu.with_memory_space_constraint(x, pltpu.HBM) for x in (docs, queries, keys, values, weight)])


def attend_next(queries, open_beside, weight, part, split, state, chunks, numbers):
    return pl.pallas_call(
        functools.partial(next_kernel, numbers, split),
        out_shape=state_shapes(queries) + (pltpu.VMEM(weight.shape, weight.dtype),),
        in_specs=[VMEM, VMEM, HBM] + [VMEM] * (4 + 2 * len(chunks)),
        out_specs=(VMEM,) * 4,
        input_output_aliases={3: 3},
        scratch_shapes=[pltpu.SemaphoreType.DMA],
        compiler_params=LIMIT,
        cost_estimate=attend_cost(queries, numbers, 2 * weight.size),
        name="attend_next",
    )(
        queries,
        open_beside,
        pltpu.with_memory_space_constraint(weight, pltpu.HBM),
        part,
        *state,
        *[x for pair in chunks for x in pair],
    )


def middle_kernel(numbers, queries, *refs):
    pairs = 2 * len(numbers)
    absorb(numbers, None, queries, pairs_of(refs[3 : 3 + pairs]), refs[:3], store_state(refs[3 + pairs :]))


def attend_middle(queries, state, chunks, numbers):
    return pl.pallas_call(
        functools.partial(middle_kernel, numbers),
        out_shape=state_shapes(queries),
        in_specs=[VMEM] * (4 + 2 * len(chunks)),
        out_specs=(VMEM,) * 3,
        compiler_params=LIMIT,
        cost_estimate=attend_cost(queries, numbers),
        name="attend_middle",
    )(queries, *state, *[x for pair in chunks for x in pair])


def last_kernel(numbers, columns, queries, weight, *refs):
    pairs = 2 * len(numbers)
    chunks = pairs_of(refs[3 : 3 + pairs])
    far, near, mine, send, attended = refs[3 + pairs :]

    def after(parts, peaks, sums):
        inverses = [1.0 / jnp.sum(total, axis=1, keepdims=True) for total, _ in sums]
        for (a, _, heads, _), inverse, (_, added) in zip(parts, inverses, sums):
            result = (added * inverse).astype(jnp.bfloat16)
            for g, head in enumerate(heads):
                attended[a * BLOCK : (a + 1) * BLOCK, head] = result[g * BLOCK : (g + 1) * BLOCK]

    absorb(numbers, None, queries, chunks, refs[:3], after)
    place = lax.axis_index("head")
    share = queries.shape[0] // 4
    for half, owners in ((far, (place ^ 2, place ^ 3)), (near, (place, place ^ 1))):
        for i, owner in enumerate(owners):
            source = pl.ds(pl.multiple_of(owner * share, share), share)
            half[i * share : (i + 1) * share, :] = attended[source, :]
    project_columns(far, weight, mine, (send,), *columns)


def attend_last(queries, weight, state, chunks, numbers, columns):
    n_query, width = queries.shape
    half = jax.ShapeDtypeStruct((n_query // 2, width), jnp.bfloat16)
    return pl.pallas_call(
        functools.partial(last_kernel, numbers, columns),
        out_shape=(half, half) + project_shapes(n_query // 4, columns[1] - columns[0]),
        in_specs=[VMEM] * (5 + 2 * len(numbers)),
        out_specs=(VMEM,) * 4,
        scratch_shapes=[pltpu.VMEM(queries.shape, jnp.bfloat16)],
        compiler_params=LIMIT,
        cost_estimate=attend_cost(queries, numbers),
        name="attend_last",
    )(queries, weight, *state, *[x for pair in chunks for x in pair])


def project_shapes(rows, count, sends=1):
    send = jax.ShapeDtypeStruct((rows, count // sends), jnp.bfloat16)
    return (jax.ShapeDtypeStruct((rows, count), jnp.float32),) + (send,) * sends


def project_columns(rows, weight, mine, sends, start, end):
    share = rows.shape[0] // 2
    width = sends[0].shape[1]
    for i, send in enumerate(sends):
        for at in range(0, width, 768):
            stop = min(at + 768, width)
            columns = weight[:, start + i * width + at : start + i * width + stop]
            product = jnp.dot(rows[...], columns, preferred_element_type=jnp.float32)
            mine[:, i * width + at : i * width + stop] = product[:share]
            send[:, at:stop] = product[share:].astype(send.dtype)


def project_kernel(columns, rows, weight, mine, *sends):
    project_columns(rows, weight, mine, sends, *columns)


def project(rows, weight, columns, sends=1):
    count = columns[1] - columns[0]
    return pl.pallas_call(
        functools.partial(project_kernel, columns),
        out_shape=project_shapes(rows.shape[0] // 2, count, sends),
        in_specs=[VMEM, VMEM],
        out_specs=(VMEM,) * (1 + sends),
        compiler_params=LIMIT,
        cost_estimate=pl.CostEstimate(
            flops=2 * rows.shape[0] * rows.shape[1] * count, bytes_accessed=0, transcendentals=0
        ),
        name="project",
    )(rows, weight)


def add_kernel(mine, theirs, *outs):
    at = 0
    for out in outs:
        columns = slice(at, at + out.shape[1])
        at += out.shape[1]
        out[...] = (mine[:, columns] + theirs[:, columns].astype(jnp.float32)).astype(out.dtype)


def add_up(mine, theirs, widths):
    return pl.pallas_call(
        add_kernel,
        out_shape=[jax.ShapeDtypeStruct((mine.shape[0], width), theirs.dtype) for width in widths],
        in_specs=[VMEM, VMEM],
        out_specs=[VMEM] * len(widths),
        compiler_params=LIMIT,
        cost_estimate=pl.CostEstimate(flops=theirs.size, bytes_accessed=0, transcendentals=0),
        name="add_up",
    )(mine, theirs)


def combine_kernel(cuts, counts, mine, *refs):
    across, refs = refs[: sum(counts)], refs[sum(counts) :]
    beside, (out, *totals, sems) = refs[: len(refs) - len(cuts) - 2], refs[len(refs) - len(cuts) - 2 :]
    copies = []
    for i, (at, total) in enumerate(zip(cuts, totals)):
        options = across[sum(counts[:i]) : sum(counts[: i + 1])]
        width = options[0].shape[1]
        left = 0
        for part in beside:
            low, high = max(left, at), min(left + part.shape[1], at + width)
            if low < high:
                piece = mine[:, low:high] + part[:, low - left : high - left].astype(jnp.float32)
                there = options[0][:, low - at : high - at].astype(jnp.float32)
                if len(options) == 2:
                    position = lax.axis_index("ctx")
                    late = functools.reduce(jnp.logical_or, [position == i for i in LATE])
                    relayed = options[1][:, low - at : high - at].astype(jnp.float32)
                    there = jnp.where(late, relayed, there)
                total[:, low - at : high - at] = (piece + there).astype(total.dtype)
            left += part.shape[1]
        copies.append(pltpu.make_async_copy(total, out.at[:, at : at + width], sems.at[i]))
        copies[-1].start()
    for copy in copies:
        copy.wait()


def combine(mine, beside, across, cuts, out=None):
    outs = [] if out is None else [out]
    across = [x if isinstance(x, tuple) else (x,) for x in across]
    arrays = [x for options in across for x in options]
    counts = [len(options) for options in across]
    inputs = 1 + len(arrays) + len(beside)

    def kernel(*refs):
        combine_kernel(cuts, counts, *refs[:inputs], *refs[inputs + len(outs) :])

    return pl.pallas_call(
        kernel,
        out_shape=jax.ShapeDtypeStruct(mine.shape, jnp.bfloat16),
        in_specs=[VMEM] * inputs + [HBM] * len(outs),
        out_specs=HBM,
        scratch_shapes=[pltpu.VMEM(options[0].shape, jnp.bfloat16) for options in across]
        + [pltpu.SemaphoreType.DMA((len(cuts),))],
        input_output_aliases={inputs: 0} if outs else {},
        compiler_params=LIMIT,
        name="combine",
    )(mine, *arrays, *beside, *outs)


def from_behind(block, axis, distance):
    devices = range(lax.axis_size(axis))
    route = [(i - distance, i) for i in devices if i - distance in devices]
    return lax.ppermute(block, axis, route)


def token_docs(doc_ids, start, count):
    blocks = (start + jnp.arange(count, dtype=jnp.int32)) // BLOCK
    table = blocks[:, None] == jnp.arange(doc_ids.shape[0], dtype=jnp.int32)[None, :]
    return jnp.sum(jnp.where(table, doc_ids[None, :], 0), axis=1)


def attend(carry, queries, q_docs, q_start, k_piece, v_piece, k_docs, k_start):
    peak, totals, accum = carry
    n_query = queries.shape[0]
    n_key = k_piece.shape[0]
    kv_heads = k_piece.shape[1] // HEAD_SIZE
    query_group = queries.shape[1] // k_piece.shape[1]
    q_heads = queries.reshape(n_query, kv_heads, query_group, HEAD_SIZE)
    k_heads = k_piece.reshape(n_key, kv_heads, HEAD_SIZE)
    v_heads = v_piece.reshape(n_key, kv_heads, HEAD_SIZE)
    scores = (
        jnp.einsum("qkgd,skd->kgqs", q_heads, k_heads, preferred_element_type=jnp.float32) * SCALE
    )
    q_pos = q_start + jnp.arange(n_query, dtype=jnp.int32)
    k_pos = k_start + jnp.arange(n_key, dtype=jnp.int32)
    allowed = (q_docs[:, None] == k_docs[None, :]) & (q_pos[:, None] >= k_pos[None, :])
    scores = jnp.where(allowed, scores, NEG)
    new_peak = jnp.maximum(peak, jnp.max(scores, axis=-1))
    shrink = jnp.exp(peak - new_peak)
    weights = jnp.exp(scores - new_peak[..., None])
    totals = totals * shrink + jnp.sum(weights, axis=-1)
    rounded = weights.astype(jnp.bfloat16)
    added = jnp.einsum("kgqs,skd->kgqd", rounded, v_heads, preferred_element_type=jnp.float32)
    accum = accum * shrink[..., None] + added
    return (new_peak, totals, accum)


def absorb_block(carry, queries, q_docs, q_start, k_piece, v_piece, k_start, doc_ids, flag):
    n_key = k_piece.shape[0]
    k_docs = token_docs(doc_ids, k_start, n_key)
    fresh = attend(carry, queries, q_docs, q_start, k_piece, v_piece, k_docs, k_start)
    return jax.tree.map(lambda new, old: jnp.where(flag, new, old), fresh, carry)


def ring_attention(queries, keys, values, doc_ids, n_ctx, position):
    n_query = queries.shape[0]
    q_start = position * n_query
    q_docs = token_docs(doc_ids, q_start, n_query)
    kv_heads = keys.shape[1] // HEAD_SIZE
    query_group = queries.shape[1] // keys.shape[1]
    carry = (
        jnp.full((kv_heads, query_group, n_query), NEG, jnp.float32),
        jnp.zeros((kv_heads, query_group, n_query), jnp.float32),
        jnp.zeros((kv_heads, query_group, n_query, HEAD_SIZE), jnp.float32),
    )
    always = jnp.array(True)
    carry = absorb_block(carry, queries, q_docs, q_start, keys, values, q_start, doc_ids, always)

    def turn_one(step, state):
        inner_state, moving = state
        moving = from_behind(moving, "ctx", 1)
        start = ((position - step) % n_ctx) * n_query
        inner_state = absorb_block(
            inner_state, queries, q_docs, q_start, moving[0], moving[1], start, doc_ids, always
        )
        return (inner_state, moving)

    _, totals, accum = lax.fori_loop(1, n_ctx, turn_one, (carry, jnp.stack((keys, values))))[0]
    result = accum / totals[..., None]
    return jnp.transpose(result, (2, 0, 1, 3)).reshape(queries.shape).astype(jnp.bfloat16)


def part_rows(attended, place):
    share = attended.shape[0] // 4
    rows = [lax.dynamic_slice_in_dim(attended, (place ^ flip) * share, share, 0) for flip in (2, 3, 0, 1)]
    return jnp.concatenate(rows[:2], axis=0), jnp.concatenate(rows[2:], axis=0)


def per_device(queries, keys, values, doc_ids, out_weight):
    n_ctx = lax.axis_size("ctx")
    heads = lax.axis_size("head")
    position = lax.axis_index("ctx")
    place = lax.axis_index("head")
    other_core = [(i, i ^ 1) for i in range(heads)]
    other_chip = [(i, i ^ 2) for i in range(heads)]
    columns = out_weight.shape[1]
    relay = columns // 8 // BLOCK * BLOCK
    early_columns = columns * 3 // 7 // BLOCK * BLOCK - BLOCK
    cuts = [0, early_columns - relay, early_columns]

    if n_ctx == 8:
        by_two = [move(x, BY_TWO) for x in (keys, values)]
        beside = [move(x, BESIDE) for x in (keys, values)]
        split = columns // 3 // BLOCK * BLOCK
        *state, fetched, open_beside, part = attend_first(
            doc_ids, queries, keys, values, out_weight, split
        )
        by_four = [move(after(x, state[0]), AGAIN) for x in by_two]
        swap_two = [
            move(after(after(by_two[0], beside[0]), state[0]), ACROSS),
            move(after(by_two[1], beside[1]), ACROSS),
        ]
        swap_four = [move(after(swap_two[0], by_four[0]), AGAIN), move(by_four[1], LAST)]
        chunks = [beside, by_two, by_four]
        *state, weight = attend_next(
            fetched, open_beside, out_weight, part, split, state, chunks, (1, 2, 3)
        )
        state = attend_middle(fetched, state, [swap_two], (4,))
        chunks = [swap_four]
        far, near, mine, send = attend_last(fetched, weight, state, chunks, (5,), (0, cuts[1]))
    else:
        weight = out_weight
        attended = ring_attention(queries, keys, values, doc_ids, n_ctx, position)
        far, near = part_rows(attended, place)
        mine, send = project(far, weight, (0, cuts[1]))
    theirs = hop(send, "head", other_core)
    later_mine, later_send = project(far, weight, (cuts[1], columns))
    (first_sum,) = add_up(mine, theirs, [cuts[1]])
    first_part = hop(first_sum, "head", other_chip)
    later_theirs = hop(after(later_send, first_sum), "head", other_core)
    later_mine = after(later_mine, first_sum)
    relay_sum, later_sum = add_up(later_mine, later_theirs, [cuts[2] - cuts[1], columns - cuts[2]])
    later_part = hop(later_sum, "head", other_chip)
    mine, *sends = project(after(near, later_sum), weight, (0, columns), 2)
    theirs = [hop(send, "head", other_core) for send in sends]
    if n_ctx == 8:
        direct = move(relay_sum, (), [i for i in range(n_ctx) if i not in LATE])
        arrived = move(after(relay_sum, mine), RELAY)
        relay_part = (direct, move(move(after(arrived, first_part), (), [ring[1] for ring in RELAY]), RELAY))
    else:
        relay_part = hop(relay_sum, "head", other_chip)
    out = combine(mine, theirs, [first_part], [0])
    return combine(mine, theirs, [later_part, relay_part], [cuts[2], cuts[1]], out)


def solution(mesh):
    placed = (P("ctx", "head"), P("ctx", "head"), P("ctx", "head"), P(), P("head", None))
    return jax.shard_map(
        per_device, mesh=mesh, in_specs=placed, out_specs=P(("ctx", "head"), None), check_vma=False
    )
```
